32 devices in a mesh: narrow: 4 (over y, x), wide: 8 (over z, core).
Axes of the slice: x: 2, y: 2, z: 4, core: 2. Of those that a mesh axis runs over, the one named last changes fastest.
Arguments:
- tokens: bfloat16 [32768, 768], P(('narrow', 'wide')), may hold values from -6 to 6
- attention_gain: bfloat16 [768], P('wide'), may hold values from 0.5 to 1.5
- query_weight: bfloat16 [768, 768], P('wide'), may hold values from -0.0546875 to 0.0546875
- key_weight: bfloat16 [768, 768], P('wide'), may hold values from -0.21875 to 0.21875
- value_weight: bfloat16 [768, 768], P('wide'), may hold values from -0.21875 to 0.21875
- output_weight: bfloat16 [768, 768], P('wide'), may hold values from -0.875 to 0.875
- bias_table: bfloat16 [384], P('wide'), may hold values from -3 to 3
- forward_gain: bfloat16 [768], P('wide'), may hold values from 0.5 to 1.5
- inner_weight: bfloat16 [768, 3072], P('wide'), may hold values from -0.21875 to 0.21875
- outer_weight: bfloat16 [3072, 768], P('wide'), may hold values from -0.15625 to 0.15625
- project_weight: bfloat16 [768, 768], P('wide'), may hold values from -0.21875 to 0.21875
- lengths: int32 [32, 8], P(('narrow', 'wide')), may hold values from 1 to 256, 1024 in all within a row
- positives: int32 [256], replicated, may hold values from 0 to 255, as said below
Outputs:
- hidden: bfloat16 [32768, 768], P(('narrow', 'wide'))
- grad_tokens: float32 [32768, 768], P(('narrow', 'wide'))
- seg_loss: float32 [32, 8], P(('narrow', 'wide'))
- grad_attention_gain: float32 [768], P('wide')
- grad_query_weight: float32 [768, 768], P('wide')
- grad_key_weight: float32 [768, 768], P('wide')
- grad_value_weight: float32 [768, 768], P('wide')
- grad_output_weight: float32 [768, 768], P('wide')
- grad_bias_table: float32 [384], P('wide')
- grad_forward_gain: float32 [768], P('wide')
- grad_inner_weight: float32 [768, 3072], P('wide')
- grad_outer_weight: float32 [3072, 768], P('wide')
- grad_project_weight: float32 [768, 768], P('wide')
The draws below stay inside these ranges and needn't reach their ends.
Inputs may be any that keep to these rules, and one draw needn't show every extreme that they name: Each row's 8 lengths sum to 1024. `positives`: A permutation of the 256 passages with no passage its own positive.
All inputs are finite; a program needn't handle non-finite values.
Results may differ from the reference program's by a relative error of at most 0.015.
Values may be sent and summed in bfloat16 or wider, within the bound.
No kernel may reach another device: no remote copies, remote signals or barrier semaphores. Data moves between devices by JAX's collectives and lax.ppermute only.
A program may use at most 256 MiB of HBM per device.

```python
import math
import jax
import jax.numpy as jnp
import numpy as np
from jax import lax

D = 768
HEADS = 12
HEAD_DIM = 64
FF = 3072
EMB = 768
BUCKETS = 32
ROW_LEN = 1024
SEGS = 8
MOST_LEN = 256
ROWS = 32
SEG_ALL = 256


def draw_positives(key, part):
    key = jax.random.fold_in(key, 7)
    order = jax.random.permutation(key, SEG_ALL).astype(jnp.int32)
    following = jnp.roll(order, -1)
    return jnp.zeros((SEG_ALL,), jnp.int32).at[order].set(following)


def block_scale(key, dims, shards, smallest, largest):
    def one(axis_at, blocks):
        heights = jax.random.uniform(jax.random.fold_in(jax.random.fold_in(key, 6), axis_at), (blocks,), jnp.float32, smallest / len(shards), largest / len(shards))
        return jnp.repeat(jnp.exp(heights), dims[axis_at] // blocks).reshape((-1,) + (1,) * (len(dims) - axis_at - 1))

    factor_of = one(*shards[0])
    for cut in shards[1:]:
        factor_of = factor_of * one(*cut)
    return factor_of


def length_profile(number_of, total, limit, lean):
    weights = [(1 << 20) // math.isqrt(standing ** lean) + 1 for standing in range(2, number_of + 1)]
    rest, given = total - limit - (number_of - 1), [1] * (number_of - 1)
    while rest > 0:
        candidates = [i for i in range(number_of - 1) if given[i] < limit]
        pool, left = sum([weights[i] for i in candidates]), rest
        for i in candidates:
            addition = min(limit - given[i], max(1, left * weights[i] // pool), rest)
            given[i] = given[i] + addition
            rest = rest - addition
    return np.array([limit] + given)


def ragged(rng, count, total, limit, slope):
    if count == 2:
        one = jax.random.randint(rng, (), max(1, total - limit), min(limit, total - 1) + 1)
        return jnp.stack([one, total - one])
    tallies = jnp.asarray(length_profile(count, total, limit, slope), jnp.int32)
    twos = (count - 1) // 2
    donor, receiver = tallies[1:1 + 2 * twos:2], tallies[2:2 + 2 * twos:2]
    slack = jnp.minimum(donor - 1, limit - receiver)
    shifted = jax.random.randint(jax.random.fold_in(rng, 1), (twos,), 0, 1 << 20) % (slack + 1)
    tallies = tallies.at[1:1 + 2 * twos:2].set(donor - shifted).at[2:2 + 2 * twos:2].set(receiver + shifted)
    return tallies[jax.random.permutation(jax.random.fold_in(rng, 2), count)]


def centred(rng, dims, scale, most, shards=(), held_as=jnp.bfloat16):
    loudness = block_scale(rng, dims, shards, -0.22, 0.18) if shards else 1.0
    result = jax.random.normal(rng, dims, jnp.float32) * scale * loudness
    return jnp.minimum(jnp.maximum(result, -most), most).astype(held_as)


def setup_inputs(seed: int = 0) -> dict:
    key_list = jax.random.split(jax.random.key(seed), 14)
    return {
        "tokens": centred(key_list[0], (ROWS * ROW_LEN, D), 1.0, 6.0, ((0, 32),)),
        "attention_gain": jnp.clip(1.0 + 0.1 * jax.random.normal(key_list[1], (D,), jnp.float32), 0.5, 1.5).astype(jnp.bfloat16),
        "query_weight": centred(key_list[2], (D, D), (D * HEAD_DIM // 4) ** -0.5, 0.0546875, ((0, 8),)),
        "key_weight": centred(key_list[3], (D, D), D ** -0.5, 0.21875, ((0, 8),)),
        "value_weight": centred(key_list[4], (D, D), D ** -0.5, 0.21875, ((0, 8),)),
        "output_weight": centred(key_list[5], (D, D), (D // 16) ** -0.5, 0.875, ((0, 8),)),
        "bias_table": centred(key_list[6], (BUCKETS * HEADS,), 0.5, 3.0, ((0, 8),)),
        "forward_gain": jnp.clip(1.0 + 0.1 * jax.random.normal(key_list[7], (D,), jnp.float32), 0.5, 1.5).astype(jnp.bfloat16),
        "inner_weight": centred(key_list[8], (D, FF), D ** -0.5, 0.21875, ((0, 8),)),
        "outer_weight": centred(key_list[9], (FF, D), (FF // 2) ** -0.5, 0.15625, ((0, 8),)),
        "project_weight": centred(key_list[10], (D, EMB), D ** -0.5, 0.21875, ((0, 8),)),
        "lengths": jax.vmap(lambda own: ragged(own, SEGS, ROW_LEN, MOST_LEN, 2))(jax.random.split(key_list[11], ROWS)).reshape((ROWS, SEGS)).astype(jnp.int32),
        "positives": draw_positives(jax.random.fold_in(key_list[13], 71), 0),
    }


@jax.custom_vjp
def low(v):
    return lax.optimization_barrier(v.astype(jnp.bfloat16)).astype(jnp.float32)

@jax.custom_vjp
def low_back(v):
    return v

def low_keep(v):
    return (low(v), None)

def low_pass(kept, grad):
    return (grad,)

def back_keep(v):
    return (v, None)

def back_low(kept, grad):
    return (low(grad),)
low.defvjp(low_keep, low_pass)
low_back.defvjp(back_keep, back_low)
precise = lax.Precision.HIGHEST
epsilon = 1e-06
logit_scale = 50.0

def bucket_of(offset):
    distance = jnp.abs(offset)
    larger = 8 + sum(((distance * distance >= 64 * 2 ** step).astype(jnp.int32) for step in range(1, 8)))
    return jnp.where(distance < 8, distance, larger) + jnp.where(offset > 0, 16, 0)

def segment_ids(len_row, row_len):
    bounds = jnp.cumsum(len_row).astype(jnp.int32)
    places = jnp.arange(row_len, dtype=jnp.int32)
    return lax.optimization_barrier(jnp.sum((places[:, None] >= bounds[None, :]).astype(jnp.int32), 1))

def rms_scale(values):
    return lax.rsqrt(lax.optimization_barrier(jnp.mean(values * values, -1, keepdims=True)) + epsilon)

def row_forward(weights, x_row, len_row):
    attention_gain, query_weight, key_weight, value_weight, output_weight, bias_table, forward_gain, inner_weight, outer_weight, project_weight = weights
    hidden_one = low(x_row * rms_scale(x_row) * attention_gain)
    query_rows = low(low_back(jnp.dot(hidden_one, query_weight, precision=precise))).reshape(ROW_LEN, HEADS, HEAD_DIM)
    key_rows = low(low_back(jnp.dot(hidden_one, key_weight, precision=precise))).reshape(ROW_LEN, HEADS, HEAD_DIM)
    value_rows = low(low_back(jnp.dot(hidden_one, value_weight, precision=precise))).reshape(ROW_LEN, HEADS, HEAD_DIM)
    segments = segment_ids(len_row, ROW_LEN)
    places = jnp.arange(ROW_LEN, dtype=jnp.int32)
    kinds = bucket_of(places[None, :] - places[:, None])
    bias = jnp.transpose(jnp.take(bias_table.reshape(BUCKETS, HEADS), kinds, axis=0), (2, 0, 1))
    scores = low_back(jnp.einsum('qhd,khd->hqk', query_rows, key_rows, precision=precise) + bias)
    scores = jnp.where((segments[:, None] == segments[None, :])[None], scores, -1000000000.0)
    highest = lax.optimization_barrier(jnp.max(scores, -1, keepdims=True))
    raised = jnp.exp(scores - highest)
    probs = raised / lax.optimization_barrier(jnp.sum(raised, -1, keepdims=True))
    mixed = jnp.einsum('hqk,khd->qhd', low(probs), value_rows, precision=precise).reshape(ROW_LEN, D)
    mixed = low(low_back(mixed))
    middle = x_row + low_back(jnp.dot(mixed, output_weight, precision=precise))
    hidden_two = low(middle * rms_scale(middle) * forward_gain)
    inner = low_back(jnp.dot(hidden_two, inner_weight, precision=precise))
    active = low(jax.nn.gelu(inner, approximate=False))
    output_rows = middle + low_back(jnp.dot(active, outer_weight, precision=precise))
    member = (segments[:, None] == jnp.arange(SEGS, dtype=jnp.int32)[None, :]).astype(jnp.float32)
    pooled = jnp.dot(member.T, output_rows, precision=precise) / len_row.astype(jnp.float32)[:, None]
    projected = jnp.dot(low(pooled), project_weight, precision=precise)
    embedded = low(projected * lax.rsqrt(lax.optimization_barrier(jnp.sum(projected * projected, -1, keepdims=True)) + epsilon))
    return (output_rows, embedded)

def contrastive(embedded, positives):
    count = embedded.shape[0]
    logits = low_back(logit_scale * jnp.dot(embedded, embedded.T, precision=precise))
    numbers = jnp.arange(count, dtype=jnp.int32)
    logits = jnp.where(numbers[:, None] == numbers[None, :], -1000000000.0, logits)
    highest = lax.optimization_barrier(jnp.max(logits, -1, keepdims=True))
    totals = highest[:, 0] + jnp.log(lax.optimization_barrier(jnp.sum(jnp.exp(logits - highest), -1)))
    target = lax.optimization_barrier(jnp.sum(jnp.where(numbers[None, :] == positives[:, None], logits, 0.0), -1))
    return (totals - target).reshape(ROWS, SEGS)

def reference(tokens, attention_gain, query_weight, key_weight, value_weight, output_weight, bias_table, forward_gain, inner_weight, outer_weight, project_weight, lengths, positives):
    weights = tuple((w.astype(jnp.float32) for w in (attention_gain, query_weight, key_weight, value_weight, output_weight, bias_table, forward_gain, inner_weight, outer_weight, project_weight)))
    inputs = tokens.astype(jnp.float32)

    def whole(weights, inputs):

        def one_row(pair):
            return row_forward(weights, pair[0], pair[1])
        outputs, embeds = lax.map(jax.checkpoint(one_row), (inputs.reshape(ROWS, ROW_LEN, D), lengths))
        losses = contrastive(embeds.reshape(SEG_ALL, EMB), positives)
        return (outputs.reshape(ROWS * ROW_LEN, D), losses)
    (outputs, losses), pull = jax.vjp(whole, weights, inputs)
    grads, grad_inputs = pull((jnp.zeros_like(outputs), jnp.ones_like(losses)))
    return (outputs.astype(jnp.bfloat16), grad_inputs, losses, grads[0], grads[1], grads[2], grads[3], grads[4], grads[5], grads[6], grads[7], grads[8], grads[9])
```

```python
import functools

import jax
import jax.numpy as jnp
from jax import lax
from jax.experimental import pallas as pl
from jax.experimental.pallas import tpu as pltpu
from jax.sharding import PartitionSpec as P

HEADS = 12
HEAD_DIM = 64
BUCKETS = 32
SPAN = 256
BLOCK = 128
WINDOW = BLOCK + 2 * SPAN
CHUNK = 512

epsilon = 1e-06
logit_scale = 50.0
root_half = 0.7071067811865476
inv_root_tau = 0.3989422804014327
MIB = 1 << 20
F32 = jnp.float32
BF16 = jnp.bfloat16


def dot_nn(left, right):
    return lax.dot_general(left, right, (((1,), (0,)), ((), ())), preferred_element_type=F32)


def dot_nt(left, right):
    return lax.dot_general(left, right, (((1,), (1,)), ((), ())), preferred_element_type=F32)


def dot_tn(left, right):
    return lax.dot_general(left, right, (((0,), (0,)), ((), ())), preferred_element_type=F32)


def split(values):
    high = values.astype(BF16)
    rest = values - high.astype(F32)
    middle = rest.astype(BF16)
    return high, middle, (rest - middle.astype(F32)).astype(BF16)


def split_two(values):
    high = values.astype(BF16)
    return high, (values - high.astype(F32)).astype(BF16)


def bucket_of(offset):
    distance = jnp.abs(offset)
    larger = jnp.full_like(distance, 8)
    for step in range(1, 8):
        larger = larger + (distance * distance >= 64 * 2**step).astype(jnp.int32)
    return jnp.where(distance < 8, distance, larger) + jnp.where(offset > 0, 16, 0)


def bounds_of(lengths_ref, count):
    bounds = []
    total = 0
    for index in range(count):
        total = total + lengths_ref[0, index]
        bounds.append(total)
    return bounds


def segment_of(places, bounds):
    segment = jnp.zeros_like(places)
    for bound in bounds:
        segment = segment + (places >= bound).astype(jnp.int32)
    return segment


def window_of(bounds, start):
    low = 0
    high = bounds[-1]
    for bound in bounds[:-1]:
        low = jnp.where(bound <= start, bound, low)
    for bound in reversed(bounds[:-1]):
        high = jnp.where(bound > start + BLOCK - 1, bound, high)
    first = (low // BLOCK) * BLOCK
    blocks = (high - first + BLOCK - 1) // BLOCK
    return first, blocks


def params(mib, grid=1):
    return pltpu.CompilerParams(
        vmem_limit_bytes=mib * MIB, dimension_semantics=("arbitrary",) * grid
    )


def whole(shape):
    return pl.BlockSpec(shape, lambda *_: (0,) * len(shape), pipeline_mode=pl.Buffered(1))


smem = pl.BlockSpec(memory_space=pltpu.SMEM)


def project_kernel(x_ref, gain_ref, wq_ref, wk_ref, wv_ref, hid_ref, q_ref, k_ref, v_ref):
    x = x_ref[...].astype(F32)
    scale = lax.rsqrt(jnp.mean(x * x, -1, keepdims=True) + epsilon)
    hidden = (x * scale * gain_ref[...].astype(F32)).astype(BF16)
    hid_ref[...] = hidden
    q_ref[...] = dot_nn(hidden, wq_ref[...]).astype(BF16)
    k_ref[...] = dot_nn(hidden, wk_ref[...]).astype(BF16)
    v_ref[...] = dot_nn(hidden, wv_ref[...]).astype(BF16)


def project(x, gain, wq, wk, wv):
    rows, width = x.shape
    block = rows // 4
    row_spec = pl.BlockSpec((block, width), lambda i: (i, 0))
    out = jax.ShapeDtypeStruct((rows, width), BF16)
    return pl.pallas_call(
        project_kernel,
        grid=(4,),
        in_specs=[row_spec, whole((1, width))] + [whole((width, width))] * 3,
        out_specs=[row_spec] * 4,
        out_shape=[out] * 4,
        compiler_params=params(48),
        cost_estimate=pl.CostEstimate(
            flops=6 * rows * width * width, bytes_accessed=10 * rows * width + 6 * width * width, transcendentals=0
        ),
        name="project_heads",
    )(x, gain, wq, wk, wv)


def attend_kernel(
    lengths_ref, table_ref, q_ref, k_ref, v_ref, mixed_ref, inv_ref, p_ref, rows_ref, tile_ref, segc_ref, segr_ref
):
    pair = pl.program_id(0)
    rows = q_ref.shape[0]
    bounds = bounds_of(lengths_ref, lengths_ref.shape[1])
    reach = WINDOW + BLOCK

    @pl.when(pair == 0)
    def _():
        segc_ref[...] = segment_of(lax.broadcasted_iota(jnp.int32, segc_ref.shape, 0), bounds)
        segr_ref[...] = segment_of(lax.broadcasted_iota(jnp.int32, segr_ref.shape, 1), bounds)
        offsets = lax.broadcasted_iota(jnp.int32, (BUCKETS, reach), 1) - (SPAN + BLOCK)
        kinds = lax.broadcasted_iota(jnp.int32, (BUCKETS, reach), 0)
        onehot = (bucket_of(offsets) == kinds).astype(F32).astype(BF16)
        rows_ref[...] = dot_tn(table_ref[...], onehot)

    for half in range(2):
        line = rows_ref[pl.ds(2 * pair + half, 1), :]
        skew = pltpu.roll(jnp.broadcast_to(line, (BLOCK, reach)), 0, 1, stride=1, stride_axis=0)
        tile_ref[half] = skew[:, BLOCK:]

    lane = lax.broadcasted_iota(jnp.int32, (BLOCK, BLOCK), 1)
    first_half = lane < HEAD_DIM

    def one(block_index, carry):
        start = pl.multiple_of(block_index * BLOCK, BLOCK)
        first, count = window_of(bounds, start)
        first = pl.multiple_of(first, BLOCK)
        shift = pl.multiple_of(first - start + SPAN, BLOCK)

        def body(blocks):
            size = blocks * BLOCK
            q = q_ref[pl.ds(start, BLOCK), :]
            k = k_ref[pl.ds(first, size), :]
            v = v_ref[pl.ds(first, size), :]
            segc = segc_ref[pl.ds(start, BLOCK), :]
            segr = segr_ref[0:1, pl.ds(first, size)]
            same = jnp.concatenate([segc] * blocks, 1) == segr
            wide_lane = lax.broadcasted_iota(jnp.int32, (size, BLOCK), 1) < HEAD_DIM
            results = []
            for half in range(2):
                mine = first_half if half == 0 else ~first_half
                scores = dot_nt(jnp.where(mine, q, jnp.zeros_like(q)), k)
                scores = scores + tile_ref[half, :, pl.ds(shift, size)]
                scores = jnp.where(same, scores, -1000000000.0)
                raised = jnp.exp(scores - jnp.max(scores, -1, keepdims=True)).astype(BF16)
                p_ref[half, pl.ds(start, BLOCK), 0:size] = raised
                keep = wide_lane if half == 0 else ~wide_lane
                results.append(dot_nn(raised, jnp.where(keep, v, jnp.ones_like(v))))
            top = jnp.where(first_half, results[0], results[1])
            total = pltpu.roll(jnp.where(first_half, results[1], results[0]), HEAD_DIM, 1)
            inverse = 1.0 / total
            mixed_ref[pl.ds(start, BLOCK), :] = (top * inverse).astype(BF16)
            inv_ref[pl.ds(start, BLOCK), :] = inverse

        for blocks in range(1, WINDOW // BLOCK + 1):
            pl.when(count == blocks)(functools.partial(body, blocks))
        return carry

    lax.fori_loop(0, rows // BLOCK, one, 0)


def attend(lengths, table, q, k, v):
    rows, width = q.shape
    pairs = HEADS // 2
    column = pl.BlockSpec((rows, BLOCK), lambda p: (0, p))
    return pl.pallas_call(
        attend_kernel,
        grid=(pairs,),
        in_specs=[smem, whole(table.shape), column, column, column],
        out_specs=[column, column, pl.BlockSpec((2, rows, WINDOW), lambda p: (p, 0, 0))],
        out_shape=[
            jax.ShapeDtypeStruct((rows, width), BF16),
            jax.ShapeDtypeStruct((rows, width), F32),
            jax.ShapeDtypeStruct((HEADS, rows, WINDOW), BF16),
        ],
        scratch_shapes=[
            pltpu.VMEM((16, WINDOW + BLOCK), F32),
            pltpu.VMEM((2, BLOCK, WINDOW), F32),
            pltpu.VMEM((rows, BLOCK), jnp.int32),
            pltpu.VMEM((8, rows), jnp.int32),
        ],
        compiler_params=params(48),
        cost_estimate=pl.CostEstimate(
            flops=12 * 4 * rows * 512 * 128, bytes_accessed=40 * MIB, transcendentals=12 * rows * 512
        ),
        name="attend",
    )(lengths, table, q, k, v)


def output_kernel(x_ref, mixed_ref, wo_ref, gain_ref, mid_ref, hid_ref):
    middle = x_ref[...].astype(F32) + dot_nn(mixed_ref[...], wo_ref[...])
    scale = lax.rsqrt(jnp.mean(middle * middle, -1, keepdims=True) + epsilon)
    mid_ref[...] = middle
    hid_ref[...] = (middle * scale * gain_ref[...].astype(F32)).astype(BF16)


def output(x, mixed, wo, gain):
    rows, width = x.shape
    block = rows // 4
    row_spec = pl.BlockSpec((block, width), lambda i: (i, 0))
    return pl.pallas_call(
        output_kernel,
        grid=(4,),
        in_specs=[row_spec, row_spec, whole((width, width)), whole((1, width))],
        out_specs=[row_spec] * 2,
        out_shape=[jax.ShapeDtypeStruct((rows, width), F32), jax.ShapeDtypeStruct((rows, width), BF16)],
        compiler_params=params(48),
        cost_estimate=pl.CostEstimate(
            flops=2 * rows * width * width, bytes_accessed=10 * rows * width + 2 * width * width, transcendentals=0
        ),
        name="output_and_norm",
    )(x, mixed, wo, gain)


def gelu_and_slope(v):
    bell = jnp.exp(-0.5 * v * v)
    t = 1.0 / (1.0 + (0.3275911 * root_half) * jnp.abs(v))
    series = t * (
        0.5 * 0.254829592
        + t * (0.5 * -0.284496736 + t * (0.5 * 1.421413741 + t * (0.5 * -1.453152027 + t * (0.5 * 1.061405429))))
    )
    tail = series * bell
    share = jnp.where(v >= 0.0, 1.0 - tail, tail)
    return v * share, share + v * bell * inv_root_tau


def member_of(lengths_ref, rows, count):
    bounds = bounds_of(lengths_ref, lengths_ref.shape[1])
    segment = segment_of(lax.broadcasted_iota(jnp.int32, (rows, count), 0), bounds)
    return (segment == lax.broadcasted_iota(jnp.int32, (rows, count), 1)).astype(F32).astype(BF16)


def member_rows(lengths_ref, rows, count):
    bounds = bounds_of(lengths_ref, lengths_ref.shape[1])
    segment = segment_of(lax.broadcasted_iota(jnp.int32, (count, rows), 1), bounds)
    return (segment == lax.broadcasted_iota(jnp.int32, (count, rows), 0)).astype(F32).astype(BF16)


def forward_kernel(
    lengths_ref, hid_ref, mid_ref, wi_ref, wo_ref, out_ref, slope_ref, active_sum_ref, pooled_ref, total_ref, member_ref
):
    step = pl.program_id(0)
    rows = hid_ref.shape[0]

    @pl.when(step == 0)
    def _():
        member_ref[...] = member_rows(lengths_ref, rows, 16)
        total_ref[...] = mid_ref[...]

    block = rows // 4
    for index in range(4):
        span = slice(index * block, (index + 1) * block)
        active, slope = gelu_and_slope(dot_nn(hid_ref[span, :], wi_ref[...]))
        active = active.astype(BF16)
        slope_ref[span, :] = slope.astype(BF16)
        total_ref[span, :] += dot_nn(active, wo_ref[...])
        part = dot_nn(member_ref[:, span], active)
        if index == 0:
            active_sum_ref[...] = part
        else:
            active_sum_ref[...] += part

    @pl.when(step == pl.num_programs(0) - 1)
    def _():
        total = total_ref[...]
        out_ref[...] = total.astype(BF16)
        member = member_ref[...]
        high, middle, low = split(total)
        pooled_ref[...] = dot_nn(member, high) + dot_nn(member, middle) + dot_nn(member, low)


def forward(lengths, hidden, middle, wi, wo):
    rows, width = hidden.shape
    units = wi.shape[1]
    full = whole((rows, width))
    return pl.pallas_call(
        forward_kernel,
        grid=(units // CHUNK,),
        in_specs=[
            smem,
            full,
            full,
            pl.BlockSpec((width, CHUNK), lambda i: (0, i)),
            pl.BlockSpec((CHUNK, width), lambda i: (i, 0)),
        ],
        out_specs=[
            pl.BlockSpec((rows, width), lambda i: (0, 0)),
            pl.BlockSpec((rows, CHUNK), lambda i: (0, i)),
            pl.BlockSpec((16, CHUNK), lambda i: (0, i)),
            pl.BlockSpec((16, width), lambda i: (0, 0)),
        ],
        out_shape=[
            jax.ShapeDtypeStruct((rows, width), BF16),
            jax.ShapeDtypeStruct((rows, units), BF16),
            jax.ShapeDtypeStruct((16, units), F32),
            jax.ShapeDtypeStruct((16, width), F32),
        ],
        scratch_shapes=[pltpu.VMEM((rows, width), F32), pltpu.VMEM((16, rows), BF16)],
        compiler_params=params(56),
        cost_estimate=pl.CostEstimate(
            flops=4 * rows * width * units, bytes_accessed=30 * MIB, transcendentals=2 * rows * units
        ),
        name="feed_forward",
    )(lengths, hidden, middle, wi, wo)


def contrast_kernel(
    place_ref, pooled_ref, len_ref, target_ref, wp_ref, loss_ref, grad_wp_ref, glow_all_ref, grows_ref, wide_ref, line_ref, full_ref
):
    count = pooled_ref.shape[0]
    first = pl.multiple_of(place_ref[0] * 8, 8)
    pooled = pooled_ref[...]
    projected = dot_nn(pooled, wp_ref[...])
    inverse = lax.rsqrt(jnp.sum(projected * projected, -1, keepdims=True) + epsilon)
    embedded = (projected * inverse).astype(BF16)
    row = lax.broadcasted_iota(jnp.int32, (count, count), 0)
    column = lax.broadcasted_iota(jnp.int32, (count, count), 1)
    logits = logit_scale * dot_nt(embedded, embedded)
    logits = jnp.where(row == column, -1000000000.0, logits)
    hit = column == target_ref[...]
    highest = jnp.max(logits, -1, keepdims=True)
    totals = highest + jnp.log(jnp.sum(jnp.exp(logits - highest), -1, keepdims=True))
    target = jnp.sum(jnp.where(hit, logits, 0.0), -1, keepdims=True)
    line_ref[...] = jnp.broadcast_to(totals - target, line_ref.shape)
    loss_ref[...] = line_ref[pl.ds(first, 8), :]
    grad_logits = (jnp.exp(logits - totals) - hit.astype(F32)).astype(BF16)
    grad_embedded = logit_scale * (dot_nn(grad_logits, embedded) + dot_tn(grad_logits, embedded))
    along = jnp.sum(grad_embedded * projected, -1, keepdims=True)
    grad_projected = inverse * grad_embedded - projected * (inverse * inverse * inverse * along)
    high, middle, low = split(grad_projected)
    full_ref[...] = dot_tn(pooled, high) + dot_tn(pooled, middle) + dot_tn(pooled, low)
    share = grad_wp_ref.shape[0]
    grad_wp_ref[...] = full_ref[pl.ds(pl.multiple_of(place_ref[1] * share, share), share), :]
    wp = wp_ref[...]
    grad_rows = (dot_nt(high, wp) + dot_nt(middle, wp) + dot_nt(low, wp)) / len_ref[...]
    glow_all_ref[...] = grad_rows.astype(BF16)
    wide_ref[...] = grad_rows
    grows_ref[...] = wide_ref[pl.ds(first, 8), :]


def contrast(place, pooled, lens, targets, wp, share):
    count, width = pooled.shape
    if count > 512 or share % 8:
        return contrast_plain(place, pooled, lens, targets, wp, share)
    return pl.pallas_call(
        contrast_kernel,
        in_specs=[smem] + [pl.BlockSpec(memory_space=pltpu.VMEM)] * 4,
        out_specs=[pl.BlockSpec(memory_space=pltpu.VMEM)] * 4,
        out_shape=[
            jax.ShapeDtypeStruct((8, 128), F32),
            jax.ShapeDtypeStruct((share, width), F32),
            jax.ShapeDtypeStruct((count, width), BF16),
            jax.ShapeDtypeStruct((8, width), F32),
        ],
        scratch_shapes=[
            pltpu.VMEM((count, width), F32),
            pltpu.VMEM((count, 128), F32),
            pltpu.VMEM((width, width), F32),
        ],
        compiler_params=pltpu.CompilerParams(vmem_limit_bytes=48 * MIB),
        cost_estimate=pl.CostEstimate(flops=4 * count * width * width, bytes_accessed=8 * MIB, transcendentals=0),
        name="contrast",
    )(place, pooled, lens, targets, wp)


def contrast_plain(place, pooled, lens, targets, wp, share):
    count, width = pooled.shape
    exact = lax.Precision.HIGHEST
    projected = jnp.dot(pooled, wp, preferred_element_type=F32)
    inverse = lax.rsqrt(jnp.sum(projected * projected, -1, keepdims=True) + epsilon)
    embedded = (projected * inverse).astype(BF16)
    numbers = jnp.arange(count, dtype=jnp.int32)
    logits = logit_scale * dot_nt(embedded, embedded)
    logits = jnp.where(numbers[:, None] == numbers[None, :], -1000000000.0, logits)
    hit = numbers[None, :] == targets
    highest = jnp.max(logits, -1, keepdims=True)
    totals = highest + jnp.log(jnp.sum(jnp.exp(logits - highest), -1, keepdims=True))
    loss = totals - jnp.sum(jnp.where(hit, logits, 0.0), -1, keepdims=True)
    grad_logits = (jnp.exp(logits - totals) - hit.astype(F32)).astype(BF16)
    grad_embedded = logit_scale * (dot_nn(grad_logits, embedded) + dot_tn(grad_logits, embedded))
    along = jnp.sum(grad_embedded * projected, -1, keepdims=True)
    grad_projected = inverse * grad_embedded - projected * (inverse * inverse * inverse * along)
    own_columns = lax.dynamic_slice_in_dim(pooled.astype(F32), place[1] * share, share, 1)
    grad_wp = lax.dot_general(own_columns, grad_projected, (((0,), (0,)), ((), ())), precision=exact)
    grad_rows = jnp.dot(grad_projected, wp.astype(F32).T, precision=exact) / lens
    first = place[0] * 8
    own = lambda a: lax.dynamic_slice_in_dim(a, first, 8, 0)
    return jnp.broadcast_to(own(loss), (8, 128)), grad_wp, grad_rows.astype(BF16), own(grad_rows)


def inner_grad_kernel(lengths_ref, glow_ref, wo_ref, slope_ref, hid_ref, grad_ref, gi_ref, member_ref):
    @pl.when(pl.program_id(0) == 0)
    def _():
        member_ref[...] = member_of(lengths_ref, member_ref.shape[0], 16)

    grad_active = dot_nt(glow_ref[...], wo_ref[...])
    high, low = split_two(grad_active)
    member = member_ref[...]
    spread = dot_nn(member, high) + dot_nn(member, low)
    grad_inner = (spread * slope_ref[...].astype(F32)).astype(BF16)
    gi_ref[...] = grad_inner
    grad_ref[...] = dot_tn(hid_ref[...], grad_inner).astype(grad_ref.dtype)


def inner_grad(lengths, glow, wo, slope, hidden):
    rows, width = hidden.shape
    units = slope.shape[1]
    return pl.pallas_call(
        inner_grad_kernel,
        grid=(units // CHUNK,),
        in_specs=[
            smem,
            whole((16, width)),
            pl.BlockSpec((CHUNK, width), lambda i: (i, 0)),
            pl.BlockSpec((rows, CHUNK), lambda i: (0, i)),
            whole((rows, width)),
        ],
        out_specs=[pl.BlockSpec((width, CHUNK), lambda i: (0, i)), pl.BlockSpec((rows, CHUNK), lambda i: (0, i))],
        out_shape=[jax.ShapeDtypeStruct((width, units), BF16), jax.ShapeDtypeStruct((rows, units), BF16)],
        scratch_shapes=[pltpu.VMEM((rows, 16), BF16)],
        compiler_params=params(48),
        cost_estimate=pl.CostEstimate(flops=2 * rows * width * units, bytes_accessed=24 * MIB, transcendentals=0),
        name="inner_grad",
    )(lengths, glow, wo, slope, hidden)


def middle_grad_kernel(
    lengths_ref, gi_ref, wi_ref, mid_ref, grows_ref, gain_ref, gmid_ref, glow_ref, ggain_ref, total_ref
):
    step = pl.program_id(0)
    rows, width = mid_ref.shape
    part = dot_nt(gi_ref[...], wi_ref[...])

    @pl.when(step == 0)
    def _():
        total_ref[...] = part

    @pl.when(step > 0)
    def _():
        total_ref[...] += part

    @pl.when(step == pl.num_programs(0) - 1)
    def _():
        bounds = bounds_of(lengths_ref, lengths_ref.shape[1])
        block = rows // 4
        gain_sum = jnp.zeros((1, width), F32)
        for index in range(4):
            span = slice(index * block, (index + 1) * block)
            middle = mid_ref[span, :]
            scale = lax.rsqrt(jnp.mean(middle * middle, -1, keepdims=True) + epsilon)
            normed = middle * scale
            grad_hidden = total_ref[span, :]
            product = grad_hidden * normed
            gain_sum = gain_sum + jnp.sum(product, 0, keepdims=True)
            scaled = grad_hidden * gain_ref[...].astype(F32)
            centre = jnp.mean(scaled * normed, -1, keepdims=True)
            segment = segment_of(lax.broadcasted_iota(jnp.int32, (block, 128), 0) + index * block, bounds)
            segment = jnp.concatenate([segment] * (width // 128), 1)
            grad_rows = jnp.zeros((block, width), F32)
            for passage in range(8):
                grad_rows = jnp.where(segment == passage, grows_ref[passage : passage + 1, :], grad_rows)
            grad_middle = grad_rows + scale * (scaled - normed * centre)
            gmid_ref[span, :] = grad_middle
            glow_ref[span, :] = grad_middle.astype(BF16)
        ggain_ref[...] = jnp.broadcast_to(gain_sum, ggain_ref.shape)


def middle_grad(lengths, gi, wi, middle, grows, gain):
    rows, width = middle.shape
    units = wi.shape[1]
    return pl.pallas_call(
        middle_grad_kernel,
        grid=(units // CHUNK,),
        in_specs=[
            smem,
            pl.BlockSpec((rows, CHUNK), lambda i: (0, i)),
            pl.BlockSpec((width, CHUNK), lambda i: (0, i)),
            whole((rows, width)),
            whole((8, width)),
            whole((1, width)),
        ],
        out_specs=[
            pl.BlockSpec((rows, width), lambda i: (0, 0)),
            pl.BlockSpec((rows, width), lambda i: (0, 0)),
            pl.BlockSpec((8, width), lambda i: (0, 0)),
        ],
        out_shape=[
            jax.ShapeDtypeStruct((rows, width), F32),
            jax.ShapeDtypeStruct((rows, width), BF16),
            jax.ShapeDtypeStruct((8, width), F32),
        ],
        scratch_shapes=[pltpu.VMEM((rows, width), F32)],
        compiler_params=params(48),
        cost_estimate=pl.CostEstimate(flops=2 * rows * width * units, bytes_accessed=20 * MIB, transcendentals=0),
        name="middle_grad",
    )(lengths, gi, wi, middle, grows, gain)


def output_grad_kernel(glow_ref, mixed_ref, wo_ref, inv_ref, grad_ref, gmix_ref):
    glow = glow_ref[...]
    grad_ref[...] = dot_tn(mixed_ref[...], glow).astype(grad_ref.dtype)
    grad_mixed = dot_nt(glow, wo_ref[...])
    gmix_ref[...] = (grad_mixed * inv_ref[...]).astype(BF16)


def output_grad(glow, mixed, wo, inv):
    rows, width = glow.shape
    block = width // 3
    column = pl.BlockSpec((rows, block), lambda i: (0, i))
    row = pl.BlockSpec((block, width), lambda i: (i, 0))
    return pl.pallas_call(
        output_grad_kernel,
        grid=(3,),
        in_specs=[whole((rows, width)), column, row, column],
        out_specs=[row, column],
        out_shape=[jax.ShapeDtypeStruct((width, width), BF16), jax.ShapeDtypeStruct((rows, width), BF16)],
        compiler_params=params(48),
        cost_estimate=pl.CostEstimate(flops=4 * rows * width * width, bytes_accessed=12 * MIB, transcendentals=0),
        name="output_grad",
    )(glow, mixed, wo, inv)


def attend_grad_kernel(
    lengths_ref, q_ref, k_ref, v_ref, gm_ref, mixed_ref, p_ref, dq_ref, dk_ref, dv_ref, diag_ref,
    qm_ref, km_ref, vx_ref, gx_ref, go_ref, ak_ref, av_ref, acc_ref,
):
    rows = q_ref.shape[0]
    bounds = bounds_of(lengths_ref, lengths_ref.shape[1])
    reach = WINDOW + BLOCK
    acc_ref[...] = jnp.zeros_like(acc_ref)
    ak_ref[...] = jnp.zeros_like(ak_ref)
    av_ref[...] = jnp.zeros_like(av_ref)

    def prepare(index, carry):
        span = pl.ds(pl.multiple_of(index * BLOCK, BLOCK), BLOCK)
        lane = lax.broadcasted_iota(jnp.int32, (BLOCK, BLOCK), 1)
        q, k, v, g = q_ref[span, :], k_ref[span, :], v_ref[span, :], gm_ref[span, :]
        product = g.astype(F32) * mixed_ref[span, :].astype(F32)
        for half in range(2):
            mine = (lane < HEAD_DIM) if half == 0 else (lane >= HEAD_DIM)
            base = HEAD_DIM * (1 - half)
            zero = jnp.zeros_like(q)
            qm_ref[half, span, :] = jnp.where(mine, q, zero)
            km_ref[half, span, :] = jnp.where(mine, k, zero)
            go_ref[half, span, :] = jnp.where(mine, g, zero)
            vx_ref[half, span, :] = jnp.where(mine, v, jnp.ones_like(v))
            centre = jnp.sum(jnp.where(mine, product, 0.0), -1, keepdims=True)
            high, low = split_two(-centre)
            high, low = high.astype(F32), low.astype(F32)
            extra = jnp.where(lane == base, high, jnp.where(lane == base + 1, low, 0.0))
            gx_ref[half, span, :] = jnp.where(mine, g.astype(F32), extra).astype(BF16)
        return carry

    lax.fori_loop(0, rows // BLOCK, prepare, 0)

    def one(block_index, carry):
        start = pl.multiple_of(block_index * BLOCK, BLOCK)
        first, count = window_of(bounds, start)
        first = pl.multiple_of(first, BLOCK)
        shift = pl.multiple_of(first - start + SPAN, BLOCK)

        def body(blocks):
            size = blocks * BLOCK
            queries = pl.ds(start, BLOCK)
            keys = pl.ds(first, size)
            parts = []
            raised = []
            for half in range(2):
                spread = dot_nt(gx_ref[half, queries, :], vx_ref[half, keys, :])
                p = p_ref[half, queries, 0:size]
                grad_scores = p.astype(F32) * spread
                acc_ref[half, :, pl.ds(shift, size)] += grad_scores
                parts.append(grad_scores.astype(BF16))
                raised.append(p)
            both = jnp.concatenate(parts, 0)
            q_both = jnp.concatenate([qm_ref[0, queries, :], qm_ref[1, queries, :]], 0)
            g_both = jnp.concatenate([go_ref[0, queries, :], go_ref[1, queries, :]], 0)
            k_both = jnp.concatenate([km_ref[0, keys, :], km_ref[1, keys, :]], 0)
            ak_ref[keys, :] += dot_tn(both, q_both)
            av_ref[keys, :] += dot_tn(jnp.concatenate(raised, 0), g_both)
            dq_ref[queries, :] = dot_nn(jnp.concatenate(parts, 1), k_both).astype(BF16)

        for blocks in range(1, WINDOW // BLOCK + 1):
            pl.when(count == blocks)(functools.partial(body, blocks))
        return carry

    lax.fori_loop(0, rows // BLOCK, one, 0)
    dk_ref[...] = ak_ref[...].astype(BF16)
    dv_ref[...] = av_ref[...].astype(BF16)
    for half in range(2):
        padded = jnp.concatenate([jnp.zeros((BLOCK, BLOCK), F32), acc_ref[half]], 1)
        group = padded[0:8]
        for index in range(1, BLOCK // 8):
            group = group + pltpu.roll(padded[8 * index : 8 * index + 8], reach - 8 * index, 1)
        line = group[0:1]
        for index in range(1, 8):
            line = line + pltpu.roll(group, reach - index, 1)[index : index + 1]
        diag_ref[0, half : half + 1, :] = line


def attend_grad(lengths, q, k, v, gm, mixed, p):
    rows, width = q.shape
    pairs = HEADS // 2
    column = pl.BlockSpec((rows, BLOCK), lambda i: (0, i))
    return pl.pallas_call(
        attend_grad_kernel,
        grid=(pairs,),
        in_specs=[smem] + [column] * 5 + [pl.BlockSpec((2, rows, WINDOW), lambda i: (i, 0, 0))],
        out_specs=[column] * 3 + [pl.BlockSpec((1, 2, WINDOW + BLOCK), lambda i: (i, 0, 0))],
        out_shape=[jax.ShapeDtypeStruct((rows, width), BF16)] * 3
        + [jax.ShapeDtypeStruct((pairs, 2, WINDOW + BLOCK), F32)],
        scratch_shapes=[pltpu.VMEM((2, rows, BLOCK), BF16)] * 5
        + [pltpu.VMEM((rows, BLOCK), F32)] * 2
        + [pltpu.VMEM((2, BLOCK, WINDOW), F32)],
        compiler_params=params(48),
        cost_estimate=pl.CostEstimate(flops=12 * 10 * rows * 512 * 64, bytes_accessed=30 * MIB, transcendentals=0),
        name="attend_grad",
    )(lengths, q, k, v, gm, mixed, p)


def head_grad_kernel(hid_ref, dq_ref, dk_ref, dv_ref, gq_ref, gk_ref, gv_ref):
    hidden = hid_ref[...]
    gq_ref[...] = dot_tn(hidden, dq_ref[...]).astype(gq_ref.dtype)
    gk_ref[...] = dot_tn(hidden, dk_ref[...]).astype(gk_ref.dtype)
    gv_ref[...] = dot_tn(hidden, dv_ref[...]).astype(gv_ref.dtype)


def head_grad(hidden, dq, dk, dv):
    rows, width = hidden.shape
    block = width // 3
    column = pl.BlockSpec((rows, block), lambda i: (0, i))
    out = pl.BlockSpec((width, block), lambda i: (0, i))
    return pl.pallas_call(
        head_grad_kernel,
        grid=(3,),
        in_specs=[whole((rows, width)), column, column, column],
        out_specs=[out] * 3,
        out_shape=[jax.ShapeDtypeStruct((width, width), BF16)] * 3,
        compiler_params=params(48),
        cost_estimate=pl.CostEstimate(flops=6 * rows * width * width, bytes_accessed=12 * MIB, transcendentals=0),
        name="head_grad",
    )(hidden, dq, dk, dv)


def token_grad_kernel(
    x_ref, gain_ref, gmid_ref, dq_ref, dk_ref, dv_ref, wq_ref, wk_ref, wv_ref, out_ref, ggain_ref
):
    x = x_ref[...].astype(F32)
    scale = lax.rsqrt(jnp.mean(x * x, -1, keepdims=True) + epsilon)
    normed = x * scale
    grad_hidden = (
        dot_nt(dq_ref[...], wq_ref[...]) + dot_nt(dk_ref[...], wk_ref[...]) + dot_nt(dv_ref[...], wv_ref[...])
    )
    part = jnp.broadcast_to(jnp.sum(grad_hidden * normed, 0, keepdims=True), ggain_ref.shape)

    @pl.when(pl.program_id(0) == 0)
    def _():
        ggain_ref[...] = part

    @pl.when(pl.program_id(0) > 0)
    def _():
        ggain_ref[...] += part

    scaled = grad_hidden * gain_ref[...].astype(F32)
    centre = jnp.mean(scaled * normed, -1, keepdims=True)
    out_ref[...] = gmid_ref[...] + scale * (scaled - normed * centre)


def token_grad(x, gain, gmid, dq, dk, dv, wq, wk, wv):
    rows, width = x.shape
    block = rows // 4
    row_spec = pl.BlockSpec((block, width), lambda i: (i, 0))
    return pl.pallas_call(
        token_grad_kernel,
        grid=(4,),
        in_specs=[row_spec, whole((1, width))] + [row_spec] * 4 + [whole((width, width))] * 3,
        out_specs=[row_spec, pl.BlockSpec((8, width), lambda i: (0, 0))],
        out_shape=[jax.ShapeDtypeStruct((rows, width), F32), jax.ShapeDtypeStruct((8, width), F32)],
        compiler_params=params(48),
        cost_estimate=pl.CostEstimate(flops=6 * rows * width * width, bytes_accessed=16 * MIB, transcendentals=0),
        name="token_grad",
    )(x, gain, gmid, dq, dk, dv, wq, wk, wv)


def outer_grad_kernel(active_ref, glow_ref, out_ref):
    high, low = split_two(active_ref[...])
    glow = glow_ref[...]
    out_ref[...] = dot_tn(high, glow) + dot_tn(low, glow)


def outer_grad(active, glow):
    return pl.pallas_call(
        outer_grad_kernel,
        out_shape=jax.ShapeDtypeStruct((active.shape[1], glow.shape[1]), F32),
        compiler_params=pltpu.CompilerParams(vmem_limit_bytes=48 * MIB),
        name="outer_grad",
    )(active, glow)


def table_grad(diag):
    reach = WINDOW + BLOCK
    offsets = jnp.arange(reach, dtype=jnp.int32) - (SPAN + BLOCK)
    onehot = (bucket_of(offsets)[:, None] == jnp.arange(BUCKETS, dtype=jnp.int32)[None, :]).astype(F32)
    sums = jnp.dot(diag.reshape(HEADS, reach), onehot, precision=lax.Precision.HIGHEST)
    return sums.T.reshape(BUCKETS * HEADS)


def layer_specs():
    both = ("narrow", "wide")
    rows, matrix, vector = P(both, None), P("wide", None), P("wide")
    ins = (rows, vector, matrix, matrix, matrix, matrix, vector, vector, matrix, matrix, matrix, rows, P())
    outs = (rows, rows, rows, vector, matrix, matrix, matrix, matrix, vector, vector, matrix, matrix, matrix)
    return ins, outs


def local(
    tokens,
    attention_gain,
    query_weight,
    key_weight,
    value_weight,
    output_weight,
    bias_table,
    forward_gain,
    inner_weight,
    outer_weight,
    project_weight,
    lengths,
    positives,
):
    both = ("narrow", "wide")
    gather = lambda a: lax.all_gather(a, "wide", axis=0, tiled=True)
    segs = lengths.shape[1]
    width = tokens.shape[1]
    wide_at = lax.axis_index("wide")
    device = lax.axis_index("narrow") * lax.axis_size("wide") + wide_at
    small = gather(jnp.concatenate([attention_gain, forward_gain, bias_table])[None])
    share = attention_gain.shape[0]
    gain_one = small[:, :share].reshape(1, width)
    gain_two = small[:, share : 2 * share].reshape(1, width)
    table = jnp.pad(small[:, 2 * share :].reshape(BUCKETS, HEADS), ((0, 0), (0, 4)))
    wq, wk, wv, wo = gather(query_weight), gather(key_weight), gather(value_weight), gather(output_weight)
    wi, wu, wp = gather(inner_weight), gather(outer_weight), gather(project_weight)

    hid, q, k, v = project(tokens, gain_one, wq, wk, wv)
    mixed, inv, p = attend(lengths, table, q, k, v)
    middle, hid_two = output(tokens, mixed, wo, gain_two)
    hidden, slope, active_sum, pooled = forward(lengths, hid_two, middle, wi, wu)
    lens = lengths.astype(F32).reshape(segs, 1)
    message = jnp.concatenate(
        [(pooled[:segs] / lens).astype(BF16), jnp.broadcast_to(lens, (segs, 128)).astype(BF16)], 1
    )
    messages = lax.all_gather(message, both, axis=0, tiled=True)
    place = jnp.stack([device, wide_at]).astype(jnp.int32)
    loss, grad_wp, glow_all, grows = contrast(
        place,
        messages[:, :width],
        messages[:, width : width + 1].astype(F32),
        positives.reshape(-1, 1),
        wp,
        project_weight.shape[0],
    )
    active_all = lax.all_gather(active_sum[:segs].astype(BF16), both, axis=0, tiled=True)
    units = outer_weight.shape[0]
    active_own = lax.dynamic_slice_in_dim(active_all, wide_at * units, units, 1)
    glow = jnp.pad(lax.dynamic_slice_in_dim(glow_all, device * segs, segs, 0), ((0, 16 - segs), (0, 0)))
    grad_wi, gi = inner_grad(lengths, glow, wu, slope, hid_two)
    gmid, gmid_low, grad_gain_two = middle_grad(lengths, gi, wi, middle, grows, gain_two)
    grad_wo, gm = output_grad(gmid_low, mixed, wo, inv)
    dq, dk, dv, diag = attend_grad(lengths, q, k, v, gm, mixed, p)
    grad_wq, grad_wk, grad_wv = head_grad(hid, dq, dk, dv)
    grad_tokens, grad_gain_one = token_grad(tokens, gain_one, gmid, dq, dk, dv, wq, wk, wv)
    grad_outer = outer_grad(active_own, glow_all)

    def total(grad):
        part = lax.psum_scatter(grad, "wide", scatter_dimension=0, tiled=True)
        return lax.psum(part.astype(F32), "narrow")

    wide = lax.axis_size("wide")
    vectors = jnp.concatenate(
        [
            grad_gain_one[0].reshape(wide, -1),
            grad_gain_two[0].reshape(wide, -1),
            table_grad(diag).reshape(wide, -1),
        ],
        1,
    )
    vectors = total(vectors)[0]
    return (
        hidden,
        grad_tokens,
        loss[:, 0].reshape(1, segs),
        vectors[:share],
        total(grad_wq),
        total(grad_wk),
        total(grad_wv),
        total(grad_wo),
        vectors[2 * share :],
        vectors[share : 2 * share],
        total(grad_wi),
        grad_outer,
        grad_wp,
    )


def solution(mesh):
    ins, outs = layer_specs()
    return jax.shard_map(local, mesh=mesh, in_specs=ins, out_specs=outs, check_vma=False)
```

```python
import functools

import jax
import jax.numpy as jnp
from jax import lax
from jax.experimental import pallas as pl
from jax.experimental.pallas import tpu as pltpu
from jax.sharding import PartitionSpec as P

HEADS = 12
HEAD_DIM = 64
BUCKETS = 32
SPAN = 256
BLOCK = 128
WINDOW = BLOCK + 2 * SPAN
CHUNK = 512

epsilon = 1e-06
logit_scale = 50.0
root_half = 0.7071067811865476
inv_root_tau = 0.3989422804014327
MIB = 1 << 20
F32 = jnp.float32
BF16 = jnp.bfloat16


def dot_nn(left, right):
    return lax.dot_general(left, right, (((1,), (0,)), ((), ())), preferred_element_type=F32)


def dot_nt(left, right):
    return lax.dot_general(left, right, (((1,), (1,)), ((), ())), preferred_element_type=F32)


def dot_tn(left, right):
    return lax.dot_general(left, right, (((0,), (0,)), ((), ())), preferred_element_type=F32)


def split(values):
    high = values.astype(BF16)
    rest = values - high.astype(F32)
    middle = rest.astype(BF16)
    return high, middle, (rest - middle.astype(F32)).astype(BF16)


def split_two(values):
    high = values.astype(BF16)
    return high, (values - high.astype(F32)).astype(BF16)


def bucket_of(offset):
    distance = jnp.abs(offset)
    larger = jnp.full_like(distance, 8)
    for step in range(1, 8):
        larger = larger + (distance * distance >= 64 * 2**step).astype(jnp.int32)
    return jnp.where(distance < 8, distance, larger) + jnp.where(offset > 0, 16, 0)


def bounds_of(lengths_ref, count):
    bounds = []
    total = 0
    for index in range(count):
        total = total + lengths_ref[0, index]
        bounds.append(total)
    return bounds


def segment_of(places, bounds):
    segment = jnp.zeros_like(places)
    for bound in bounds:
        segment = segment + (places >= bound).astype(jnp.int32)
    return segment


def window_of(bounds, start):
    low = 0
    high = bounds[-1]
    for bound in bounds[:-1]:
        low = jnp.where(bound <= start, bound, low)
    for bound in reversed(bounds[:-1]):
        high = jnp.where(bound > start + BLOCK - 1, bound, high)
    first = (low // BLOCK) * BLOCK
    blocks = (high - first + BLOCK - 1) // BLOCK
    return first, blocks


def params(grid=1):
    return pltpu.CompilerParams(vmem_limit_bytes=60 * MIB, dimension_semantics=("arbitrary",) * grid)


def whole(shape):
    return pl.BlockSpec(shape, lambda *_: (0,) * len(shape), pipeline_mode=pl.Buffered(1))


smem = pl.BlockSpec(memory_space=pltpu.SMEM)
anywhere = pl.BlockSpec(memory_space=pl.ANY)


def owner_of(place_ref, far, other):
    return 2 * (place_ref[3] ^ far) + (place_ref[4] ^ other)


def start_copies(pairs, sems, first=0):
    pending = [pltpu.make_async_copy(source, target, sems.at[first + at]) for at, (source, target) in enumerate(pairs)]
    for copy in pending:
        copy.start()
    return pending


def wait_copies(pending):
    for copy in pending:
        copy.wait()


def head_copies(place_ref, refs, whole_ref):
    rows = refs[0].shape[1]
    for other in range(2):
        start = pl.multiple_of(owner_of(place_ref, 0, other) * rows, 16)
        yield refs[other], whole_ref.at[:, pl.ds(start, rows), :]
        for near in range(4):
            piece = refs[2 + 4 * other + near]
            for far in range(1, 4):
                start = pl.multiple_of(owner_of(place_ref, far, other) * rows, 16)
                yield piece.at[far - 1], whole_ref.at[place_ref[2] ^ near, pl.ds(start, rows), :]


def project_kernel(place_ref, x_ref, gain_ref, *refs):
    *pieces, hid_ref, q_ref, k_ref, v_ref, w_ref, sems = refs

    @pl.when(pl.program_id(0) == 0)
    def _():
        if len(pieces) == 1:
            pairs = [(pieces[0], w_ref)]
        else:
            pairs = list(head_copies(place_ref, pieces, w_ref))
        wait_copies(start_copies(pairs, sems))

    x = x_ref[...].astype(F32)
    scale = lax.rsqrt(jnp.mean(x * x, -1, keepdims=True) + epsilon)
    hidden = (x * scale * gain_ref[...].astype(F32)).astype(BF16)
    hid_ref[...] = hidden
    q_ref[...] = dot_nn(hidden, w_ref[0]).astype(BF16)
    k_ref[...] = dot_nn(hidden, w_ref[1]).astype(BF16)
    v_ref[...] = dot_nn(hidden, w_ref[2]).astype(BF16)


def project(place, x, gain, pieces):
    rows, width = x.shape
    block = rows // 4
    row_spec = pl.BlockSpec((block, width), lambda i: (i, 0))
    out = jax.ShapeDtypeStruct((rows, width), BF16)
    return pl.pallas_call(
        project_kernel,
        grid=(4,),
        in_specs=[smem, row_spec, whole((1, width))] + [anywhere] * len(pieces),
        out_specs=[row_spec] * 4 + [pl.BlockSpec((4, width, width), lambda i: (0, 0, 0))],
        out_shape=[out] * 4 + [jax.ShapeDtypeStruct((4, width, width), BF16)],
        scratch_shapes=[pltpu.SemaphoreType.DMA((26,))],
        compiler_params=params(),
        cost_estimate=pl.CostEstimate(
            flops=6 * rows * width * width, bytes_accessed=10 * rows * width + 16 * width * width, transcendentals=0
        ),
        name="project_heads",
    )(place, x, gain, *pieces)


def attend_kernel(first_pair, lengths_ref, table_ref, q_ref, k_ref, v_ref, *refs):
    mixed_ref, inv_ref, p_ref, rows_ref, tile_ref, segc_ref, segr_ref = refs[-7:]
    pair = first_pair + pl.program_id(0)
    rows = q_ref.shape[0]
    bounds = bounds_of(lengths_ref, lengths_ref.shape[1])
    reach = WINDOW + BLOCK

    @pl.when(pl.program_id(0) == 0)
    def _():
        segc_ref[...] = segment_of(lax.broadcasted_iota(jnp.int32, segc_ref.shape, 0), bounds)
        segr_ref[...] = segment_of(lax.broadcasted_iota(jnp.int32, segr_ref.shape, 1), bounds)
        offsets = lax.broadcasted_iota(jnp.int32, (BUCKETS, reach), 1) - (SPAN + BLOCK)
        kinds = lax.broadcasted_iota(jnp.int32, (BUCKETS, reach), 0)
        onehot = (bucket_of(offsets) == kinds).astype(F32).astype(BF16)
        rows_ref[...] = dot_tn(table_ref[...], onehot)

    for half in range(2):
        line = rows_ref[pl.ds(2 * pair + half, 1), :]
        skew = pltpu.roll(jnp.broadcast_to(line, (BLOCK, reach)), 0, 1, stride=1, stride_axis=0)
        tile_ref[half] = skew[:, BLOCK:]

    lane = lax.broadcasted_iota(jnp.int32, (BLOCK, BLOCK), 1)
    first_half = lane < HEAD_DIM

    def one(block_index, carry):
        start = pl.multiple_of(block_index * BLOCK, BLOCK)
        first, count = window_of(bounds, start)
        first = pl.multiple_of(first, BLOCK)
        shift = pl.multiple_of(first - start + SPAN, BLOCK)

        def body(blocks):
            size = blocks * BLOCK
            q = q_ref[pl.ds(start, BLOCK), :]
            k = k_ref[pl.ds(first, size), :]
            v = v_ref[pl.ds(first, size), :]
            segc = segc_ref[pl.ds(start, BLOCK), :]
            segr = segr_ref[0:1, pl.ds(first, size)]
            same = jnp.concatenate([segc] * blocks, 1) == segr
            wide_lane = lax.broadcasted_iota(jnp.int32, (size, BLOCK), 1) < HEAD_DIM
            results = []
            for half in range(2):
                mine = first_half if half == 0 else ~first_half
                scores = dot_nt(jnp.where(mine, q, jnp.zeros_like(q)), k)
                scores = scores + tile_ref[half, :, pl.ds(shift, size)]
                scores = jnp.where(same, scores, -1000000000.0)
                raised = jnp.exp(scores - jnp.max(scores, -1, keepdims=True)).astype(BF16)
                p_ref[half, pl.ds(start, BLOCK), 0:size] = raised
                keep = wide_lane if half == 0 else ~wide_lane
                results.append(dot_nn(raised, jnp.where(keep, v, jnp.ones_like(v))))
            top = jnp.where(first_half, results[0], results[1])
            total = pltpu.roll(jnp.where(first_half, results[1], results[0]), HEAD_DIM, 1)
            inverse = 1.0 / total
            mixed_ref[pl.ds(start, BLOCK), :] = (top * inverse).astype(BF16)
            inv_ref[pl.ds(start, BLOCK), :] = inverse

        for blocks in range(1, WINDOW // BLOCK + 1):
            pl.when(count == blocks)(functools.partial(body, blocks))
        return carry

    lax.fori_loop(0, rows // BLOCK, one, 0)


def attend(lengths, table, q, k, v, first_pair, pairs, before=()):
    rows, width = q.shape
    column = pl.BlockSpec((rows, BLOCK), lambda p: (0, first_pair + p))
    return pl.pallas_call(
        functools.partial(attend_kernel, first_pair),
        grid=(pairs,),
        in_specs=[smem, whole(table.shape), column, column, column] + [anywhere] * len(before),
        out_specs=[column, column, pl.BlockSpec((2, rows, WINDOW), lambda p: (first_pair + p, 0, 0))],
        out_shape=[
            jax.ShapeDtypeStruct((rows, width), BF16),
            jax.ShapeDtypeStruct((rows, width), F32),
            jax.ShapeDtypeStruct((HEADS, rows, WINDOW), BF16),
        ],
        scratch_shapes=[
            pltpu.VMEM((16, WINDOW + BLOCK), F32),
            pltpu.VMEM((2, BLOCK, WINDOW), F32),
            pltpu.VMEM((rows, BLOCK), jnp.int32),
            pltpu.VMEM((8, rows), jnp.int32),
        ],
        input_output_aliases={5 + index: index for index in range(len(before))},
        compiler_params=params(),
        cost_estimate=pl.CostEstimate(
            flops=pairs * 8 * rows * 512 * 128, bytes_accessed=pairs * 6 * MIB, transcendentals=2 * pairs * rows * 512
        ),
        name="attend",
    )(lengths, table, q, k, v, *before)


def output_kernel(x_ref, mixed_ref, wo_ref, gain_ref, mid_ref, hid_ref):
    middle = x_ref[...].astype(F32) + dot_nn(mixed_ref[...], wo_ref[0])
    scale = lax.rsqrt(jnp.mean(middle * middle, -1, keepdims=True) + epsilon)
    mid_ref[...] = middle
    hid_ref[...] = (middle * scale * gain_ref[...].astype(F32)).astype(BF16)


def output(x, mixed, wo, gain):
    rows, width = x.shape
    block = rows // 4
    row_spec = pl.BlockSpec((block, width), lambda i: (i, 0))
    return pl.pallas_call(
        output_kernel,
        grid=(4,),
        in_specs=[
            row_spec,
            row_spec,
            pl.BlockSpec((1, width, width), lambda i: (3, 0, 0), pipeline_mode=pl.Buffered(1)),
            whole((1, width)),
        ],
        out_specs=[row_spec] * 2,
        out_shape=[jax.ShapeDtypeStruct((rows, width), F32), jax.ShapeDtypeStruct((rows, width), BF16)],
        compiler_params=params(),
        cost_estimate=pl.CostEstimate(
            flops=2 * rows * width * width, bytes_accessed=10 * rows * width + 2 * width * width, transcendentals=0
        ),
        name="output_and_norm",
    )(x, mixed, wo, gain)


def gelu_and_slope(v):
    bell = jnp.exp(-0.5 * v * v)
    t = 1.0 / (1.0 + (0.3275911 * root_half) * jnp.abs(v))
    series = t * (
        0.5 * 0.254829592
        + t * (0.5 * -0.284496736 + t * (0.5 * 1.421413741 + t * (0.5 * -1.453152027 + t * (0.5 * 1.061405429))))
    )
    tail = series * bell
    share = jnp.where(v >= 0.0, 1.0 - tail, tail)
    return v * share, share + v * bell * inv_root_tau


def member_of(lengths_ref, rows, count):
    bounds = bounds_of(lengths_ref, lengths_ref.shape[1])
    segment = segment_of(lax.broadcasted_iota(jnp.int32, (rows, count), 0), bounds)
    return (segment == lax.broadcasted_iota(jnp.int32, (rows, count), 1)).astype(F32).astype(BF16)


def member_rows(lengths_ref, rows, count):
    bounds = bounds_of(lengths_ref, lengths_ref.shape[1])
    segment = segment_of(lax.broadcasted_iota(jnp.int32, (count, rows), 1), bounds)
    return (segment == lax.broadcasted_iota(jnp.int32, (count, rows), 0)).astype(F32).astype(BF16)


def forward_copies(place_ref, refs, inner_ref, outer_ref, project_ref):
    rows = refs[0].shape[0]
    share, width = refs[2].shape
    half = rows // 2
    inner, outer, last = [], [], []
    for other in range(2):
        owner = owner_of(place_ref, 0, other)
        inner.append((refs[other], inner_ref.at[pl.ds(pl.multiple_of(owner * rows, 16), rows), :]))
        outer.append((refs[2 + other], outer_ref.at[pl.ds(pl.multiple_of(owner * share, 16), share), :]))
        last.append((refs[4 + other], project_ref.at[pl.ds(pl.multiple_of(owner * rows, 16), rows), :]))
        for near in range(4):
            piece = refs[6 + 4 * other + near]
            quarter = place_ref[2] ^ near
            for far in range(1, 4):
                owner = owner_of(place_ref, far, other)
                row = pl.ds(pl.multiple_of(owner * rows, 16), rows)
                column = pl.ds(pl.multiple_of(quarter * width, 128), width)
                inner.append((piece.at[far - 1, pl.ds(0, rows), :], inner_ref.at[row, column]))
                row = pl.ds(pl.multiple_of(owner * share + quarter * rows, 16), rows)
                outer.append((piece.at[far - 1, pl.ds(rows, rows), :], outer_ref.at[row, :]))
                if near < 2:
                    row = pl.ds(pl.multiple_of(owner * rows + (quarter % 2) * half, 16), half)
                    last.append((piece.at[far - 1, pl.ds(2 * rows, half), :], project_ref.at[row, :]))
    return inner, outer, last


def forward_kernel(place_ref, lengths_ref, hid_ref, mid_ref, *refs):
    *pieces, out_ref, slope_ref, active_sum_ref, pooled_ref, wi_out, wu_out, wp_out = refs[:-7]
    total_ref, member_ref, wi_ref, wu_ref, wp_ref, sems, out_sems = refs[-7:]
    step = pl.program_id(0)
    rows = hid_ref.shape[0]
    outs = ((wi_ref, wi_out), (wu_ref, wu_out), (wp_ref, wp_out))

    @pl.when(step == 0)
    def _():
        if len(pieces) == 3:
            groups = [[pair] for pair in zip(pieces, (wi_ref, wu_ref, wp_ref))]
        else:
            groups = forward_copies(place_ref, pieces, wi_ref, wu_ref, wp_ref)
        pending = []
        first = 0
        for group in groups:
            pending.append(start_copies(group, sems, first))
            first += len(group)
        member_ref[...] = member_rows(lengths_ref, rows, 16)
        total_ref[...] = mid_ref[...]
        for group, out in zip(pending, outs):
            wait_copies(group)
        for index, (source, target) in enumerate(outs):
            pltpu.make_async_copy(source, target, out_sems.at[index]).start()

    block = rows // 4
    columns = pl.ds(pl.multiple_of(step * CHUNK, CHUNK), CHUNK)
    for index in range(4):
        span = slice(index * block, (index + 1) * block)
        active, slope = gelu_and_slope(dot_nn(hid_ref[span, :], wi_ref[:, columns]))
        active = active.astype(BF16)
        slope_ref[span, :] = slope.astype(BF16)
        total_ref[span, :] += dot_nn(active, wu_ref[columns, :])
        part = dot_nn(member_ref[:, span], active)
        if index == 0:
            active_sum_ref[...] = part
        else:
            active_sum_ref[...] += part

    @pl.when(step == pl.num_programs(0) - 1)
    def _():
        total = total_ref[...]
        out_ref[...] = total.astype(BF16)
        member = member_ref[...]
        high, middle, low = split(total)
        pooled_ref[...] = dot_nn(member, high) + dot_nn(member, middle) + dot_nn(member, low)
        for index, (source, target) in enumerate(outs):
            pltpu.make_async_copy(source, target, out_sems.at[index]).wait()


def forward(place, lengths, hidden, middle, units, pieces):
    rows, width = hidden.shape
    full = whole((rows, width))
    weights = [
        jax.ShapeDtypeStruct((width, units), BF16),
        jax.ShapeDtypeStruct((units, width), BF16),
        jax.ShapeDtypeStruct((width, width), BF16),
    ]
    return pl.pallas_call(
        forward_kernel,
        grid=(units // CHUNK,),
        in_specs=[smem, smem, full, full] + [anywhere] * len(pieces),
        out_specs=[
            pl.BlockSpec((rows, width), lambda i: (0, 0)),
            pl.BlockSpec((rows, CHUNK), lambda i: (0, i)),
            pl.BlockSpec((16, CHUNK), lambda i: (0, i)),
            pl.BlockSpec((16, width), lambda i: (0, 0)),
        ]
        + [anywhere] * 3,
        out_shape=[
            jax.ShapeDtypeStruct((rows, width), BF16),
            jax.ShapeDtypeStruct((rows, units), BF16),
            jax.ShapeDtypeStruct((16, units), F32),
            jax.ShapeDtypeStruct((16, width), F32),
        ]
        + weights,
        scratch_shapes=[pltpu.VMEM((rows, width), F32), pltpu.VMEM((16, rows), BF16)]
        + [pltpu.VMEM(weight.shape, BF16) for weight in weights]
        + [pltpu.SemaphoreType.DMA((72,)), pltpu.SemaphoreType.DMA((3,))],
        compiler_params=params(),
        cost_estimate=pl.CostEstimate(
            flops=4 * rows * width * units, bytes_accessed=30 * MIB, transcendentals=2 * rows * units
        ),
        name="feed_forward",
    )(place, lengths, hidden, middle, *pieces)


def contrast_kernel(
    place_ref, pooled_ref, len_ref, target_ref, wp_ref, loss_ref, grad_wp_ref, glow_all_ref, grows_ref, wide_ref, line_ref, full_ref
):
    count = pooled_ref.shape[0]
    first = pl.multiple_of(place_ref[0] * 8, 8)
    pooled = pooled_ref[...]
    projected = dot_nn(pooled, wp_ref[...])
    inverse = lax.rsqrt(jnp.sum(projected * projected, -1, keepdims=True) + epsilon)
    embedded = (projected * inverse).astype(BF16)
    row = lax.broadcasted_iota(jnp.int32, (count, count), 0)
    column = lax.broadcasted_iota(jnp.int32, (count, count), 1)
    logits = logit_scale * dot_nt(embedded, embedded)
    logits = jnp.where(row == column, -1000000000.0, logits)
    hit = column == target_ref[...]
    highest = jnp.max(logits, -1, keepdims=True)
    totals = highest + jnp.log(jnp.sum(jnp.exp(logits - highest), -1, keepdims=True))
    target = jnp.sum(jnp.where(hit, logits, 0.0), -1, keepdims=True)
    line_ref[...] = jnp.broadcast_to(totals - target, line_ref.shape)
    loss_ref[...] = line_ref[pl.ds(first, 8), :]
    grad_logits = (jnp.exp(logits - totals) - hit.astype(F32)).astype(BF16)
    grad_embedded = logit_scale * (dot_nn(grad_logits, embedded) + dot_tn(grad_logits, embedded))
    along = jnp.sum(grad_embedded * projected, -1, keepdims=True)
    grad_projected = inverse * grad_embedded - projected * (inverse * inverse * inverse * along)
    high, middle, low = split(grad_projected)
    full_ref[...] = dot_tn(pooled, high) + dot_tn(pooled, middle) + dot_tn(pooled, low)
    share = grad_wp_ref.shape[0]
    grad_wp_ref[...] = full_ref[pl.ds(pl.multiple_of(place_ref[1] * share, share), share), :]
    wp = wp_ref[...]
    grad_rows = (dot_nt(high, wp) + dot_nt(middle, wp) + dot_nt(low, wp)) / len_ref[...]
    glow_all_ref[...] = grad_rows.astype(BF16)
    wide_ref[...] = grad_rows
    grows_ref[...] = wide_ref[pl.ds(first, 8), :]


def contrast(place, pooled, lens, targets, wp, share):
    count, width = pooled.shape
    if count > 512 or share % 8:
        return contrast_plain(place, pooled, lens, targets, wp, share)
    return pl.pallas_call(
        contrast_kernel,
        in_specs=[smem] + [pl.BlockSpec(memory_space=pltpu.VMEM)] * 4,
        out_specs=[pl.BlockSpec(memory_space=pltpu.VMEM)] * 4,
        out_shape=[
            jax.ShapeDtypeStruct((8, 128), F32),
            jax.ShapeDtypeStruct((share, width), F32),
            jax.ShapeDtypeStruct((count, width), BF16),
            jax.ShapeDtypeStruct((8, width), F32),
        ],
        scratch_shapes=[
            pltpu.VMEM((count, width), F32),
            pltpu.VMEM((count, 128), F32),
            pltpu.VMEM((width, width), F32),
        ],
        compiler_params=pltpu.CompilerParams(vmem_limit_bytes=60 * MIB),
        cost_estimate=pl.CostEstimate(flops=4 * count * width * width, bytes_accessed=8 * MIB, transcendentals=0),
        name="contrast",
    )(place, pooled, lens, targets, wp)


def contrast_plain(place, pooled, lens, targets, wp, share):
    count, width = pooled.shape
    exact = lax.Precision.HIGHEST
    projected = jnp.dot(pooled, wp, preferred_element_type=F32)
    inverse = lax.rsqrt(jnp.sum(projected * projected, -1, keepdims=True) + epsilon)
    embedded = (projected * inverse).astype(BF16)
    numbers = jnp.arange(count, dtype=jnp.int32)
    logits = logit_scale * dot_nt(embedded, embedded)
    logits = jnp.where(numbers[:, None] == numbers[None, :], -1000000000.0, logits)
    hit = numbers[None, :] == targets
    highest = jnp.max(logits, -1, keepdims=True)
    totals = highest + jnp.log(jnp.sum(jnp.exp(logits - highest), -1, keepdims=True))
    loss = totals - jnp.sum(jnp.where(hit, logits, 0.0), -1, keepdims=True)
    grad_logits = (jnp.exp(logits - totals) - hit.astype(F32)).astype(BF16)
    grad_embedded = logit_scale * (dot_nn(grad_logits, embedded) + dot_tn(grad_logits, embedded))
    along = jnp.sum(grad_embedded * projected, -1, keepdims=True)
    grad_projected = inverse * grad_embedded - projected * (inverse * inverse * inverse * along)
    own_columns = lax.dynamic_slice_in_dim(pooled.astype(F32), place[1] * share, share, 1)
    grad_wp = lax.dot_general(own_columns, grad_projected, (((0,), (0,)), ((), ())), precision=exact)
    grad_rows = jnp.dot(grad_projected, wp.astype(F32).T, precision=exact) / lens
    first = place[0] * 8
    own = lambda a: lax.dynamic_slice_in_dim(a, first, 8, 0)
    return jnp.broadcast_to(own(loss), (8, 128)), grad_wp, grad_rows.astype(BF16), own(grad_rows)


def fold(result_ref, keep_ref, send_ref, place_ref, column_half, column):
    narrow, plane, core = place_ref[2], place_ref[3], place_ref[4]
    rows = keep_ref.shape[2]
    for near in range(2):
        quarter = 2 * ((narrow // 2) ^ column_half) + near
        half = (narrow % 2) ^ near
        for far in range(4):
            for ref, owner in ((keep_ref, core), (send_ref, 1 - core)):
                start = pl.multiple_of((2 * (plane ^ far) + owner) * 2 * rows + half * rows, 16)
                block = result_ref[pl.ds(start, rows), :].astype(BF16)
                ref[quarter, far, :, pl.ds(column, block.shape[1])] = block


def inner_grad_kernel(lengths_ref, place_ref, glow_ref, wo_ref, slope_ref, hid_ref, gi_ref, *refs):
    member_ref = refs[-1]

    @pl.when(pl.program_id(0) == 0)
    def _():
        member_ref[...] = member_of(lengths_ref, member_ref.shape[0], 16)

    grad_active = dot_nt(glow_ref[...], wo_ref[...])
    high, low = split_two(grad_active)
    member = member_ref[...]
    spread = dot_nn(member, high) + dot_nn(member, low)
    grad_inner = (spread * slope_ref[...].astype(F32)).astype(BF16)
    gi_ref[...] = grad_inner
    grad = dot_tn(hid_ref[...], grad_inner)
    if len(refs) == 2:
        refs[0][...] = grad.astype(BF16)
    else:
        keep_ref, send_ref, result_ref = refs[:3]
        step = pl.program_id(0)
        result_ref[...] = grad
        half = pl.num_programs(0) // 2
        fold(result_ref, keep_ref, send_ref, place_ref, step // half, pl.multiple_of((step % half) * CHUNK, CHUNK))


def inner_grad(lengths, place, glow, wo, slope, hidden, folded):
    rows, width = hidden.shape
    units = slope.shape[1]
    out_specs = [pl.BlockSpec((rows, CHUNK), lambda i: (0, i))]
    out_shape = [jax.ShapeDtypeStruct((rows, units), BF16)]
    scratch = []
    if folded:
        slab = (4, 4, width // 16, units // 2)
        out_specs += [pl.BlockSpec(slab, lambda i: (0, 0, 0, 0))] * 2
        out_shape += [jax.ShapeDtypeStruct(slab, BF16)] * 2
        scratch = [pltpu.VMEM((width, CHUNK), F32)]
    else:
        out_specs += [pl.BlockSpec((width, CHUNK), lambda i: (0, i))]
        out_shape += [jax.ShapeDtypeStruct((width, units), BF16)]
    return pl.pallas_call(
        inner_grad_kernel,
        grid=(units // CHUNK,),
        in_specs=[
            smem,
            smem,
            whole((16, width)),
            pl.BlockSpec((CHUNK, width), lambda i: (i, 0)),
            pl.BlockSpec((rows, CHUNK), lambda i: (0, i)),
            whole((rows, width)),
        ],
        out_specs=out_specs,
        out_shape=out_shape,
        scratch_shapes=scratch + [pltpu.VMEM((rows, 16), BF16)],
        compiler_params=params(),
        cost_estimate=pl.CostEstimate(flops=2 * rows * width * units, bytes_accessed=24 * MIB, transcendentals=0),
        name="inner_grad",
    )(lengths, place, glow, wo, slope, hidden)


def middle_grad_kernel(
    lengths_ref, gi_ref, wi_ref, mid_ref, grows_ref, gain_ref, gmid_ref, glow_ref, total_ref
):
    step = pl.program_id(0)
    rows, width = mid_ref.shape
    part = dot_nt(gi_ref[...], wi_ref[...])

    @pl.when(step == 0)
    def _():
        total_ref[...] = part

    @pl.when(step > 0)
    def _():
        total_ref[...] += part

    @pl.when(step == pl.num_programs(0) - 1)
    def _():
        bounds = bounds_of(lengths_ref, lengths_ref.shape[1])
        block = rows // 4
        for index in range(4):
            span = slice(index * block, (index + 1) * block)
            middle = mid_ref[span, :]
            scale = lax.rsqrt(jnp.mean(middle * middle, -1, keepdims=True) + epsilon)
            normed = middle * scale
            grad_hidden = total_ref[span, :]
            scaled = grad_hidden * gain_ref[...].astype(F32)
            centre = jnp.mean(scaled * normed, -1, keepdims=True)
            segment = segment_of(lax.broadcasted_iota(jnp.int32, (block, 128), 0) + index * block, bounds)
            segment = jnp.concatenate([segment] * (width // 128), 1)
            grad_rows = jnp.zeros((block, width), F32)
            for passage in range(8):
                grad_rows = jnp.where(segment == passage, grows_ref[passage : passage + 1, :], grad_rows)
            grad_middle = grad_rows + scale * (scaled - normed * centre)
            gmid_ref[span, :] = grad_middle
            glow_ref[span, :] = grad_middle.astype(BF16)


def middle_grad(lengths, gi, wi, middle, grows, gain):
    rows, width = middle.shape
    units = wi.shape[1]
    return pl.pallas_call(
        middle_grad_kernel,
        grid=(units // CHUNK,),
        in_specs=[
            smem,
            pl.BlockSpec((rows, CHUNK), lambda i: (0, i)),
            pl.BlockSpec((width, CHUNK), lambda i: (0, i)),
            whole((rows, width)),
            whole((8, width)),
            whole((1, width)),
        ],
        out_specs=[
            pl.BlockSpec((rows, width), lambda i: (0, 0)),
            pl.BlockSpec((rows, width), lambda i: (0, 0)),
        ],
        out_shape=[jax.ShapeDtypeStruct((rows, width), F32), jax.ShapeDtypeStruct((rows, width), BF16)],
        scratch_shapes=[pltpu.VMEM((rows, width), F32)],
        compiler_params=params(),
        cost_estimate=pl.CostEstimate(flops=2 * rows * width * units, bytes_accessed=20 * MIB, transcendentals=0),
        name="middle_grad",
    )(lengths, gi, wi, middle, grows, gain)


def output_grad_kernel(glow_ref, mixed_ref, wo_ref, inv_ref, grad_ref, gmix_ref):
    glow = glow_ref[...]
    grad_ref[...] = dot_tn(mixed_ref[...], glow).astype(grad_ref.dtype)
    grad_mixed = dot_nt(glow, wo_ref[0])
    gmix_ref[...] = (grad_mixed * inv_ref[...]).astype(BF16)


def output_grad(glow, mixed, wo, inv):
    rows, width = glow.shape
    block = width // 3
    column = pl.BlockSpec((rows, block), lambda i: (0, i))
    row = pl.BlockSpec((block, width), lambda i: (i, 0))
    weight = pl.BlockSpec((1, block, width), lambda i: (3, i, 0))
    return pl.pallas_call(
        output_grad_kernel,
        grid=(3,),
        in_specs=[whole((rows, width)), column, weight, column],
        out_specs=[row, column],
        out_shape=[jax.ShapeDtypeStruct((width, width), BF16), jax.ShapeDtypeStruct((rows, width), BF16)],
        compiler_params=params(),
        cost_estimate=pl.CostEstimate(flops=4 * rows * width * width, bytes_accessed=12 * MIB, transcendentals=0),
        name="output_grad",
    )(glow, mixed, wo, inv)


def attend_grad_kernel(lengths_ref, q_ref, k_ref, v_ref, gm_ref, mixed_ref, p_ref, *refs):
    grad_ref, diag_ref, qm_ref, km_ref, vx_ref, gx_ref, go_ref, ak_ref, av_ref, acc_ref = refs[-10:]
    rows = q_ref.shape[0]
    bounds = bounds_of(lengths_ref, lengths_ref.shape[1])
    reach = WINDOW + BLOCK
    acc_ref[...] = jnp.zeros_like(acc_ref)
    ak_ref[...] = jnp.zeros_like(ak_ref)
    av_ref[...] = jnp.zeros_like(av_ref)

    def prepare(index, carry):
        span = pl.ds(pl.multiple_of(index * BLOCK, BLOCK), BLOCK)
        lane = lax.broadcasted_iota(jnp.int32, (BLOCK, BLOCK), 1)
        q, k, v, g = q_ref[span, :], k_ref[span, :], v_ref[span, :], gm_ref[span, :]
        product = g.astype(F32) * mixed_ref[span, :].astype(F32)
        for half in range(2):
            mine = (lane < HEAD_DIM) if half == 0 else (lane >= HEAD_DIM)
            base = HEAD_DIM * (1 - half)
            zero = jnp.zeros_like(q)
            qm_ref[half, span, :] = jnp.where(mine, q, zero)
            km_ref[half, span, :] = jnp.where(mine, k, zero)
            go_ref[half, span, :] = jnp.where(mine, g, zero)
            vx_ref[half, span, :] = jnp.where(mine, v, jnp.ones_like(v))
            centre = jnp.sum(jnp.where(mine, product, 0.0), -1, keepdims=True)
            high, low = split_two(-centre)
            high, low = high.astype(F32), low.astype(F32)
            extra = jnp.where(lane == base, high, jnp.where(lane == base + 1, low, 0.0))
            gx_ref[half, span, :] = jnp.where(mine, g.astype(F32), extra).astype(BF16)
        return carry

    lax.fori_loop(0, rows // BLOCK, prepare, 0)

    def one(block_index, carry):
        start = pl.multiple_of(block_index * BLOCK, BLOCK)
        first, count = window_of(bounds, start)
        first = pl.multiple_of(first, BLOCK)
        shift = pl.multiple_of(first - start + SPAN, BLOCK)

        def body(blocks):
            size = blocks * BLOCK
            queries = pl.ds(start, BLOCK)
            keys = pl.ds(first, size)
            parts = []
            raised = []
            for half in range(2):
                spread = dot_nt(gx_ref[half, queries, :], vx_ref[half, keys, :])
                p = p_ref[half, queries, 0:size]
                grad_scores = p.astype(F32) * spread
                acc_ref[half, :, pl.ds(shift, size)] += grad_scores
                parts.append(grad_scores.astype(BF16))
                raised.append(p)
            both = jnp.concatenate(parts, 0)
            q_both = jnp.concatenate([qm_ref[0, queries, :], qm_ref[1, queries, :]], 0)
            g_both = jnp.concatenate([go_ref[0, queries, :], go_ref[1, queries, :]], 0)
            k_both = jnp.concatenate([km_ref[0, keys, :], km_ref[1, keys, :]], 0)
            ak_ref[keys, :] += dot_tn(both, q_both)
            av_ref[keys, :] += dot_tn(jnp.concatenate(raised, 0), g_both)
            grad_ref[0, queries, :] = dot_nn(jnp.concatenate(parts, 1), k_both).astype(BF16)

        for blocks in range(1, WINDOW // BLOCK + 1):
            pl.when(count == blocks)(functools.partial(body, blocks))
        return carry

    lax.fori_loop(0, rows // BLOCK, one, 0)
    grad_ref[1] = ak_ref[...].astype(BF16)
    grad_ref[2] = av_ref[...].astype(BF16)
    for half in range(2):
        padded = jnp.concatenate([jnp.zeros((BLOCK, BLOCK), F32), acc_ref[half]], 1)
        group = padded[0:8]
        for index in range(1, BLOCK // 8):
            group = group + pltpu.roll(padded[8 * index : 8 * index + 8], reach - 8 * index, 1)
        line = group[0:1]
        for index in range(1, 8):
            line = line + pltpu.roll(group, reach - index, 1)[index : index + 1]
        diag_ref[0, half : half + 1, :] = line


def attend_grad(lengths, q, k, v, gm, mixed, p, first_pair, pairs, before=()):
    rows, width = q.shape
    column = pl.BlockSpec((rows, BLOCK), lambda i: (0, first_pair + i))
    return pl.pallas_call(
        attend_grad_kernel,
        grid=(pairs,),
        in_specs=[smem]
        + [column] * 5
        + [pl.BlockSpec((2, rows, WINDOW), lambda i: (first_pair + i, 0, 0))]
        + [anywhere] * len(before),
        out_specs=[
            pl.BlockSpec((3, rows, BLOCK), lambda i: (0, 0, first_pair + i)),
            pl.BlockSpec((1, 2, WINDOW + BLOCK), lambda i: (first_pair + i, 0, 0)),
        ],
        out_shape=[
            jax.ShapeDtypeStruct((3, rows, width), BF16),
            jax.ShapeDtypeStruct((HEADS // 2, 2, WINDOW + BLOCK), F32),
        ],
        scratch_shapes=[pltpu.VMEM((2, rows, BLOCK), BF16)] * 5
        + [pltpu.VMEM((rows, BLOCK), F32)] * 2
        + [pltpu.VMEM((2, BLOCK, WINDOW), F32)],
        input_output_aliases={7 + index: index for index in range(len(before))},
        compiler_params=params(),
        cost_estimate=pl.CostEstimate(
            flops=pairs * 20 * rows * 512 * 64, bytes_accessed=pairs * 5 * MIB, transcendentals=0
        ),
        name="attend_grad",
    )(lengths, q, k, v, gm, mixed, p, *before)


def head_grad_kernel(place_ref, hid_ref, gh_ref, go_ref, table_ref, keep_ref, send_ref, result_ref):
    step = pl.program_id(0)
    count = pl.num_programs(0) - 2
    half = pl.num_programs(0) // 2
    block = result_ref.shape[1]

    @pl.when(step < count)
    def _():
        result_ref[...] = dot_tn(hid_ref[...], gh_ref[0])

    @pl.when(step >= count)
    def _():
        result_ref[...] = go_ref[...].astype(F32)

    fold(result_ref, keep_ref, send_ref, place_ref, step // half, pl.multiple_of((step % half) * block, 128))

    @pl.when(step == 0)
    def _():
        plane, core = place_ref[3], place_ref[4]
        rows = keep_ref.shape[2]
        for far in range(4):
            for ref, owner in ((keep_ref, core), (send_ref, 1 - core)):
                line = jnp.broadcast_to(table_ref[pl.ds(2 * (plane ^ far) + owner, 1), :], (rows, 128)).astype(BF16)
                for quarter in range(4):
                    ref[quarter, far, :, half * block :] = line


def head_grad(place, hidden, grads, grad_out, table):
    rows, width = hidden.shape
    block = width // 2
    slab = (4, 4, width // 16, 2 * width + 128)
    return pl.pallas_call(
        head_grad_kernel,
        grid=(8,),
        in_specs=[
            smem,
            whole((rows, width)),
            pl.BlockSpec((1, rows, block), lambda i: (jnp.minimum(i // 2, 2), 0, jnp.where(i < 6, i % 2, 1))),
            pl.BlockSpec((width, block), lambda i: (0, jnp.where(i < 6, 0, i % 2))),
            whole(table.shape),
        ],
        out_specs=[pl.BlockSpec(slab, lambda i: (0, 0, 0, 0))] * 2,
        out_shape=[jax.ShapeDtypeStruct(slab, BF16)] * 2,
        scratch_shapes=[pltpu.VMEM((width, block), F32)],
        compiler_params=params(),
        cost_estimate=pl.CostEstimate(flops=6 * rows * width * width, bytes_accessed=12 * MIB, transcendentals=0),
        name="head_grad",
    )(place, hidden, grads, grad_out, table)


def token_grad_kernel(x_ref, gain_ref, gmid_ref, grad_ref, w_ref, out_ref):
    x = x_ref[...].astype(F32)
    scale = lax.rsqrt(jnp.mean(x * x, -1, keepdims=True) + epsilon)
    normed = x * scale
    grad_hidden = dot_nt(grad_ref[0], w_ref[0]) + dot_nt(grad_ref[1], w_ref[1]) + dot_nt(grad_ref[2], w_ref[2])
    scaled = grad_hidden * gain_ref[...].astype(F32)
    centre = jnp.mean(scaled * normed, -1, keepdims=True)
    out_ref[...] = gmid_ref[...] + scale * (scaled - normed * centre)


def token_grad(x, gain, gmid, grads, weights):
    rows, width = x.shape
    block = rows // 4
    row_spec = pl.BlockSpec((block, width), lambda i: (i, 0))
    return pl.pallas_call(
        token_grad_kernel,
        grid=(4,),
        in_specs=[
            row_spec,
            whole((1, width)),
            row_spec,
            pl.BlockSpec((3, block, width), lambda i: (0, i, 0)),
            whole((3, width, width)),
        ],
        out_specs=row_spec,
        out_shape=jax.ShapeDtypeStruct((rows, width), F32),
        compiler_params=params(),
        cost_estimate=pl.CostEstimate(flops=6 * rows * width * width, bytes_accessed=16 * MIB, transcendentals=0),
        name="token_grad",
    )(x, gain, gmid, grads, weights)


def outer_grad_kernel(place_ref, *refs):
    *pieces, glow_ref, out_ref, active_ref = refs
    if len(pieces) == 1:
        active = pieces[0][...].astype(F32)
    else:
        for near, ref in enumerate(pieces):
            for far in range(4):
                for other in range(2):
                    device = (place_ref[2] ^ near) * 8 + owner_of(place_ref, far, other)
                    active_ref[pl.ds(pl.multiple_of(device * 8, 8), 8), :] = ref[far, other]
        active = active_ref[...]
    high, low = split_two(active)
    glow = glow_ref[...]
    out_ref[...] = dot_tn(high, glow) + dot_tn(low, glow)


def outer_grad(place, pieces, glow):
    units = pieces[0].shape[-1]
    return pl.pallas_call(
        outer_grad_kernel,
        grid=(1,),
        in_specs=[smem] + [whole(piece.shape) for piece in pieces] + [whole(glow.shape)],
        out_specs=pl.BlockSpec((units, glow.shape[1]), lambda i: (0, 0)),
        out_shape=jax.ShapeDtypeStruct((units, glow.shape[1]), F32),
        scratch_shapes=[pltpu.VMEM((glow.shape[0], units), F32)],
        compiler_params=params(),
        name="outer_grad",
    )(place, *pieces, glow)


def table_grad(diag):
    reach = WINDOW + BLOCK
    offsets = jnp.arange(reach, dtype=jnp.int32) - (SPAN + BLOCK)
    onehot = (bucket_of(offsets)[:, None] == jnp.arange(BUCKETS, dtype=jnp.int32)[None, :]).astype(F32)
    sums = jnp.dot(diag.reshape(HEADS, reach), onehot, precision=lax.Precision.HIGHEST)
    return sums.T.reshape(BUCKETS * HEADS)


def exchange(value, narrow=0, plane=0, core=0):
    bits = narrow * 8 + plane * 2 + core
    return lax.ppermute(value, ("narrow", "wide"), [(i, i ^ bits) for i in range(32)])


def spread(value):
    return [value] + [exchange(value, narrow=near) for near in range(1, 4)]


def sum_core_kernel(keep_ref, got_ref, *out_refs):
    for quarter, out_ref in enumerate(out_refs):
        out_ref[...] = (keep_ref[quarter].astype(F32) + got_ref[quarter].astype(F32)).astype(BF16)


def sum_four_kernel(a_ref, b_ref, c_ref, d_ref, *out_refs):
    total = a_ref[...].astype(F32) + b_ref[...].astype(F32) + c_ref[...].astype(F32) + d_ref[...].astype(F32)
    if len(out_refs) == 1:
        out_refs[0][...] = total.astype(BF16)
    else:
        for far, out_ref in enumerate(out_refs):
            out_ref[...] = total[far].astype(BF16)


def sum_core(keep, got):
    _, _, rows, columns = keep.shape
    slab = pl.BlockSpec((4, 1, rows, columns), lambda i: (0, i, 0, 0))
    part = pl.BlockSpec((1, rows, columns), lambda i: (i, 0, 0))
    return pl.pallas_call(
        sum_core_kernel,
        grid=(4,),
        in_specs=[slab, slab],
        out_specs=[part] * 4,
        out_shape=[jax.ShapeDtypeStruct((4, rows, columns), BF16)] * 4,
        compiler_params=params(),
        cost_estimate=pl.CostEstimate(flops=0, bytes_accessed=3 * keep.size * 2, transcendentals=0),
        name="sum_core",
    )(keep, got)


def sum_four(parts, outs, name):
    return pl.pallas_call(
        sum_four_kernel,
        grid=(1,),
        in_specs=[whole(part.shape) for part in parts],
        out_specs=[pl.BlockSpec(parts[0].shape[-2:], lambda i: (0, 0))] * outs,
        out_shape=[jax.ShapeDtypeStruct(parts[0].shape[-2:], BF16)] * outs,
        compiler_params=params(),
        cost_estimate=pl.CostEstimate(flops=0, bytes_accessed=10 * parts[0].size, transcendentals=0),
        name=name,
    )(*parts)


def sum_narrow(parts):
    return sum_four(parts, 4, "sum_narrow")


def sum_planes(parts):
    return sum_four(parts, 1, "sum_planes")[0]


def finish_inner_kernel(place_ref, weight_ref, gain_ref, a_ref, b_ref, c_ref, d_ref, out_ref, ggain_ref):
    rows, columns = a_ref.shape
    for near, ref in enumerate((a_ref, b_ref, c_ref, d_ref)):
        quarter = place_ref[2] ^ near
        row = pl.multiple_of((quarter % 2) * rows, rows)
        column = pl.multiple_of((quarter // 2) * columns, 128)
        out_ref[pl.ds(row, rows), pl.ds(column, columns)] = ref[...].astype(F32)
    along = jnp.sum(out_ref[...] * weight_ref[...].astype(F32), -1, keepdims=True)
    ggain_ref[...] = jnp.broadcast_to(along / gain_ref[...].astype(F32), ggain_ref.shape)


def finish_inner(place, weight, gain, parts):
    rows, units = weight.shape
    vmem = pl.BlockSpec(memory_space=pltpu.VMEM)
    return pl.pallas_call(
        finish_inner_kernel,
        in_specs=[smem] + [vmem] * 6,
        out_shape=[jax.ShapeDtypeStruct((rows, units), F32), jax.ShapeDtypeStruct((rows, 128), F32)],
        compiler_params=pltpu.CompilerParams(vmem_limit_bytes=60 * MIB),
        cost_estimate=pl.CostEstimate(flops=0, bytes_accessed=3 * MIB, transcendentals=0),
        name="finish_inner",
    )(place, weight, gain, *parts)


def finish_heads_kernel(place_ref, weight_ref, gain_ref, a_ref, b_ref, c_ref, d_ref, *refs):
    *out_refs, table_ref, ggain_ref, result_ref = refs
    rows = a_ref.shape[0]
    width = weight_ref.shape[2]
    for near, ref in enumerate((a_ref, b_ref, c_ref, d_ref)):
        quarter = place_ref[2] ^ near
        row = pl.multiple_of((quarter % 2) * rows, rows)
        column = pl.multiple_of((quarter // 2) * (2 * width), 128)
        result_ref[pl.ds(row, rows), pl.ds(column, 2 * width)] = ref[:, : 2 * width].astype(F32)

        @pl.when(quarter == 0)
        def _():
            table_ref[...] = ref[0:16, 2 * width :].astype(F32)

    along = jnp.zeros((2 * rows, 1), F32)
    for index, out_ref in enumerate(out_refs):
        grad = result_ref[:, index * width : (index + 1) * width]
        out_ref[...] = grad
        if index < 3:
            along = along + jnp.sum(grad * weight_ref[index].astype(F32), -1, keepdims=True)
    ggain_ref[...] = jnp.broadcast_to(along / gain_ref[...].astype(F32), ggain_ref.shape)


def finish_heads(place, weights, gain, parts):
    _, rows, width = weights.shape
    vmem = pl.BlockSpec(memory_space=pltpu.VMEM)
    return pl.pallas_call(
        finish_heads_kernel,
        in_specs=[smem] + [vmem] * 6,
        out_shape=[jax.ShapeDtypeStruct((rows, width), F32)] * 4
        + [jax.ShapeDtypeStruct((16, 128), F32), jax.ShapeDtypeStruct((rows, 128), F32)],
        scratch_shapes=[pltpu.VMEM((rows, 4 * width), F32)],
        compiler_params=pltpu.CompilerParams(vmem_limit_bytes=60 * MIB),
        cost_estimate=pl.CostEstimate(flops=0, bytes_accessed=3 * MIB, transcendentals=0),
        name="finish_heads",
    )(place, weights, gain, *parts)


def order_small_kernel(place_ref, own_ref, got_ref, out_ref):
    for other, ref in enumerate((own_ref, got_ref)):
        for far in range(4):
            out_ref[pl.ds(owner_of(place_ref, far, other), 1), :] = ref[far, 0:1, :]


def gather_small(place, small):
    line = jnp.broadcast_to(small[None], (8, small.shape[0]))
    planes = jnp.stack([line] + [exchange(line, plane=far) for far in range(1, 4)])
    got = exchange(planes, core=1)
    vmem = pl.BlockSpec(memory_space=pltpu.VMEM)
    return pl.pallas_call(
        order_small_kernel,
        in_specs=[smem, vmem, vmem],
        out_shape=jax.ShapeDtypeStruct((8, small.shape[0]), F32),
        name="order_small",
    )(place, planes, got)


def order_messages_kernel(place_ref, own_ref, got_ref, pooled_ref, lens_ref, left_ref, right_ref):
    for other, ref in enumerate((own_ref, got_ref)):
        for far in range(4):
            for near in range(4):
                device = (place_ref[2] ^ near) * 8 + owner_of(place_ref, far, other)
                start = pl.multiple_of(device * 8, 8)
                piece = ref[far, near].astype(F32)
                left_ref[pl.ds(start, 8), :] = piece[0:8]
                right_ref[pl.ds(start, 8), :] = piece[8:16]
    half = left_ref.shape[1]
    pooled_ref[:, 0:half] = left_ref[...].astype(BF16)
    rest = pooled_ref.shape[1] - half
    pooled_ref[:, half:] = right_ref[:, 0:rest].astype(BF16)
    lens_ref[...] = right_ref[:, rest : rest + 128]


def gather_messages(place, pooled, lens):
    wide = jnp.broadcast_to(lens, (8, 256))
    message = jnp.concatenate([pooled[:, :512], jnp.concatenate([pooled[:, 512:], wide], 1)], 0).astype(BF16)
    near = jnp.stack(spread(message))
    planes = jnp.stack([near] + [exchange(near, plane=far) for far in range(1, 4)])
    got = exchange(planes, core=1)
    vmem = pl.BlockSpec(memory_space=pltpu.VMEM)
    pooled_all, lens_all = pl.pallas_call(
        order_messages_kernel,
        in_specs=[smem, vmem, vmem],
        out_shape=[jax.ShapeDtypeStruct((256, pooled.shape[1]), BF16), jax.ShapeDtypeStruct((256, 128), F32)],
        scratch_shapes=[pltpu.VMEM((256, 512), F32)] * 2,
        name="order_messages",
    )(place, planes, got)
    return pooled_all, lens_all[:, :1]


def tie(first, then):
    first, then = lax.optimization_barrier((first, then))
    return first, then


def gather_heads(narrow, own):
    heads = jnp.stack(own)
    quarter = lax.dynamic_index_in_dim(heads, narrow, 0, keepdims=False)
    far = jnp.stack([exchange(quarter, plane=far) for far in range(1, 4)])
    other = exchange(heads, core=1)
    near = spread(far)
    return far, near, [heads, other] + near + [exchange(piece, core=1) for piece in near]


def forward_far(narrow, inner_weight, outer_weight, project_weight):
    rows = inner_weight.shape[0]
    width = outer_weight.shape[1]
    half = rows // 2
    quarter = jnp.concatenate(
        [
            lax.dynamic_slice_in_dim(inner_weight, narrow * width, width, 1),
            lax.dynamic_slice_in_dim(outer_weight, narrow * rows, rows, 0),
            lax.dynamic_slice_in_dim(project_weight, (narrow % 2) * half, half, 0),
        ]
    )
    return jnp.stack([exchange(quarter, plane=far) for far in range(1, 4)])


def gather_active(place, active_sum):
    share = active_sum.shape[1] // 8
    slabs = active_sum.reshape(8, 4, 2, share).transpose(1, 2, 0, 3)
    order = place[3] ^ jnp.arange(4, dtype=jnp.int32)
    slabs = slabs[order]
    keep = lax.dynamic_index_in_dim(slabs, place[4], 1, keepdims=False)
    got = exchange(lax.dynamic_index_in_dim(slabs, 1 - place[4], 1, keepdims=False), core=1)
    both = jnp.stack([keep, got], 1)
    planes = jnp.stack([both[0]] + [exchange(both[far], plane=far) for far in range(1, 4)])
    return spread(planes)


def layer_specs():
    both = ("narrow", "wide")
    rows, matrix, vector = P(both, None), P("wide", None), P("wide")
    ins = (rows, vector, matrix, matrix, matrix, matrix, vector, vector, matrix, matrix, matrix, rows, P())
    outs = (rows, rows, rows, vector, matrix, matrix, matrix, matrix, vector, vector, matrix, matrix, matrix)
    return ins, outs


def local_permuted(tokens, *arguments):
    *weights_own, lengths, positives = arguments
    attention_gain, query_weight, key_weight, value_weight, output_weight = weights_own[:5]
    bias_table, forward_gain, inner_weight, outer_weight, project_weight = weights_own[5:]
    segs = lengths.shape[1]
    width = tokens.shape[1]
    units = inner_weight.shape[1]
    wide_at = lax.axis_index("wide")
    narrow_at = lax.axis_index("narrow")
    device = narrow_at * 8 + wide_at
    place = jnp.stack([device, wide_at, narrow_at, wide_at // 2, wide_at % 2]).astype(jnp.int32)
    share = attention_gain.shape[0]

    small = jnp.concatenate([attention_gain, forward_gain, bias_table]).astype(F32)
    small = gather_small(place, jnp.pad(small, (0, 256 - small.shape[0])))
    gain_one = small[:, :share].reshape(1, width)
    gain_two = small[:, share : 2 * share].reshape(1, width)
    table = small[:, 2 * share : 2 * share + bias_table.shape[0]].reshape(BUCKETS, HEADS)
    table = jnp.pad(table, ((0, 0), (0, 4))).astype(BF16)
    heads_far, heads_near, head_pieces = gather_heads(narrow_at, (query_weight, key_weight, value_weight, output_weight))
    _, own_forward = tie(heads_far, (inner_weight, outer_weight, project_weight))
    far = forward_far(narrow_at, *own_forward)
    _, far = tie(heads_near, far)
    near = spread(far)
    own_pieces = []
    for own in own_forward:
        own_pieces += [own, exchange(own, core=1)]

    hid, q, k, v, weights = project(place, tokens, gain_one, head_pieces)
    some = attend(lengths, table, q, k, v, 0, 4)
    some, near = tie(some, near)
    near_other = [exchange(piece, core=1) for piece in near]
    mixed, inv, p = attend(lengths, table, q, k, v, 4, 2, some)
    middle, hid_two = output(tokens, mixed, weights, gain_two)
    hidden, slope, active_sum, pooled, wi, wu, wp = forward(
        place, lengths, hid_two, middle, units, own_pieces + near + near_other
    )
    lens = lengths.astype(F32).reshape(segs, 1)
    pooled_all, lens_all = gather_messages(place, pooled[:segs] / lens, lens)
    loss, grad_wp, glow_all, grows = contrast(
        place, pooled_all, lens_all, positives.reshape(-1, 1), wp, project_weight.shape[0]
    )
    glow = jnp.pad(grows.astype(BF16), ((0, 16 - segs), (0, 0)))
    gi, keep, send = inner_grad(lengths, place, glow, wu, slope, hid_two, True)

    got = exchange(send, core=1)
    gmid, gmid_low = middle_grad(lengths, gi, wi, middle, grows, gain_two)
    got, gmid_low = tie(got, gmid_low)
    quarters = sum_core(keep, got)
    arrived = [quarters[0]] + [exchange(quarters[near], narrow=near) for near in range(1, 4)]
    quarters, gmid_low = tie(quarters, gmid_low)
    grad_wo, gm = output_grad(gmid_low, mixed, weights, inv)
    active_pieces = gather_active(place, active_sum[:segs])
    some = attend_grad(lengths, q, k, v, gm, mixed, p, 0, 3)
    some, arrived = tie(some, arrived)
    planes = sum_narrow(arrived)
    arrived = [planes[0]] + [exchange(planes[far], plane=far) for far in range(1, 4)]
    planes, some = tie(planes, some)
    grad_heads, diag = attend_grad(lengths, q, k, v, gm, mixed, p, 3, 3, some)
    grad_heads, arrived = tie(grad_heads, arrived)
    total = sum_planes(arrived)
    grad_table = table_grad(diag).reshape(8, -1)
    rows_table = jnp.pad(grad_table, ((0, 0), (0, 128 - grad_table.shape[1])))
    total, grad_heads = tie(total, grad_heads)
    inner_parts = spread(total)
    keep, send = head_grad(place, hid, grad_heads, grad_wo, rows_table)
    got = exchange(send, core=1)
    quarters = sum_core(keep, got)
    quarters, gmid = tie(quarters, gmid)
    arrived = [quarters[0]] + [exchange(quarters[near], narrow=near) for near in range(1, 4)]
    grad_tokens = token_grad(tokens, gain_one, gmid, grad_heads, weights)
    grad_outer = outer_grad(place, active_pieces, glow_all)
    grad_inner, gain_two_grad = finish_inner(place, inner_weight, forward_gain[:, None], inner_parts)
    planes = sum_narrow(arrived)
    total = sum_planes([planes[0]] + [exchange(planes[far], plane=far) for far in range(1, 4)])
    own_heads = jnp.stack([query_weight, key_weight, value_weight])
    *grads, table_own, gain_one_grad = finish_heads(place, own_heads, attention_gain[:, None], spread(total))
    return (
        hidden,
        grad_tokens,
        loss[:, 0].reshape(1, segs),
        gain_one_grad[:, 0],
        *grads,
        table_own[0, : bias_table.shape[0]],
        gain_two_grad[:, 0],
        grad_inner,
        grad_outer,
        grad_wp,
    )


def local_plain(tokens, *arguments):
    *weights_own, lengths, positives = arguments
    attention_gain, query_weight, key_weight, value_weight, output_weight = weights_own[:5]
    bias_table, forward_gain, inner_weight, outer_weight, project_weight = weights_own[5:]
    both = ("narrow", "wide")
    segs = lengths.shape[1]
    width = tokens.shape[1]
    wide_at = lax.axis_index("wide")
    device = lax.axis_index("narrow") * lax.axis_size("wide") + wide_at
    place = jnp.stack([device, wide_at]).astype(jnp.int32)
    share = attention_gain.shape[0]
    gather = lambda a: lax.all_gather(a, "wide", axis=0, tiled=True)
    small = gather(jnp.concatenate([attention_gain, forward_gain, bias_table])[None])
    gain_one = small[:, :share].reshape(1, width)
    gain_two = small[:, share : 2 * share].reshape(1, width)
    table = jnp.pad(small[:, 2 * share :].reshape(BUCKETS, HEADS), ((0, 0), (0, 4)))
    weights = jnp.stack([gather(w) for w in (query_weight, key_weight, value_weight, output_weight)])
    pieces = [gather(inner_weight), gather(outer_weight), gather(project_weight)]
    hid, q, k, v, weights = project(place, tokens, gain_one, [weights])
    mixed, inv, p = attend(lengths, table, q, k, v, 0, HEADS // 2)
    middle, hid_two = output(tokens, mixed, weights, gain_two)
    hidden, slope, active_sum, pooled, wi, wu, wp = forward(
        place, lengths, hid_two, middle, inner_weight.shape[1], pieces
    )
    lens = lengths.astype(F32).reshape(segs, 1)
    pooled_all = lax.all_gather((pooled[:segs] / lens).astype(BF16), both, axis=0, tiled=True)
    lens_all = lax.all_gather(lens, both, axis=0, tiled=True)
    loss, grad_wp, glow_all, grows = contrast(
        place, pooled_all, lens_all, positives.reshape(-1, 1), wp, project_weight.shape[0]
    )
    active_all = lax.all_gather(active_sum[:segs], both, axis=0, tiled=True)
    active_own = lax.dynamic_slice_in_dim(active_all, wide_at * outer_weight.shape[0], outer_weight.shape[0], 1)
    grad_outer = dot_tn(active_own, glow_all.astype(F32))
    glow = jnp.pad(grows.astype(BF16), ((0, 16 - segs), (0, 0)))
    gi, grad_wi = inner_grad(lengths, place, glow, wu, slope, hid_two, False)
    gmid, gmid_low = middle_grad(lengths, gi, wi, middle, grows, gain_two)
    grad_wo, gm = output_grad(gmid_low, mixed, weights, inv)
    grad_heads, diag = attend_grad(lengths, q, k, v, gm, mixed, p, 0, HEADS // 2)
    grad_tokens = token_grad(tokens, gain_one, gmid, grad_heads, weights)

    def total(grad):
        part = lax.psum_scatter(grad, "wide", scatter_dimension=0, tiled=True)
        return lax.psum(part.astype(F32), "narrow")

    grads = [total(dot_tn(hid, grad).astype(BF16)) for grad in grad_heads] + [total(grad_wo)]
    grad_inner = total(grad_wi)
    table_own = total(table_grad(diag).reshape(lax.axis_size("wide"), -1))[0]
    own_heads = jnp.stack([query_weight, key_weight, value_weight])
    along = jnp.sum(jnp.stack(grads[:3]) * own_heads.astype(F32), (0, 2))
    return (
        hidden,
        grad_tokens,
        loss[:, 0].reshape(1, segs),
        along / attention_gain.astype(F32),
        *grads,
        table_own,
        jnp.sum(grad_inner * inner_weight.astype(F32), 1) / forward_gain.astype(F32),
        grad_inner,
        grad_outer,
        grad_wp,
    )


def solution(mesh):
    ins, outs = layer_specs()
    permuted = (mesh.shape["narrow"], mesh.shape["wide"]) == (4, 8)
    body = local_permuted if permuted else local_plain
    return jax.shard_map(body, mesh=mesh, in_specs=ins, out_specs=outs, check_vma=False)
```

```python
import functools

import jax
import jax.numpy as jnp
from jax import lax
from jax.experimental import pallas as pl
from jax.experimental.pallas import tpu as pltpu
from jax.sharding import PartitionSpec as P

HEADS = 12
HEAD_DIM = 64
BUCKETS = 32
SPAN = 256
BLOCK = 128
WINDOW = BLOCK + 2 * SPAN
CHUNK = 512
TOGETHER = 3

epsilon = 1e-06
logit_scale = 50.0
root_half = 0.7071067811865476
inv_root_tau = 0.3989422804014327
MIB = 1 << 20
F32 = jnp.float32
BF16 = jnp.bfloat16


def dot_nn(left, right):
    return lax.dot_general(left, right, (((1,), (0,)), ((), ())), preferred_element_type=F32)


def dot_nt(left, right):
    return lax.dot_general(left, right, (((1,), (1,)), ((), ())), preferred_element_type=F32)


def dot_tn(left, right):
    return lax.dot_general(left, right, (((0,), (0,)), ((), ())), preferred_element_type=F32)


def split(values):
    high = values.astype(BF16)
    rest = values - high.astype(F32)
    middle = rest.astype(BF16)
    return high, middle, (rest - middle.astype(F32)).astype(BF16)


def split_two(values):
    high = values.astype(BF16)
    return high, (values - high.astype(F32)).astype(BF16)


def bucket_of(offset):
    distance = jnp.abs(offset)
    larger = jnp.full_like(distance, 8)
    for step in range(1, 8):
        larger = larger + (distance * distance >= 64 * 2**step).astype(jnp.int32)
    return jnp.where(distance < 8, distance, larger) + jnp.where(offset > 0, 16, 0)


def bounds_of(lengths_ref, count):
    bounds = []
    total = 0
    for index in range(count):
        total = total + lengths_ref[0, index]
        bounds.append(total)
    return bounds


def segment_of(places, bounds):
    segment = jnp.zeros_like(places)
    for bound in bounds:
        segment = segment + (places >= bound).astype(jnp.int32)
    return segment


def window_of(bounds, start):
    low = 0
    high = bounds[-1]
    for bound in bounds[:-1]:
        low = jnp.where(bound <= start, bound, low)
    for bound in reversed(bounds[:-1]):
        high = jnp.where(bound > start + BLOCK - 1, bound, high)
    first = (low // BLOCK) * BLOCK
    blocks = (high - first + BLOCK - 1) // BLOCK
    return first, blocks


def params(grid=1):
    return pltpu.CompilerParams(vmem_limit_bytes=60 * MIB, dimension_semantics=("arbitrary",) * grid)


def whole(shape):
    return pl.BlockSpec(shape, lambda *_: (0,) * len(shape), pipeline_mode=pl.Buffered(1))


smem = pl.BlockSpec(memory_space=pltpu.SMEM)
anywhere = pl.BlockSpec(memory_space=pl.ANY)


def owner_of(place_ref, far, other):
    return 2 * (place_ref[3] ^ far) + (place_ref[4] ^ other)


def start_copies(pairs, sems, first=0):
    pending = [pltpu.make_async_copy(source, target, sems.at[first + at]) for at, (source, target) in enumerate(pairs)]
    for copy in pending:
        copy.start()
    return pending


def wait_copies(pending):
    for copy in pending:
        copy.wait()


def head_copies(place_ref, refs, whole_ref):
    rows = whole_ref.shape[1] // 8
    mine = pl.ds(0, rows)
    for other in range(2):
        start = pl.multiple_of(owner_of(place_ref, 0, other) * rows, 16)
        yield refs[other].at[:, mine, :], whole_ref.at[:, pl.ds(start, rows), :]
        for near in range(4):
            piece = refs[2 + 4 * other + near]
            for far in range(1, 4):
                start = pl.multiple_of(owner_of(place_ref, far, other) * rows, 16)
                yield piece.at[far - 1, mine, :], whole_ref.at[place_ref[2] ^ near, pl.ds(start, rows), :]


def project_kernel(place_ref, x_ref, gain_ref, *refs):
    *pieces, hid_ref, q_ref, k_ref, v_ref, out_ref, w_ref, sems, out_sem = refs
    step = pl.program_id(0)
    if len(pieces) == 1:
        pairs = [(pieces[0], w_ref)]
    else:
        pairs = list(head_copies(place_ref, pieces, w_ref))
    whole_copy = pltpu.make_async_copy(w_ref, out_ref, out_sem)

    @pl.when(step == 0)
    def _():
        start_copies(pairs, sems)

    x = x_ref[...].astype(F32)
    scale = lax.rsqrt(jnp.mean(x * x, -1, keepdims=True) + epsilon)
    hidden = (x * scale * gain_ref[...].astype(F32)).astype(BF16)
    hid_ref[...] = hidden

    @pl.when(step == 0)
    def _():
        wait_copies([pltpu.make_async_copy(*pair, sems.at[index]) for index, pair in enumerate(pairs)])
        whole_copy.start()

    q_ref[...] = dot_nn(hidden, w_ref[0]).astype(BF16)
    k_ref[...] = dot_nn(hidden, w_ref[1]).astype(BF16)
    v_ref[...] = dot_nn(hidden, w_ref[2]).astype(BF16)

    @pl.when(step == pl.num_programs(0) - 1)
    def _():
        whole_copy.wait()


def project(place, x, gain, pieces):
    rows, width = x.shape
    block = rows // 4
    row_spec = pl.BlockSpec((block, width), lambda i: (i, 0))
    out = jax.ShapeDtypeStruct((rows, width), BF16)
    return pl.pallas_call(
        project_kernel,
        grid=(4,),
        in_specs=[smem, row_spec, whole((1, width))] + [anywhere] * len(pieces),
        out_specs=[row_spec] * 4 + [anywhere],
        out_shape=[out] * 4 + [jax.ShapeDtypeStruct((4, width, width), BF16)],
        scratch_shapes=[
            pltpu.VMEM((4, width, width), BF16),
            pltpu.SemaphoreType.DMA((26,)),
            pltpu.SemaphoreType.DMA(()),
        ],
        compiler_params=params(),
        cost_estimate=pl.CostEstimate(
            flops=6 * rows * width * width, bytes_accessed=10 * rows * width + 16 * width * width, transcendentals=0
        ),
        name="project_heads",
    )(place, x, gain, *pieces)


def attend_kernel(first_pair, lengths_ref, table_ref, q_ref, k_ref, v_ref, *refs):
    mixed_ref, inv_ref, p_ref, rows_ref, tile_ref, segc_ref, segr_ref = refs[-7:]
    together = q_ref.shape[1] // BLOCK
    pair = first_pair + together * pl.program_id(0)
    rows = q_ref.shape[0]
    bounds = bounds_of(lengths_ref, lengths_ref.shape[1])
    reach = WINDOW + BLOCK

    @pl.when(pl.program_id(0) == 0)
    def _():
        segc_ref[...] = segment_of(lax.broadcasted_iota(jnp.int32, segc_ref.shape, 0), bounds)
        segr_ref[...] = segment_of(lax.broadcasted_iota(jnp.int32, segr_ref.shape, 1), bounds)
        offsets = lax.broadcasted_iota(jnp.int32, (BUCKETS, reach), 1) - (SPAN + BLOCK)
        kinds = lax.broadcasted_iota(jnp.int32, (BUCKETS, reach), 0)
        onehot = (bucket_of(offsets) == kinds).astype(F32).astype(BF16)
        rows_ref[...] = dot_tn(table_ref[...], onehot)

    for head in range(2 * together):
        line = rows_ref[pl.ds(2 * pair + head, 1), :]
        skew = pltpu.roll(jnp.broadcast_to(line, (BLOCK, reach)), 0, 1, stride=1, stride_axis=0)
        tile_ref[head] = skew[:, BLOCK:]

    lane = lax.broadcasted_iota(jnp.int32, (BLOCK, BLOCK), 1)
    first_half = lane < HEAD_DIM

    def one(block_index, carry):
        start = pl.multiple_of(block_index * BLOCK, BLOCK)
        first, count = window_of(bounds, start)
        first = pl.multiple_of(first, BLOCK)
        shift = pl.multiple_of(first - start + SPAN, BLOCK)

        def body(blocks):
            size = blocks * BLOCK
            queries = pl.ds(start, BLOCK)
            keys = pl.ds(first, size)
            segc = segc_ref[queries, :]
            segr = segr_ref[0:1, keys]
            same = jnp.concatenate([segc] * blocks, 1) == segr
            wide_lane = lax.broadcasted_iota(jnp.int32, (size, BLOCK), 1) < HEAD_DIM
            scores = []
            for head in range(2 * together):
                lanes = slice(head // 2 * BLOCK, head // 2 * BLOCK + BLOCK)
                mine = first_half if head % 2 == 0 else ~first_half
                q = q_ref[queries, lanes]
                scores.append(dot_nt(jnp.where(mine, q, jnp.zeros_like(q)), k_ref[keys, lanes]))
            raised = []
            for head in range(2 * together):
                score = jnp.where(same, scores[head] + tile_ref[head, :, pl.ds(shift, size)], -1000000000.0)
                power = jnp.exp(score - jnp.max(score, -1, keepdims=True)).astype(BF16)
                p_ref[head, queries, 0:size] = power
                raised.append(power)
            for near in range(together):
                lanes = slice(near * BLOCK, near * BLOCK + BLOCK)
                v = v_ref[keys, lanes]
                one = jnp.ones_like(v)
                left = dot_nn(raised[2 * near], jnp.where(wide_lane, v, one))
                right = dot_nn(raised[2 * near + 1], jnp.where(wide_lane, one, v))
                total = pltpu.roll(jnp.where(first_half, right, left), HEAD_DIM, 1)
                inverse = 1.0 / total
                mixed_ref[queries, lanes] = (jnp.where(first_half, left, right) * inverse).astype(BF16)
                inv_ref[queries, lanes] = inverse

        for blocks in range(1, WINDOW // BLOCK + 1):
            pl.when(count == blocks)(functools.partial(body, blocks))
        return carry

    lax.fori_loop(0, rows // BLOCK, one, 0)


def attend(lengths, table, q, k, v, first_pair, pairs, before=()):
    rows, width = q.shape
    together = TOGETHER if pairs % TOGETHER == 0 and first_pair % TOGETHER == 0 else 1
    column = pl.BlockSpec((rows, BLOCK * together), lambda p: (0, first_pair // together + p))
    return pl.pallas_call(
        functools.partial(attend_kernel, first_pair),
        grid=(pairs // together,),
        in_specs=[smem, whole(table.shape), column, column, column] + [anywhere] * len(before),
        out_specs=[
            column,
            column,
            pl.BlockSpec((2 * together, rows, WINDOW), lambda p: (first_pair // together + p, 0, 0)),
        ],
        out_shape=[
            jax.ShapeDtypeStruct((rows, width), BF16),
            jax.ShapeDtypeStruct((rows, width), F32),
            jax.ShapeDtypeStruct((HEADS, rows, WINDOW), BF16),
        ],
        scratch_shapes=[
            pltpu.VMEM((16, WINDOW + BLOCK), F32),
            pltpu.VMEM((2 * together, BLOCK, WINDOW), F32),
            pltpu.VMEM((rows, BLOCK), jnp.int32),
            pltpu.VMEM((8, rows), jnp.int32),
        ],
        input_output_aliases={5 + index: index for index in range(len(before))},
        compiler_params=params(),
        cost_estimate=pl.CostEstimate(
            flops=pairs * 8 * rows * 512 * 128, bytes_accessed=pairs * 6 * MIB, transcendentals=2 * pairs * rows * 512
        ),
        name="attend",
    )(lengths, table, q, k, v, *before)


def gelu_and_slope(v):
    bell = jnp.exp(-0.5 * v * v)
    t = 1.0 / (1.0 + (0.3275911 * root_half) * jnp.abs(v))
    series = t * (
        0.5 * 0.254829592
        + t * (0.5 * -0.284496736 + t * (0.5 * 1.421413741 + t * (0.5 * -1.453152027 + t * (0.5 * 1.061405429))))
    )
    tail = series * bell
    share = jnp.where(v >= 0.0, 1.0 - tail, tail)
    return v * share, share + v * bell * inv_root_tau


def member_of(lengths_ref, rows, count):
    bounds = bounds_of(lengths_ref, lengths_ref.shape[1])
    segment = segment_of(lax.broadcasted_iota(jnp.int32, (rows, count), 0), bounds)
    return (segment == lax.broadcasted_iota(jnp.int32, (rows, count), 1)).astype(F32).astype(BF16)


def member_rows(lengths_ref, rows, count):
    bounds = bounds_of(lengths_ref, lengths_ref.shape[1])
    segment = segment_of(lax.broadcasted_iota(jnp.int32, (count, rows), 1), bounds)
    return (segment == lax.broadcasted_iota(jnp.int32, (count, rows), 0)).astype(F32).astype(BF16)


def forward_copies(place_ref, refs, inner_ref, outer_ref):
    rows = refs[0].shape[0]
    share, width = refs[2].shape
    inner, outer = [], []
    for other in range(2):
        owner = owner_of(place_ref, 0, other)
        inner.append((refs[other], inner_ref.at[pl.ds(pl.multiple_of(owner * rows, 16), rows), :]))
        outer.append((refs[2 + other], outer_ref.at[pl.ds(pl.multiple_of(owner * share, 16), share), :]))
        for near in range(4):
            piece = refs[4 + 4 * other + near]
            quarter = place_ref[2] ^ near
            for far in range(1, 4):
                owner = owner_of(place_ref, far, other)
                row = pl.ds(pl.multiple_of(owner * rows, 16), rows)
                column = pl.ds(pl.multiple_of(quarter * width, 128), width)
                inner.append((piece.at[far - 1, pl.ds(0, rows), :], inner_ref.at[row, column]))
                row = pl.ds(pl.multiple_of(owner * share + quarter * rows, 16), rows)
                outer.append((piece.at[far - 1, pl.ds(rows, rows), :], outer_ref.at[row, :]))
    return inner, outer


def forward_kernel(place_ref, lengths_ref, x_ref, mixed_ref, gain_ref, heads_ref, *refs):
    *pieces, out_ref, slope_ref, active_sum_ref, pooled_ref, mid_out, hid_out, wi_out, wu_out = refs[:-12]
    total_ref, mid_ref, hid_ref, member_ref, wo_ref, inner_ref, active_ref = refs[-12:-5]
    wi_ref, wu_ref, sems, out_sems, last_sems = refs[-5:]
    step = pl.program_id(0)
    rows = hid_ref.shape[0]
    block = rows // 4
    outs = ((wi_ref, wi_out), (wu_ref, wu_out), (hid_ref, hid_out), (mid_ref, mid_out))
    if len(pieces) == 2:
        groups = [[pair] for pair in zip(pieces, (wi_ref, wu_ref))]
    else:
        groups = forward_copies(place_ref, pieces, wi_ref, wu_ref)
    firsts = [0, len(groups[0])]
    spans = [slice(index * block, (index + 1) * block) for index in range(4)]

    def arrive(index):
        pairs = groups[index]
        wait_copies([pltpu.make_async_copy(*pair, sems.at[firsts[index] + at]) for at, pair in enumerate(pairs)])
        pltpu.make_async_copy(*outs[index], out_sems.at[index]).start()

    @pl.when(step == 0)
    def _():
        output_copy = pltpu.make_async_copy(heads_ref.at[3], wo_ref, last_sems.at[0])
        output_copy.start()
        for group, first in zip(groups, firsts):
            start_copies(group, sems, first)
        member_ref[...] = member_rows(lengths_ref, rows, 16)
        output_copy.wait()
        for span in spans:
            middle = x_ref[span, :].astype(F32) + dot_nn(mixed_ref[span, :], wo_ref[...])
            scale = lax.rsqrt(jnp.mean(middle * middle, -1, keepdims=True) + epsilon)
            total_ref[span, :] = middle
            mid_ref[span, :] = middle
            hid_ref[span, :] = (middle * scale * gain_ref[...].astype(F32)).astype(BF16)
        for index in (2, 3):
            pltpu.make_async_copy(*outs[index], out_sems.at[index]).start()
        arrive(0)

    columns = pl.ds(pl.multiple_of(step * CHUNK, CHUNK), CHUNK)

    def first(span):
        inner_ref[span, :] = dot_nn(hid_ref[span, :], wi_ref[:, columns])

    def second(span):
        for at in range(span.start, span.stop, 32):
            active, slope = gelu_and_slope(inner_ref[at : at + 32, :])
            active_ref[at : at + 32, :] = active.astype(BF16)
            slope_ref[at : at + 32, :] = slope.astype(BF16)

    first(spans[0])
    first(spans[1])
    second(spans[0])

    @pl.when(step == 0)
    def _():
        arrive(1)

    for index, span in enumerate(spans):
        total_ref[span, :] += dot_nn(active_ref[span, :], wu_ref[columns, :])
        if index + 2 < 4:
            first(spans[index + 2])
        if index + 1 < 4:
            second(spans[index + 1])
    active_sum_ref[...] = dot_nn(member_ref[...], active_ref[...])

    @pl.when(step == pl.num_programs(0) - 1)
    def _():
        out_ref[...] = total_ref[...].astype(BF16)
        member = member_ref[...]
        pooled = jnp.zeros(pooled_ref.shape, F32)
        for span in spans:
            for piece in split(total_ref[span, :]):
                pooled = pooled + dot_nn(member[:, span], piece)
        pooled_ref[...] = pooled
        for index, pair in enumerate(outs):
            pltpu.make_async_copy(*pair, out_sems.at[index]).wait()


def forward(place, lengths, x, mixed, gain, heads, units, pieces):
    rows, width = x.shape
    full = whole((rows, width))
    weights = [
        jax.ShapeDtypeStruct((width, units), BF16),
        jax.ShapeDtypeStruct((units, width), BF16),
    ]
    return pl.pallas_call(
        forward_kernel,
        grid=(units // CHUNK,),
        in_specs=[smem, smem, full, full, whole((1, width)), anywhere] + [anywhere] * len(pieces),
        out_specs=[
            pl.BlockSpec((rows, width), lambda i: (0, 0)),
            pl.BlockSpec((rows, CHUNK), lambda i: (0, i)),
            pl.BlockSpec((16, CHUNK), lambda i: (0, i)),
            pl.BlockSpec((16, width), lambda i: (0, 0)),
        ]
        + [anywhere] * 4,
        out_shape=[
            jax.ShapeDtypeStruct((rows, width), BF16),
            jax.ShapeDtypeStruct((rows, units), BF16),
            jax.ShapeDtypeStruct((16, units), F32),
            jax.ShapeDtypeStruct((16, width), F32),
            jax.ShapeDtypeStruct((rows, width), F32),
            jax.ShapeDtypeStruct((rows, width), BF16),
        ]
        + weights,
        scratch_shapes=[
            pltpu.VMEM((rows, width), F32),
            pltpu.VMEM((rows, width), F32),
            pltpu.VMEM((rows, width), BF16),
            pltpu.VMEM((16, rows), BF16),
            pltpu.VMEM((width, width), BF16),
            pltpu.VMEM((rows, CHUNK), F32),
            pltpu.VMEM((rows, CHUNK), BF16),
        ]
        + [pltpu.VMEM(weight.shape, BF16) for weight in weights]
        + [pltpu.SemaphoreType.DMA((52,)), pltpu.SemaphoreType.DMA((4,)), pltpu.SemaphoreType.DMA((1,))],
        compiler_params=params(),
        cost_estimate=pl.CostEstimate(
            flops=4 * rows * width * units, bytes_accessed=30 * MIB, transcendentals=2 * rows * units
        ),
        name="feed_forward",
    )(place, lengths, x, mixed, gain, heads, *pieces)


def contrast_kernel(place_ref, pooled_ref, len_ref, target_ref, *refs):
    *pieces, loss_ref, grad_wp_ref, glow_all_ref, grows_ref, wide_ref, line_ref, full_ref, wp_ref, sems = refs
    count = pooled_ref.shape[0]
    if len(pieces) == 1:
        pairs = [(pieces[0], wp_ref)]
    else:
        pairs = []
        rows = pieces[0].shape[0]
        for far in range(4):
            for other in range(2):
                start = pl.multiple_of(owner_of(place_ref, far, other) * rows, 16)
                source = pieces[2 + other].at[far - 1] if far else pieces[other]
                pairs.append((source, wp_ref.at[pl.ds(start, rows), :]))
    wait_copies(start_copies(pairs, sems))
    first = pl.multiple_of(place_ref[0] * 8, 8)
    pooled = pooled_ref[...]
    projected = dot_nn(pooled, wp_ref[...])
    inverse = lax.rsqrt(jnp.sum(projected * projected, -1, keepdims=True) + epsilon)
    embedded = (projected * inverse).astype(BF16)
    row = lax.broadcasted_iota(jnp.int32, (count, count), 0)
    column = lax.broadcasted_iota(jnp.int32, (count, count), 1)
    logits = logit_scale * dot_nt(embedded, embedded)
    logits = jnp.where(row == column, -1000000000.0, logits)
    hit = column == target_ref[...]
    highest = jnp.max(logits, -1, keepdims=True)
    totals = highest + jnp.log(jnp.sum(jnp.exp(logits - highest), -1, keepdims=True))
    target = jnp.sum(jnp.where(hit, logits, 0.0), -1, keepdims=True)
    line_ref[...] = jnp.broadcast_to(totals - target, line_ref.shape)
    loss_ref[...] = line_ref[pl.ds(first, 8), :]
    grad_logits = (jnp.exp(logits - totals) - hit.astype(F32)).astype(BF16)
    grad_embedded = logit_scale * (dot_nn(grad_logits, embedded) + dot_tn(grad_logits, embedded))
    along = jnp.sum(grad_embedded * projected, -1, keepdims=True)
    grad_projected = inverse * grad_embedded - projected * (inverse * inverse * inverse * along)
    high, middle, low = split(grad_projected)
    full_ref[...] = dot_tn(pooled, high) + dot_tn(pooled, middle) + dot_tn(pooled, low)
    share = grad_wp_ref.shape[0]
    grad_wp_ref[...] = full_ref[pl.ds(pl.multiple_of(place_ref[1] * share, share), share), :]
    wp = wp_ref[...]
    grad_rows = (dot_nt(high, wp) + dot_nt(middle, wp) + dot_nt(low, wp)) / len_ref[...]
    glow_all_ref[...] = grad_rows.astype(BF16)
    wide_ref[...] = grad_rows
    grows_ref[...] = wide_ref[pl.ds(first, 8), :]


def contrast(place, pooled, lens, targets, pieces, share):
    count, width = pooled.shape
    if count > 512 or share % 8:
        return contrast_plain(place, pooled, lens, targets, pieces[0], share)
    return pl.pallas_call(
        contrast_kernel,
        in_specs=[smem] + [pl.BlockSpec(memory_space=pltpu.VMEM)] * 3 + [anywhere] * len(pieces),
        out_specs=[pl.BlockSpec(memory_space=pltpu.VMEM)] * 4,
        out_shape=[
            jax.ShapeDtypeStruct((8, 128), F32),
            jax.ShapeDtypeStruct((share, width), F32),
            jax.ShapeDtypeStruct((count, width), BF16),
            jax.ShapeDtypeStruct((8, width), F32),
        ],
        scratch_shapes=[
            pltpu.VMEM((count, width), F32),
            pltpu.VMEM((count, 128), F32),
            pltpu.VMEM((width, width), F32),
            pltpu.VMEM((width, width), BF16),
            pltpu.SemaphoreType.DMA((8,)),
        ],
        compiler_params=pltpu.CompilerParams(vmem_limit_bytes=60 * MIB),
        cost_estimate=pl.CostEstimate(flops=4 * count * width * width, bytes_accessed=8 * MIB, transcendentals=0),
        name="contrast",
    )(place, pooled, lens, targets, *pieces)


def contrast_plain(place, pooled, lens, targets, wp, share):
    count, width = pooled.shape
    exact = lax.Precision.HIGHEST
    projected = jnp.dot(pooled, wp, preferred_element_type=F32)
    inverse = lax.rsqrt(jnp.sum(projected * projected, -1, keepdims=True) + epsilon)
    embedded = (projected * inverse).astype(BF16)
    numbers = jnp.arange(count, dtype=jnp.int32)
    logits = logit_scale * dot_nt(embedded, embedded)
    logits = jnp.where(numbers[:, None] == numbers[None, :], -1000000000.0, logits)
    hit = numbers[None, :] == targets
    highest = jnp.max(logits, -1, keepdims=True)
    totals = highest + jnp.log(jnp.sum(jnp.exp(logits - highest), -1, keepdims=True))
    loss = totals - jnp.sum(jnp.where(hit, logits, 0.0), -1, keepdims=True)
    grad_logits = (jnp.exp(logits - totals) - hit.astype(F32)).astype(BF16)
    grad_embedded = logit_scale * (dot_nn(grad_logits, embedded) + dot_tn(grad_logits, embedded))
    along = jnp.sum(grad_embedded * projected, -1, keepdims=True)
    grad_projected = inverse * grad_embedded - projected * (inverse * inverse * inverse * along)
    own_columns = lax.dynamic_slice_in_dim(pooled.astype(F32), place[1] * share, share, 1)
    grad_wp = lax.dot_general(own_columns, grad_projected, (((0,), (0,)), ((), ())), precision=exact)
    grad_rows = jnp.dot(grad_projected, wp.astype(F32).T, precision=exact) / lens
    first = place[0] * 8
    own = lambda a: lax.dynamic_slice_in_dim(a, first, 8, 0)
    return jnp.broadcast_to(own(loss), (8, 128)), grad_wp, grad_rows.astype(BF16), own(grad_rows)


def fold(result_ref, keep_ref, send_ref, place_ref, column_half, column):
    narrow, plane, core = place_ref[2], place_ref[3], place_ref[4]
    rows = keep_ref.shape[2]
    for near in range(2):
        quarter = 2 * ((narrow // 2) ^ column_half) + near
        half = (narrow % 2) ^ near
        for far in range(4):
            for ref, owner in ((keep_ref, core), (send_ref, 1 - core)):
                start = pl.multiple_of((2 * (plane ^ far) + owner) * 2 * rows + half * rows, 16)
                block = result_ref[pl.ds(start, rows), :].astype(BF16)
                ref[quarter, far, :, pl.ds(column, block.shape[1])] = block


def back_kernel(
    lengths_ref, place_ref, glow_ref, grows_ref, gain_ref, hid_ref, active_ref, wu_ref, slope_ref, wi_ref,
    mid_any, mixed_any, inv_any, heads_any, gmid_any, gmix_ref, *refs,
):
    *grad_refs, result_ref, total_ref, member_ref, mid_ref, mixed_ref, inv_ref, wo_ref, sems, out_sems = refs
    step = pl.program_id(0)
    last = pl.num_programs(0) - 1
    rows, width = total_ref.shape
    folded = len(grad_refs) == 4
    late = [(mid_any, mid_ref), (mixed_any, mixed_ref), (inv_any, inv_ref), (heads_any.at[3], wo_ref)]

    @pl.when(step == 0)
    def _():
        member = member_of(lengths_ref, rows, 16)
        member_ref[...] = jnp.concatenate([member, member], 1)

    @pl.when(step == 2)
    def _():
        start_copies(late, sems)

    high, low = split_two(dot_nt(glow_ref[...], wu_ref[...]))
    spread = dot_nn(member_ref[...], jnp.concatenate([high, low], 0))
    grad_inner = (spread * slope_ref[...].astype(F32)).astype(BF16)
    part = dot_nt(grad_inner, wi_ref[...])
    result_ref[:, :CHUNK] = dot_tn(hid_ref[...], grad_inner)

    @pl.when(step == 0)
    def _():
        total_ref[...] = part

    @pl.when(step > 0)
    def _():
        total_ref[...] += part

    if folded:
        keep_any, send_any, keep_ref, send_ref = grad_refs
        half = pl.num_programs(0) // 2
        fold(
            result_ref.at[:, 0:CHUNK], keep_ref, send_ref, place_ref, step // half, pl.multiple_of((step % half) * CHUNK, CHUNK)
        )

        @pl.when(step == 0)
        def _():
            share = active_ref.shape[1] // 8
            empty = jnp.zeros((8, 128), F32)
            for far in range(4):
                for ref, other in ((keep_ref, 0), (send_ref, 1)):
                    owner = owner_of(place_ref, far, other)
                    for part_at in range(share // 128):
                        column = pl.multiple_of(owner * share + part_at * 128, 128)
                        sums = active_ref[0:8, pl.ds(column, 128)]
                        block = jnp.concatenate([empty, sums] if other else [sums, empty], 0).astype(BF16)
                        for quarter in range(4):
                            ref[quarter, far, 16 * part_at : 16 * part_at + 16, -128:] = block
    else:
        grad_refs[0][:, pl.ds(pl.multiple_of(step * CHUNK, CHUNK), CHUNK)] = result_ref[:, :CHUNK].astype(BF16)

    @pl.when(step == last)
    def _():
        pending = []
        if folded:
            inner_columns = pl.ds(0, 3 * CHUNK)
            rest = pl.ds(3 * CHUNK, keep_ref.shape[3] - 3 * CHUNK)
            for index, (source, target) in enumerate(((keep_ref, keep_any), (send_ref, send_any))):
                copy = pltpu.make_async_copy(
                    source.at[:, :, :, inner_columns], target.at[:, :, :, inner_columns], out_sems.at[index]
                )
                copy.start()
                pending.append(copy)
        wait_copies([pltpu.make_async_copy(*pair, sems.at[index]) for index, pair in enumerate(late)])
        bounds = bounds_of(lengths_ref, lengths_ref.shape[1])
        block = rows // 8
        for index in range(8):
            span = slice(index * block, (index + 1) * block)
            middle = mid_ref[span, :]
            scale = lax.rsqrt(jnp.mean(middle * middle, -1, keepdims=True) + epsilon)
            normed = middle * scale
            scaled = total_ref[span, :] * gain_ref[...].astype(F32)
            centre = jnp.mean(scaled * normed, -1, keepdims=True)
            segment = segment_of(lax.broadcasted_iota(jnp.int32, (block, 128), 0) + index * block, bounds)
            segment = jnp.concatenate([segment] * (width // 128), 1)
            grad_rows = jnp.zeros((block, width), F32)
            for passage in range(8):
                grad_rows = jnp.where(segment == passage, grows_ref[passage : passage + 1, :], grad_rows)
            total_ref[span, :] = grad_rows + scale * (scaled - normed * centre)
        copy = pltpu.make_async_copy(total_ref, gmid_any, out_sems.at[2])
        copy.start()
        pending.append(copy)
        columns = width // 2
        for side in range(2):
            grad = dot_tn(mixed_ref[...], total_ref[:, side * columns : (side + 1) * columns].astype(BF16))
            if folded:
                result_ref[:, 0:columns] = grad
                fold(result_ref.at[:, 0:columns], keep_ref, send_ref, place_ref, side, 3 * CHUNK)
            else:
                grad_refs[1][:, side * columns : (side + 1) * columns] = grad.astype(BF16)
        if folded:
            for index, (source, target) in enumerate(((keep_ref, keep_any), (send_ref, send_any))):
                copy = pltpu.make_async_copy(source.at[:, :, :, rest], target.at[:, :, :, rest], out_sems.at[3 + index])
                copy.start()
                pending.append(copy)
        for index in range(4):
            span = slice(index * 2 * block, (index + 1) * 2 * block)
            low_rows = total_ref[span, :].astype(BF16)
            gmix_ref[span, :] = (dot_nt(low_rows, wo_ref[...]) * inv_ref[span, :]).astype(BF16)
        wait_copies(pending)


def back(lengths, place, glow, grows, gain, hidden, active_sum, wu, slope, wi, middle, mixed, inv, heads, folded):
    rows, width = hidden.shape
    units = slope.shape[1]
    full = pl.BlockSpec((rows, width), lambda i: (0, 0))
    if folded:
        slabs = [(4, 4, width // 16, units // 2 + width // 2 + 128)] * 2
        grad_shape = [pltpu.HBM(slab, BF16) for slab in slabs]
        grad_specs = [anywhere] * 2
        grad_scratch = [pltpu.VMEM(slab, BF16) for slab in slabs]
    else:
        shapes = [(width, units), (width, width)]
        grad_shape = [jax.ShapeDtypeStruct(shape, BF16) for shape in shapes]
        grad_specs = [pl.BlockSpec(shape, lambda i: (0, 0)) for shape in shapes]
        grad_scratch = []
    return pl.pallas_call(
        back_kernel,
        grid=(units // CHUNK,),
        in_specs=[
            smem,
            smem,
            whole((16, width)),
            whole((8, width)),
            whole((1, width)),
            whole((rows, width)),
            whole(active_sum.shape),
            pl.BlockSpec((CHUNK, width), lambda i: (i, 0)),
            pl.BlockSpec((rows, CHUNK), lambda i: (0, i)),
            pl.BlockSpec((width, CHUNK), lambda i: (0, i)),
        ]
        + [anywhere] * 4,
        out_specs=[anywhere, full] + grad_specs,
        out_shape=[jax.ShapeDtypeStruct((rows, width), F32), jax.ShapeDtypeStruct((rows, width), BF16)] + grad_shape,
        scratch_shapes=grad_scratch
        + [
            pltpu.VMEM((width, CHUNK), F32),
            pltpu.VMEM((rows, width), F32),
            pltpu.VMEM((rows, 32), BF16),
            pltpu.VMEM((rows, width), F32),
            pltpu.VMEM((rows, width), BF16),
            pltpu.VMEM((rows, width), F32),
            pltpu.VMEM((width, width), BF16),
            pltpu.SemaphoreType.DMA((4,)),
            pltpu.SemaphoreType.DMA((5,)),
        ],
        compiler_params=params(),
        cost_estimate=pl.CostEstimate(flops=5 * rows * width * units, bytes_accessed=40 * MIB, transcendentals=0),
        name="back",
    )(lengths, place, glow, grows, gain, hidden, active_sum, wu, slope, wi, middle, mixed, inv, heads)


def attend_grad_kernel(lengths_ref, q_ref, k_ref, v_ref, gm_ref, mixed_ref, p_ref, *refs):
    grad_ref, diag_ref, qm_ref, km_ref, vx_ref, gx_ref, go_ref, ak_ref, av_ref, acc_ref = refs[-10:]
    together = q_ref.shape[1] // BLOCK
    rows = q_ref.shape[0]
    bounds = bounds_of(lengths_ref, lengths_ref.shape[1])
    reach = WINDOW + BLOCK
    acc_ref[...] = jnp.zeros_like(acc_ref)
    ak_ref[...] = jnp.zeros_like(ak_ref)
    av_ref[...] = jnp.zeros_like(av_ref)

    def prepare(index, carry):
        span = pl.ds(pl.multiple_of(index * BLOCK, BLOCK), BLOCK)
        lane = lax.broadcasted_iota(jnp.int32, (BLOCK, BLOCK), 1)
        for near in range(together):
            lanes = slice(near * BLOCK, near * BLOCK + BLOCK)
            q, k, v, g = q_ref[span, lanes], k_ref[span, lanes], v_ref[span, lanes], gm_ref[span, lanes]
            product = g.astype(F32) * mixed_ref[span, lanes].astype(F32)
            for half in range(2):
                head = 2 * near + half
                mine = (lane < HEAD_DIM) if half == 0 else (lane >= HEAD_DIM)
                base = HEAD_DIM * (1 - half)
                zero = jnp.zeros_like(q)
                qm_ref[head, span, :] = jnp.where(mine, q, zero)
                km_ref[head, span, :] = jnp.where(mine, k, zero)
                go_ref[head, span, :] = jnp.where(mine, g, zero)
                vx_ref[head, span, :] = jnp.where(mine, v, jnp.ones_like(v))
                centre = jnp.sum(jnp.where(mine, product, 0.0), -1, keepdims=True)
                high, low = split_two(-centre)
                high, low = high.astype(F32), low.astype(F32)
                extra = jnp.where(lane == base, high, jnp.where(lane == base + 1, low, 0.0))
                gx_ref[head, span, :] = jnp.where(mine, g.astype(F32), extra).astype(BF16)
        return carry

    lax.fori_loop(0, rows // BLOCK, prepare, 0)

    def one(block_index, carry):
        start = pl.multiple_of(block_index * BLOCK, BLOCK)
        first, count = window_of(bounds, start)
        first = pl.multiple_of(first, BLOCK)
        shift = pl.multiple_of(first - start + SPAN, BLOCK)

        def body(blocks):
            size = blocks * BLOCK
            queries = pl.ds(start, BLOCK)
            keys = pl.ds(first, size)
            spread = [dot_nt(gx_ref[head, queries, :], vx_ref[head, keys, :]) for head in range(2 * together)]
            for near in range(together):
                heads = (2 * near, 2 * near + 1)
                lanes = slice(near * BLOCK, near * BLOCK + BLOCK)
                parts = []
                raised = []
                for head in heads:
                    p = p_ref[head, queries, 0:size]
                    grad_scores = p.astype(F32) * spread[head]
                    acc_ref[head, :, pl.ds(shift, size)] += grad_scores
                    parts.append(grad_scores.astype(BF16))
                    raised.append(p)
                q_both = jnp.concatenate([qm_ref[head, queries, :] for head in heads], 0)
                g_both = jnp.concatenate([go_ref[head, queries, :] for head in heads], 0)
                k_both = jnp.concatenate([km_ref[head, keys, :] for head in heads], 0)
                ak_ref[keys, lanes] += dot_tn(jnp.concatenate(parts, 0), q_both)
                av_ref[keys, lanes] += dot_tn(jnp.concatenate(raised, 0), g_both)
                grad_ref[0, queries, lanes] = dot_nn(jnp.concatenate(parts, 1), k_both).astype(BF16)

        for blocks in range(1, WINDOW // BLOCK + 1):
            pl.when(count == blocks)(functools.partial(body, blocks))
        return carry

    lax.fori_loop(0, rows // BLOCK, one, 0)
    grad_ref[1] = ak_ref[...].astype(BF16)
    grad_ref[2] = av_ref[...].astype(BF16)
    for head in range(2 * together):
        padded = jnp.concatenate([jnp.zeros((BLOCK, BLOCK), F32), acc_ref[head]], 1)
        group = padded[0:8]
        for index in range(1, BLOCK // 8):
            group = group + pltpu.roll(padded[8 * index : 8 * index + 8], reach - 8 * index, 1)
        line = group[0:1]
        for index in range(1, 8):
            line = line + pltpu.roll(group, reach - index, 1)[index : index + 1]
        diag_ref[head // 2, head % 2 : head % 2 + 1, :] = line


def attend_grad(lengths, q, k, v, gm, mixed, p, first_pair, pairs, before=()):
    rows, width = q.shape
    together = TOGETHER if pairs % TOGETHER == 0 and first_pair % TOGETHER == 0 else 1
    at = first_pair // together
    column = pl.BlockSpec((rows, BLOCK * together), lambda i: (0, at + i))
    return pl.pallas_call(
        attend_grad_kernel,
        grid=(pairs // together,),
        in_specs=[smem]
        + [column] * 5
        + [pl.BlockSpec((2 * together, rows, WINDOW), lambda i: (at + i, 0, 0))]
        + [anywhere] * len(before),
        out_specs=[
            pl.BlockSpec((3, rows, BLOCK * together), lambda i: (0, 0, at + i)),
            pl.BlockSpec((together, 2, WINDOW + BLOCK), lambda i: (at + i, 0, 0)),
        ],
        out_shape=[
            jax.ShapeDtypeStruct((3, rows, width), BF16),
            jax.ShapeDtypeStruct((HEADS // 2, 2, WINDOW + BLOCK), F32),
        ],
        scratch_shapes=[pltpu.VMEM((2 * together, rows, BLOCK), BF16)] * 5
        + [pltpu.VMEM((rows, BLOCK * together), F32)] * 2
        + [pltpu.VMEM((2 * together, BLOCK, WINDOW), F32)],
        input_output_aliases={7 + index: index for index in range(len(before))},
        compiler_params=params(),
        cost_estimate=pl.CostEstimate(
            flops=pairs * 20 * rows * 512 * 64, bytes_accessed=pairs * 5 * MIB, transcendentals=0
        ),
        name="attend_grad",
    )(lengths, q, k, v, gm, mixed, p, *before)


def head_grad_kernel(place_ref, hid_ref, grad_ref, table_ref, keep_ref, send_ref, result_ref):
    step = pl.program_id(0)
    half = pl.num_programs(0) // 2
    block = result_ref.shape[1]
    result_ref[...] = dot_tn(hid_ref[...], grad_ref[0])
    fold(result_ref, keep_ref, send_ref, place_ref, step // half, pl.multiple_of((step % half) * block, 128))

    @pl.when(step == 0)
    def _():
        rows = keep_ref.shape[2]
        for far in range(4):
            for ref, other in ((keep_ref, 0), (send_ref, 1)):
                line = table_ref[pl.ds(owner_of(place_ref, far, other), 1), :]
                block_of = jnp.broadcast_to(line, (rows, 128)).astype(BF16)
                for quarter in range(4):
                    ref[quarter, far, :, half * block :] = block_of


def head_grad(place, hidden, grads, table):
    rows, width = hidden.shape
    block = width // 2
    slab = (4, 4, width // 16, 3 * block + 128)
    return pl.pallas_call(
        head_grad_kernel,
        grid=(6,),
        in_specs=[
            smem,
            whole((rows, width)),
            pl.BlockSpec((1, rows, block), lambda i: (i // 2, 0, i % 2)),
            whole(table.shape),
        ],
        out_specs=[pl.BlockSpec(slab, lambda i: (0, 0, 0, 0))] * 2,
        out_shape=[pltpu.HBM(slab, BF16)] * 2,
        scratch_shapes=[pltpu.VMEM((width, block), F32)],
        compiler_params=params(),
        cost_estimate=pl.CostEstimate(flops=6 * rows * width * width, bytes_accessed=12 * MIB, transcendentals=0),
        name="head_grad",
    )(place, hidden, grads, table)


def token_grad_kernel(x_ref, gain_ref, gmid_ref, grad_ref, w_ref, out_ref):
    x = x_ref[...].astype(F32)
    scale = lax.rsqrt(jnp.mean(x * x, -1, keepdims=True) + epsilon)
    normed = x * scale
    grad_hidden = dot_nt(grad_ref[0], w_ref[0]) + dot_nt(grad_ref[1], w_ref[1]) + dot_nt(grad_ref[2], w_ref[2])
    scaled = grad_hidden * gain_ref[...].astype(F32)
    centre = jnp.mean(scaled * normed, -1, keepdims=True)
    out_ref[...] = gmid_ref[...] + scale * (scaled - normed * centre)


def token_grad(x, gain, gmid, grads, weights):
    rows, width = x.shape
    block = rows // 4
    row_spec = pl.BlockSpec((block, width), lambda i: (i, 0))
    return pl.pallas_call(
        token_grad_kernel,
        grid=(4,),
        in_specs=[
            row_spec,
            whole((1, width)),
            row_spec,
            pl.BlockSpec((3, block, width), lambda i: (0, i, 0)),
            whole((3, width, width)),
        ],
        out_specs=row_spec,
        out_shape=jax.ShapeDtypeStruct((rows, width), F32),
        compiler_params=params(),
        cost_estimate=pl.CostEstimate(flops=6 * rows * width * width, bytes_accessed=16 * MIB, transcendentals=0),
        name="token_grad",
    )(x, gain, gmid, grads, weights)


def outer_grad_kernel(place_ref, pieces_ref, glow_ref, out_ref, active_ref):
    for far in range(4):
        for near in range(4):
            for part in range(active_ref.shape[1] // 128):
                block = pieces_ref[far, 16 * part : 16 * part + 16, 128 * near : 128 * near + 128].astype(F32)
                for other in range(2):
                    device = (place_ref[2] ^ near) * 8 + owner_of(place_ref, far, other)
                    start = pl.multiple_of(device * 8, 8)
                    active_ref[pl.ds(start, 8), 128 * part : 128 * part + 128] = block[8 * other : 8 * other + 8]
    out_ref[...] = dot_tn(active_ref[...].astype(BF16), glow_ref[...])


def outer_grad(place, pieces, glow):
    count, width = glow.shape
    units = 8 * pieces.shape[1]
    return pl.pallas_call(
        outer_grad_kernel,
        grid=(1,),
        in_specs=[smem, whole(pieces.shape), whole(glow.shape)],
        out_specs=pl.BlockSpec((units, width), lambda i: (0, 0)),
        out_shape=jax.ShapeDtypeStruct((units, width), F32),
        scratch_shapes=[pltpu.VMEM((count, units), F32)],
        compiler_params=params(),
        cost_estimate=pl.CostEstimate(flops=2 * count * units * width, bytes_accessed=3 * MIB, transcendentals=0),
        name="outer_grad",
    )(place, pieces, glow)


def table_grad(diag):
    reach = WINDOW + BLOCK
    offsets = jnp.arange(reach, dtype=jnp.int32) - (SPAN + BLOCK)
    onehot = (bucket_of(offsets)[:, None] == jnp.arange(BUCKETS, dtype=jnp.int32)[None, :]).astype(F32)
    sums = jnp.dot(diag.reshape(HEADS, reach), onehot, precision=lax.Precision.HIGHEST)
    return sums.T.reshape(BUCKETS * HEADS)


def exchange(value, narrow=0, plane=0, core=0):
    bits = narrow * 8 + plane * 2 + core
    return lax.ppermute(value, ("narrow", "wide"), [(i, i ^ bits) for i in range(32)])


def spread(value):
    return [value] + [exchange(value, narrow=near) for near in range(1, 4)]


def sum_core_kernel(*refs):
    pairs, out_refs = refs[:-4], refs[-4:]
    for quarter, out_ref in enumerate(out_refs):
        column = 0
        tail = None
        for keep_ref, got_ref in zip(pairs[0::2], pairs[1::2]):
            total = (keep_ref[quarter].astype(F32) + got_ref[quarter].astype(F32)).astype(BF16)
            if tail is None:
                tail = total[:, :, -128:]
                total = total[:, :, :-128]
            out_ref[:, :, column : column + total.shape[2]] = total
            column += total.shape[2]
        out_ref[:, :, column:] = tail


def sum_core(*pairs):
    rows = pairs[0].shape[2]
    columns = sum(array.shape[3] for array in pairs[0::2])
    specs = [pl.BlockSpec((4, 1) + array.shape[2:], lambda i: (0, i, 0, 0)) for array in pairs]
    return pl.pallas_call(
        sum_core_kernel,
        grid=(4,),
        in_specs=specs,
        out_specs=[pl.BlockSpec((1, rows, columns), lambda i: (i, 0, 0))] * 4,
        out_shape=[pltpu.HBM((4, rows, columns), BF16)] * 4,
        compiler_params=params(),
        cost_estimate=pl.CostEstimate(flops=0, bytes_accessed=96 * rows * columns, transcendentals=0),
        name="sum_core",
    )(*pairs)


def sum_narrow_kernel(apart, a_ref, b_ref, c_ref, d_ref, *out_refs):
    refs = (a_ref, b_ref, c_ref, d_ref)
    columns = a_ref.shape[2] - (128 if apart else 0)
    for far, out_ref in enumerate(out_refs):
        total = sum(ref[far, :, :columns].astype(F32) for ref in refs)
        out_ref[:, :columns] = total.astype(BF16)
        if apart:
            for near, ref in enumerate(refs):
                out_ref[:, columns + 128 * near : columns + 128 * near + 128] = ref[far, :, columns:]


def sum_narrow(parts, apart):
    _, rows, columns = parts[0].shape
    columns += 3 * 128 if apart else 0
    return pl.pallas_call(
        functools.partial(sum_narrow_kernel, apart),
        grid=(1,),
        in_specs=[whole(part.shape) for part in parts],
        out_specs=[pl.BlockSpec((rows, columns), lambda i: (0, 0))] * 4,
        out_shape=[pltpu.HBM((rows, columns), BF16)] * 4,
        compiler_params=params(),
        cost_estimate=pl.CostEstimate(flops=0, bytes_accessed=40 * rows * columns, transcendentals=0),
        name="sum_narrow",
    )(*parts)


def sum_planes_kernel(a_ref, b_ref, c_ref, d_ref, total_ref, *apart_refs):
    refs = (a_ref, b_ref, c_ref, d_ref)
    columns = total_ref.shape[1]
    total_ref[...] = sum(ref[:, :columns].astype(F32) for ref in refs).astype(BF16)
    for apart_ref in apart_refs:
        for far, ref in enumerate(refs):
            apart_ref[far] = ref[:, columns:]


def sum_planes(parts, apart):
    rows, columns = parts[0].shape
    kept = 4 * 128 if apart else 0
    out_specs = [pl.BlockSpec((rows, columns - kept), lambda i: (0, 0))]
    out_shape = [pltpu.HBM((rows, columns - kept), BF16)]
    if apart:
        out_specs.append(pl.BlockSpec((4, rows, kept), lambda i: (0, 0, 0)))
        out_shape.append(jax.ShapeDtypeStruct((4, rows, kept), BF16))
    return pl.pallas_call(
        sum_planes_kernel,
        grid=(1,),
        in_specs=[whole(part.shape) for part in parts],
        out_specs=out_specs,
        out_shape=out_shape,
        compiler_params=params(),
        cost_estimate=pl.CostEstimate(flops=0, bytes_accessed=10 * rows * columns, transcendentals=0),
        name="sum_planes",
    )(*parts)


def finish_inner_kernel(place_ref, weight_ref, gain_ref, a_ref, b_ref, c_ref, d_ref, out_ref, last_ref, ggain_ref):
    rows = a_ref.shape[0]
    units = weight_ref.shape[1] // 2
    width = last_ref.shape[1] // 2
    for near, ref in enumerate((a_ref, b_ref, c_ref, d_ref)):
        quarter = place_ref[2] ^ near
        row = pl.ds(pl.multiple_of((quarter % 2) * rows, rows), rows)
        half = quarter // 2
        out_ref[row, pl.ds(pl.multiple_of(half * units, 128), units)] = ref[:, :units].astype(F32)
        last_ref[row, pl.ds(pl.multiple_of(half * width, 128), width)] = ref[:, units:].astype(F32)
    along = jnp.sum(out_ref[...] * weight_ref[...].astype(F32), -1, keepdims=True)
    ggain_ref[...] = jnp.broadcast_to(along / gain_ref[...].astype(F32), ggain_ref.shape)


def finish_inner(place, weight, gain, parts, width):
    rows, units = weight.shape
    ins = [weight, gain] + list(parts)
    outs = [jax.ShapeDtypeStruct((rows, columns), F32) for columns in (units, width, 128)]
    return pl.pallas_call(
        finish_inner_kernel,
        grid=(1,),
        in_specs=[smem] + [whole(array.shape) for array in ins],
        out_specs=[pl.BlockSpec(out.shape, lambda i: (0, 0)) for out in outs],
        out_shape=outs,
        compiler_params=params(),
        cost_estimate=pl.CostEstimate(flops=0, bytes_accessed=3 * MIB, transcendentals=0),
        name="finish_inner",
    )(place, *ins)


def finish_heads_kernel(place_ref, weight_ref, gain_ref, a_ref, b_ref, c_ref, d_ref, *refs):
    *out_refs, table_ref, ggain_ref, result_ref = refs
    rows = a_ref.shape[0]
    width = weight_ref.shape[2]
    half = 3 * width // 2
    for near, ref in enumerate((a_ref, b_ref, c_ref, d_ref)):
        quarter = place_ref[2] ^ near
        row = pl.multiple_of((quarter % 2) * rows, rows)
        column = pl.multiple_of((quarter // 2) * half, 128)
        result_ref[pl.ds(row, rows), pl.ds(column, half)] = ref[:, :half].astype(F32)

        @pl.when(quarter == 0)
        def _():
            table_ref[...] = ref[0:16, half:].astype(F32)

    along = jnp.zeros((2 * rows, 1), F32)
    for index, out_ref in enumerate(out_refs):
        grad = result_ref[:, index * width : (index + 1) * width]
        out_ref[...] = grad
        along = along + jnp.sum(grad * weight_ref[index].astype(F32), -1, keepdims=True)
    ggain_ref[...] = jnp.broadcast_to(along / gain_ref[...].astype(F32), ggain_ref.shape)


def finish_heads(place, weights, gain, parts):
    _, rows, width = weights.shape
    ins = [weights, gain] + list(parts)
    outs = [jax.ShapeDtypeStruct((rows, width), F32)] * 3
    outs += [jax.ShapeDtypeStruct((16, 128), F32), jax.ShapeDtypeStruct((rows, 128), F32)]
    return pl.pallas_call(
        finish_heads_kernel,
        grid=(1,),
        in_specs=[smem] + [whole(array.shape) for array in ins],
        out_specs=[pl.BlockSpec(out.shape, lambda i: (0, 0)) for out in outs],
        out_shape=outs,
        scratch_shapes=[pltpu.VMEM((rows, 3 * width), F32)],
        compiler_params=params(),
        cost_estimate=pl.CostEstimate(flops=0, bytes_accessed=3 * MIB, transcendentals=0),
        name="finish_heads",
    )(place, *ins)


def order_small_kernel(place_ref, own_ref, got_ref, out_ref):
    for other, ref in enumerate((own_ref, got_ref)):
        for far in range(4):
            out_ref[pl.ds(owner_of(place_ref, far, other), 1), :] = ref[far, 0:1, :]


def order_small(place, own, got):
    return pl.pallas_call(
        order_small_kernel,
        grid=(1,),
        in_specs=[smem, whole(own.shape), whole(got.shape)],
        out_specs=pl.BlockSpec((8, own.shape[2]), lambda i: (0, 0)),
        out_shape=jax.ShapeDtypeStruct((8, own.shape[2]), F32),
        name="order_small",
    )(place, own, got)


def order_messages_kernel(place_ref, own_ref, got_ref, pooled_ref, lens_ref, left_ref, right_ref):
    for other, ref in enumerate((own_ref, got_ref)):
        for far in range(4):
            for near in range(4):
                device = (place_ref[2] ^ near) * 8 + owner_of(place_ref, far, other)
                start = pl.multiple_of(device * 8, 8)
                piece = ref[far, near].astype(F32)
                left_ref[pl.ds(start, 8), :] = piece[0:8]
                right_ref[pl.ds(start, 8), :] = piece[8:16]
    half = left_ref.shape[1]
    pooled_ref[:, 0:half] = left_ref[...].astype(BF16)
    rest = pooled_ref.shape[1] - half
    pooled_ref[:, half:] = right_ref[:, 0:rest].astype(BF16)
    lens_ref[...] = right_ref[:, rest : rest + 128]


def gather_messages(place, pooled, lens):
    wide = jnp.broadcast_to(lens, (8, 256))
    message = jnp.concatenate([pooled[:, :512], jnp.concatenate([pooled[:, 512:], wide], 1)], 0).astype(BF16)
    near = jnp.stack(spread(message))
    planes = jnp.stack([near] + [exchange(near, plane=far) for far in range(1, 4)])
    got = exchange(planes, core=1)
    vmem = pl.BlockSpec(memory_space=pltpu.VMEM)
    pooled_all, lens_all = pl.pallas_call(
        order_messages_kernel,
        in_specs=[smem, vmem, vmem],
        out_shape=[jax.ShapeDtypeStruct((256, pooled.shape[1]), BF16), jax.ShapeDtypeStruct((256, 128), F32)],
        scratch_shapes=[pltpu.VMEM((256, 512), F32)] * 2,
        name="order_messages",
    )(place, planes, got)
    return pooled_all, lens_all[:, :1]


def tie(first, then):
    first, then = lax.optimization_barrier((first, then))
    return first, then


def gather_heads(place, own, small):
    rows, width = own[0].shape
    line = jnp.broadcast_to(jnp.pad(small, (0, width - small.shape[0])), (8, width))
    heads = jnp.stack([jnp.concatenate([weight, line]) for weight in own])
    quarter = lax.dynamic_index_in_dim(heads, place[2], 0, keepdims=False)
    far = jnp.stack([exchange(quarter, plane=distance) for distance in range(1, 4)])
    far, heads = tie(far, heads)
    near = spread(far)
    other = exchange(heads, core=1)
    far_other = exchange(far, core=1)
    lines = lambda first, rest: jnp.concatenate([first[:1, rows:, :256], rest[:, rows:, :256]]).astype(F32)
    ordered = order_small(place, lines(heads, far), lines(other, far_other))
    return near, [heads, other], far_other, ordered


def forward_far(narrow, inner_weight, outer_weight):
    rows = inner_weight.shape[0]
    width = outer_weight.shape[1]
    quarter = jnp.concatenate(
        [
            lax.dynamic_slice_in_dim(inner_weight, narrow * width, width, 1),
            lax.dynamic_slice_in_dim(outer_weight, narrow * rows, rows, 0),
        ]
    )
    return [exchange(quarter, plane=far) for far in range(1, 4)]


def layer_specs():
    both = ("narrow", "wide")
    rows, matrix, vector = P(both, None), P("wide", None), P("wide")
    ins = (rows, vector, matrix, matrix, matrix, matrix, vector, vector, matrix, matrix, matrix, rows, P())
    outs = (rows, rows, rows, vector, matrix, matrix, matrix, matrix, vector, vector, matrix, matrix, matrix)
    return ins, outs


def local_permuted(tokens, *arguments):
    *weights_own, lengths, positives = arguments
    attention_gain, query_weight, key_weight, value_weight, output_weight = weights_own[:5]
    bias_table, forward_gain, inner_weight, outer_weight, project_weight = weights_own[5:]
    segs = lengths.shape[1]
    width = tokens.shape[1]
    units = inner_weight.shape[1]
    wide_at = lax.axis_index("wide")
    narrow_at = lax.axis_index("narrow")
    device = narrow_at * 8 + wide_at
    place = jnp.stack([device, wide_at, narrow_at, wide_at // 2, wide_at % 2]).astype(jnp.int32)
    share = attention_gain.shape[0]

    own_heads = (query_weight, key_weight, value_weight, output_weight)
    small = jnp.concatenate([attention_gain, forward_gain, bias_table])
    near, both_heads, far_other, small = gather_heads(place, own_heads, small)
    gain_one = small[:, :share].reshape(1, width)
    gain_two = small[:, share : 2 * share].reshape(1, width)
    table = small[:, 2 * share : 2 * share + bias_table.shape[0]].reshape(BUCKETS, HEADS)
    table = jnp.pad(table, ((0, 0), (0, 4))).astype(BF16)
    _, own_forward = tie(both_heads[1], (inner_weight, outer_weight))
    far = jnp.stack(forward_far(narrow_at, *own_forward))
    (gain_one, gain_two, table), near = tie((gain_one, gain_two, table), near)
    near, far = tie(near, far)
    head_pieces = both_heads + near + [far_other] + [exchange(piece, core=1) for piece in near[1:]]
    near = spread(far)
    own_pieces = []
    for own in own_forward:
        own_pieces += [own, exchange(own, core=1)]

    hid, q, k, v, weights = project(place, tokens, gain_one, head_pieces)
    mixed, inv, p = attend(lengths, table, q, k, v, 0, 6)
    mixed, near, last_own = lax.optimization_barrier((mixed, near, project_weight))
    near_other = [exchange(piece, core=1) for piece in near]
    last_other = exchange(last_own, core=1)
    last_far = [exchange(last_own, plane=far) for far in range(1, 4)]
    hidden, slope, active_sum, pooled, middle, hid_two, wi, wu = forward(
        place, lengths, tokens, mixed, gain_two, weights, units, own_pieces + near + near_other
    )
    lens = lengths.astype(F32).reshape(segs, 1)
    hidden, last_far = tie(hidden, last_far)
    last_far = jnp.stack(last_far)
    last_pieces = [last_own, last_other, last_far, exchange(last_far, core=1)]
    pooled_all, lens_all = gather_messages(place, pooled[:segs] / lens, lens)
    loss, grad_wp, glow_all, grows = contrast(
        place, pooled_all, lens_all, positives.reshape(-1, 1), last_pieces, project_weight.shape[0]
    )
    glow = jnp.pad(grows.astype(BF16), ((0, 16 - segs), (0, 0)))
    gmid, gm, keep, send = back(
        lengths, place, glow, grows, gain_two, hid_two, active_sum, wu, slope, wi, middle, mixed, inv, weights, True
    )

    got = exchange(send, core=1)
    some = attend_grad(lengths, q, k, v, gm, mixed, p, 0, 3)
    some, got = tie(some, got)
    quarters = sum_core(keep, got)
    quarters, some = tie(quarters, some)
    arrived = [quarters[0]] + [exchange(quarters[near], narrow=near) for near in range(1, 4)]
    grad_heads, diag = attend_grad(lengths, q, k, v, gm, mixed, p, 3, 3, some)
    grad_table = table_grad(diag).reshape(8, -1)
    rows_table = jnp.pad(grad_table, ((0, 0), (0, 128 - grad_table.shape[1])))
    keep, send = head_grad(place, hid, grad_heads, rows_table)
    keep, send, arrived = lax.optimization_barrier((keep, send, arrived))
    got = exchange(send, core=1)
    planes = sum_narrow(arrived, True)
    inner_far = [planes[0]] + [exchange(planes[far], plane=far) for far in range(1, 4)]
    planes, got = tie(planes, got)
    quarters = sum_core(keep, got)
    quarters, gmid = tie(quarters, gmid)
    arrived = [quarters[0]] + [exchange(quarters[near], narrow=near) for near in range(1, 4)]
    grad_tokens = token_grad(tokens, gain_one, gmid, grad_heads, weights)
    grad_tokens, inner_far = tie(grad_tokens, inner_far)
    total, active_pieces = sum_planes(inner_far, True)
    inner_parts = spread(total)
    grad_outer = outer_grad(place, active_pieces, glow_all)
    grad_outer, arrived = tie(grad_outer, arrived)
    planes = sum_narrow(arrived, False)
    planes, inner_parts = tie(planes, inner_parts)
    arrived = [planes[0]] + [exchange(planes[far], plane=far) for far in range(1, 4)]
    grad_inner, grad_out, gain_two_grad = finish_inner(place, inner_weight, forward_gain[:, None], inner_parts, width)
    grad_inner, arrived = tie(grad_inner, arrived)
    (total,) = sum_planes(arrived, False)
    *grads, table_own, gain_one_grad = finish_heads(
        place, jnp.stack(own_heads[:3]), attention_gain[:, None], spread(total)
    )
    grads.append(grad_out)
    return (
        hidden,
        grad_tokens,
        loss[:, 0].reshape(1, segs),
        gain_one_grad[:, 0],
        *grads,
        table_own[0, : bias_table.shape[0]],
        gain_two_grad[:, 0],
        grad_inner,
        grad_outer,
        grad_wp,
    )


def local_plain(tokens, *arguments):
    *weights_own, lengths, positives = arguments
    attention_gain, query_weight, key_weight, value_weight, output_weight = weights_own[:5]
    bias_table, forward_gain, inner_weight, outer_weight, project_weight = weights_own[5:]
    both = ("narrow", "wide")
    segs = lengths.shape[1]
    width = tokens.shape[1]
    wide_at = lax.axis_index("wide")
    device = lax.axis_index("narrow") * lax.axis_size("wide") + wide_at
    place = jnp.stack([device, wide_at]).astype(jnp.int32)
    share = attention_gain.shape[0]
    gather = lambda a: lax.all_gather(a, "wide", axis=0, tiled=True)
    small = gather(jnp.concatenate([attention_gain, forward_gain, bias_table])[None])
    gain_one = small[:, :share].reshape(1, width)
    gain_two = small[:, share : 2 * share].reshape(1, width)
    table = jnp.pad(small[:, 2 * share :].reshape(BUCKETS, HEADS), ((0, 0), (0, 4)))
    weights = jnp.stack([gather(w) for w in (query_weight, key_weight, value_weight, output_weight)])
    pieces = [gather(inner_weight), gather(outer_weight)]
    hid, q, k, v, weights = project(place, tokens, gain_one, [weights])
    mixed, inv, p = attend(lengths, table, q, k, v, 0, HEADS // 2)
    hidden, slope, active_sum, pooled, middle, hid_two, wi, wu = forward(
        place, lengths, tokens, mixed, gain_two, weights, inner_weight.shape[1], pieces
    )
    lens = lengths.astype(F32).reshape(segs, 1)
    pooled_all = lax.all_gather((pooled[:segs] / lens).astype(BF16), both, axis=0, tiled=True)
    lens_all = lax.all_gather(lens, both, axis=0, tiled=True)
    loss, grad_wp, glow_all, grows = contrast(
        place, pooled_all, lens_all, positives.reshape(-1, 1), [gather(project_weight)], project_weight.shape[0]
    )
    active_all = lax.all_gather(active_sum[:segs], both, axis=0, tiled=True)
    active_own = lax.dynamic_slice_in_dim(active_all, wide_at * outer_weight.shape[0], outer_weight.shape[0], 1)
    grad_outer = dot_tn(active_own, glow_all.astype(F32))
    glow = jnp.pad(grows.astype(BF16), ((0, 16 - segs), (0, 0)))
    gmid, gm, grad_wi, grad_wo = back(
        lengths, place, glow, grows, gain_two, hid_two, active_sum, wu, slope, wi, middle, mixed, inv, weights, False
    )
    grad_heads, diag = attend_grad(lengths, q, k, v, gm, mixed, p, 0, HEADS // 2)
    grad_tokens = token_grad(tokens, gain_one, gmid, grad_heads, weights)

    def total(grad):
        part = lax.psum_scatter(grad, "wide", scatter_dimension=0, tiled=True)
        return lax.psum(part.astype(F32), "narrow")

    grads = [total(dot_tn(hid, grad).astype(BF16)) for grad in grad_heads] + [total(grad_wo)]
    grad_inner = total(grad_wi)
    table_own = total(table_grad(diag).reshape(lax.axis_size("wide"), -1))[0]
    own_heads = jnp.stack([query_weight, key_weight, value_weight])
    along = jnp.sum(jnp.stack(grads[:3]) * own_heads.astype(F32), (0, 2))
    return (
        hidden,
        grad_tokens,
        loss[:, 0].reshape(1, segs),
        along / attention_gain.astype(F32),
        *grads,
        table_own,
        jnp.sum(grad_inner * inner_weight.astype(F32), 1) / forward_gain.astype(F32),
        grad_inner,
        grad_outer,
        grad_wp,
    )


def solution(mesh):
    ins, outs = layer_specs()
    permuted = (mesh.shape["narrow"], mesh.shape["wide"]) == (4, 8)
    body = local_permuted if permuted else local_plain
    return jax.shard_map(body, mesh=mesh, in_specs=ins, out_specs=outs, check_vma=False)
```

```python
import functools

import jax
import jax.numpy as jnp
from jax import lax
from jax.experimental import pallas as pl
from jax.experimental.pallas import tpu as pltpu
from jax.sharding import PartitionSpec as P

HEADS = 12
HEAD_DIM = 64
BUCKETS = 32
SPAN = 256
BLOCK = 128
WINDOW = BLOCK + 2 * SPAN
SLOTS = 4
CHUNK = 512

epsilon = 1e-06
logit_scale = 50.0
root_half = 0.7071067811865476
inv_root_tau = 0.3989422804014327
MIB = 1 << 20
F32 = jnp.float32
BF16 = jnp.bfloat16


def dot_nn(left, right):
    return lax.dot_general(left, right, (((1,), (0,)), ((), ())), preferred_element_type=F32)


def dot_nt(left, right):
    return lax.dot_general(left, right, (((1,), (1,)), ((), ())), preferred_element_type=F32)


def dot_tn(left, right):
    return lax.dot_general(left, right, (((0,), (0,)), ((), ())), preferred_element_type=F32)


def split(values):
    high = values.astype(BF16)
    rest = values - high.astype(F32)
    middle = rest.astype(BF16)
    return high, middle, (rest - middle.astype(F32)).astype(BF16)


def split_two(values):
    high = values.astype(BF16)
    return high, (values - high.astype(F32)).astype(BF16)


def bucket_of(offset):
    distance = jnp.abs(offset)
    larger = jnp.full_like(distance, 8)
    for step in range(1, 8):
        larger = larger + (distance * distance >= 64 * 2**step).astype(jnp.int32)
    return jnp.where(distance < 8, distance, larger) + jnp.where(offset > 0, 16, 0)


def bounds_of(lengths_ref, count):
    bounds = []
    total = 0
    for index in range(count):
        total = total + lengths_ref[0, index]
        bounds.append(total)
    return bounds


def segment_of(places, bounds):
    segment = jnp.zeros_like(places)
    for bound in bounds:
        segment = segment + (places >= bound).astype(jnp.int32)
    return segment


def window_of(bounds, start):
    low = 0
    high = bounds[-1]
    for bound in bounds[:-1]:
        low = jnp.where(bound <= start, bound, low)
    for bound in reversed(bounds[:-1]):
        high = jnp.where(bound > start + BLOCK - 1, bound, high)
    first = (low // BLOCK) * BLOCK
    blocks = (high - first + BLOCK - 1) // BLOCK
    return first, blocks


def params(mib=60, grid=1):
    return pltpu.CompilerParams(vmem_limit_bytes=mib * MIB, dimension_semantics=("arbitrary",) * grid)


def whole(shape):
    return pl.BlockSpec(shape, lambda *_: (0,) * len(shape), pipeline_mode=pl.Buffered(1))


smem = pl.BlockSpec(memory_space=pltpu.SMEM)
anywhere = pl.BlockSpec(memory_space=pl.ANY)
in_hbm = pl.BlockSpec(memory_space=pltpu.HBM)
in_vmem = pl.BlockSpec(memory_space=pltpu.VMEM)
small = pltpu.CompilerParams(vmem_limit_bytes=12 * MIB)


def owner_of(place_ref, far, other):
    return 2 * (place_ref[3] ^ far) + (place_ref[4] ^ other)


def start_copies(pairs, sems, first=0):
    pending = [pltpu.make_async_copy(source, target, sems.at[first + at]) for at, (source, target) in enumerate(pairs)]
    for copy in pending:
        copy.start()
    return pending


def wait_copies(pending):
    for copy in pending:
        copy.wait()


def head_copies(place_ref, refs, whole_ref):
    rows = whole_ref.shape[1] // 8
    mine = pl.ds(0, rows)
    for other in range(2):
        start = pl.multiple_of(owner_of(place_ref, 0, other) * rows, 16)
        yield refs[other].at[:, mine, :], whole_ref.at[:, pl.ds(start, rows), :]
        for near in range(4):
            piece = refs[2 + 4 * other + near]
            for far in range(1, 4):
                start = pl.multiple_of(owner_of(place_ref, far, other) * rows, 16)
                yield piece.at[far - 1, mine, :], whole_ref.at[place_ref[2] ^ near, pl.ds(start, rows), :]


def project_kernel(place_ref, x_ref, gain_ref, *refs):
    *pieces, hid_ref, q_ref, k_ref, v_ref, out_ref, w_ref, sems, out_sem = refs
    step = pl.program_id(0)
    if len(pieces) == 1:
        pairs = [(pieces[0], w_ref)]
    else:
        pairs = list(head_copies(place_ref, pieces, w_ref))
    whole_copy = pltpu.make_async_copy(w_ref, out_ref, out_sem)

    @pl.when(step == 0)
    def _():
        start_copies(pairs, sems)

    x = x_ref[...].astype(F32)
    scale = lax.rsqrt(jnp.mean(x * x, -1, keepdims=True) + epsilon)
    hidden = (x * scale * gain_ref[...].astype(F32)).astype(BF16)
    hid_ref[...] = hidden

    @pl.when(step == 0)
    def _():
        wait_copies([pltpu.make_async_copy(*pair, sems.at[index]) for index, pair in enumerate(pairs)])
        whole_copy.start()

    q_ref[...] = dot_nn(hidden, w_ref[0]).astype(BF16)
    k_ref[...] = dot_nn(hidden, w_ref[1]).astype(BF16)
    v_ref[...] = dot_nn(hidden, w_ref[2]).astype(BF16)

    @pl.when(step == pl.num_programs(0) - 1)
    def _():
        whole_copy.wait()


def project(place, x, gain, pieces):
    rows, width = x.shape
    block = rows // 4
    row_spec = pl.BlockSpec((block, width), lambda i: (i, 0))
    out = jax.ShapeDtypeStruct((rows, width), BF16)
    return pl.pallas_call(
        project_kernel,
        grid=(4,),
        in_specs=[smem, row_spec, whole((1, width))] + [in_hbm] * len(pieces),
        out_specs=[row_spec] * 4 + [anywhere],
        out_shape=[out] * 4 + [jax.ShapeDtypeStruct((4, width, width), BF16)],
        scratch_shapes=[
            pltpu.VMEM((4, width, width), BF16),
            pltpu.SemaphoreType.DMA((26,)),
            pltpu.SemaphoreType.DMA(()),
        ],
        compiler_params=params(),
        cost_estimate=pl.CostEstimate(
            flops=6 * rows * width * width, bytes_accessed=10 * rows * width + 16 * width * width, transcendentals=0
        ),
        name="project_heads",
    )(place, x, gain, *pieces)


def attend_kernel(first_pair, lengths_ref, table_ref, q_ref, k_ref, v_ref, *refs):
    mixed_ref, inv_ref, p_any, rows_ref, tile_ref, segc_ref, segr_ref, p_ref, sems = refs[-9:]
    together = q_ref.shape[1] // BLOCK
    pair = first_pair + together * pl.program_id(0)
    rows = q_ref.shape[0]
    bounds = bounds_of(lengths_ref, lengths_ref.shape[1])
    reach = WINDOW + BLOCK

    @pl.when(pl.program_id(0) == 0)
    def _():
        segc_ref[...] = segment_of(lax.broadcasted_iota(jnp.int32, segc_ref.shape, 0), bounds)
        segr_ref[...] = segment_of(lax.broadcasted_iota(jnp.int32, segr_ref.shape, 1), bounds)
        offsets = lax.broadcasted_iota(jnp.int32, (BUCKETS, reach), 1) - (SPAN + BLOCK)
        kinds = lax.broadcasted_iota(jnp.int32, (BUCKETS, reach), 0)
        onehot = (bucket_of(offsets) == kinds).astype(F32).astype(BF16)
        rows_ref[...] = dot_tn(table_ref[...], onehot)

    for head in range(2 * together):
        line = rows_ref[pl.ds(2 * pair + head, 1), :]
        skew = pltpu.roll(jnp.broadcast_to(line, (BLOCK, reach)), 0, 1, stride=1, stride_axis=0)
        tile_ref[head] = skew[:, BLOCK:]

    lane = lax.broadcasted_iota(jnp.int32, (BLOCK, BLOCK), 1)
    first_half = lane < HEAD_DIM

    def out_copy(block_index):
        slot = block_index % SLOTS
        target = p_any.at[pl.ds(2 * pair, 2 * together), pl.ds(pl.multiple_of(block_index * BLOCK, BLOCK), BLOCK), :]
        return pltpu.make_async_copy(p_ref.at[slot], target, sems.at[slot])

    def one(block_index, carry):
        slot = block_index % SLOTS
        start = pl.multiple_of(block_index * BLOCK, BLOCK)

        @pl.when(block_index >= SLOTS)
        def _():
            out_copy(block_index - SLOTS).wait()

        first, count = window_of(bounds, start)
        first = pl.multiple_of(first, BLOCK)
        shift = pl.multiple_of(first - start + SPAN, BLOCK)

        def body(blocks):
            size = blocks * BLOCK
            queries = pl.ds(start, BLOCK)
            keys = pl.ds(first, size)
            segc = segc_ref[queries, :]
            segr = segr_ref[0:1, keys]
            same = jnp.concatenate([segc] * blocks, 1) == segr
            wide_lane = lax.broadcasted_iota(jnp.int32, (size, BLOCK), 1) < HEAD_DIM
            scores = []
            for head in range(2 * together):
                lanes = slice(head // 2 * BLOCK, head // 2 * BLOCK + BLOCK)
                mine = first_half if head % 2 == 0 else ~first_half
                q = q_ref[queries, lanes]
                scores.append(dot_nt(jnp.where(mine, q, jnp.zeros_like(q)), k_ref[keys, lanes]))
            raised = []
            for head in range(2 * together):
                score = jnp.where(same, scores[head] + tile_ref[head, :, pl.ds(shift, size)], -1000000000.0)
                power = jnp.exp(score - jnp.max(score, -1, keepdims=True)).astype(BF16)
                p_ref[slot, head, :, 0:size] = power
                raised.append(power)
            for near in range(together):
                lanes = slice(near * BLOCK, near * BLOCK + BLOCK)
                v = v_ref[keys, lanes]
                one = jnp.ones_like(v)
                left = dot_nn(raised[2 * near], jnp.where(wide_lane, v, one))
                right = dot_nn(raised[2 * near + 1], jnp.where(wide_lane, one, v))
                total = pltpu.roll(jnp.where(first_half, right, left), HEAD_DIM, 1)
                inverse = 1.0 / total
                mixed_ref[queries, lanes] = (jnp.where(first_half, left, right) * inverse).astype(BF16)
                inv_ref[queries, lanes] = inverse

        for blocks in range(1, WINDOW // BLOCK + 1):
            pl.when(count == blocks)(functools.partial(body, blocks))
        out_copy(block_index).start()
        return carry

    lax.fori_loop(0, rows // BLOCK, one, 0)
    for block_index in range(rows // BLOCK - SLOTS, rows // BLOCK):
        out_copy(block_index).wait()


def attend(lengths, table, q, k, v, first_pair, pairs, before=()):
    rows, width = q.shape
    together = max(size for size in (1, 2, 3) if pairs % size == 0 and first_pair % size == 0)
    column = pl.BlockSpec((rows, BLOCK * together), lambda p: (0, first_pair // together + p))
    return pl.pallas_call(
        functools.partial(attend_kernel, first_pair),
        grid=(pairs // together,),
        in_specs=[smem, whole(table.shape), column, column, column] + [anywhere] * len(before),
        out_specs=[column, column, anywhere],
        out_shape=[
            jax.ShapeDtypeStruct((rows, width), BF16),
            jax.ShapeDtypeStruct((rows, width), F32),
            jax.ShapeDtypeStruct((HEADS, rows, WINDOW), BF16),
        ],
        scratch_shapes=[
            pltpu.VMEM((16, WINDOW + BLOCK), F32),
            pltpu.VMEM((2 * together, BLOCK, WINDOW), F32),
            pltpu.VMEM((rows, BLOCK), jnp.int32),
            pltpu.VMEM((8, rows), jnp.int32),
            pltpu.VMEM((SLOTS, 2 * together, BLOCK, WINDOW), BF16),
            pltpu.SemaphoreType.DMA((SLOTS,)),
        ],
        input_output_aliases={5 + index: index for index in range(len(before))},
        compiler_params=params(),
        cost_estimate=pl.CostEstimate(
            flops=pairs * 8 * rows * 512 * 128, bytes_accessed=pairs * 6 * MIB, transcendentals=2 * pairs * rows * 512
        ),
        name="attend",
    )(lengths, table, q, k, v, *before)


def gelu_and_slope(v):
    bell = jnp.exp(-0.5 * v * v)
    t = 1.0 / (1.0 + (0.3275911 * root_half) * jnp.abs(v))
    series = t * (
        0.5 * 0.254829592
        + t * (0.5 * -0.284496736 + t * (0.5 * 1.421413741 + t * (0.5 * -1.453152027 + t * (0.5 * 1.061405429))))
    )
    tail = series * bell
    share = jnp.where(v >= 0.0, 1.0 - tail, tail)
    return v * share, share + v * bell * inv_root_tau


def member_of(lengths_ref, rows, count):
    bounds = bounds_of(lengths_ref, lengths_ref.shape[1])
    segment = segment_of(lax.broadcasted_iota(jnp.int32, (rows, count), 0), bounds)
    return (segment == lax.broadcasted_iota(jnp.int32, (rows, count), 1)).astype(F32).astype(BF16)


def member_rows(lengths_ref, rows, count):
    bounds = bounds_of(lengths_ref, lengths_ref.shape[1])
    segment = segment_of(lax.broadcasted_iota(jnp.int32, (count, rows), 1), bounds)
    return (segment == lax.broadcasted_iota(jnp.int32, (count, rows), 0)).astype(F32).astype(BF16)


def inner_copies(place_ref, refs, inner_ref):
    rows = refs[0].shape[0]
    width = inner_ref.shape[0]
    for other in range(2):
        owner = owner_of(place_ref, 0, other)
        yield refs[other], inner_ref.at[pl.ds(pl.multiple_of(owner * rows, 16), rows), :]
        for near in range(4):
            piece = refs[2 + 4 * other + near]
            quarter = place_ref[2] ^ near
            for far in range(1, 4):
                owner = owner_of(place_ref, far, other)
                row = pl.ds(pl.multiple_of(owner * rows, 16), rows)
                column = pl.ds(pl.multiple_of(quarter * width, 128), width)
                yield piece.at[far - 1], inner_ref.at[row, column]


def forward_kernel(place_ref, lengths_ref, x_ref, mixed_ref, gain_ref, heads_ref, wu_any, *refs):
    *pieces, out_ref, slope_ref, active_sum_ref, message_ref, mid_out, hid_out, wi_out = refs[:-12]
    total_ref, mid_ref, hid_ref, member_ref, wo_ref, inner_ref, active_ref = refs[-12:-5]
    wi_ref, wu_ref, sems, out_sems, last_sems = refs[-5:]
    step = pl.program_id(0)
    rows, width = hid_ref.shape
    block = rows // 4
    outs = ((wi_ref, wi_out), (hid_ref, hid_out), (mid_ref, mid_out))
    if len(pieces) == 1:
        groups = [[(pieces[0], wi_ref)], [(wu_any, wu_ref)]]
    else:
        groups = [list(inner_copies(place_ref, pieces, wi_ref)), [(wu_any, wu_ref)]]
    firsts = [0, len(groups[0])]
    spans = [slice(index * block, (index + 1) * block) for index in range(4)]

    def arrive(index):
        pairs = groups[index]
        wait_copies([pltpu.make_async_copy(*pair, sems.at[firsts[index] + at]) for at, pair in enumerate(pairs)])

    @pl.when(step == 0)
    def _():
        output_copy = pltpu.make_async_copy(heads_ref.at[3], wo_ref, last_sems.at[0])
        output_copy.start()
        for group, first in zip(groups, firsts):
            start_copies(group, sems, first)
        member_ref[...] = member_rows(lengths_ref, rows, 16)
        output_copy.wait()
        for span in spans:
            middle = x_ref[span, :].astype(F32) + dot_nn(mixed_ref[span, :], wo_ref[...])
            scale = lax.rsqrt(jnp.mean(middle * middle, -1, keepdims=True) + epsilon)
            total_ref[span, :] = middle
            mid_ref[span, :] = middle
            hid_ref[span, :] = (middle * scale * gain_ref[...].astype(F32)).astype(BF16)
        arrive(0)
        for index, pair in enumerate(outs):
            pltpu.make_async_copy(*pair, out_sems.at[index]).start()

    columns = pl.ds(pl.multiple_of(step * CHUNK, CHUNK), CHUNK)

    def first(span):
        inner_ref[span, :] = dot_nn(hid_ref[span, :], wi_ref[:, columns])

    def second(span):
        for at in range(span.start, span.stop, 32):
            active, slope = gelu_and_slope(inner_ref[at : at + 32, :])
            active_ref[at : at + 32, :] = active.astype(BF16)
            slope_ref[at : at + 32, :] = slope.astype(BF16)

    first(spans[0])
    first(spans[1])
    second(spans[0])

    @pl.when(step == 0)
    def _():
        arrive(1)

    for index, span in enumerate(spans):
        total_ref[span, :] += dot_nn(active_ref[span, :], wu_ref[columns, :])
        if index + 2 < 4:
            first(spans[index + 2])
        if index + 1 < 4:
            second(spans[index + 1])
    active_sum_ref[...] = dot_nn(member_ref[...], active_ref[...])

    @pl.when(step == pl.num_programs(0) - 1)
    def _():
        out_ref[...] = total_ref[...].astype(BF16)
        member = member_ref[...]
        pooled = jnp.zeros((16, width), F32)
        for span in spans:
            for piece in split(total_ref[span, :]):
                pooled = pooled + dot_nn(member[:, span], piece)
        row = lax.broadcasted_iota(jnp.int32, (8, 128), 0)
        lens = jnp.zeros((8, 128), jnp.int32)
        for index in range(8):
            lens = jnp.where(row == index, lengths_ref[0, index], lens)
        lens = lens.astype(F32)
        mean = pooled[0:8] / jnp.concatenate([lens] * (width // 128), 1)
        lower = jnp.concatenate([mean[:, 512:], lens, lens], 1)
        message_ref[...] = jnp.concatenate([mean[:, :512], lower], 0).astype(BF16)
        for index, pair in enumerate(outs):
            pltpu.make_async_copy(*pair, out_sems.at[index]).wait()


def forward(place, lengths, x, mixed, gain, heads, wu, units, pieces):
    rows, width = x.shape
    full = whole((rows, width))
    return pl.pallas_call(
        forward_kernel,
        grid=(units // CHUNK,),
        in_specs=[smem, smem, full, full, whole((1, width)), in_hbm, in_hbm] + [in_hbm] * len(pieces),
        out_specs=[
            pl.BlockSpec((rows, width), lambda i: (0, 0)),
            pl.BlockSpec((rows, CHUNK), lambda i: (0, i)),
            pl.BlockSpec((16, CHUNK), lambda i: (0, i)),
            pl.BlockSpec((16, 512), lambda i: (0, 0)),
        ]
        + [anywhere] * 3,
        out_shape=[
            jax.ShapeDtypeStruct((rows, width), BF16),
            jax.ShapeDtypeStruct((rows, units), BF16),
            jax.ShapeDtypeStruct((16, units), F32),
            pltpu.HBM((16, 512), BF16),
            jax.ShapeDtypeStruct((rows, width), F32),
            jax.ShapeDtypeStruct((rows, width), BF16),
            jax.ShapeDtypeStruct((width, units), BF16),
        ],
        scratch_shapes=[
            pltpu.VMEM((rows, width), F32),
            pltpu.VMEM((rows, width), F32),
            pltpu.VMEM((rows, width), BF16),
            pltpu.VMEM((16, rows), BF16),
            pltpu.VMEM((width, width), BF16),
            pltpu.VMEM((rows, CHUNK), F32),
            pltpu.VMEM((rows, CHUNK), BF16),
            pltpu.VMEM((width, units), BF16),
            pltpu.VMEM((units, width), BF16),
            pltpu.SemaphoreType.DMA((27,)),
            pltpu.SemaphoreType.DMA((3,)),
            pltpu.SemaphoreType.DMA((1,)),
        ],
        compiler_params=params(),
        cost_estimate=pl.CostEstimate(
            flops=4 * rows * width * units, bytes_accessed=30 * MIB, transcendentals=2 * rows * units
        ),
        name="feed_forward",
    )(place, lengths, x, mixed, gain, heads, wu, *pieces)


def contrast_kernel(place_ref, own_ref, got_ref, target_ref, wp_any, *refs):
    loss_ref, grad_wp_ref, glow_all_ref, grows_ref, glow_ref = refs[:-7]
    wide_ref, line_ref, full_ref, wp_ref, left_ref, right_ref, sems = refs[-7:]
    count, width = wide_ref.shape
    pending = start_copies([(wp_any, wp_ref)], sems)
    for other, ref in enumerate((own_ref, got_ref)):
        for far in range(4):
            for near in range(4):
                device = (place_ref[2] ^ near) * 8 + owner_of(place_ref, far, other)
                start = pl.multiple_of(device * 8, 8)
                piece = ref[far, near].astype(F32)
                left_ref[pl.ds(start, 8), :] = piece[0:8]
                right_ref[pl.ds(start, 8), :] = piece[8:16]
    rest = width - left_ref.shape[1]
    pooled = jnp.concatenate([left_ref[...], right_ref[:, 0:rest]], 1).astype(BF16)
    lens = right_ref[:, rest : rest + 1]
    wait_copies(pending)
    first = pl.multiple_of(place_ref[0] * 8, 8)
    projected = dot_nn(pooled, wp_ref[...])
    inverse = lax.rsqrt(jnp.sum(projected * projected, -1, keepdims=True) + epsilon)
    embedded = (projected * inverse).astype(BF16)
    row = lax.broadcasted_iota(jnp.int32, (count, count), 0)
    column = lax.broadcasted_iota(jnp.int32, (count, count), 1)
    logits = logit_scale * dot_nt(embedded, embedded)
    logits = jnp.where(row == column, -1000000000.0, logits)
    hit = column == target_ref[...]
    highest = jnp.max(logits, -1, keepdims=True)
    totals = highest + jnp.log(jnp.sum(jnp.exp(logits - highest), -1, keepdims=True))
    target = jnp.sum(jnp.where(hit, logits, 0.0), -1, keepdims=True)
    line_ref[...] = jnp.broadcast_to(totals - target, line_ref.shape)
    loss_ref[...] = line_ref[pl.ds(first, 8), :]
    grad_logits = (jnp.exp(logits - totals) - hit.astype(F32)).astype(BF16)
    grad_embedded = logit_scale * (dot_nn(grad_logits, embedded) + dot_tn(grad_logits, embedded))
    along = jnp.sum(grad_embedded * projected, -1, keepdims=True)
    grad_projected = inverse * grad_embedded - projected * (inverse * inverse * inverse * along)
    high, middle, low = split(grad_projected)
    full_ref[...] = dot_tn(pooled, high) + dot_tn(pooled, middle) + dot_tn(pooled, low)
    share = grad_wp_ref.shape[0]
    grad_wp_ref[...] = full_ref[pl.ds(pl.multiple_of(place_ref[1] * share, share), share), :]
    wp = wp_ref[...]
    grad_rows = (dot_nt(high, wp) + dot_nt(middle, wp) + dot_nt(low, wp)) / lens
    glow_all_ref[...] = grad_rows.astype(BF16)
    wide_ref[...] = grad_rows
    own_rows = wide_ref[pl.ds(first, 8), :]
    grows_ref[...] = own_rows
    glow_ref[...] = jnp.concatenate([own_rows, jnp.zeros_like(own_rows)], 0).astype(BF16)


def contrast(place, own, got, targets, wp, share):
    count = targets.shape[0]
    width = wp.shape[1]
    ins = [own, got, targets]
    outs = [
        jax.ShapeDtypeStruct((8, 128), F32),
        jax.ShapeDtypeStruct((share, width), F32),
        jax.ShapeDtypeStruct((count, width), BF16),
        jax.ShapeDtypeStruct((8, width), F32),
        jax.ShapeDtypeStruct((16, width), BF16),
    ]
    return pl.pallas_call(
        contrast_kernel,
        grid=(1,),
        in_specs=[smem] + [whole(array.shape) for array in ins] + [in_hbm],
        out_specs=[pl.BlockSpec(out.shape, lambda i: (0, 0)) for out in outs],
        out_shape=outs,
        scratch_shapes=[
            pltpu.VMEM((count, width), F32),
            pltpu.VMEM((count, 128), F32),
            pltpu.VMEM((width, width), F32),
            pltpu.VMEM((width, width), BF16),
            pltpu.VMEM((count, 512), F32),
            pltpu.VMEM((count, 512), F32),
            pltpu.SemaphoreType.DMA((1,)),
        ],
        compiler_params=params(),
        cost_estimate=pl.CostEstimate(flops=4 * count * width * width, bytes_accessed=8 * MIB, transcendentals=0),
        name="contrast",
    )(place, *ins, wp)


def contrast_plain(place, pooled, lens, targets, wp, share):
    count, width = pooled.shape
    exact = lax.Precision.HIGHEST
    projected = jnp.dot(pooled, wp, preferred_element_type=F32)
    inverse = lax.rsqrt(jnp.sum(projected * projected, -1, keepdims=True) + epsilon)
    embedded = (projected * inverse).astype(BF16)
    numbers = jnp.arange(count, dtype=jnp.int32)
    logits = logit_scale * dot_nt(embedded, embedded)
    logits = jnp.where(numbers[:, None] == numbers[None, :], -1000000000.0, logits)
    hit = numbers[None, :] == targets
    highest = jnp.max(logits, -1, keepdims=True)
    totals = highest + jnp.log(jnp.sum(jnp.exp(logits - highest), -1, keepdims=True))
    loss = totals - jnp.sum(jnp.where(hit, logits, 0.0), -1, keepdims=True)
    grad_logits = (jnp.exp(logits - totals) - hit.astype(F32)).astype(BF16)
    grad_embedded = logit_scale * (dot_nn(grad_logits, embedded) + dot_tn(grad_logits, embedded))
    along = jnp.sum(grad_embedded * projected, -1, keepdims=True)
    grad_projected = inverse * grad_embedded - projected * (inverse * inverse * inverse * along)
    own_columns = lax.dynamic_slice_in_dim(pooled.astype(F32), place[1] * share, share, 1)
    grad_wp = lax.dot_general(own_columns, grad_projected, (((0,), (0,)), ((), ())), precision=exact)
    grad_rows = jnp.dot(grad_projected, wp.astype(F32).T, precision=exact) / lens
    first = place[0] * 8
    own = lambda a: lax.dynamic_slice_in_dim(a, first, 8, 0)
    return jnp.broadcast_to(own(loss), (8, 128)), grad_wp, grad_rows.astype(BF16), own(grad_rows)


def fold(result_ref, keep_ref, send_ref, place_ref, column_half, column):
    narrow, plane, core = place_ref[2], place_ref[3], place_ref[4]
    rows = keep_ref.shape[2]
    for near in range(2):
        quarter = 2 * ((narrow // 2) ^ column_half) + near
        half = (narrow % 2) ^ near
        for far in range(4):
            for ref, owner in ((keep_ref, core), (send_ref, 1 - core)):
                start = pl.multiple_of((2 * (plane ^ far) + owner) * 2 * rows + half * rows, 16)
                block = result_ref[pl.ds(start, rows), :].astype(BF16)
                ref[quarter, far, :, pl.ds(column, block.shape[1])] = block


def back_kernel(
    lengths_ref, place_ref, glow_ref, grows_ref, gain_ref, hid_ref, active_ref, wu_ref, slope_ref, wi_ref,
    mid_any, mixed_any, inv_any, heads_any, gmid_any, gmix_ref, *refs,
):
    *grad_refs, result_ref, total_ref, member_ref, mid_ref, mixed_ref, inv_ref, wo_ref, sems, out_sems = refs
    step = pl.program_id(0)
    last = pl.num_programs(0) - 1
    rows, width = total_ref.shape
    folded = len(grad_refs) == 4
    late = [(mid_any, mid_ref), (mixed_any, mixed_ref), (inv_any, inv_ref), (heads_any.at[3], wo_ref)]

    @pl.when(step == 0)
    def _():
        member = member_of(lengths_ref, rows, 16)
        member_ref[...] = jnp.concatenate([member, member], 1)

    @pl.when(step == 2)
    def _():
        start_copies(late, sems)

    high, low = split_two(dot_nt(glow_ref[...], wu_ref[...]))
    spread = dot_nn(member_ref[...], jnp.concatenate([high, low], 0))
    grad_inner = (spread * slope_ref[...].astype(F32)).astype(BF16)
    part = dot_nt(grad_inner, wi_ref[...])
    result_ref[:, :CHUNK] = dot_tn(hid_ref[...], grad_inner)

    @pl.when(step == 0)
    def _():
        total_ref[...] = part

    @pl.when(step > 0)
    def _():
        total_ref[...] += part

    if folded:
        keep_any, send_any, keep_ref, send_ref = grad_refs
        half = pl.num_programs(0) // 2
        fold(
            result_ref.at[:, 0:CHUNK], keep_ref, send_ref, place_ref, step // half, pl.multiple_of((step % half) * CHUNK, CHUNK)
        )

        @pl.when(step == 0)
        def _():
            share = active_ref.shape[1] // 8
            empty = jnp.zeros((8, 128), F32)
            for far in range(4):
                for ref, other in ((keep_ref, 0), (send_ref, 1)):
                    owner = owner_of(place_ref, far, other)
                    for part_at in range(share // 128):
                        column = pl.multiple_of(owner * share + part_at * 128, 128)
                        sums = active_ref[0:8, pl.ds(column, 128)]
                        block = jnp.concatenate([empty, sums] if other else [sums, empty], 0).astype(BF16)
                        for quarter in range(4):
                            ref[quarter, far, 16 * part_at : 16 * part_at + 16, -128:] = block
    else:
        grad_refs[0][:, pl.ds(pl.multiple_of(step * CHUNK, CHUNK), CHUNK)] = result_ref[:, :CHUNK].astype(BF16)

    @pl.when(step == last)
    def _():
        pending = []
        if folded:
            inner_columns = pl.ds(0, 3 * CHUNK)
            rest = pl.ds(3 * CHUNK, keep_ref.shape[3] - 3 * CHUNK)
            for index, (source, target) in enumerate(((keep_ref, keep_any), (send_ref, send_any))):
                copy = pltpu.make_async_copy(
                    source.at[:, :, :, inner_columns], target.at[:, :, :, inner_columns], out_sems.at[index]
                )
                copy.start()
                pending.append(copy)
        wait_copies([pltpu.make_async_copy(*pair, sems.at[index]) for index, pair in enumerate(late)])
        bounds = bounds_of(lengths_ref, lengths_ref.shape[1])
        block = rows // 8
        for index in range(8):
            span = slice(index * block, (index + 1) * block)
            middle = mid_ref[span, :]
            scale = lax.rsqrt(jnp.mean(middle * middle, -1, keepdims=True) + epsilon)
            normed = middle * scale
            scaled = total_ref[span, :] * gain_ref[...].astype(F32)
            centre = jnp.mean(scaled * normed, -1, keepdims=True)
            segment = segment_of(lax.broadcasted_iota(jnp.int32, (block, 128), 0) + index * block, bounds)
            segment = jnp.concatenate([segment] * (width // 128), 1)
            grad_rows = jnp.zeros((block, width), F32)
            for passage in range(8):
                grad_rows = jnp.where(segment == passage, grows_ref[passage : passage + 1, :], grad_rows)
            total_ref[span, :] = grad_rows + scale * (scaled - normed * centre)
        copy = pltpu.make_async_copy(total_ref, gmid_any, out_sems.at[2])
        copy.start()
        pending.append(copy)
        columns = width // 2
        for side in range(2):
            grad = dot_tn(mixed_ref[...], total_ref[:, side * columns : (side + 1) * columns].astype(BF16))
            if folded:
                result_ref[:, 0:columns] = grad
                fold(result_ref.at[:, 0:columns], keep_ref, send_ref, place_ref, side, 3 * CHUNK)
            else:
                grad_refs[1][:, side * columns : (side + 1) * columns] = grad.astype(BF16)
        if folded:
            for index, (source, target) in enumerate(((keep_ref, keep_any), (send_ref, send_any))):
                copy = pltpu.make_async_copy(source.at[:, :, :, rest], target.at[:, :, :, rest], out_sems.at[3 + index])
                copy.start()
                pending.append(copy)
        for index in range(4):
            span = slice(index * 2 * block, (index + 1) * 2 * block)
            low_rows = total_ref[span, :].astype(BF16)
            gmix_ref[span, :] = (dot_nt(low_rows, wo_ref[...]) * inv_ref[span, :]).astype(BF16)
        wait_copies(pending)


def back(lengths, place, glow, grows, gain, hidden, active_sum, wu, slope, wi, middle, mixed, inv, heads, folded):
    rows, width = hidden.shape
    units = slope.shape[1]
    full = pl.BlockSpec((rows, width), lambda i: (0, 0))
    if folded:
        slabs = [(4, 4, width // 16, units // 2 + width // 2 + 128)] * 2
        grad_shape = [pltpu.HBM(slab, BF16) for slab in slabs]
        grad_specs = [anywhere] * 2
        grad_scratch = [pltpu.VMEM(slab, BF16) for slab in slabs]
    else:
        shapes = [(width, units), (width, width)]
        grad_shape = [jax.ShapeDtypeStruct(shape, BF16) for shape in shapes]
        grad_specs = [pl.BlockSpec(shape, lambda i: (0, 0)) for shape in shapes]
        grad_scratch = []
    return pl.pallas_call(
        back_kernel,
        grid=(units // CHUNK,),
        in_specs=[
            smem,
            smem,
            whole((16, width)),
            whole((8, width)),
            whole((1, width)),
            whole((rows, width)),
            whole(active_sum.shape),
            pl.BlockSpec((CHUNK, width), lambda i: (i, 0)),
            pl.BlockSpec((rows, CHUNK), lambda i: (0, i)),
            pl.BlockSpec((width, CHUNK), lambda i: (0, i)),
        ]
        + [anywhere] * 4,
        out_specs=[anywhere, full] + grad_specs,
        out_shape=[jax.ShapeDtypeStruct((rows, width), F32), jax.ShapeDtypeStruct((rows, width), BF16)] + grad_shape,
        scratch_shapes=grad_scratch
        + [
            pltpu.VMEM((width, CHUNK), F32),
            pltpu.VMEM((rows, width), F32),
            pltpu.VMEM((rows, 32), BF16),
            pltpu.VMEM((rows, width), F32),
            pltpu.VMEM((rows, width), BF16),
            pltpu.VMEM((rows, width), F32),
            pltpu.VMEM((width, width), BF16),
            pltpu.SemaphoreType.DMA((4,)),
            pltpu.SemaphoreType.DMA((5,)),
        ],
        compiler_params=params(),
        cost_estimate=pl.CostEstimate(flops=5 * rows * width * units, bytes_accessed=40 * MIB, transcendentals=0),
        name="back",
    )(lengths, place, glow, grows, gain, hidden, active_sum, wu, slope, wi, middle, mixed, inv, heads)


def attend_grad_kernel(first_pair, lengths_ref, q_ref, k_ref, v_ref, gm_ref, mixed_ref, p_any, *refs):
    grad_ref, diag_ref, qm_ref, km_ref, vx_ref, gx_ref, go_ref, ak_ref, av_ref, acc_ref, p_ref, sems = refs[-12:]
    together = q_ref.shape[1] // BLOCK
    rows = q_ref.shape[0]
    first_head = 2 * (first_pair + together * pl.program_id(0))

    def in_copy(block_index):
        slot = block_index % SLOTS
        source = p_any.at[pl.ds(first_head, 2 * together), pl.ds(pl.multiple_of(block_index * BLOCK, BLOCK), BLOCK), :]
        return pltpu.make_async_copy(source, p_ref.at[slot], sems.at[slot])

    for block_index in range(SLOTS - 1):
        in_copy(block_index).start()
    bounds = bounds_of(lengths_ref, lengths_ref.shape[1])
    reach = WINDOW + BLOCK
    acc_ref[...] = jnp.zeros_like(acc_ref)
    ak_ref[...] = jnp.zeros_like(ak_ref)
    av_ref[...] = jnp.zeros_like(av_ref)

    lane = lax.broadcasted_iota(jnp.int32, (BLOCK, BLOCK), 1)
    row = lax.broadcasted_iota(jnp.int32, (BLOCK, BLOCK), 0)
    across = jnp.where((row < HEAD_DIM) != (lane < HEAD_DIM), -1.0, 0.0).astype(BF16)

    def prepare(index, carry):
        span = pl.ds(pl.multiple_of(index * BLOCK, BLOCK), BLOCK)
        for near in range(together):
            lanes = slice(near * BLOCK, near * BLOCK + BLOCK)
            q, k, v, g = q_ref[span, lanes], k_ref[span, lanes], v_ref[span, lanes], gm_ref[span, lanes]
            product = split_two(g.astype(F32) * mixed_ref[span, lanes].astype(F32))
            centre = dot_nn(product[0], across) + dot_nn(product[1], across)
            high, low = split_two(centre)
            first = (lane == 0) | (lane == HEAD_DIM)
            second = (lane == 1) | (lane == HEAD_DIM + 1)
            zero = jnp.zeros_like(q)
            extra = jnp.where(first, high, jnp.where(second, low, zero))
            one = jnp.ones_like(v)
            for half in range(2):
                head = 2 * near + half
                mine = (lane < HEAD_DIM) if half == 0 else (lane >= HEAD_DIM)
                qm_ref[head, span, :] = jnp.where(mine, q, zero)
                km_ref[head, span, :] = jnp.where(mine, k, zero)
                go_ref[head, span, :] = jnp.where(mine, g, zero)
                vx_ref[head, span, :] = jnp.where(mine, v, one)
                gx_ref[head, span, :] = jnp.where(mine, g, extra)
        return carry

    lax.fori_loop(0, rows // BLOCK, prepare, 0)

    def one(block_index, carry):
        slot = block_index % SLOTS
        start = pl.multiple_of(block_index * BLOCK, BLOCK)
        in_copy(block_index).wait()

        @pl.when(block_index + SLOTS - 1 < rows // BLOCK)
        def _():
            in_copy(block_index + SLOTS - 1).start()

        first, count = window_of(bounds, start)
        first = pl.multiple_of(first, BLOCK)
        shift = pl.multiple_of(first - start + SPAN, BLOCK)

        def body(blocks):
            size = blocks * BLOCK
            queries = pl.ds(start, BLOCK)
            keys = pl.ds(first, size)
            spread = [dot_nt(gx_ref[head, queries, :], vx_ref[head, keys, :]) for head in range(2 * together)]
            for near in range(together):
                heads = (2 * near, 2 * near + 1)
                lanes = slice(near * BLOCK, near * BLOCK + BLOCK)
                parts = []
                raised = []
                for head in heads:
                    p = p_ref[slot, head, :, 0:size]
                    grad_scores = p.astype(F32) * spread[head]
                    acc_ref[head, :, pl.ds(shift, size)] += grad_scores
                    parts.append(grad_scores.astype(BF16))
                    raised.append(p)
                q_both = jnp.concatenate([qm_ref[head, queries, :] for head in heads], 0)
                g_both = jnp.concatenate([go_ref[head, queries, :] for head in heads], 0)
                k_both = jnp.concatenate([km_ref[head, keys, :] for head in heads], 0)
                ak_ref[lanes, keys] += dot_tn(q_both, jnp.concatenate(parts, 0))
                av_ref[lanes, keys] += dot_tn(g_both, jnp.concatenate(raised, 0))
                grad_ref[0, queries, lanes] = dot_nn(jnp.concatenate(parts, 1), k_both).astype(BF16)

        for blocks in range(1, WINDOW // BLOCK + 1):
            pl.when(count == blocks)(functools.partial(body, blocks))
        return carry

    lax.fori_loop(0, rows // BLOCK, one, 0)
    for near in range(together):
        lanes = slice(near * BLOCK, near * BLOCK + BLOCK)
        grad_ref[1, :, lanes] = jnp.transpose(ak_ref[lanes, :]).astype(BF16)
        grad_ref[2, :, lanes] = jnp.transpose(av_ref[lanes, :]).astype(BF16)
    for head in range(2 * together):
        padded = jnp.concatenate([jnp.zeros((BLOCK, BLOCK), F32), acc_ref[head]], 1)
        group = padded[0:8]
        for index in range(1, BLOCK // 8):
            group = group + pltpu.roll(padded[8 * index : 8 * index + 8], reach - 8 * index, 1)
        line = group[0:1]
        for index in range(1, 8):
            line = line + pltpu.roll(group, reach - index, 1)[index : index + 1]
        diag_ref[head // 2, head % 2 : head % 2 + 1, :] = line


def attend_grad(lengths, q, k, v, gm, mixed, p, first_pair, pairs, before=()):
    rows, width = q.shape
    together = max(size for size in (1, 2, 3) if pairs % size == 0 and first_pair % size == 0)
    at = first_pair // together
    column = pl.BlockSpec((rows, BLOCK * together), lambda i: (0, at + i))
    return pl.pallas_call(
        functools.partial(attend_grad_kernel, first_pair),
        grid=(pairs // together,),
        in_specs=[smem]
        + [column] * 5
        + [in_hbm]
        + [anywhere] * len(before),
        out_specs=[
            pl.BlockSpec((3, rows, BLOCK * together), lambda i: (0, 0, at + i)),
            pl.BlockSpec((together, 2, WINDOW + BLOCK), lambda i: (at + i, 0, 0)),
        ],
        out_shape=[
            jax.ShapeDtypeStruct((3, rows, width), BF16),
            jax.ShapeDtypeStruct((HEADS // 2, 2, WINDOW + BLOCK), F32),
        ],
        scratch_shapes=[pltpu.VMEM((2 * together, rows, BLOCK), BF16)] * 5
        + [pltpu.VMEM((BLOCK * together, rows), F32)] * 2
        + [
            pltpu.VMEM((2 * together, BLOCK, WINDOW), F32),
            pltpu.VMEM((SLOTS, 2 * together, BLOCK, WINDOW), BF16),
            pltpu.SemaphoreType.DMA((SLOTS,)),
        ],
        input_output_aliases={7 + index: index for index in range(len(before))},
        compiler_params=params(),
        cost_estimate=pl.CostEstimate(
            flops=pairs * 20 * rows * 512 * 64, bytes_accessed=pairs * 5 * MIB, transcendentals=0
        ),
        name="attend_grad",
    )(lengths, q, k, v, gm, mixed, p, *before)


def head_grad_kernel(place_ref, hid_ref, grad_ref, table_ref, keep_ref, send_ref, result_ref):
    step = pl.program_id(0)
    half = pl.num_programs(0) // 2
    block = result_ref.shape[1]
    result_ref[...] = dot_tn(hid_ref[...], grad_ref[0])
    fold(result_ref, keep_ref, send_ref, place_ref, step // half, pl.multiple_of((step % half) * block, 128))

    @pl.when(step == 0)
    def _():
        rows = keep_ref.shape[2]
        for far in range(4):
            for ref, other in ((keep_ref, 0), (send_ref, 1)):
                line = table_ref[pl.ds(owner_of(place_ref, far, other), 1), :]
                block_of = jnp.broadcast_to(line, (rows, 128)).astype(BF16)
                for quarter in range(4):
                    ref[quarter, far, :, half * block :] = block_of


def head_grad(place, hidden, grads, table):
    rows, width = hidden.shape
    block = width // 2
    slab = (4, 4, width // 16, 3 * block + 128)
    return pl.pallas_call(
        head_grad_kernel,
        grid=(6,),
        in_specs=[
            smem,
            whole((rows, width)),
            pl.BlockSpec((1, rows, block), lambda i: (i // 2, 0, i % 2)),
            whole(table.shape),
        ],
        out_specs=[pl.BlockSpec(slab, lambda i: (0, 0, 0, 0))] * 2,
        out_shape=[pltpu.HBM(slab, BF16)] * 2,
        scratch_shapes=[pltpu.VMEM((width, block), F32)],
        compiler_params=params(),
        cost_estimate=pl.CostEstimate(flops=6 * rows * width * width, bytes_accessed=12 * MIB, transcendentals=0),
        name="head_grad",
    )(place, hidden, grads, table)


def token_grad_kernel(x_ref, gain_ref, gmid_ref, grad_ref, w_ref, out_ref):
    x = x_ref[...].astype(F32)
    scale = lax.rsqrt(jnp.mean(x * x, -1, keepdims=True) + epsilon)
    normed = x * scale
    grad_hidden = dot_nt(grad_ref[0], w_ref[0]) + dot_nt(grad_ref[1], w_ref[1]) + dot_nt(grad_ref[2], w_ref[2])
    scaled = grad_hidden * gain_ref[...].astype(F32)
    centre = jnp.mean(scaled * normed, -1, keepdims=True)
    out_ref[...] = gmid_ref[...] + scale * (scaled - normed * centre)


def token_grad(x, gain, gmid, grads, weights):
    rows, width = x.shape
    block = rows // 4
    row_spec = pl.BlockSpec((block, width), lambda i: (i, 0))
    return pl.pallas_call(
        token_grad_kernel,
        grid=(4,),
        in_specs=[
            row_spec,
            whole((1, width)),
            row_spec,
            pl.BlockSpec((3, block, width), lambda i: (0, i, 0)),
            whole((3, width, width)),
        ],
        out_specs=row_spec,
        out_shape=jax.ShapeDtypeStruct((rows, width), F32),
        compiler_params=params(),
        cost_estimate=pl.CostEstimate(flops=6 * rows * width * width, bytes_accessed=16 * MIB, transcendentals=0),
        name="token_grad",
    )(x, gain, gmid, grads, weights)


def outer_grad_kernel(place_ref, pieces_ref, glow_ref, out_ref, active_ref):
    for far in range(4):
        for near in range(4):
            for part in range(active_ref.shape[1] // 128):
                block = pieces_ref[far, 16 * part : 16 * part + 16, 128 * near : 128 * near + 128].astype(F32)
                for other in range(2):
                    device = (place_ref[2] ^ near) * 8 + owner_of(place_ref, far, other)
                    start = pl.multiple_of(device * 8, 8)
                    active_ref[pl.ds(start, 8), 128 * part : 128 * part + 128] = block[8 * other : 8 * other + 8]
    out_ref[...] = dot_tn(active_ref[...].astype(BF16), glow_ref[...])


def outer_grad(place, pieces, glow):
    count, width = glow.shape
    units = 8 * pieces.shape[1]
    return pl.pallas_call(
        outer_grad_kernel,
        grid=(1,),
        in_specs=[smem, whole(pieces.shape), whole(glow.shape)],
        out_specs=pl.BlockSpec((units, width), lambda i: (0, 0)),
        out_shape=jax.ShapeDtypeStruct((units, width), F32),
        scratch_shapes=[pltpu.VMEM((count, units), F32)],
        compiler_params=params(),
        cost_estimate=pl.CostEstimate(flops=2 * count * units * width, bytes_accessed=3 * MIB, transcendentals=0),
        name="outer_grad",
    )(place, pieces, glow)


def table_grad(diag):
    reach = WINDOW + BLOCK
    offsets = jnp.arange(reach, dtype=jnp.int32) - (SPAN + BLOCK)
    onehot = (bucket_of(offsets)[:, None] == jnp.arange(BUCKETS, dtype=jnp.int32)[None, :]).astype(F32)
    sums = jnp.dot(diag.reshape(HEADS, reach), onehot, precision=lax.Precision.HIGHEST)
    return sums.T.reshape(BUCKETS * HEADS)


def exchange(value, narrow=0, plane=0, core=0):
    bits = narrow * 8 + plane * 2 + core
    return lax.ppermute(value, ("narrow", "wide"), [(i, i ^ bits) for i in range(32)])


def spread(value):
    return [value] + [exchange(value, narrow=near) for near in range(1, 4)]


def sum_core_kernel(keep_ref, got_ref, *out_refs):
    for quarter, out_ref in enumerate(out_refs):
        for far in range(4):
            out_ref[far] = (keep_ref[quarter, far].astype(F32) + got_ref[quarter, far].astype(F32)).astype(BF16)


def sum_core(keep, got):
    _, _, rows, columns = keep.shape
    return pl.pallas_call(
        sum_core_kernel,
        in_specs=[in_vmem] * 2,
        out_specs=[in_vmem] * 4,
        out_shape=[jax.ShapeDtypeStruct((4, rows, columns), BF16)] * 4,
        compiler_params=small,
        cost_estimate=pl.CostEstimate(flops=0, bytes_accessed=96 * rows * columns, transcendentals=0),
        name="sum_core",
    )(keep, got)


def sum_narrow_kernel(apart, a_ref, b_ref, c_ref, d_ref, *out_refs):
    refs = (a_ref, b_ref, c_ref, d_ref)
    columns = a_ref.shape[2] - (128 if apart else 0)
    for far, out_ref in enumerate(out_refs):
        total = sum(ref[far, :, :columns].astype(F32) for ref in refs)
        out_ref[:, :columns] = total.astype(BF16)
        if apart:
            for near, ref in enumerate(refs):
                out_ref[:, columns + 128 * near : columns + 128 * near + 128] = ref[far, :, columns:]


def sum_narrow(parts, apart):
    _, rows, columns = parts[0].shape
    columns += 3 * 128 if apart else 0
    return pl.pallas_call(
        functools.partial(sum_narrow_kernel, apart),
        in_specs=[in_vmem] * 4,
        out_specs=[in_vmem] * 4,
        out_shape=[jax.ShapeDtypeStruct((rows, columns), BF16)] * 4,
        compiler_params=small,
        cost_estimate=pl.CostEstimate(flops=0, bytes_accessed=40 * rows * columns, transcendentals=0),
        name="sum_narrow",
    )(*parts)


def sum_planes_kernel(a_ref, b_ref, c_ref, d_ref, total_ref, *apart_refs):
    refs = (a_ref, b_ref, c_ref, d_ref)
    columns = total_ref.shape[1]
    total_ref[...] = sum(ref[:, :columns].astype(F32) for ref in refs).astype(BF16)
    for apart_ref in apart_refs:
        for far, ref in enumerate(refs):
            apart_ref[far] = ref[:, columns:]


def sum_planes(parts, apart):
    rows, columns = parts[0].shape
    kept = 4 * 128 if apart else 0
    out_shape = [jax.ShapeDtypeStruct((rows, columns - kept), BF16)]
    if apart:
        out_shape.append(jax.ShapeDtypeStruct((4, rows, kept), BF16))
    return pl.pallas_call(
        sum_planes_kernel,
        in_specs=[in_vmem] * 4,
        out_specs=[in_vmem] * len(out_shape),
        out_shape=out_shape,
        compiler_params=small,
        cost_estimate=pl.CostEstimate(flops=0, bytes_accessed=10 * rows * columns, transcendentals=0),
        name="sum_planes",
    )(*parts)


def as_row(column):
    return jnp.transpose(jnp.broadcast_to(column, (column.shape[0], 128)))[0:1]


def finish_inner_kernel(place_ref, weight_ref, gain_ref, a_ref, b_ref, c_ref, d_ref, out_ref, last_ref, ggain_ref):
    rows = a_ref.shape[0]
    units = weight_ref.shape[1] // 2
    width = last_ref.shape[1] // 2
    for near, ref in enumerate((a_ref, b_ref, c_ref, d_ref)):
        quarter = place_ref[2] ^ near
        row = pl.ds(pl.multiple_of((quarter % 2) * rows, rows), rows)
        half = quarter // 2
        out_ref[row, pl.ds(pl.multiple_of(half * units, 128), units)] = ref[:, :units].astype(F32)
        last_ref[row, pl.ds(pl.multiple_of(half * width, 128), width)] = ref[:, units:].astype(F32)
    along = jnp.sum(out_ref[...] * weight_ref[...].astype(F32), -1, keepdims=True)
    ggain_ref[...] = as_row(along) / gain_ref[...].astype(F32)


def finish_inner(place, weight, gain, parts, width):
    rows, units = weight.shape
    ins = [weight, gain] + list(parts)
    outs = [jax.ShapeDtypeStruct(shape, F32) for shape in ((rows, units), (rows, width), (1, rows))]
    return pl.pallas_call(
        finish_inner_kernel,
        in_specs=[smem] + [in_vmem] * len(ins),
        out_specs=[in_vmem] * len(outs),
        out_shape=outs,
        compiler_params=small,
        cost_estimate=pl.CostEstimate(flops=0, bytes_accessed=3 * MIB, transcendentals=0),
        name="finish_inner",
    )(place, *ins)


def finish_heads_kernel(place_ref, wq_ref, wk_ref, wv_ref, gain_ref, a_ref, b_ref, c_ref, d_ref, *refs):
    *out_refs, table_ref, ggain_ref, result_ref = refs
    rows = a_ref.shape[0]
    width = wq_ref.shape[1]
    half = 3 * width // 2
    for near, ref in enumerate((a_ref, b_ref, c_ref, d_ref)):
        quarter = place_ref[2] ^ near
        row = pl.multiple_of((quarter % 2) * rows, rows)
        column = pl.multiple_of((quarter // 2) * half, 128)
        result_ref[pl.ds(row, rows), pl.ds(column, half)] = ref[:, :half].astype(F32)

        @pl.when(quarter == 0)
        def _():
            table_ref[...] = ref[0:16, half:].astype(F32)[0:1, : table_ref.shape[1]]

    along = jnp.zeros((2 * rows, 1), F32)
    for index, (out_ref, weight_ref) in enumerate(zip(out_refs, (wq_ref, wk_ref, wv_ref))):
        grad = result_ref[:, index * width : (index + 1) * width]
        out_ref[...] = grad
        along = along + jnp.sum(grad * weight_ref[...].astype(F32), -1, keepdims=True)
    ggain_ref[...] = as_row(along) / gain_ref[...].astype(F32)


def finish_heads(place, weights, gain, parts, table_share):
    rows, width = weights[0].shape
    ins = list(weights) + [gain] + list(parts)
    outs = [jax.ShapeDtypeStruct((rows, width), F32)] * 3
    outs += [jax.ShapeDtypeStruct((1, table_share), F32), jax.ShapeDtypeStruct((1, rows), F32)]
    return pl.pallas_call(
        finish_heads_kernel,
        in_specs=[smem] + [in_vmem] * len(ins),
        out_specs=[in_vmem] * len(outs),
        out_shape=outs,
        scratch_shapes=[pltpu.VMEM((rows, 3 * width), F32)],
        compiler_params=small,
        cost_estimate=pl.CostEstimate(flops=0, bytes_accessed=3 * MIB, transcendentals=0),
        name="finish_heads",
    )(place, *ins)


def order_small_kernel(place_ref, own_ref, got_ref, out_ref):
    for other, ref in enumerate((own_ref, got_ref)):
        for far in range(4):
            out_ref[pl.ds(owner_of(place_ref, far, other), 1), :] = ref[far, 0:1, :]


def order_small(place, own, got):
    return pl.pallas_call(
        order_small_kernel,
        grid=(1,),
        in_specs=[smem, whole(own.shape), whole(got.shape)],
        out_specs=pl.BlockSpec((8, own.shape[2]), lambda i: (0, 0)),
        out_shape=jax.ShapeDtypeStruct((8, own.shape[2]), F32),
        name="order_small",
    )(place, own, got)


def gather_messages(message):
    near = jnp.stack(spread(message))
    planes = jnp.stack([near] + [exchange(near, plane=far) for far in range(1, 4)])
    return planes, exchange(planes, core=1)


def tie(first, then):
    first, then = lax.optimization_barrier((first, then))
    return first, then


def gather_heads(place, own, small):
    rows, width = own[0].shape
    line = jnp.broadcast_to(jnp.pad(small, (0, width - small.shape[0])), (8, width))
    heads = jnp.stack([jnp.concatenate([weight, line]) for weight in own])
    quarter = lax.dynamic_index_in_dim(heads, place[2], 0, keepdims=False)
    far = jnp.stack([exchange(quarter, plane=distance) for distance in range(1, 4)])
    far, heads = tie(far, heads)
    near = spread(far)
    other = exchange(heads, core=1)
    far_other = exchange(far, core=1)
    lines = lambda first, rest: jnp.concatenate([first[:1, rows:, :256], rest[:, rows:, :256]]).astype(F32)
    ordered = order_small(place, lines(heads, far), lines(other, far_other))
    return near, [heads, other], far_other, ordered


def fetch_inner(narrow, inner_weight, width):
    quarter = lax.dynamic_slice_in_dim(inner_weight, narrow * width, width, 1)
    return [exchange(quarter, plane=far) for far in range(1, 4)]


def layer_specs():
    both = ("narrow", "wide")
    rows, matrix, vector = P(both, None), P("wide", None), P("wide")
    ins = (rows, vector, matrix, matrix, matrix, matrix, vector, vector, matrix, matrix, matrix, rows, P())
    outs = (rows, rows, rows, vector, matrix, matrix, matrix, matrix, vector, vector, matrix, matrix, matrix)
    return ins, outs


def local_permuted(tokens, *arguments):
    *weights_own, lengths, positives = arguments
    attention_gain, query_weight, key_weight, value_weight, output_weight = weights_own[:5]
    bias_table, forward_gain, inner_weight, outer_weight, project_weight = weights_own[5:]
    segs = lengths.shape[1]
    width = tokens.shape[1]
    units = inner_weight.shape[1]
    wide_at = lax.axis_index("wide")
    narrow_at = lax.axis_index("narrow")
    device = narrow_at * 8 + wide_at
    place = jnp.stack([device, wide_at, narrow_at, wide_at // 2, wide_at % 2]).astype(jnp.int32)
    share = attention_gain.shape[0]

    own_heads = (query_weight, key_weight, value_weight, output_weight)
    small = jnp.concatenate([attention_gain, forward_gain, bias_table])
    near, both_heads, far_other, small = gather_heads(place, own_heads, small)
    gain_one = small[:, :share].reshape(1, width)
    gain_two = small[:, share : 2 * share].reshape(1, width)
    table = small[:, 2 * share : 2 * share + bias_table.shape[0]].reshape(BUCKETS, HEADS)
    table = jnp.pad(table, ((0, 0), (0, 4))).astype(BF16)
    _, own_inner = tie(both_heads[1], inner_weight)
    _, own_outer = tie(far_other, outer_weight)
    wu = lax.all_gather(own_outer, "wide", axis=0, tiled=True)
    far = jnp.stack(fetch_inner(narrow_at, own_inner, width))
    (gain_one, gain_two, table), near = tie((gain_one, gain_two, table), near)
    near, far = tie(near, far)
    head_pieces = both_heads + near + [far_other] + [exchange(piece, core=1) for piece in near[1:]]
    near = spread(far)
    other_inner = exchange(own_inner, core=1)

    hid, q, k, v, weights = project(place, tokens, gain_one, head_pieces)
    q, own_last = tie(q, project_weight)
    wp = lax.all_gather(own_last, "wide", axis=0, tiled=True)
    mixed, inv, p = attend(lengths, table, q, k, v, 0, 6)
    mixed, inv, p, near = lax.optimization_barrier((mixed, inv, p, near))
    near_other = [exchange(piece, core=1) for piece in near]
    hidden, slope, active_sum, message, middle, hid_two, wi = forward(
        place, lengths, tokens, mixed, gain_two, weights, wu, units, [own_inner, other_inner] + near + near_other
    )
    loss, grad_wp, glow_all, grows, glow = contrast(
        place, *gather_messages(message), positives.reshape(-1, 1), wp, project_weight.shape[0]
    )
    gmid, gm, keep, send = back(
        lengths, place, glow, grows, gain_two, hid_two, active_sum, wu, slope, wi, middle, mixed, inv, weights, True
    )

    got = exchange(send, core=1)
    some = attend_grad(lengths, q, k, v, gm, mixed, p, 0, 2)
    some, got = tie(some, got)
    quarters = sum_core(keep, got)
    quarters, some = tie(quarters, some)
    arrived = [quarters[0]] + [exchange(quarters[near], narrow=near) for near in range(1, 4)]
    grad_heads, diag = attend_grad(lengths, q, k, v, gm, mixed, p, 2, 4, some)
    grad_table = table_grad(diag).reshape(8, -1)
    rows_table = jnp.pad(grad_table, ((0, 0), (0, 128 - grad_table.shape[1])))
    keep, send = head_grad(place, hid, grad_heads, rows_table)
    keep, send, arrived = lax.optimization_barrier((keep, send, arrived))
    got = exchange(send, core=1)
    planes = sum_narrow(arrived, True)
    inner_far = [planes[0]] + [exchange(planes[far], plane=far) for far in range(1, 4)]
    planes, got = tie(planes, got)
    quarters = sum_core(keep, got)
    quarters, gmid = tie(quarters, gmid)
    arrived = [quarters[0]] + [exchange(quarters[near], narrow=near) for near in range(1, 4)]
    grad_tokens = token_grad(tokens, gain_one, gmid, grad_heads, weights)
    grad_tokens, inner_far = tie(grad_tokens, inner_far)
    total, active_pieces = sum_planes(inner_far, True)
    inner_parts = spread(total)
    grad_outer = outer_grad(place, active_pieces, glow_all)
    grad_outer, arrived = tie(grad_outer, arrived)
    planes = sum_narrow(arrived, False)
    planes, inner_parts = tie(planes, inner_parts)
    arrived = [planes[0]] + [exchange(planes[far], plane=far) for far in range(1, 4)]
    grad_inner, grad_out, gain_two_grad = finish_inner(place, inner_weight, forward_gain[None], inner_parts, width)
    grad_inner, arrived = tie(grad_inner, arrived)
    (total,) = sum_planes(arrived, False)
    *grads, table_own, gain_one_grad = finish_heads(
        place, own_heads[:3], attention_gain[None], spread(total), bias_table.shape[0]
    )
    grads.append(grad_out)
    return (
        hidden,
        grad_tokens,
        loss[:, 0].reshape(1, segs),
        gain_one_grad[0],
        *grads,
        table_own[0],
        gain_two_grad[0],
        grad_inner,
        grad_outer,
        grad_wp,
    )


def local_plain(tokens, *arguments):
    *weights_own, lengths, positives = arguments
    attention_gain, query_weight, key_weight, value_weight, output_weight = weights_own[:5]
    bias_table, forward_gain, inner_weight, outer_weight, project_weight = weights_own[5:]
    both = ("narrow", "wide")
    segs = lengths.shape[1]
    width = tokens.shape[1]
    wide_at = lax.axis_index("wide")
    device = lax.axis_index("narrow") * lax.axis_size("wide") + wide_at
    place = jnp.stack([device, wide_at]).astype(jnp.int32)
    share = attention_gain.shape[0]
    gather = lambda a: lax.all_gather(a, "wide", axis=0, tiled=True)
    small = gather(jnp.concatenate([attention_gain, forward_gain, bias_table])[None])
    gain_one = small[:, :share].reshape(1, width)
    gain_two = small[:, share : 2 * share].reshape(1, width)
    table = jnp.pad(small[:, 2 * share :].reshape(BUCKETS, HEADS), ((0, 0), (0, 4)))
    weights = jnp.stack([gather(w) for w in (query_weight, key_weight, value_weight, output_weight)])
    wu = gather(outer_weight)
    hid, q, k, v, weights = project(place, tokens, gain_one, [weights])
    mixed, inv, p = attend(lengths, table, q, k, v, 0, HEADS // 2)
    hidden, slope, active_sum, message, middle, hid_two, wi = forward(
        place, lengths, tokens, mixed, gain_two, weights, wu, inner_weight.shape[1], [gather(inner_weight)]
    )
    messages = lax.all_gather(message, both, axis=0, tiled=True).reshape(-1, 2, 8, 512)
    messages = messages.transpose(0, 2, 1, 3).reshape(-1, 1024)
    loss, grad_wp, glow_all, grows = contrast_plain(
        place,
        messages[:, :width],
        messages[:, width : width + 1].astype(F32),
        positives.reshape(-1, 1),
        gather(project_weight),
        project_weight.shape[0],
    )
    active_all = lax.all_gather(active_sum[:segs], both, axis=0, tiled=True)
    active_own = lax.dynamic_slice_in_dim(active_all, wide_at * outer_weight.shape[0], outer_weight.shape[0], 1)
    grad_outer = dot_tn(active_own, glow_all.astype(F32))
    glow = jnp.pad(grows.astype(BF16), ((0, 16 - segs), (0, 0)))
    gmid, gm, grad_wi, grad_wo = back(
        lengths, place, glow, grows, gain_two, hid_two, active_sum, wu, slope, wi, middle, mixed, inv, weights, False
    )
    grad_heads, diag = attend_grad(lengths, q, k, v, gm, mixed, p, 0, HEADS // 2)
    grad_tokens = token_grad(tokens, gain_one, gmid, grad_heads, weights)

    def total(grad):
        part = lax.psum_scatter(grad, "wide", scatter_dimension=0, tiled=True)
        return lax.psum(part.astype(F32), "narrow")

    grads = [total(dot_tn(hid, grad).astype(BF16)) for grad in grad_heads] + [total(grad_wo)]
    grad_inner = total(grad_wi)
    table_own = total(table_grad(diag).reshape(lax.axis_size("wide"), -1))[0]
    own_heads = jnp.stack([query_weight, key_weight, value_weight])
    along = jnp.sum(jnp.stack(grads[:3]) * own_heads.astype(F32), (0, 2))
    return (
        hidden,
        grad_tokens,
        loss[:, 0].reshape(1, segs),
        along / attention_gain.astype(F32),
        *grads,
        table_own,
        jnp.sum(grad_inner * inner_weight.astype(F32), 1) / forward_gain.astype(F32),
        grad_inner,
        grad_outer,
        grad_wp,
    )


def solution(mesh):
    ins, outs = layer_specs()
    permuted = (mesh.shape["narrow"], mesh.shape["wide"]) == (4, 8)
    body = local_permuted if permuted else local_plain
    return jax.shard_map(body, mesh=mesh, in_specs=ins, out_specs=outs, check_vma=False)
```

```python
import functools

import jax
import jax.numpy as jnp
from jax import lax
from jax.experimental import pallas as pl
from jax.experimental.pallas import tpu as pltpu
from jax.sharding import PartitionSpec as P

HEADS = 12
HEAD_DIM = 64
BUCKETS = 32
SPAN = 256
BLOCK = 128
WINDOW = BLOCK + 2 * SPAN
SLOTS = 4
CHUNK = 512

epsilon = 1e-06
logit_scale = 50.0
root_half = 0.7071067811865476
inv_root_tau = 0.3989422804014327
MIB = 1 << 20
F32 = jnp.float32
BF16 = jnp.bfloat16


def dot_nn(left, right):
    return lax.dot_general(left, right, (((1,), (0,)), ((), ())), preferred_element_type=F32)


def dot_nt(left, right):
    return lax.dot_general(left, right, (((1,), (1,)), ((), ())), preferred_element_type=F32)


def dot_tn(left, right):
    return lax.dot_general(left, right, (((0,), (0,)), ((), ())), preferred_element_type=F32)


def split(values):
    high = values.astype(BF16)
    rest = values - high.astype(F32)
    middle = rest.astype(BF16)
    return high, middle, (rest - middle.astype(F32)).astype(BF16)


def split_two(values):
    high = values.astype(BF16)
    return high, (values - high.astype(F32)).astype(BF16)


def bucket_of(offset):
    distance = jnp.abs(offset)
    larger = jnp.full_like(distance, 8)
    for step in range(1, 8):
        larger = larger + (distance * distance >= 64 * 2**step).astype(jnp.int32)
    return jnp.where(distance < 8, distance, larger) + jnp.where(offset > 0, 16, 0)


def bounds_of(lengths_ref, count):
    bounds = []
    total = 0
    for index in range(count):
        total = total + lengths_ref[0, index]
        bounds.append(total)
    return bounds


def segment_of(places, bounds):
    segment = jnp.zeros_like(places)
    for bound in bounds:
        segment = segment + (places >= bound).astype(jnp.int32)
    return segment


def window_of(bounds, start):
    low = 0
    high = bounds[-1]
    for bound in bounds[:-1]:
        low = jnp.where(bound <= start, bound, low)
    for bound in reversed(bounds[:-1]):
        high = jnp.where(bound > start + BLOCK - 1, bound, high)
    first = (low // BLOCK) * BLOCK
    blocks = (high - first + BLOCK - 1) // BLOCK
    return first, blocks


def params(mib=60, grid=1):
    return pltpu.CompilerParams(vmem_limit_bytes=mib * MIB, dimension_semantics=("arbitrary",) * grid)


def whole(shape):
    return pl.BlockSpec(shape, lambda *_: (0,) * len(shape), pipeline_mode=pl.Buffered(1))


smem = pl.BlockSpec(memory_space=pltpu.SMEM)
anywhere = pl.BlockSpec(memory_space=pl.ANY)
in_hbm = pl.BlockSpec(memory_space=pltpu.HBM)
in_vmem = pl.BlockSpec(memory_space=pltpu.VMEM)
small = pltpu.CompilerParams(vmem_limit_bytes=12 * MIB)


def owner_of(place_ref, far, other):
    return 2 * (place_ref[3] ^ far) + (place_ref[4] ^ other)


def start_copies(pairs, sems, first=0):
    pending = [pltpu.make_async_copy(source, target, sems.at[first + at]) for at, (source, target) in enumerate(pairs)]
    for copy in pending:
        copy.start()
    return pending


def wait_copies(pending):
    for copy in pending:
        copy.wait()


def head_copies(place_ref, refs, whole_ref):
    rows = whole_ref.shape[1] // 8
    mine = pl.ds(0, rows)
    for other in range(2):
        start = pl.multiple_of(owner_of(place_ref, 0, other) * rows, 16)
        yield refs[other].at[:, mine, :], whole_ref.at[:, pl.ds(start, rows), :]
        for near in range(4):
            piece = refs[2 + 4 * other + near]
            for far in range(1, 4):
                start = pl.multiple_of(owner_of(place_ref, far, other) * rows, 16)
                yield piece.at[far - 1, mine, :], whole_ref.at[place_ref[2] ^ near, pl.ds(start, rows), :]


def project_kernel(place_ref, x_ref, gain_ref, *refs):
    *pieces, hid_ref, q_ref, k_ref, v_ref, out_ref, w_ref, sems, out_sem = refs
    step = pl.program_id(0)
    if len(pieces) == 1:
        pairs = [(pieces[0], w_ref)]
    else:
        pairs = list(head_copies(place_ref, pieces, w_ref))
    whole_copy = pltpu.make_async_copy(w_ref, out_ref, out_sem)

    @pl.when(step == 0)
    def _():
        start_copies(pairs, sems)

    x = x_ref[...].astype(F32)
    scale = lax.rsqrt(jnp.mean(x * x, -1, keepdims=True) + epsilon)
    hidden = (x * scale * gain_ref[...].astype(F32)).astype(BF16)
    hid_ref[...] = hidden

    @pl.when(step == 0)
    def _():
        wait_copies([pltpu.make_async_copy(*pair, sems.at[index]) for index, pair in enumerate(pairs)])
        whole_copy.start()

    q_ref[...] = dot_nn(hidden, w_ref[0]).astype(BF16)
    k_ref[...] = dot_nn(hidden, w_ref[1]).astype(BF16)
    v_ref[...] = dot_nn(hidden, w_ref[2]).astype(BF16)

    @pl.when(step == pl.num_programs(0) - 1)
    def _():
        whole_copy.wait()


def project(place, x, gain, pieces):
    rows, width = x.shape
    block = rows // 4
    row_spec = pl.BlockSpec((block, width), lambda i: (i, 0))
    out = jax.ShapeDtypeStruct((rows, width), BF16)
    return pl.pallas_call(
        project_kernel,
        grid=(4,),
        in_specs=[smem, row_spec, whole((1, width))] + [in_hbm] * len(pieces),
        out_specs=[row_spec] * 4 + [anywhere],
        out_shape=[out] * 4 + [jax.ShapeDtypeStruct((4, width, width), BF16)],
        scratch_shapes=[
            pltpu.VMEM((4, width, width), BF16),
            pltpu.SemaphoreType.DMA((26,)),
            pltpu.SemaphoreType.DMA(()),
        ],
        compiler_params=params(),
        cost_estimate=pl.CostEstimate(
            flops=6 * rows * width * width, bytes_accessed=10 * rows * width + 16 * width * width, transcendentals=0
        ),
        name="project_heads",
    )(place, x, gain, *pieces)


def attend_kernel(first_pair, lengths_ref, table_ref, q_ref, k_ref, v_ref, *refs):
    mixed_ref, inv_ref, p_any, rows_ref, tile_ref, segc_ref, segr_ref, p_ref, sems = refs[-9:]
    together = q_ref.shape[1] // BLOCK
    pair = first_pair + together * pl.program_id(0)
    rows = q_ref.shape[0]
    bounds = bounds_of(lengths_ref, lengths_ref.shape[1])
    reach = WINDOW + BLOCK

    @pl.when(pl.program_id(0) == 0)
    def _():
        segc_ref[...] = segment_of(lax.broadcasted_iota(jnp.int32, segc_ref.shape, 0), bounds)
        segr_ref[...] = segment_of(lax.broadcasted_iota(jnp.int32, segr_ref.shape, 1), bounds)
        offsets = lax.broadcasted_iota(jnp.int32, (BUCKETS, reach), 1) - (SPAN + BLOCK)
        kinds = lax.broadcasted_iota(jnp.int32, (BUCKETS, reach), 0)
        onehot = (bucket_of(offsets) == kinds).astype(F32).astype(BF16)
        rows_ref[...] = dot_tn(table_ref[...], onehot)

    for head in range(2 * together):
        line = rows_ref[pl.ds(2 * pair + head, 1), :]
        skew = pltpu.roll(jnp.broadcast_to(line, (BLOCK, reach)), 0, 1, stride=1, stride_axis=0)
        tile_ref[head] = skew[:, BLOCK:]

    lane = lax.broadcasted_iota(jnp.int32, (BLOCK, BLOCK), 1)
    first_half = lane < HEAD_DIM

    def out_copy(block_index):
        slot = block_index % SLOTS
        target = p_any.at[pl.ds(2 * pair, 2 * together), pl.ds(pl.multiple_of(block_index * BLOCK, BLOCK), BLOCK), :]
        return pltpu.make_async_copy(p_ref.at[slot], target, sems.at[slot])

    def one(block_index, carry):
        slot = block_index % SLOTS
        start = pl.multiple_of(block_index * BLOCK, BLOCK)

        @pl.when(block_index >= SLOTS)
        def _():
            out_copy(block_index - SLOTS).wait()

        first, count = window_of(bounds, start)
        first = pl.multiple_of(first, BLOCK)
        shift = pl.multiple_of(first - start + SPAN, BLOCK)

        def body(blocks):
            size = blocks * BLOCK
            queries = pl.ds(start, BLOCK)
            keys = pl.ds(first, size)
            segc = segc_ref[queries, :]
            segr = segr_ref[0:1, keys]
            same = jnp.concatenate([segc] * blocks, 1) == segr
            wide_lane = lax.broadcasted_iota(jnp.int32, (size, BLOCK), 1) < HEAD_DIM
            scores = []
            for head in range(2 * together):
                lanes = slice(head // 2 * BLOCK, head // 2 * BLOCK + BLOCK)
                mine = first_half if head % 2 == 0 else ~first_half
                q = q_ref[queries, lanes]
                scores.append(dot_nt(jnp.where(mine, q, jnp.zeros_like(q)), k_ref[keys, lanes]))
            raised = []
            for head in range(2 * together):
                score = jnp.where(same, scores[head] + tile_ref[head, :, pl.ds(shift, size)], -1000000000.0)
                power = jnp.exp(score - jnp.max(score, -1, keepdims=True)).astype(BF16)
                p_ref[slot, head, :, 0:size] = power
                raised.append(power)
            for near in range(together):
                lanes = slice(near * BLOCK, near * BLOCK + BLOCK)
                v = v_ref[keys, lanes]
                one = jnp.ones_like(v)
                left = dot_nn(raised[2 * near], jnp.where(wide_lane, v, one))
                right = dot_nn(raised[2 * near + 1], jnp.where(wide_lane, one, v))
                total = pltpu.roll(jnp.where(first_half, right, left), HEAD_DIM, 1)
                inverse = 1.0 / total
                mixed_ref[queries, lanes] = (jnp.where(first_half, left, right) * inverse).astype(BF16)
                inv_ref[queries, lanes] = inverse

        for blocks in range(1, WINDOW // BLOCK + 1):
            pl.when(count == blocks)(functools.partial(body, blocks))
        out_copy(block_index).start()
        return carry

    lax.fori_loop(0, rows // BLOCK, one, 0)
    for block_index in range(rows // BLOCK - SLOTS, rows // BLOCK):
        out_copy(block_index).wait()


def attend(lengths, table, q, k, v, first_pair, pairs, before=()):
    rows, width = q.shape
    together = max(size for size in (1, 2, 3) if pairs % size == 0 and first_pair % size == 0)
    column = pl.BlockSpec((rows, BLOCK * together), lambda p: (0, first_pair // together + p))
    return pl.pallas_call(
        functools.partial(attend_kernel, first_pair),
        grid=(pairs // together,),
        in_specs=[smem, whole(table.shape), column, column, column] + [anywhere] * len(before),
        out_specs=[column, column, anywhere],
        out_shape=[
            jax.ShapeDtypeStruct((rows, width), BF16),
            jax.ShapeDtypeStruct((rows, width), F32),
            jax.ShapeDtypeStruct((HEADS, rows, WINDOW), BF16),
        ],
        scratch_shapes=[
            pltpu.VMEM((16, WINDOW + BLOCK), F32),
            pltpu.VMEM((2 * together, BLOCK, WINDOW), F32),
            pltpu.VMEM((rows, BLOCK), jnp.int32),
            pltpu.VMEM((8, rows), jnp.int32),
            pltpu.VMEM((SLOTS, 2 * together, BLOCK, WINDOW), BF16),
            pltpu.SemaphoreType.DMA((SLOTS,)),
        ],
        input_output_aliases={5 + index: index for index in range(len(before))},
        compiler_params=params(),
        cost_estimate=pl.CostEstimate(
            flops=pairs * 8 * rows * 512 * 128, bytes_accessed=pairs * 6 * MIB, transcendentals=2 * pairs * rows * 512
        ),
        name="attend",
    )(lengths, table, q, k, v, *before)


def gelu_and_slope(v):
    bell = jnp.exp(-0.5 * v * v)
    t = 1.0 / (1.0 + (0.3275911 * root_half) * jnp.abs(v))
    series = t * (
        0.5 * 0.254829592
        + t * (0.5 * -0.284496736 + t * (0.5 * 1.421413741 + t * (0.5 * -1.453152027 + t * (0.5 * 1.061405429))))
    )
    tail = series * bell
    share = jnp.where(v >= 0.0, 1.0 - tail, tail)
    return v * share, share + v * bell * inv_root_tau


def member_of(lengths_ref, rows, count):
    bounds = bounds_of(lengths_ref, lengths_ref.shape[1])
    segment = segment_of(lax.broadcasted_iota(jnp.int32, (rows, count), 0), bounds)
    return (segment == lax.broadcasted_iota(jnp.int32, (rows, count), 1)).astype(F32).astype(BF16)


def member_rows(lengths_ref, rows, count):
    bounds = bounds_of(lengths_ref, lengths_ref.shape[1])
    segment = segment_of(lax.broadcasted_iota(jnp.int32, (count, rows), 1), bounds)
    return (segment == lax.broadcasted_iota(jnp.int32, (count, rows), 0)).astype(F32).astype(BF16)


def inner_copies(place_ref, refs, inner_ref):
    rows = refs[0].shape[0]
    width = inner_ref.shape[0]
    for other in range(2):
        owner = owner_of(place_ref, 0, other)
        yield refs[other], inner_ref.at[pl.ds(pl.multiple_of(owner * rows, 16), rows), :]
        for near in range(4):
            piece = refs[2 + 4 * other + near]
            quarter = place_ref[2] ^ near
            for far in range(1, 4):
                owner = owner_of(place_ref, far, other)
                row = pl.ds(pl.multiple_of(owner * rows, 16), rows)
                column = pl.ds(pl.multiple_of(quarter * width, 128), width)
                yield piece.at[far - 1], inner_ref.at[row, column]


def forward_kernel(place_ref, lengths_ref, x_ref, mixed_ref, gain_ref, heads_ref, wu_any, *refs):
    *pieces, out_ref, slope_ref, active_sum_ref, message_ref, mid_out, hid_out, wi_out = refs[:-12]
    total_ref, mid_ref, hid_ref, member_ref, wo_ref, inner_ref, active_ref = refs[-12:-5]
    wi_ref, wu_ref, sems, out_sems, last_sems = refs[-5:]
    step = pl.program_id(0)
    rows, width = hid_ref.shape
    block = rows // 4
    outs = ((wi_ref, wi_out), (hid_ref, hid_out), (mid_ref, mid_out))
    if len(pieces) == 1:
        groups = [[(pieces[0], wi_ref)], [(wu_any, wu_ref)]]
    else:
        groups = [list(inner_copies(place_ref, pieces, wi_ref)), [(wu_any, wu_ref)]]
    firsts = [0, len(groups[0])]
    spans = [slice(index * block, (index + 1) * block) for index in range(4)]

    def arrive(index):
        pairs = groups[index]
        wait_copies([pltpu.make_async_copy(*pair, sems.at[firsts[index] + at]) for at, pair in enumerate(pairs)])

    @pl.when(step == 0)
    def _():
        output_copy = pltpu.make_async_copy(heads_ref.at[3], wo_ref, last_sems.at[0])
        output_copy.start()
        for group, first in zip(groups, firsts):
            start_copies(group, sems, first)
        member_ref[...] = member_rows(lengths_ref, rows, 16)
        output_copy.wait()
        for span in spans:
            middle = x_ref[span, :].astype(F32) + dot_nn(mixed_ref[span, :], wo_ref[...])
            scale = lax.rsqrt(jnp.mean(middle * middle, -1, keepdims=True) + epsilon)
            total_ref[span, :] = middle
            mid_ref[span, :] = middle
            hid_ref[span, :] = (middle * scale * gain_ref[...].astype(F32)).astype(BF16)
        arrive(0)
        for index, pair in enumerate(outs):
            pltpu.make_async_copy(*pair, out_sems.at[index]).start()

    columns = pl.ds(pl.multiple_of(step * CHUNK, CHUNK), CHUNK)

    def first(span):
        inner_ref[span, :] = dot_nn(hid_ref[span, :], wi_ref[:, columns])

    def second(span):
        for at in range(span.start, span.stop, 32):
            active, slope = gelu_and_slope(inner_ref[at : at + 32, :])
            active_ref[at : at + 32, :] = active.astype(BF16)
            slope_ref[at : at + 32, :] = slope.astype(BF16)

    first(spans[0])
    first(spans[1])
    second(spans[0])

    @pl.when(step == 0)
    def _():
        arrive(1)

    for index, span in enumerate(spans):
        total_ref[span, :] += dot_nn(active_ref[span, :], wu_ref[columns, :])
        if index + 2 < 4:
            first(spans[index + 2])
        if index + 1 < 4:
            second(spans[index + 1])
    active_sum_ref[...] = dot_nn(member_ref[...], active_ref[...])

    @pl.when(step == pl.num_programs(0) - 1)
    def _():
        out_ref[...] = total_ref[...].astype(BF16)
        member = member_ref[...]
        pooled = jnp.zeros((16, width), F32)
        for span in spans:
            for piece in split_two(total_ref[span, :]):
                pooled = pooled + dot_nn(member[:, span], piece)
        row = lax.broadcasted_iota(jnp.int32, (8, 128), 0)
        lens = jnp.zeros((8, 128), jnp.int32)
        for index in range(8):
            lens = jnp.where(row == index, lengths_ref[0, index], lens)
        lens = lens.astype(F32)
        mean = pooled[0:8] / jnp.concatenate([lens] * (width // 128), 1)
        lower = jnp.concatenate([mean[:, 512:], lens, lens], 1)
        message_ref[...] = jnp.concatenate([mean[:, :512], lower], 0).astype(BF16)
        for index, pair in enumerate(outs):
            pltpu.make_async_copy(*pair, out_sems.at[index]).wait()


def forward(place, lengths, x, mixed, gain, heads, wu, units, pieces):
    rows, width = x.shape
    full = whole((rows, width))
    return pl.pallas_call(
        forward_kernel,
        grid=(units // CHUNK,),
        in_specs=[smem, smem, full, full, whole((1, width)), in_hbm, in_hbm] + [in_hbm] * len(pieces),
        out_specs=[
            pl.BlockSpec((rows, width), lambda i: (0, 0)),
            pl.BlockSpec((rows, CHUNK), lambda i: (0, i)),
            pl.BlockSpec((16, CHUNK), lambda i: (0, i)),
            pl.BlockSpec((16, 512), lambda i: (0, 0)),
        ]
        + [anywhere] * 3,
        out_shape=[
            jax.ShapeDtypeStruct((rows, width), BF16),
            jax.ShapeDtypeStruct((rows, units), BF16),
            jax.ShapeDtypeStruct((16, units), F32),
            pltpu.HBM((16, 512), BF16),
            jax.ShapeDtypeStruct((rows, width), F32),
            jax.ShapeDtypeStruct((rows, width), BF16),
            jax.ShapeDtypeStruct((width, units), BF16),
        ],
        scratch_shapes=[
            pltpu.VMEM((rows, width), F32),
            pltpu.VMEM((rows, width), F32),
            pltpu.VMEM((rows, width), BF16),
            pltpu.VMEM((16, rows), BF16),
            pltpu.VMEM((width, width), BF16),
            pltpu.VMEM((rows, CHUNK), F32),
            pltpu.VMEM((rows, CHUNK), BF16),
            pltpu.VMEM((width, units), BF16),
            pltpu.VMEM((units, width), BF16),
            pltpu.SemaphoreType.DMA((27,)),
            pltpu.SemaphoreType.DMA((3,)),
            pltpu.SemaphoreType.DMA((1,)),
        ],
        compiler_params=params(),
        cost_estimate=pl.CostEstimate(
            flops=4 * rows * width * units, bytes_accessed=30 * MIB, transcendentals=2 * rows * units
        ),
        name="feed_forward",
    )(place, lengths, x, mixed, gain, heads, wu, *pieces)


def contrast_kernel(place_ref, own_ref, got_ref, target_ref, wp_any, *refs):
    loss_ref, grad_wp_ref, glow_all_ref, grows_ref, glow_ref = refs[:-7]
    wide_ref, line_ref, full_ref, wp_ref, left_ref, right_ref, sems = refs[-7:]
    count, width = wide_ref.shape
    pending = start_copies([(wp_any, wp_ref)], sems)
    for other, ref in enumerate((own_ref, got_ref)):
        for far in range(4):
            for near in range(4):
                device = (place_ref[2] ^ near) * 8 + owner_of(place_ref, far, other)
                start = pl.multiple_of(device * 8, 8)
                piece = ref[near, far].astype(F32)
                left_ref[pl.ds(start, 8), :] = piece[0:8]
                right_ref[pl.ds(start, 8), :] = piece[8:16]
    rest = width - left_ref.shape[1]
    pooled = jnp.concatenate([left_ref[...], right_ref[:, 0:rest]], 1).astype(BF16)
    lens = right_ref[:, rest : rest + 1]
    wait_copies(pending)
    first = pl.multiple_of(place_ref[0] * 8, 8)
    projected = dot_nn(pooled, wp_ref[...])
    inverse = lax.rsqrt(jnp.sum(projected * projected, -1, keepdims=True) + epsilon)
    embedded = (projected * inverse).astype(BF16)
    row = lax.broadcasted_iota(jnp.int32, (count, count), 0)
    column = lax.broadcasted_iota(jnp.int32, (count, count), 1)
    logits = logit_scale * dot_nt(embedded, embedded)
    logits = jnp.where(row == column, -1000000000.0, logits)
    target_at = jnp.sum(jnp.where(row == column, target_ref[...], 0), -1, keepdims=True)
    hit = column == target_at
    highest = jnp.max(logits, -1, keepdims=True)
    totals = highest + jnp.log(jnp.sum(jnp.exp(logits - highest), -1, keepdims=True))
    target = jnp.sum(jnp.where(hit, logits, 0.0), -1, keepdims=True)
    line_ref[...] = jnp.broadcast_to(totals - target, line_ref.shape)
    loss_ref[...] = line_ref[pl.ds(first, 8), :]
    grad_logits = (jnp.exp(logits - totals) - hit.astype(F32)).astype(BF16)
    grad_embedded = logit_scale * (dot_nn(grad_logits, embedded) + dot_tn(grad_logits, embedded))
    along = jnp.sum(grad_embedded * projected, -1, keepdims=True)
    grad_projected = inverse * grad_embedded - projected * (inverse * inverse * inverse * along)
    high, low = split_two(grad_projected)
    full_ref[...] = dot_tn(pooled, high) + dot_tn(pooled, low)
    share = grad_wp_ref.shape[0]
    grad_wp_ref[...] = full_ref[pl.ds(pl.multiple_of(place_ref[1] * share, share), share), :]
    wp = wp_ref[...]
    grad_rows = (dot_nt(high, wp) + dot_nt(low, wp)) / lens
    glow_all_ref[...] = grad_rows.astype(BF16)
    wide_ref[...] = grad_rows
    own_rows = wide_ref[pl.ds(first, 8), :]
    grows_ref[...] = own_rows
    glow_ref[...] = jnp.concatenate([own_rows, jnp.zeros_like(own_rows)], 0).astype(BF16)


def contrast(place, own, got, targets, wp, share):
    count = targets.shape[1]
    width = wp.shape[1]
    ins = [own, got, targets]
    outs = [
        jax.ShapeDtypeStruct((8, 128), F32),
        jax.ShapeDtypeStruct((share, width), F32),
        jax.ShapeDtypeStruct((count, width), BF16),
        jax.ShapeDtypeStruct((8, width), F32),
        jax.ShapeDtypeStruct((16, width), BF16),
    ]
    return pl.pallas_call(
        contrast_kernel,
        grid=(1,),
        in_specs=[smem] + [whole(array.shape) for array in ins] + [in_hbm],
        out_specs=[pl.BlockSpec(out.shape, lambda i: (0, 0)) for out in outs],
        out_shape=outs,
        scratch_shapes=[
            pltpu.VMEM((count, width), F32),
            pltpu.VMEM((count, 128), F32),
            pltpu.VMEM((width, width), F32),
            pltpu.VMEM((width, width), BF16),
            pltpu.VMEM((count, 512), F32),
            pltpu.VMEM((count, 512), F32),
            pltpu.SemaphoreType.DMA((1,)),
        ],
        compiler_params=params(),
        cost_estimate=pl.CostEstimate(flops=4 * count * width * width, bytes_accessed=8 * MIB, transcendentals=0),
        name="contrast",
    )(place, *ins, wp)


def contrast_plain(place, pooled, lens, targets, wp, share):
    count, width = pooled.shape
    exact = lax.Precision.HIGHEST
    projected = jnp.dot(pooled, wp, preferred_element_type=F32)
    inverse = lax.rsqrt(jnp.sum(projected * projected, -1, keepdims=True) + epsilon)
    embedded = (projected * inverse).astype(BF16)
    numbers = jnp.arange(count, dtype=jnp.int32)
    logits = logit_scale * dot_nt(embedded, embedded)
    logits = jnp.where(numbers[:, None] == numbers[None, :], -1000000000.0, logits)
    hit = numbers[None, :] == targets
    highest = jnp.max(logits, -1, keepdims=True)
    totals = highest + jnp.log(jnp.sum(jnp.exp(logits - highest), -1, keepdims=True))
    loss = totals - jnp.sum(jnp.where(hit, logits, 0.0), -1, keepdims=True)
    grad_logits = (jnp.exp(logits - totals) - hit.astype(F32)).astype(BF16)
    grad_embedded = logit_scale * (dot_nn(grad_logits, embedded) + dot_tn(grad_logits, embedded))
    along = jnp.sum(grad_embedded * projected, -1, keepdims=True)
    grad_projected = inverse * grad_embedded - projected * (inverse * inverse * inverse * along)
    own_columns = lax.dynamic_slice_in_dim(pooled.astype(F32), place[1] * share, share, 1)
    grad_wp = lax.dot_general(own_columns, grad_projected, (((0,), (0,)), ((), ())), precision=exact)
    grad_rows = jnp.dot(grad_projected, wp.astype(F32).T, precision=exact) / lens
    first = place[0] * 8
    own = lambda a: lax.dynamic_slice_in_dim(a, first, 8, 0)
    return jnp.broadcast_to(own(loss), (8, 128)), grad_wp, grad_rows.astype(BF16), own(grad_rows)


def fold(result_ref, keep_ref, send_ref, place_ref, column_half, column):
    narrow, plane, core = place_ref[2], place_ref[3], place_ref[4]
    rows = keep_ref.shape[2]
    for near in range(2):
        quarter = 2 * ((narrow // 2) ^ column_half) + near
        half = (narrow % 2) ^ near
        for far in range(4):
            for ref, owner in ((keep_ref, core), (send_ref, 1 - core)):
                start = pl.multiple_of((2 * (plane ^ far) + owner) * 2 * rows + half * rows, 16)
                block = result_ref[pl.ds(start, rows), :].astype(BF16)
                ref[quarter, far, :, pl.ds(column, block.shape[1])] = block


def back_kernel(
    lengths_ref, place_ref, glow_ref, grows_ref, gain_ref, hid_ref, active_ref, wu_ref, slope_ref, wi_ref,
    mid_any, mixed_any, inv_any, heads_any, gmid_any, gmix_ref, *refs,
):
    *grad_refs, result_ref, total_ref, member_ref, mid_ref, mixed_ref, inv_ref, wo_ref, sems, out_sems, gi_ref = refs
    step = pl.program_id(0)
    last = pl.num_programs(0) - 1
    rows, width = total_ref.shape
    folded = len(grad_refs) == 2 and len(grad_refs[1].shape) == 3
    late = [(mid_any, mid_ref), (mixed_any, mixed_ref), (inv_any, inv_ref), (heads_any.at[3], wo_ref)]

    @pl.when(step == 0)
    def _():
        member = member_of(lengths_ref, rows, 16)
        member_ref[...] = jnp.concatenate([member, member], 1)

    @pl.when(step == 0)
    def _():
        total_ref[...] = jnp.zeros_like(total_ref)

    @pl.when(step == 2)
    def _():
        start_copies(late, sems)

    high, low = split_two(dot_nt(glow_ref[...], wu_ref[...]))
    both = jnp.concatenate([high, low], 0)
    spans = (slice(0, rows // 2), slice(rows // 2, rows))
    for span in spans:
        spread = dot_nn(member_ref[span, :], both)
        gi_ref[span, :] = (spread * slope_ref[span, :].astype(F32)).astype(BF16)
    for span in spans:
        total_ref[span, :] += dot_nt(gi_ref[span, :], wi_ref[...])
    result_ref[:, :CHUNK] = dot_tn(hid_ref[...], gi_ref[...])

    if folded:
        grad_any, grad_ref = grad_refs
        owners, lines, _ = grad_ref.shape
        lines = lines - 8
        units = active_ref.shape[1]
        columns = pl.ds(pl.multiple_of(step * CHUNK, CHUNK), CHUNK)
        for owner in range(owners):
            grad_ref[owner, 0:lines, columns] = result_ref[owner * lines : (owner + 1) * lines, :CHUNK].astype(BF16)

        @pl.when(step == 0)
        def _():
            share = units // owners
            start = pl.multiple_of(place_ref[1] * share, 128)
            for owner in range(owners):
                grad_ref[owner, lines:, 0:units] = jnp.zeros((8, units), BF16)
                grad_ref[owner, lines:, pl.ds(start, share)] = active_ref[0:8, owner * share : (owner + 1) * share].astype(BF16)
    else:
        grad_refs[0][:, pl.ds(pl.multiple_of(step * CHUNK, CHUNK), CHUNK)] = result_ref[:, :CHUNK].astype(BF16)

    @pl.when(step == last)
    def _():
        pending = []
        if folded:
            inner_columns = pl.ds(0, units)
            copy = pltpu.make_async_copy(
                grad_ref.at[:, :, inner_columns], grad_any.at[:, :, inner_columns], out_sems.at[0]
            )
            copy.start()
            pending.append(copy)
        wait_copies([pltpu.make_async_copy(*pair, sems.at[index]) for index, pair in enumerate(late)])
        bounds = bounds_of(lengths_ref, lengths_ref.shape[1])
        block = rows // 8
        for index in range(8):
            span = slice(index * block, (index + 1) * block)
            middle = mid_ref[span, :]
            scale = lax.rsqrt(jnp.mean(middle * middle, -1, keepdims=True) + epsilon)
            normed = middle * scale
            scaled = total_ref[span, :] * gain_ref[...].astype(F32)
            centre = jnp.mean(scaled * normed, -1, keepdims=True)
            segment = segment_of(lax.broadcasted_iota(jnp.int32, (block, 128), 0) + index * block, bounds)
            segment = jnp.concatenate([segment] * (width // 128), 1)
            grad_rows = jnp.zeros((block, width), F32)
            for passage in range(8):
                grad_rows = jnp.where(segment == passage, grows_ref[passage : passage + 1, :], grad_rows)
            total_ref[span, :] = grad_rows + scale * (scaled - normed * centre)
        copy = pltpu.make_async_copy(total_ref, gmid_any, out_sems.at[2])
        copy.start()
        pending.append(copy)
        columns = width // 2
        for side in range(2):
            grad = dot_tn(mixed_ref[...], total_ref[:, side * columns : (side + 1) * columns].astype(BF16))
            if folded:
                span = slice(units + side * columns, units + (side + 1) * columns)
                for owner in range(owners):
                    grad_ref[owner, 0:lines, span] = grad[owner * lines : (owner + 1) * lines].astype(BF16)
            else:
                grad_refs[1][:, side * columns : (side + 1) * columns] = grad.astype(BF16)
        if folded:
            rest = pl.ds(units, width)
            copy = pltpu.make_async_copy(grad_ref.at[:, :, rest], grad_any.at[:, :, rest], out_sems.at[1])
            copy.start()
            pending.append(copy)
        for index in range(4):
            span = slice(index * 2 * block, (index + 1) * 2 * block)
            low_rows = total_ref[span, :].astype(BF16)
            gmix_ref[span, :] = (dot_nt(low_rows, wo_ref[...]) * inv_ref[span, :]).astype(BF16)
        wait_copies(pending)


def back(lengths, place, glow, grows, gain, hidden, active_sum, wu, slope, wi, middle, mixed, inv, heads, folded):
    rows, width = hidden.shape
    units = slope.shape[1]
    full = pl.BlockSpec((rows, width), lambda i: (0, 0))
    if folded:
        slab = (8, width // 8 + 8, units + width)
        grad_shape = [pltpu.HBM(slab, BF16)]
        grad_specs = [anywhere]
        grad_scratch = [pltpu.VMEM(slab, BF16)]
    else:
        shapes = [(width, units), (width, width)]
        grad_shape = [jax.ShapeDtypeStruct(shape, BF16) for shape in shapes]
        grad_specs = [pl.BlockSpec(shape, lambda i: (0, 0)) for shape in shapes]
        grad_scratch = []
    return pl.pallas_call(
        back_kernel,
        grid=(units // CHUNK,),
        in_specs=[
            smem,
            smem,
            whole((16, width)),
            whole((8, width)),
            whole((1, width)),
            whole((rows, width)),
            whole(active_sum.shape),
            pl.BlockSpec((CHUNK, width), lambda i: (i, 0)),
            pl.BlockSpec((rows, CHUNK), lambda i: (0, i)),
            pl.BlockSpec((width, CHUNK), lambda i: (0, i)),
        ]
        + [anywhere] * 4,
        out_specs=[anywhere, full] + grad_specs,
        out_shape=[jax.ShapeDtypeStruct((rows, width), F32), jax.ShapeDtypeStruct((rows, width), BF16)] + grad_shape,
        scratch_shapes=grad_scratch
        + [
            pltpu.VMEM((width, CHUNK), F32),
            pltpu.VMEM((rows, width), F32),
            pltpu.VMEM((rows, 32), BF16),
            pltpu.VMEM((rows, width), F32),
            pltpu.VMEM((rows, width), BF16),
            pltpu.VMEM((rows, width), F32),
            pltpu.VMEM((width, width), BF16),
            pltpu.SemaphoreType.DMA((4,)),
            pltpu.SemaphoreType.DMA((5,)),
            pltpu.VMEM((rows, CHUNK), BF16),
        ],
        compiler_params=params(),
        cost_estimate=pl.CostEstimate(flops=5 * rows * width * units, bytes_accessed=40 * MIB, transcendentals=0),
        name="back",
    )(lengths, place, glow, grows, gain, hidden, active_sum, wu, slope, wi, middle, mixed, inv, heads)


def attend_grad_kernel(first_pair, lengths_ref, q_ref, k_ref, v_ref, gm_ref, mixed_ref, p_any, *refs):
    grad_ref, diag_ref, qm_ref, km_ref, vx_ref, gx_ref, go_ref, ak_ref, av_ref, acc_ref, p_ref, sems = refs[-12:]
    together = q_ref.shape[1] // BLOCK
    rows = q_ref.shape[0]
    first_head = 2 * (first_pair + together * pl.program_id(0))

    def in_copy(block_index):
        slot = block_index % SLOTS
        source = p_any.at[pl.ds(first_head, 2 * together), pl.ds(pl.multiple_of(block_index * BLOCK, BLOCK), BLOCK), :]
        return pltpu.make_async_copy(source, p_ref.at[slot], sems.at[slot])

    for block_index in range(SLOTS - 1):
        in_copy(block_index).start()
    bounds = bounds_of(lengths_ref, lengths_ref.shape[1])
    reach = WINDOW + BLOCK
    acc_ref[...] = jnp.zeros_like(acc_ref)
    ak_ref[...] = jnp.zeros_like(ak_ref)
    av_ref[...] = jnp.zeros_like(av_ref)

    lane = lax.broadcasted_iota(jnp.int32, (BLOCK, BLOCK), 1)
    row = lax.broadcasted_iota(jnp.int32, (BLOCK, BLOCK), 0)
    across = jnp.where((row < HEAD_DIM) != (lane < HEAD_DIM), -1.0, 0.0).astype(BF16)

    def prepare(index, carry):
        span = pl.ds(pl.multiple_of(index * BLOCK, BLOCK), BLOCK)
        for near in range(together):
            lanes = slice(near * BLOCK, near * BLOCK + BLOCK)
            q, k, v, g = q_ref[span, lanes], k_ref[span, lanes], v_ref[span, lanes], gm_ref[span, lanes]
            product = split_two(g.astype(F32) * mixed_ref[span, lanes].astype(F32))
            centre = dot_nn(product[0], across) + dot_nn(product[1], across)
            high, low = split_two(centre)
            first = (lane == 0) | (lane == HEAD_DIM)
            second = (lane == 1) | (lane == HEAD_DIM + 1)
            zero = jnp.zeros_like(q)
            extra = jnp.where(first, high, jnp.where(second, low, zero))
            one = jnp.ones_like(v)
            for half in range(2):
                head = 2 * near + half
                mine = (lane < HEAD_DIM) if half == 0 else (lane >= HEAD_DIM)
                qm_ref[head, span, :] = jnp.where(mine, q, zero)
                km_ref[head, span, :] = jnp.where(mine, k, zero)
                go_ref[head, span, :] = jnp.where(mine, g, zero)
                vx_ref[head, span, :] = jnp.where(mine, v, one)
                gx_ref[head, span, :] = jnp.where(mine, g, extra)
        return carry

    lax.fori_loop(0, rows // BLOCK, prepare, 0)

    def one(block_index, carry):
        slot = block_index % SLOTS
        start = pl.multiple_of(block_index * BLOCK, BLOCK)
        in_copy(block_index).wait()

        @pl.when(block_index + SLOTS - 1 < rows // BLOCK)
        def _():
            in_copy(block_index + SLOTS - 1).start()

        first, count = window_of(bounds, start)
        first = pl.multiple_of(first, BLOCK)
        shift = pl.multiple_of(first - start + SPAN, BLOCK)

        def body(blocks):
            size = blocks * BLOCK
            queries = pl.ds(start, BLOCK)
            keys = pl.ds(first, size)
            spread = [dot_nt(gx_ref[head, queries, :], vx_ref[head, keys, :]) for head in range(2 * together)]
            for near in range(together):
                heads = (2 * near, 2 * near + 1)
                lanes = slice(near * BLOCK, near * BLOCK + BLOCK)
                parts = []
                raised = []
                for head in heads:
                    p = p_ref[slot, head, :, 0:size]
                    grad_scores = p.astype(F32) * spread[head]
                    acc_ref[head, :, pl.ds(shift, size)] += grad_scores
                    parts.append(grad_scores.astype(BF16))
                    raised.append(p)
                q_both = jnp.concatenate([qm_ref[head, queries, :] for head in heads], 0)
                g_both = jnp.concatenate([go_ref[head, queries, :] for head in heads], 0)
                k_both = jnp.concatenate([km_ref[head, keys, :] for head in heads], 0)
                ak_ref[lanes, keys] += dot_tn(q_both, jnp.concatenate(parts, 0))
                av_ref[lanes, keys] += dot_tn(g_both, jnp.concatenate(raised, 0))
                grad_ref[0, queries, lanes] = dot_nn(jnp.concatenate(parts, 1), k_both).astype(BF16)

        for blocks in range(1, WINDOW // BLOCK + 1):
            pl.when(count == blocks)(functools.partial(body, blocks))
        return carry

    lax.fori_loop(0, rows // BLOCK, one, 0)
    for near in range(together):
        lanes = slice(near * BLOCK, near * BLOCK + BLOCK)
        grad_ref[1, :, lanes] = jnp.transpose(ak_ref[lanes, :]).astype(BF16)
        grad_ref[2, :, lanes] = jnp.transpose(av_ref[lanes, :]).astype(BF16)
    for head in range(2 * together):
        padded = jnp.concatenate([jnp.zeros((BLOCK, BLOCK), F32), acc_ref[head]], 1)
        group = padded[0:8]
        for index in range(1, BLOCK // 8):
            group = group + pltpu.roll(padded[8 * index : 8 * index + 8], reach - 8 * index, 1)
        line = group[0:1]
        for index in range(1, 8):
            line = line + pltpu.roll(group, reach - index, 1)[index : index + 1]
        diag_ref[head // 2, head % 2 : head % 2 + 1, :] = line


def attend_grad(lengths, q, k, v, gm, mixed, p, first_pair, pairs, before=()):
    rows, width = q.shape
    together = max(size for size in (1, 2, 3) if pairs % size == 0 and first_pair % size == 0)
    at = first_pair // together
    column = pl.BlockSpec((rows, BLOCK * together), lambda i: (0, at + i))
    return pl.pallas_call(
        functools.partial(attend_grad_kernel, first_pair),
        grid=(pairs // together,),
        in_specs=[smem]
        + [column] * 5
        + [in_hbm]
        + [anywhere] * len(before),
        out_specs=[
            pl.BlockSpec((3, rows, BLOCK * together), lambda i: (0, 0, at + i)),
            pl.BlockSpec((together, 2, WINDOW + BLOCK), lambda i: (at + i, 0, 0)),
        ],
        out_shape=[
            jax.ShapeDtypeStruct((3, rows, width), BF16),
            jax.ShapeDtypeStruct((HEADS // 2, 2, WINDOW + BLOCK), F32),
        ],
        scratch_shapes=[pltpu.VMEM((2 * together, rows, BLOCK), BF16)] * 5
        + [pltpu.VMEM((BLOCK * together, rows), F32)] * 2
        + [
            pltpu.VMEM((2 * together, BLOCK, WINDOW), F32),
            pltpu.VMEM((SLOTS, 2 * together, BLOCK, WINDOW), BF16),
            pltpu.SemaphoreType.DMA((SLOTS,)),
        ],
        input_output_aliases={7 + index: index for index in range(len(before))},
        compiler_params=params(),
        cost_estimate=pl.CostEstimate(
            flops=pairs * 20 * rows * 512 * 64, bytes_accessed=pairs * 5 * MIB, transcendentals=0
        ),
        name="attend_grad",
    )(lengths, q, k, v, gm, mixed, p, *before)


def head_grad_kernel(place_ref, hid_any, grad_any, table_ref, keep_ref, send_ref, hid_ref, grad_ref, result_ref, sems):
    block = result_ref.shape[2]
    pairs = [(hid_any, hid_ref)]
    for matrix in range(3):
        for side in range(2):
            columns = pl.ds(side * block, block)
            pairs.append((grad_any.at[matrix, :, columns], grad_ref.at[matrix, :, columns]))
    pending = start_copies(pairs, sems)
    rows = keep_ref.shape[2]
    for far in range(4):
        for ref, other in ((keep_ref, 0), (send_ref, 1)):
            line = table_ref[pl.ds(owner_of(place_ref, far, other), 1), :]
            block_of = jnp.broadcast_to(line, (rows, 128)).astype(BF16)
            for quarter in range(4):
                ref[quarter, far, :, 3 * block :] = block_of
    pending[0].wait()
    for step in range(6):
        pending[1 + step].wait()
        columns = slice(step % 2 * block, step % 2 * block + block)
        result_ref[step % 2] = dot_tn(hid_ref[...], grad_ref[step // 2, :, columns])
        fold(result_ref.at[step % 2], keep_ref, send_ref, place_ref, step // 3, step % 3 * block)


def head_grad(place, hidden, grads, table):
    rows, width = hidden.shape
    block = width // 2
    slab = (4, 4, width // 16, 3 * block + 128)
    return pl.pallas_call(
        head_grad_kernel,
        in_specs=[smem, in_hbm, in_hbm, in_vmem],
        out_specs=[in_vmem] * 2,
        out_shape=[jax.ShapeDtypeStruct(slab, BF16)] * 2,
        scratch_shapes=[
            pltpu.VMEM((rows, width), BF16),
            pltpu.VMEM((3, rows, width), BF16),
            pltpu.VMEM((2, width, block), F32),
            pltpu.SemaphoreType.DMA((7,)),
        ],
        compiler_params=pltpu.CompilerParams(vmem_limit_bytes=28 * MIB),
        cost_estimate=pl.CostEstimate(flops=6 * rows * width * width, bytes_accessed=12 * MIB, transcendentals=0),
        name="head_grad",
    )(place, hidden, grads, table)


def token_grad_kernel(x_ref, gain_ref, gmid_ref, grad_ref, w_ref, out_ref):
    x = x_ref[...].astype(F32)
    scale = lax.rsqrt(jnp.mean(x * x, -1, keepdims=True) + epsilon)
    normed = x * scale
    grad_hidden = dot_nt(grad_ref[0], w_ref[0]) + dot_nt(grad_ref[1], w_ref[1]) + dot_nt(grad_ref[2], w_ref[2])
    scaled = grad_hidden * gain_ref[...].astype(F32)
    centre = jnp.mean(scaled * normed, -1, keepdims=True)
    out_ref[...] = gmid_ref[...] + scale * (scaled - normed * centre)


def token_grad(x, gain, gmid, grads, weights):
    rows, width = x.shape
    block = rows // 4
    row_spec = pl.BlockSpec((block, width), lambda i: (i, 0))
    return pl.pallas_call(
        token_grad_kernel,
        grid=(4,),
        in_specs=[
            row_spec,
            whole((1, width)),
            row_spec,
            pl.BlockSpec((3, block, width), lambda i: (0, i, 0)),
            whole((3, width, width)),
        ],
        out_specs=row_spec,
        out_shape=jax.ShapeDtypeStruct((rows, width), F32),
        compiler_params=params(),
        cost_estimate=pl.CostEstimate(flops=6 * rows * width * width, bytes_accessed=16 * MIB, transcendentals=0),
        name="token_grad",
    )(x, gain, gmid, grads, weights)


def outer_grad_kernel(place_ref, pieces_ref, glow_ref, out_ref, active_ref):
    units = active_ref.shape[1]
    for near in range(4):
        start = pl.multiple_of((place_ref[2] ^ near) * 64, 64)
        for owner in range(8):
            half = 8 * (owner // 4)
            column = owner % 4 * units
            block = pieces_ref[near].astype(F32)[half : half + 8, column : column + units]
            active_ref[pl.ds(start + 8 * owner, 8), :] = block
    out_ref[...] = dot_tn(active_ref[...].astype(BF16), glow_ref[...])


def outer_grad(place, pieces, glow):
    count, width = glow.shape
    units = pieces.shape[2] // 4
    return pl.pallas_call(
        outer_grad_kernel,
        grid=(1,),
        in_specs=[smem, whole(pieces.shape), whole(glow.shape)],
        out_specs=pl.BlockSpec((units, width), lambda i: (0, 0)),
        out_shape=jax.ShapeDtypeStruct((units, width), F32),
        scratch_shapes=[pltpu.VMEM((count, units), F32)],
        compiler_params=params(),
        cost_estimate=pl.CostEstimate(flops=2 * count * units * width, bytes_accessed=3 * MIB, transcendentals=0),
        name="outer_grad",
    )(place, pieces, glow)


def table_grad(diag):
    reach = WINDOW + BLOCK
    offsets = jnp.arange(reach, dtype=jnp.int32) - (SPAN + BLOCK)
    onehot = (bucket_of(offsets)[:, None] == jnp.arange(BUCKETS, dtype=jnp.int32)[None, :]).astype(F32)
    sums = jnp.dot(diag.reshape(HEADS, reach), onehot, precision=lax.Precision.HIGHEST)
    return sums.T.reshape(BUCKETS * HEADS)


def exchange(value, narrow=0, plane=0, core=0):
    bits = narrow * 8 + plane * 2 + core
    return lax.ppermute(value, ("narrow", "wide"), [(i, i ^ bits) for i in range(32)])


def spread(value):
    return [value] + [exchange(value, narrow=near) for near in range(1, 4)]


def sum_core_kernel(keep_ref, got_ref, *out_refs):
    for quarter, out_ref in enumerate(out_refs):
        for far in range(4):
            out_ref[far] = (keep_ref[quarter, far].astype(F32) + got_ref[quarter, far].astype(F32)).astype(BF16)


def sum_core(keep, got):
    _, _, rows, columns = keep.shape
    return pl.pallas_call(
        sum_core_kernel,
        in_specs=[in_vmem] * 2,
        out_specs=[in_vmem] * 4,
        out_shape=[jax.ShapeDtypeStruct((4, rows, columns), BF16)] * 4,
        compiler_params=small,
        cost_estimate=pl.CostEstimate(flops=0, bytes_accessed=96 * rows * columns, transcendentals=0),
        name="sum_core",
    )(keep, got)


def sum_narrow_kernel(apart, a_ref, b_ref, c_ref, d_ref, *out_refs):
    refs = (a_ref, b_ref, c_ref, d_ref)
    columns = a_ref.shape[2] - (128 if apart else 0)
    for far, out_ref in enumerate(out_refs):
        total = sum(ref[far, :, :columns].astype(F32) for ref in refs)
        out_ref[:, :columns] = total.astype(BF16)
        if apart:
            for near, ref in enumerate(refs):
                out_ref[:, columns + 128 * near : columns + 128 * near + 128] = ref[far, :, columns:]


def sum_narrow(parts, apart):
    _, rows, columns = parts[0].shape
    columns += 3 * 128 if apart else 0
    return pl.pallas_call(
        functools.partial(sum_narrow_kernel, apart),
        in_specs=[in_vmem] * 4,
        out_specs=[in_vmem] * 4,
        out_shape=[jax.ShapeDtypeStruct((rows, columns), BF16)] * 4,
        compiler_params=small,
        cost_estimate=pl.CostEstimate(flops=0, bytes_accessed=40 * rows * columns, transcendentals=0),
        name="sum_narrow",
    )(*parts)


def sum_planes_kernel(a_ref, b_ref, c_ref, d_ref, total_ref, *apart_refs):
    refs = (a_ref, b_ref, c_ref, d_ref)
    columns = total_ref.shape[1]
    total_ref[...] = sum(ref[:, :columns].astype(F32) for ref in refs).astype(BF16)
    for apart_ref in apart_refs:
        for far, ref in enumerate(refs):
            apart_ref[far] = ref[:, columns:]


def sum_planes(parts, apart):
    rows, columns = parts[0].shape
    kept = 4 * 128 if apart else 0
    out_shape = [jax.ShapeDtypeStruct((rows, columns - kept), BF16)]
    if apart:
        out_shape.append(jax.ShapeDtypeStruct((4, rows, kept), BF16))
    return pl.pallas_call(
        sum_planes_kernel,
        in_specs=[in_vmem] * 4,
        out_specs=[in_vmem] * len(out_shape),
        out_shape=out_shape,
        compiler_params=small,
        cost_estimate=pl.CostEstimate(flops=0, bytes_accessed=10 * rows * columns, transcendentals=0),
        name="sum_planes",
    )(*parts)


def cut_kernel(place_ref, part_ref, *out_refs):
    rows, columns = out_refs[0].shape
    rows = rows - 16
    total = part_ref.shape[1]
    units = total * 4 // 5
    for near, out_ref in enumerate(out_refs):
        quarter = place_ref[2] ^ near
        row = pl.ds(pl.multiple_of((quarter % 2) * rows, 16), rows)
        column = pl.multiple_of((quarter // 2) * (units // 2), 128)
        out_ref[0:rows, 0 : units // 2] = part_ref[row, pl.ds(column, units // 2)]
        column = pl.multiple_of(units + (quarter // 2) * (columns - units // 2), 128)
        out_ref[0:rows, units // 2 :] = part_ref[row, pl.ds(column, columns - units // 2)]
        sums = part_ref[2 * rows :, 0:units].astype(F32)
        sums = jnp.concatenate([sums[:, : units // 2], sums[:, units // 2 :]], 0)
        out_ref[rows:, 0 : units // 2] = sums.astype(BF16)
        out_ref[rows:, units // 2 :] = jnp.zeros((16, columns - units // 2), BF16)


def cut(place, part):
    rows, total = part.shape
    shape = ((rows - 8) // 2 + 16, total // 2)
    return pl.pallas_call(
        cut_kernel,
        in_specs=[smem, in_vmem],
        out_specs=[in_vmem] * 4,
        out_shape=[jax.ShapeDtypeStruct(shape, BF16)] * 4,
        compiler_params=small,
        cost_estimate=pl.CostEstimate(flops=0, bytes_accessed=2 * MIB, transcendentals=0),
        name="cut",
    )(place, part)


def sum_quarter_kernel(a_ref, b_ref, c_ref, d_ref, total_ref, apart_ref):
    refs = (a_ref, b_ref, c_ref, d_ref)
    rows = total_ref.shape[0]
    total_ref[...] = sum(ref[0:rows, :].astype(F32) for ref in refs).astype(BF16)
    for near, ref in enumerate(refs):
        apart_ref[near] = ref[rows:, : apart_ref.shape[2]]


def sum_quarter(parts):
    rows, columns = parts[0].shape
    return pl.pallas_call(
        sum_quarter_kernel,
        in_specs=[in_vmem] * 4,
        out_specs=[in_vmem] * 2,
        out_shape=[
            jax.ShapeDtypeStruct((rows - 16, columns), BF16),
            jax.ShapeDtypeStruct((4, 16, columns * 4 // 5), BF16),
        ],
        compiler_params=small,
        cost_estimate=pl.CostEstimate(flops=0, bytes_accessed=2 * MIB, transcendentals=0),
        name="sum_quarter",
    )(*parts)


def as_row(column):
    return jnp.transpose(jnp.broadcast_to(column, (column.shape[0], 128)))[0:1]


def finish_inner_kernel(place_ref, weight_ref, gain_ref, a_ref, b_ref, c_ref, d_ref, out_ref, last_ref, ggain_ref):
    rows = a_ref.shape[0]
    units = weight_ref.shape[1] // 2
    width = last_ref.shape[1] // 2
    for near, ref in enumerate((a_ref, b_ref, c_ref, d_ref)):
        quarter = place_ref[2] ^ near
        row = pl.ds(pl.multiple_of((quarter % 2) * rows, rows), rows)
        half = quarter // 2
        out_ref[row, pl.ds(pl.multiple_of(half * units, 128), units)] = ref[:, :units].astype(F32)
        last_ref[row, pl.ds(pl.multiple_of(half * width, 128), width)] = ref[:, units:].astype(F32)
    along = jnp.sum(out_ref[...] * weight_ref[...].astype(F32), -1, keepdims=True)
    ggain_ref[...] = as_row(along) / gain_ref[...].astype(F32)


def finish_inner(place, weight, gain, parts, width):
    rows, units = weight.shape
    ins = [weight, gain] + list(parts)
    outs = [jax.ShapeDtypeStruct(shape, F32) for shape in ((rows, units), (rows, width), (1, rows))]
    return pl.pallas_call(
        finish_inner_kernel,
        in_specs=[smem] + [in_vmem] * len(ins),
        out_specs=[in_vmem] * len(outs),
        out_shape=outs,
        compiler_params=small,
        cost_estimate=pl.CostEstimate(flops=0, bytes_accessed=3 * MIB, transcendentals=0),
        name="finish_inner",
    )(place, *ins)


def finish_heads_kernel(place_ref, wq_ref, wk_ref, wv_ref, gain_ref, a_ref, b_ref, c_ref, d_ref, *refs):
    *out_refs, table_ref, ggain_ref, result_ref = refs
    rows = a_ref.shape[0]
    width = wq_ref.shape[1]
    half = 3 * width // 2
    for near, ref in enumerate((a_ref, b_ref, c_ref, d_ref)):
        quarter = place_ref[2] ^ near
        row = pl.multiple_of((quarter % 2) * rows, rows)
        column = pl.multiple_of((quarter // 2) * half, 128)
        result_ref[pl.ds(row, rows), pl.ds(column, half)] = ref[:, :half].astype(F32)

        @pl.when(quarter == 0)
        def _():
            table_ref[...] = ref[0:16, half:].astype(F32)[0:1, : table_ref.shape[1]]

    along = jnp.zeros((2 * rows, 1), F32)
    for index, (out_ref, weight_ref) in enumerate(zip(out_refs, (wq_ref, wk_ref, wv_ref))):
        grad = result_ref[:, index * width : (index + 1) * width]
        out_ref[...] = grad
        along = along + jnp.sum(grad * weight_ref[...].astype(F32), -1, keepdims=True)
    ggain_ref[...] = as_row(along) / gain_ref[...].astype(F32)


def finish_heads(place, weights, gain, parts, table_share):
    rows, width = weights[0].shape
    ins = list(weights) + [gain] + list(parts)
    outs = [jax.ShapeDtypeStruct((rows, width), F32)] * 3
    outs += [jax.ShapeDtypeStruct((1, table_share), F32), jax.ShapeDtypeStruct((1, rows), F32)]
    return pl.pallas_call(
        finish_heads_kernel,
        in_specs=[smem] + [in_vmem] * len(ins),
        out_specs=[in_vmem] * len(outs),
        out_shape=outs,
        scratch_shapes=[pltpu.VMEM((rows, 3 * width), F32)],
        compiler_params=small,
        cost_estimate=pl.CostEstimate(flops=0, bytes_accessed=3 * MIB, transcendentals=0),
        name="finish_heads",
    )(place, *ins)


def order_small_kernel(place_ref, own_ref, got_ref, out_ref):
    for other, ref in enumerate((own_ref, got_ref)):
        for far in range(4):
            out_ref[pl.ds(owner_of(place_ref, far, other), 1), :] = ref[far, 0:1, :]


def order_small(place, own, got):
    return pl.pallas_call(
        order_small_kernel,
        grid=(1,),
        in_specs=[smem, whole(own.shape), whole(got.shape)],
        out_specs=pl.BlockSpec((8, own.shape[2]), lambda i: (0, 0)),
        out_shape=jax.ShapeDtypeStruct((8, own.shape[2]), F32),
        name="order_small",
    )(place, own, got)


def gather_messages(message):
    far = jnp.stack([message] + [exchange(message, plane=distance) for distance in range(1, 4)])
    near = jnp.stack(spread(far))
    return near, exchange(near, core=1)


def tie(first, then):
    first, then = lax.optimization_barrier((first, then))
    return first, then


def gather_heads(place, own, small):
    rows, width = own[0].shape
    line = jnp.broadcast_to(jnp.pad(small, (0, width - small.shape[0])), (8, width))
    heads = jnp.stack([jnp.concatenate([weight, line]) for weight in own])
    quarter = lax.dynamic_index_in_dim(heads, place[2], 0, keepdims=False)
    far = jnp.stack([exchange(quarter, plane=distance) for distance in range(1, 4)])
    far, heads = tie(far, heads)
    near = spread(far)
    other = exchange(heads, core=1)
    far_other = exchange(far, core=1)
    lines = lambda first, rest: jnp.concatenate([first[:1, rows:, :256], rest[:, rows:, :256]]).astype(F32)
    ordered = order_small(place, lines(heads, far), lines(other, far_other))
    return near, [heads, other], far_other, ordered


def fetch_inner(narrow, inner_weight, width):
    quarter = lax.dynamic_slice_in_dim(inner_weight, narrow * width, width, 1)
    return [exchange(quarter, plane=far) for far in range(1, 4)]


def layer_specs():
    both = ("narrow", "wide")
    rows, matrix, vector = P(both, None), P("wide", None), P("wide")
    ins = (rows, vector, matrix, matrix, matrix, matrix, vector, vector, matrix, matrix, matrix, rows, P())
    outs = (rows, rows, rows, vector, matrix, matrix, matrix, matrix, vector, vector, matrix, matrix, matrix)
    return ins, outs


def local_permuted(tokens, *arguments):
    *weights_own, lengths, positives = arguments
    attention_gain, query_weight, key_weight, value_weight, output_weight = weights_own[:5]
    bias_table, forward_gain, inner_weight, outer_weight, project_weight = weights_own[5:]
    segs = lengths.shape[1]
    width = tokens.shape[1]
    units = inner_weight.shape[1]
    wide_at = lax.axis_index("wide")
    narrow_at = lax.axis_index("narrow")
    device = narrow_at * 8 + wide_at
    place = jnp.stack([device, wide_at, narrow_at, wide_at // 2, wide_at % 2]).astype(jnp.int32)
    share = attention_gain.shape[0]

    own_heads = (query_weight, key_weight, value_weight, output_weight)
    small = jnp.concatenate([attention_gain, forward_gain, bias_table])
    near, both_heads, far_other, small = gather_heads(place, own_heads, small)
    gain_one = small[:, :share].reshape(1, width)
    gain_two = small[:, share : 2 * share].reshape(1, width)
    table = small[:, 2 * share : 2 * share + bias_table.shape[0]].reshape(BUCKETS, HEADS)
    table = jnp.pad(table, ((0, 0), (0, 4))).astype(BF16)
    _, own_inner = tie(both_heads[1], inner_weight)
    _, own_outer = tie(far_other, outer_weight)
    wu = lax.all_gather(own_outer, "wide", axis=0, tiled=True)
    far = jnp.stack(fetch_inner(narrow_at, own_inner, width))
    (gain_one, gain_two, table), near = tie((gain_one, gain_two, table), near)
    near, far = tie(near, far)
    head_pieces = both_heads + near + [far_other] + [exchange(piece, core=1) for piece in near[1:]]
    near = spread(far)
    other_inner = exchange(own_inner, core=1)

    hid, q, k, v, weights = project(place, tokens, gain_one, head_pieces)
    q, own_last = tie(q, project_weight)
    wp = lax.all_gather(own_last, "wide", axis=0, tiled=True)
    mixed, inv, p = attend(lengths, table, q, k, v, 0, 6)
    mixed, inv, p, near = lax.optimization_barrier((mixed, inv, p, near))
    near_other = [exchange(piece, core=1) for piece in near]
    hidden, slope, active_sum, message, middle, hid_two, wi = forward(
        place, lengths, tokens, mixed, gain_two, weights, wu, units, [own_inner, other_inner] + near + near_other
    )
    loss, grad_wp, glow_all, grows, glow = contrast(
        place, *gather_messages(message), positives[None], wp, project_weight.shape[0]
    )
    gmid, gm, grads_out = back(
        lengths, place, glow, grows, gain_two, hid_two, active_sum, wu, slope, wi, middle, mixed, inv, weights, True
    )

    part = lax.psum_scatter(grads_out.reshape(-1, units + width), "wide", scatter_dimension=0, tiled=True)
    grad_heads, diag = attend_grad(lengths, q, k, v, gm, mixed, p, 0, 6)
    grad_table = table_grad(diag).reshape(8, -1)
    rows_table = jnp.pad(grad_table, ((0, 0), (0, 128 - grad_table.shape[1])))
    keep, send = head_grad(place, hid, grad_heads, rows_table)
    got = exchange(send, core=1)
    quarters = sum_core(keep, got)
    quarters, gmid = tie(quarters, gmid)
    arrived = [quarters[0]] + [exchange(quarters[near], narrow=near) for near in range(1, 4)]
    grad_tokens = token_grad(tokens, gain_one, gmid, grad_heads, weights)
    grad_tokens, part = tie(grad_tokens, part)
    pieces = cut(place, part)
    pieces = [pieces[0]] + [exchange(pieces[near], narrow=near) for near in range(1, 4)]
    planes = sum_narrow(arrived, False)
    arrived = [planes[0]] + [exchange(planes[far], plane=far) for far in range(1, 4)]
    total, active_pieces = sum_quarter(pieces)
    inner_parts = spread(total)
    grad_outer = outer_grad(place, active_pieces, glow_all)
    grad_outer, arrived = tie(grad_outer, arrived)
    (total,) = sum_planes(arrived, False)
    last_parts = spread(total)
    grad_inner, grad_out, gain_two_grad = finish_inner(place, inner_weight, forward_gain[None], inner_parts, width)
    *grads, table_own, gain_one_grad = finish_heads(
        place, own_heads[:3], attention_gain[None], last_parts, bias_table.shape[0]
    )
    grads.append(grad_out)
    return (
        hidden,
        grad_tokens,
        loss[:, 0].reshape(1, segs),
        gain_one_grad[0],
        *grads,
        table_own[0],
        gain_two_grad[0],
        grad_inner,
        grad_outer,
        grad_wp,
    )


def local_plain(tokens, *arguments):
    *weights_own, lengths, positives = arguments
    attention_gain, query_weight, key_weight, value_weight, output_weight = weights_own[:5]
    bias_table, forward_gain, inner_weight, outer_weight, project_weight = weights_own[5:]
    both = ("narrow", "wide")
    segs = lengths.shape[1]
    width = tokens.shape[1]
    wide_at = lax.axis_index("wide")
    device = lax.axis_index("narrow") * lax.axis_size("wide") + wide_at
    place = jnp.stack([device, wide_at]).astype(jnp.int32)
    share = attention_gain.shape[0]
    gather = lambda a: lax.all_gather(a, "wide", axis=0, tiled=True)
    small = gather(jnp.concatenate([attention_gain, forward_gain, bias_table])[None])
    gain_one = small[:, :share].reshape(1, width)
    gain_two = small[:, share : 2 * share].reshape(1, width)
    table = jnp.pad(small[:, 2 * share :].reshape(BUCKETS, HEADS), ((0, 0), (0, 4)))
    weights = jnp.stack([gather(w) for w in (query_weight, key_weight, value_weight, output_weight)])
    wu = gather(outer_weight)
    hid, q, k, v, weights = project(place, tokens, gain_one, [weights])
    mixed, inv, p = attend(lengths, table, q, k, v, 0, HEADS // 2)
    hidden, slope, active_sum, message, middle, hid_two, wi = forward(
        place, lengths, tokens, mixed, gain_two, weights, wu, inner_weight.shape[1], [gather(inner_weight)]
    )
    messages = lax.all_gather(message, both, axis=0, tiled=True).reshape(-1, 2, 8, 512)
    messages = messages.transpose(0, 2, 1, 3).reshape(-1, 1024)
    loss, grad_wp, glow_all, grows = contrast_plain(
        place,
        messages[:, :width],
        messages[:, width : width + 1].astype(F32),
        positives.reshape(-1, 1),
        gather(project_weight),
        project_weight.shape[0],
    )
    active_all = lax.all_gather(active_sum[:segs], both, axis=0, tiled=True)
    active_own = lax.dynamic_slice_in_dim(active_all, wide_at * outer_weight.shape[0], outer_weight.shape[0], 1)
    grad_outer = dot_tn(active_own, glow_all.astype(F32))
    glow = jnp.pad(grows.astype(BF16), ((0, 16 - segs), (0, 0)))
    gmid, gm, grad_wi, grad_wo = back(
        lengths, place, glow, grows, gain_two, hid_two, active_sum, wu, slope, wi, middle, mixed, inv, weights, False
    )
    grad_heads, diag = attend_grad(lengths, q, k, v, gm, mixed, p, 0, HEADS // 2)
    grad_tokens = token_grad(tokens, gain_one, gmid, grad_heads, weights)

    def total(grad):
        part = lax.psum_scatter(grad, "wide", scatter_dimension=0, tiled=True)
        return lax.psum(part.astype(F32), "narrow")

    grads = [total(dot_tn(hid, grad).astype(BF16)) for grad in grad_heads] + [total(grad_wo)]
    grad_inner = total(grad_wi)
    table_own = total(table_grad(diag).reshape(lax.axis_size("wide"), -1))[0]
    own_heads = jnp.stack([query_weight, key_weight, value_weight])
    along = jnp.sum(jnp.stack(grads[:3]) * own_heads.astype(F32), (0, 2))
    return (
        hidden,
        grad_tokens,
        loss[:, 0].reshape(1, segs),
        along / attention_gain.astype(F32),
        *grads,
        table_own,
        jnp.sum(grad_inner * inner_weight.astype(F32), 1) / forward_gain.astype(F32),
        grad_inner,
        grad_outer,
        grad_wp,
    )


def solution(mesh):
    ins, outs = layer_specs()
    permuted = (mesh.shape["narrow"], mesh.shape["wide"]) == (4, 8)
    body = local_permuted if permuted else local_plain
    return jax.shard_map(body, mesh=mesh, in_specs=ins, out_specs=outs, check_vma=False)
```

```python
import functools

import jax
import jax.numpy as jnp
from jax import lax
from jax.experimental import pallas as pl
from jax.experimental.pallas import tpu as pltpu
from jax.sharding import PartitionSpec as P

HEADS = 12
HEAD_DIM = 64
BUCKETS = 32
SPAN = 256
BLOCK = 128
WINDOW = BLOCK + 2 * SPAN
SLOTS = 4
CHUNK = 1024

epsilon = 1e-06
logit_scale = 50.0
root_half = 0.7071067811865476
inv_root_tau = 0.3989422804014327
MIB = 1 << 20
F32 = jnp.float32
BF16 = jnp.bfloat16


def dot_nn(left, right):
    return lax.dot_general(left, right, (((1,), (0,)), ((), ())), preferred_element_type=F32)


def dot_nt(left, right):
    return lax.dot_general(left, right, (((1,), (1,)), ((), ())), preferred_element_type=F32)


def dot_tn(left, right):
    return lax.dot_general(left, right, (((0,), (0,)), ((), ())), preferred_element_type=F32)


def split(values):
    high = values.astype(BF16)
    rest = values - high.astype(F32)
    middle = rest.astype(BF16)
    return high, middle, (rest - middle.astype(F32)).astype(BF16)


def split_two(values):
    high = values.astype(BF16)
    return high, (values - high.astype(F32)).astype(BF16)


def bucket_of(offset):
    distance = jnp.abs(offset)
    larger = jnp.full_like(distance, 8)
    for step in range(1, 8):
        larger = larger + (distance * distance >= 64 * 2**step).astype(jnp.int32)
    return jnp.where(distance < 8, distance, larger) + jnp.where(offset > 0, 16, 0)


def bounds_of(lengths_ref, count):
    bounds = []
    total = 0
    for index in range(count):
        total = total + lengths_ref[0, index]
        bounds.append(total)
    return bounds


def segment_of(places, bounds):
    segment = jnp.zeros_like(places)
    for bound in bounds:
        segment = segment + (places >= bound).astype(jnp.int32)
    return segment


def window_of(bounds, start):
    low = 0
    high = bounds[-1]
    for bound in bounds[:-1]:
        low = jnp.where(bound <= start, bound, low)
    for bound in reversed(bounds[:-1]):
        high = jnp.where(bound > start + BLOCK - 1, bound, high)
    first = (low // BLOCK) * BLOCK
    blocks = (high - first + BLOCK - 1) // BLOCK
    return first, blocks


def params(mib=60, grid=1):
    return pltpu.CompilerParams(vmem_limit_bytes=mib * MIB, dimension_semantics=("arbitrary",) * grid)


def whole(shape):
    return pl.BlockSpec(shape, lambda *_: (0,) * len(shape), pipeline_mode=pl.Buffered(1))


smem = pl.BlockSpec(memory_space=pltpu.SMEM)
anywhere = pl.BlockSpec(memory_space=pl.ANY)
in_hbm = pl.BlockSpec(memory_space=pltpu.HBM)
in_vmem = pl.BlockSpec(memory_space=pltpu.VMEM)
small = pltpu.CompilerParams(vmem_limit_bytes=12 * MIB)


def owner_of(place_ref, far, other):
    return 2 * (place_ref[3] ^ far) + (place_ref[4] ^ other)


def start_copies(pairs, sems, first=0):
    pending = [pltpu.make_async_copy(source, target, sems.at[first + at]) for at, (source, target) in enumerate(pairs)]
    for copy in pending:
        copy.start()
    return pending


def wait_copies(pending):
    for copy in pending:
        copy.wait()


def head_copies(place_ref, refs, whole_ref):
    rows = whole_ref.shape[1] // 8
    mine = pl.ds(0, rows)
    for other in range(2):
        start = pl.multiple_of(owner_of(place_ref, 0, other) * rows, 16)
        yield refs[other].at[:, mine, :], whole_ref.at[:, pl.ds(start, rows), :]
        for near in range(4):
            piece = refs[2 + 4 * other + near]
            for far in range(1, 4):
                start = pl.multiple_of(owner_of(place_ref, far, other) * rows, 16)
                yield piece.at[far - 1, mine, :], whole_ref.at[place_ref[2] ^ near, pl.ds(start, rows), :]


def project_kernel(place_ref, x_ref, gain_ref, *refs):
    *pieces, hid_ref, q_ref, k_ref, v_ref, out_ref, w_ref, sems, out_sem = refs
    step = pl.program_id(0)
    if len(pieces) == 1:
        pairs = [(pieces[0], w_ref)]
    else:
        pairs = list(head_copies(place_ref, pieces, w_ref))
    whole_copy = pltpu.make_async_copy(w_ref, out_ref, out_sem)

    @pl.when(step == 0)
    def _():
        start_copies(pairs, sems)

    x = x_ref[...].astype(F32)
    scale = lax.rsqrt(jnp.mean(x * x, -1, keepdims=True) + epsilon)
    hidden = (x * scale * gain_ref[...].astype(F32)).astype(BF16)
    hid_ref[...] = hidden

    @pl.when(step == 0)
    def _():
        wait_copies([pltpu.make_async_copy(*pair, sems.at[index]) for index, pair in enumerate(pairs)])
        whole_copy.start()

    q_ref[...] = dot_nn(hidden, w_ref[0]).astype(BF16)
    k_ref[...] = dot_nn(hidden, w_ref[1]).astype(BF16)
    v_ref[...] = dot_nn(hidden, w_ref[2]).astype(BF16)

    @pl.when(step == pl.num_programs(0) - 1)
    def _():
        whole_copy.wait()


def project(place, x, gain, pieces):
    rows, width = x.shape
    block = rows // 4
    row_spec = pl.BlockSpec((block, width), lambda i: (i, 0))
    out = jax.ShapeDtypeStruct((rows, width), BF16)
    return pl.pallas_call(
        project_kernel,
        grid=(4,),
        in_specs=[smem, row_spec, whole((1, width))] + [in_hbm] * len(pieces),
        out_specs=[row_spec] * 4 + [anywhere],
        out_shape=[out] * 4 + [jax.ShapeDtypeStruct((4, width, width), BF16)],
        scratch_shapes=[
            pltpu.VMEM((4, width, width), BF16),
            pltpu.SemaphoreType.DMA((26,)),
            pltpu.SemaphoreType.DMA(()),
        ],
        compiler_params=params(),
        cost_estimate=pl.CostEstimate(
            flops=6 * rows * width * width, bytes_accessed=10 * rows * width + 16 * width * width, transcendentals=0
        ),
        name="project_heads",
    )(place, x, gain, *pieces)


def attend_kernel(first_pair, lengths_ref, table_ref, q_ref, k_ref, v_ref, *refs):
    mixed_ref, inv_ref, p_any, rows_ref, tile_ref, segc_ref, segr_ref, p_ref, sems = refs[-9:]
    together = q_ref.shape[1] // BLOCK
    pair = first_pair + together * pl.program_id(0)
    rows = q_ref.shape[0]
    bounds = bounds_of(lengths_ref, lengths_ref.shape[1])
    reach = WINDOW + BLOCK

    @pl.when(pl.program_id(0) == 0)
    def _():
        segc_ref[...] = segment_of(lax.broadcasted_iota(jnp.int32, segc_ref.shape, 0), bounds)
        segr_ref[...] = segment_of(lax.broadcasted_iota(jnp.int32, segr_ref.shape, 1), bounds)
        offsets = lax.broadcasted_iota(jnp.int32, (BUCKETS, reach), 1) - (SPAN + BLOCK)
        kinds = lax.broadcasted_iota(jnp.int32, (BUCKETS, reach), 0)
        onehot = (bucket_of(offsets) == kinds).astype(F32).astype(BF16)
        rows_ref[...] = dot_tn(table_ref[...], onehot)

    for head in range(2 * together):
        line = rows_ref[pl.ds(2 * pair + head, 1), :]
        skew = pltpu.roll(jnp.broadcast_to(line, (BLOCK, reach)), 0, 1, stride=1, stride_axis=0)
        tile_ref[head] = skew[:, BLOCK:]

    lane = lax.broadcasted_iota(jnp.int32, (BLOCK, BLOCK), 1)
    first_half = lane < HEAD_DIM

    def out_copy(block_index):
        slot = block_index % SLOTS
        target = p_any.at[pl.ds(2 * pair, 2 * together), pl.ds(pl.multiple_of(block_index * BLOCK, BLOCK), BLOCK), :]
        return pltpu.make_async_copy(p_ref.at[slot], target, sems.at[slot])

    def one(block_index, carry):
        slot = block_index % SLOTS
        start = pl.multiple_of(block_index * BLOCK, BLOCK)

        @pl.when(block_index >= SLOTS)
        def _():
            out_copy(block_index - SLOTS).wait()

        first, count = window_of(bounds, start)
        first = pl.multiple_of(first, BLOCK)
        shift = pl.multiple_of(first - start + SPAN, BLOCK)

        def body(blocks):
            size = blocks * BLOCK
            queries = pl.ds(start, BLOCK)
            keys = pl.ds(first, size)
            segc = segc_ref[queries, :]
            segr = segr_ref[0:1, keys]
            same = jnp.concatenate([segc] * blocks, 1) == segr
            wide_lane = lax.broadcasted_iota(jnp.int32, (size, BLOCK), 1) < HEAD_DIM
            scores = []
            for head in range(2 * together):
                lanes = slice(head // 2 * BLOCK, head // 2 * BLOCK + BLOCK)
                mine = first_half if head % 2 == 0 else ~first_half
                q = q_ref[queries, lanes]
                scores.append(dot_nt(jnp.where(mine, q, jnp.zeros_like(q)), k_ref[keys, lanes]))
            raised = []
            for head in range(2 * together):
                score = jnp.where(same, scores[head] + tile_ref[head, :, pl.ds(shift, size)], -1000000000.0)
                power = jnp.exp(score - jnp.max(score, -1, keepdims=True)).astype(BF16)
                p_ref[slot, head, :, 0:size] = power
                raised.append(power)
            for near in range(together):
                lanes = slice(near * BLOCK, near * BLOCK + BLOCK)
                v = v_ref[keys, lanes]
                one = jnp.ones_like(v)
                left = dot_nn(raised[2 * near], jnp.where(wide_lane, v, one))
                right = dot_nn(raised[2 * near + 1], jnp.where(wide_lane, one, v))
                total = pltpu.roll(jnp.where(first_half, right, left), HEAD_DIM, 1)
                inverse = 1.0 / total
                mixed_ref[queries, lanes] = (jnp.where(first_half, left, right) * inverse).astype(BF16)
                inv_ref[queries, lanes] = inverse

        for blocks in range(1, WINDOW // BLOCK + 1):
            pl.when(count == blocks)(functools.partial(body, blocks))
        out_copy(block_index).start()
        return carry

    lax.fori_loop(0, rows // BLOCK, one, 0)
    for block_index in range(rows // BLOCK - SLOTS, rows // BLOCK):
        out_copy(block_index).wait()


def attend(lengths, table, q, k, v, first_pair, pairs, before=()):
    rows, width = q.shape
    together = max(size for size in (1, 2, 3) if pairs % size == 0 and first_pair % size == 0)
    column = pl.BlockSpec((rows, BLOCK * together), lambda p: (0, first_pair // together + p))
    return pl.pallas_call(
        functools.partial(attend_kernel, first_pair),
        grid=(pairs // together,),
        in_specs=[smem, whole(table.shape), column, column, column] + [anywhere] * len(before),
        out_specs=[column, column, anywhere],
        out_shape=[
            jax.ShapeDtypeStruct((rows, width), BF16),
            jax.ShapeDtypeStruct((rows, width), F32),
            jax.ShapeDtypeStruct((HEADS, rows, WINDOW), BF16),
        ],
        scratch_shapes=[
            pltpu.VMEM((16, WINDOW + BLOCK), F32),
            pltpu.VMEM((2 * together, BLOCK, WINDOW), F32),
            pltpu.VMEM((rows, BLOCK), jnp.int32),
            pltpu.VMEM((8, rows), jnp.int32),
            pltpu.VMEM((SLOTS, 2 * together, BLOCK, WINDOW), BF16),
            pltpu.SemaphoreType.DMA((SLOTS,)),
        ],
        input_output_aliases={5 + index: index for index in range(len(before))},
        compiler_params=params(),
        cost_estimate=pl.CostEstimate(
            flops=pairs * 8 * rows * 512 * 128, bytes_accessed=pairs * 6 * MIB, transcendentals=2 * pairs * rows * 512
        ),
        name="attend",
    )(lengths, table, q, k, v, *before)


def gelu_and_slope(v):
    bell = jnp.exp(-0.5 * v * v)
    t = 1.0 / (1.0 + (0.3275911 * root_half) * jnp.abs(v))
    series = t * (
        0.5 * 0.254829592
        + t * (0.5 * -0.284496736 + t * (0.5 * 1.421413741 + t * (0.5 * -1.453152027 + t * (0.5 * 1.061405429))))
    )
    tail = series * bell
    share = jnp.where(v >= 0.0, 1.0 - tail, tail)
    return v * share, share + v * bell * inv_root_tau


def member_of(lengths_ref, rows, count):
    bounds = bounds_of(lengths_ref, lengths_ref.shape[1])
    segment = segment_of(lax.broadcasted_iota(jnp.int32, (rows, count), 0), bounds)
    return (segment == lax.broadcasted_iota(jnp.int32, (rows, count), 1)).astype(F32).astype(BF16)


def member_rows(lengths_ref, rows, count):
    bounds = bounds_of(lengths_ref, lengths_ref.shape[1])
    segment = segment_of(lax.broadcasted_iota(jnp.int32, (count, rows), 1), bounds)
    return (segment == lax.broadcasted_iota(jnp.int32, (count, rows), 0)).astype(F32).astype(BF16)


def inner_copies(place_ref, refs, inner_ref):
    rows = refs[0].shape[0]
    width = inner_ref.shape[0]
    for other in range(2):
        owner = owner_of(place_ref, 0, other)
        yield refs[other], inner_ref.at[pl.ds(pl.multiple_of(owner * rows, 16), rows), :]
        for near in range(4):
            piece = refs[2 + 4 * other + near]
            quarter = place_ref[2] ^ near
            for far in range(1, 4):
                owner = owner_of(place_ref, far, other)
                row = pl.ds(pl.multiple_of(owner * rows, 16), rows)
                column = pl.ds(pl.multiple_of(quarter * width, 128), width)
                yield piece.at[far - 1], inner_ref.at[row, column]


def forward_kernel(place_ref, lengths_ref, x_ref, mixed_ref, gain_ref, heads_ref, wu_any, *refs):
    *pieces, out_ref, slope_ref, active_sum_ref, message_ref, mid_out, hid_out, wi_out = refs[:-12]
    total_ref, mid_ref, hid_ref, member_ref, wo_ref, inner_ref, active_ref = refs[-12:-5]
    wi_ref, wu_ref, sems, out_sems, last_sems = refs[-5:]
    step = pl.program_id(0)
    rows, width = hid_ref.shape
    block = rows // 4
    outs = ((wi_ref, wi_out), (hid_ref, hid_out), (mid_ref, mid_out))
    if len(pieces) == 1:
        groups = [[(pieces[0], wi_ref)], [(wu_any, wu_ref)]]
    else:
        groups = [list(inner_copies(place_ref, pieces, wi_ref)), [(wu_any, wu_ref)]]
    firsts = [0, len(groups[0])]
    spans = [slice(index * block, (index + 1) * block) for index in range(4)]

    def arrive(index):
        pairs = groups[index]
        wait_copies([pltpu.make_async_copy(*pair, sems.at[firsts[index] + at]) for at, pair in enumerate(pairs)])

    @pl.when(step == 0)
    def _():
        output_copy = pltpu.make_async_copy(heads_ref.at[3], wo_ref, last_sems.at[0])
        output_copy.start()
        for group, first in zip(groups, firsts):
            start_copies(group, sems, first)
        member_ref[...] = member_rows(lengths_ref, rows, 16)
        output_copy.wait()
        for span in spans:
            middle = x_ref[span, :].astype(F32) + dot_nn(mixed_ref[span, :], wo_ref[...])
            scale = lax.rsqrt(jnp.mean(middle * middle, -1, keepdims=True) + epsilon)
            total_ref[span, :] = middle
            mid_ref[span, :] = middle
            hid_ref[span, :] = (middle * scale * gain_ref[...].astype(F32)).astype(BF16)
        arrive(0)
        for index, pair in enumerate(outs):
            pltpu.make_async_copy(*pair, out_sems.at[index]).start()

    columns = pl.ds(pl.multiple_of(step * CHUNK, CHUNK), CHUNK)

    def first(span):
        inner_ref[span, :] = dot_nn(hid_ref[span, :], wi_ref[:, columns])

    def second(span):
        for at in range(span.start, span.stop, 32):
            active, slope = gelu_and_slope(inner_ref[at : at + 32, :])
            active_ref[at : at + 32, :] = active.astype(BF16)
            slope_ref[at : at + 32, :] = slope.astype(BF16)

    first(spans[0])
    first(spans[1])
    second(spans[0])

    @pl.when(step == 0)
    def _():
        arrive(1)

    for index, span in enumerate(spans):
        total_ref[span, :] += dot_nn(active_ref[span, :], wu_ref[columns, :])
        if index + 2 < 4:
            first(spans[index + 2])
        if index + 1 < 4:
            second(spans[index + 1])
    active_sum_ref[...] = dot_nn(member_ref[...], active_ref[...])

    @pl.when(step == pl.num_programs(0) - 1)
    def _():
        out_ref[...] = total_ref[...].astype(BF16)
        member = member_ref[...]
        pooled = jnp.zeros((16, width), F32)
        for span in spans:
            for piece in split_two(total_ref[span, :]):
                pooled = pooled + dot_nn(member[:, span], piece)
        row = lax.broadcasted_iota(jnp.int32, (8, 128), 0)
        lens = jnp.zeros((8, 128), jnp.int32)
        for index in range(8):
            lens = jnp.where(row == index, lengths_ref[0, index], lens)
        lens = lens.astype(F32)
        mean = pooled[0:8] / jnp.concatenate([lens] * (width // 128), 1)
        lower = jnp.concatenate([mean[:, 512:], lens, lens], 1)
        message_ref[...] = jnp.concatenate([mean[:, :512], lower], 0).astype(BF16)
        for index, pair in enumerate(outs):
            pltpu.make_async_copy(*pair, out_sems.at[index]).wait()


def forward(place, lengths, x, mixed, gain, heads, wu, units, pieces):
    rows, width = x.shape
    full = whole((rows, width))
    return pl.pallas_call(
        forward_kernel,
        grid=(units // CHUNK,),
        in_specs=[smem, smem, full, full, whole((1, width)), in_hbm, in_hbm] + [in_hbm] * len(pieces),
        out_specs=[
            pl.BlockSpec((rows, width), lambda i: (0, 0)),
            pl.BlockSpec((rows, CHUNK), lambda i: (0, i)),
            pl.BlockSpec((16, CHUNK), lambda i: (0, i)),
            pl.BlockSpec((16, 512), lambda i: (0, 0)),
        ]
        + [anywhere] * 3,
        out_shape=[
            jax.ShapeDtypeStruct((rows, width), BF16),
            jax.ShapeDtypeStruct((rows, units), BF16),
            jax.ShapeDtypeStruct((16, units), F32),
            pltpu.HBM((16, 512), BF16),
            jax.ShapeDtypeStruct((rows, width), F32),
            jax.ShapeDtypeStruct((rows, width), BF16),
            jax.ShapeDtypeStruct((width, units), BF16),
        ],
        scratch_shapes=[
            pltpu.VMEM((rows, width), F32),
            pltpu.VMEM((rows, width), F32),
            pltpu.VMEM((rows, width), BF16),
            pltpu.VMEM((16, rows), BF16),
            pltpu.VMEM((width, width), BF16),
            pltpu.VMEM((rows, CHUNK), F32),
            pltpu.VMEM((rows, CHUNK), BF16),
            pltpu.VMEM((width, units), BF16),
            pltpu.VMEM((units, width), BF16),
            pltpu.SemaphoreType.DMA((27,)),
            pltpu.SemaphoreType.DMA((3,)),
            pltpu.SemaphoreType.DMA((1,)),
        ],
        compiler_params=params(),
        cost_estimate=pl.CostEstimate(
            flops=4 * rows * width * units, bytes_accessed=30 * MIB, transcendentals=2 * rows * units
        ),
        name="feed_forward",
    )(place, lengths, x, mixed, gain, heads, wu, *pieces)


def contrast_kernel(place_ref, own_ref, got_ref, target_ref, wp_any, *refs):
    loss_ref, grad_wp_ref, glow_all_ref, grows_ref, glow_ref = refs[:-7]
    wide_ref, line_ref, full_ref, wp_ref, left_ref, right_ref, sems = refs[-7:]
    count, width = wide_ref.shape
    pending = start_copies([(wp_any, wp_ref)], sems)
    for other, ref in enumerate((own_ref, got_ref)):
        for far in range(4):
            for near in range(4):
                device = (place_ref[2] ^ near) * 8 + owner_of(place_ref, far, other)
                start = pl.multiple_of(device * 8, 8)
                piece = ref[near, far].astype(F32)
                left_ref[pl.ds(start, 8), :] = piece[0:8]
                right_ref[pl.ds(start, 8), :] = piece[8:16]
    rest = width - left_ref.shape[1]
    pooled = jnp.concatenate([left_ref[...], right_ref[:, 0:rest]], 1).astype(BF16)
    lens = right_ref[:, rest : rest + 1]
    wait_copies(pending)
    first = pl.multiple_of(place_ref[0] * 8, 8)
    projected = dot_nn(pooled, wp_ref[...])
    inverse = lax.rsqrt(jnp.sum(projected * projected, -1, keepdims=True) + epsilon)
    embedded = (projected * inverse).astype(BF16)
    row = lax.broadcasted_iota(jnp.int32, (count, count), 0)
    column = lax.broadcasted_iota(jnp.int32, (count, count), 1)
    logits = logit_scale * dot_nt(embedded, embedded)
    logits = jnp.where(row == column, -1000000000.0, logits)
    target_at = jnp.sum(jnp.where(row == column, target_ref[...], 0), -1, keepdims=True)
    hit = column == target_at
    highest = jnp.max(logits, -1, keepdims=True)
    totals = highest + jnp.log(jnp.sum(jnp.exp(logits - highest), -1, keepdims=True))
    target = jnp.sum(jnp.where(hit, logits, 0.0), -1, keepdims=True)
    line_ref[...] = jnp.broadcast_to(totals - target, line_ref.shape)
    loss_ref[...] = line_ref[pl.ds(first, 8), :]
    grad_logits = (jnp.exp(logits - totals) - hit.astype(F32)).astype(BF16)
    grad_embedded = logit_scale * (dot_nn(grad_logits, embedded) + dot_tn(grad_logits, embedded))
    along = jnp.sum(grad_embedded * projected, -1, keepdims=True)
    grad_projected = inverse * grad_embedded - projected * (inverse * inverse * inverse * along)
    high, low = split_two(grad_projected)
    full_ref[...] = dot_tn(pooled, high) + dot_tn(pooled, low)
    share = grad_wp_ref.shape[0]
    grad_wp_ref[...] = full_ref[pl.ds(pl.multiple_of(place_ref[1] * share, share), share), :]
    wp = wp_ref[...]
    grad_rows = (dot_nt(high, wp) + dot_nt(low, wp)) / lens
    glow_all_ref[...] = grad_rows.astype(BF16)
    wide_ref[...] = grad_rows
    own_rows = wide_ref[pl.ds(first, 8), :]
    grows_ref[...] = own_rows
    glow_ref[...] = jnp.concatenate([own_rows, jnp.zeros_like(own_rows)], 0).astype(BF16)


def contrast_plain(place, pooled, lens, targets, wp, share):
    count, width = pooled.shape
    exact = lax.Precision.HIGHEST
    projected = jnp.dot(pooled, wp, preferred_element_type=F32)
    inverse = lax.rsqrt(jnp.sum(projected * projected, -1, keepdims=True) + epsilon)
    embedded = (projected * inverse).astype(BF16)
    numbers = jnp.arange(count, dtype=jnp.int32)
    logits = logit_scale * dot_nt(embedded, embedded)
    logits = jnp.where(numbers[:, None] == numbers[None, :], -1000000000.0, logits)
    hit = numbers[None, :] == targets
    highest = jnp.max(logits, -1, keepdims=True)
    totals = highest + jnp.log(jnp.sum(jnp.exp(logits - highest), -1, keepdims=True))
    loss = totals - jnp.sum(jnp.where(hit, logits, 0.0), -1, keepdims=True)
    grad_logits = (jnp.exp(logits - totals) - hit.astype(F32)).astype(BF16)
    grad_embedded = logit_scale * (dot_nn(grad_logits, embedded) + dot_tn(grad_logits, embedded))
    along = jnp.sum(grad_embedded * projected, -1, keepdims=True)
    grad_projected = inverse * grad_embedded - projected * (inverse * inverse * inverse * along)
    own_columns = lax.dynamic_slice_in_dim(pooled.astype(F32), place[1] * share, share, 1)
    grad_wp = lax.dot_general(own_columns, grad_projected, (((0,), (0,)), ((), ())), precision=exact)
    grad_rows = jnp.dot(grad_projected, wp.astype(F32).T, precision=exact) / lens
    first = place[0] * 8
    own = lambda a: lax.dynamic_slice_in_dim(a, first, 8, 0)
    return jnp.broadcast_to(own(loss), (8, 128)), grad_wp, grad_rows.astype(BF16), own(grad_rows)


def fold(result_ref, keep_ref, send_ref, place_ref, column_half, column):
    narrow, plane, core = place_ref[2], place_ref[3], place_ref[4]
    rows = keep_ref.shape[2]
    for near in range(2):
        quarter = 2 * ((narrow // 2) ^ column_half) + near
        half = (narrow % 2) ^ near
        for far in range(4):
            for ref, owner in ((keep_ref, core), (send_ref, 1 - core)):
                start = pl.multiple_of((2 * (plane ^ far) + owner) * 2 * rows + half * rows, 16)
                block = result_ref[pl.ds(start, rows), :].astype(BF16)
                ref[quarter, far, :, pl.ds(column, block.shape[1])] = block


def back_kernel(
    lengths_ref, place_ref, glow_ref, grows_ref, gain_ref, hid_ref, active_ref, wu_ref, slope_ref, wi_ref,
    mid_any, mixed_any, inv_any, heads_any, gmid_any, gmix_ref, *refs,
):
    *grad_refs, result_ref, total_ref, member_ref, mid_ref, mixed_ref, inv_ref, wo_ref, sems, out_sems, gi_ref = refs
    step = pl.program_id(0)
    last = pl.num_programs(0) - 1
    rows, width = total_ref.shape
    folded = len(grad_refs) == 2 and len(grad_refs[1].shape) == 3
    late = [(mid_any, mid_ref), (mixed_any, mixed_ref), (inv_any, inv_ref), (heads_any.at[3], wo_ref)]

    @pl.when(step == 0)
    def _():
        member = member_of(lengths_ref, rows, 16)
        member_ref[...] = jnp.concatenate([member, member], 1)

    @pl.when(step == 0)
    def _():
        total_ref[...] = jnp.zeros_like(total_ref)

    @pl.when(step == 2)
    def _():
        start_copies(late, sems)

    high, low = split_two(dot_nt(glow_ref[...], wu_ref[...]))
    both = jnp.concatenate([high, low], 0)
    spans = (slice(0, rows // 2), slice(rows // 2, rows))
    for span in spans:
        spread = dot_nn(member_ref[span, :], both)
        gi_ref[span, :] = (spread * slope_ref[span, :].astype(F32)).astype(BF16)
    for span in spans:
        total_ref[span, :] += dot_nt(gi_ref[span, :], wi_ref[...])
    result_ref[:, :CHUNK] = dot_tn(hid_ref[...], gi_ref[...])

    if folded:
        grad_any, grad_ref = grad_refs
        owners, lines, _ = grad_ref.shape
        lines = lines - 8
        units = active_ref.shape[1]
        columns = pl.ds(pl.multiple_of(step * CHUNK, CHUNK), CHUNK)
        for owner in range(owners):
            grad_ref[owner, 0:lines, columns] = result_ref[owner * lines : (owner + 1) * lines, :CHUNK].astype(BF16)

        @pl.when(step == 0)
        def _():
            share = units // owners
            start = pl.multiple_of(place_ref[1] * share, 128)
            for owner in range(owners):
                grad_ref[owner, lines:, 0:units] = jnp.zeros((8, units), BF16)
                grad_ref[owner, lines:, pl.ds(start, share)] = active_ref[0:8, owner * share : (owner + 1) * share].astype(BF16)
    else:
        grad_refs[0][:, pl.ds(pl.multiple_of(step * CHUNK, CHUNK), CHUNK)] = result_ref[:, :CHUNK].astype(BF16)

    @pl.when(step == last)
    def _():
        pending = []
        if folded:
            inner_columns = pl.ds(0, units)
            copy = pltpu.make_async_copy(
                grad_ref.at[:, :, inner_columns], grad_any.at[:, :, inner_columns], out_sems.at[0]
            )
            copy.start()
            pending.append(copy)
        wait_copies([pltpu.make_async_copy(*pair, sems.at[index]) for index, pair in enumerate(late)])
        bounds = bounds_of(lengths_ref, lengths_ref.shape[1])
        block = rows // 8
        for index in range(8):
            span = slice(index * block, (index + 1) * block)
            middle = mid_ref[span, :]
            scale = lax.rsqrt(jnp.mean(middle * middle, -1, keepdims=True) + epsilon)
            normed = middle * scale
            scaled = total_ref[span, :] * gain_ref[...].astype(F32)
            centre = jnp.mean(scaled * normed, -1, keepdims=True)
            segment = segment_of(lax.broadcasted_iota(jnp.int32, (block, 128), 0) + index * block, bounds)
            segment = jnp.concatenate([segment] * (width // 128), 1)
            grad_rows = jnp.zeros((block, width), F32)
            for passage in range(8):
                grad_rows = jnp.where(segment == passage, grows_ref[passage : passage + 1, :], grad_rows)
            total_ref[span, :] = grad_rows + scale * (scaled - normed * centre)
        copy = pltpu.make_async_copy(total_ref, gmid_any, out_sems.at[2])
        copy.start()
        pending.append(copy)
        columns = width // 2
        for side in range(2):
            grad = dot_tn(mixed_ref[...], total_ref[:, side * columns : (side + 1) * columns].astype(BF16))
            if folded:
                span = slice(units + side * columns, units + (side + 1) * columns)
                for owner in range(owners):
                    grad_ref[owner, 0:lines, span] = grad[owner * lines : (owner + 1) * lines].astype(BF16)
            else:
                grad_refs[1][:, side * columns : (side + 1) * columns] = grad.astype(BF16)
        if folded:
            rest = pl.ds(units, width)
            copy = pltpu.make_async_copy(grad_ref.at[:, :, rest], grad_any.at[:, :, rest], out_sems.at[1])
            copy.start()
            pending.append(copy)
        for index in range(4):
            span = slice(index * 2 * block, (index + 1) * 2 * block)
            low_rows = total_ref[span, :].astype(BF16)
            gmix_ref[span, :] = (dot_nt(low_rows, wo_ref[...]) * inv_ref[span, :]).astype(BF16)
        wait_copies(pending)


def back(lengths, place, glow, grows, gain, hidden, active_sum, wu, slope, wi, middle, mixed, inv, heads, folded):
    rows, width = hidden.shape
    units = slope.shape[1]
    full = pl.BlockSpec((rows, width), lambda i: (0, 0))
    if folded:
        slab = (8, width // 8 + 8, units + width)
        grad_shape = [pltpu.HBM(slab, BF16)]
        grad_specs = [anywhere]
        grad_scratch = [pltpu.VMEM(slab, BF16)]
    else:
        shapes = [(width, units), (width, width)]
        grad_shape = [jax.ShapeDtypeStruct(shape, BF16) for shape in shapes]
        grad_specs = [pl.BlockSpec(shape, lambda i: (0, 0)) for shape in shapes]
        grad_scratch = []
    return pl.pallas_call(
        back_kernel,
        grid=(units // CHUNK,),
        in_specs=[
            smem,
            smem,
            whole((16, width)),
            whole((8, width)),
            whole((1, width)),
            whole((rows, width)),
            whole(active_sum.shape),
            pl.BlockSpec((CHUNK, width), lambda i: (i, 0)),
            pl.BlockSpec((rows, CHUNK), lambda i: (0, i)),
            pl.BlockSpec((width, CHUNK), lambda i: (0, i)),
        ]
        + [anywhere] * 4,
        out_specs=[anywhere, full] + grad_specs,
        out_shape=[jax.ShapeDtypeStruct((rows, width), F32), jax.ShapeDtypeStruct((rows, width), BF16)] + grad_shape,
        scratch_shapes=grad_scratch
        + [
            pltpu.VMEM((width, CHUNK), F32),
            pltpu.VMEM((rows, width), F32),
            pltpu.VMEM((rows, 32), BF16),
            pltpu.VMEM((rows, width), F32),
            pltpu.VMEM((rows, width), BF16),
            pltpu.VMEM((rows, width), F32),
            pltpu.VMEM((width, width), BF16),
            pltpu.SemaphoreType.DMA((4,)),
            pltpu.SemaphoreType.DMA((5,)),
            pltpu.VMEM((rows, CHUNK), BF16),
        ],
        compiler_params=params(),
        cost_estimate=pl.CostEstimate(flops=5 * rows * width * units, bytes_accessed=40 * MIB, transcendentals=0),
        name="back",
    )(lengths, place, glow, grows, gain, hidden, active_sum, wu, slope, wi, middle, mixed, inv, heads)


def contrast_back_kernel(
    lengths_ref, place_ref, own_ref, got_ref, target_ref, wp_any, gain_ref, hid_ref, active_ref, wu_ref, slope_ref, wi_ref,
    mid_any, mixed_any, inv_any, heads_any, loss_ref, grad_wp_ref, glow_all_ref, gmid_any, gmix_ref, grad_any, *refs,
):
    back_refs, (grows_ref, glow_ref, *contrast_refs) = refs[:11], refs[11:]

    @pl.when(pl.program_id(0) == 0)
    def _():
        contrast_kernel(
            place_ref, own_ref, got_ref, target_ref, wp_any,
            loss_ref, grad_wp_ref, glow_all_ref, grows_ref, glow_ref, *contrast_refs,
        )

    back_kernel(
        lengths_ref, place_ref, glow_ref, grows_ref, gain_ref, hid_ref, active_ref, wu_ref, slope_ref, wi_ref,
        mid_any, mixed_any, inv_any, heads_any, gmid_any, gmix_ref, grad_any, *back_refs,
    )


def contrast_back(
    lengths, place, own, got, targets, wp, gain, hidden, active_sum, wu, slope, wi, middle, mixed, inv, heads, share
):
    rows, width = hidden.shape
    units = slope.shape[1]
    count = targets.shape[1]
    slab = (8, width // 8 + 8, units + width)
    fixed = lambda shape: pl.BlockSpec(shape, lambda i: (0,) * len(shape))
    return pl.pallas_call(
        contrast_back_kernel,
        grid=(units // CHUNK,),
        in_specs=[smem, smem, whole(own.shape), whole(got.shape), whole(targets.shape), in_hbm]
        + [whole((1, width)), whole((rows, width)), whole(active_sum.shape)]
        + [
            pl.BlockSpec((CHUNK, width), lambda i: (i, 0)),
            pl.BlockSpec((rows, CHUNK), lambda i: (0, i)),
            pl.BlockSpec((width, CHUNK), lambda i: (0, i)),
        ]
        + [anywhere] * 4,
        out_specs=[fixed((8, 128)), fixed((share, width)), fixed((count, width)), anywhere, fixed((rows, width)), anywhere],
        out_shape=[
            jax.ShapeDtypeStruct((8, 128), F32),
            jax.ShapeDtypeStruct((share, width), F32),
            jax.ShapeDtypeStruct((count, width), BF16),
            jax.ShapeDtypeStruct((rows, width), F32),
            jax.ShapeDtypeStruct((rows, width), BF16),
            pltpu.HBM(slab, BF16),
        ],
        scratch_shapes=[
            pltpu.VMEM(slab, BF16),
            pltpu.VMEM((width, CHUNK), F32),
            pltpu.VMEM((rows, width), F32),
            pltpu.VMEM((rows, 32), BF16),
            pltpu.VMEM((rows, width), F32),
            pltpu.VMEM((rows, width), BF16),
            pltpu.VMEM((rows, width), F32),
            pltpu.VMEM((width, width), BF16),
            pltpu.SemaphoreType.DMA((4,)),
            pltpu.SemaphoreType.DMA((5,)),
            pltpu.VMEM((rows, CHUNK), BF16),
            pltpu.VMEM((8, width), F32),
            pltpu.VMEM((16, width), BF16),
            pltpu.VMEM((count, width), F32),
            pltpu.VMEM((count, 128), F32),
            pltpu.VMEM((width, width), F32),
            pltpu.VMEM((width, width), BF16),
            pltpu.VMEM((count, 512), F32),
            pltpu.VMEM((count, 512), F32),
            pltpu.SemaphoreType.DMA((1,)),
        ],
        compiler_params=params(),
        cost_estimate=pl.CostEstimate(flops=5 * rows * width * units, bytes_accessed=40 * MIB, transcendentals=0),
        name="contrast_back",
    )(lengths, place, own, got, targets, wp, gain, hidden, active_sum, wu, slope, wi, middle, mixed, inv, heads)


def attend_grad_kernel(first_pair, lengths_ref, q_ref, k_ref, v_ref, gm_ref, mixed_ref, p_any, *refs):
    grad_ref, diag_ref, qm_ref, km_ref, vx_ref, gx_ref, go_ref, ak_ref, av_ref, acc_ref, p_ref, sems = refs[-12:]
    together = q_ref.shape[1] // BLOCK
    rows = q_ref.shape[0]
    first_head = 2 * (first_pair + together * pl.program_id(0))

    def in_copy(block_index):
        slot = block_index % SLOTS
        source = p_any.at[pl.ds(first_head, 2 * together), pl.ds(pl.multiple_of(block_index * BLOCK, BLOCK), BLOCK), :]
        return pltpu.make_async_copy(source, p_ref.at[slot], sems.at[slot])

    for block_index in range(SLOTS - 1):
        in_copy(block_index).start()
    bounds = bounds_of(lengths_ref, lengths_ref.shape[1])
    reach = WINDOW + BLOCK
    acc_ref[...] = jnp.zeros_like(acc_ref)
    ak_ref[...] = jnp.zeros_like(ak_ref)
    av_ref[...] = jnp.zeros_like(av_ref)

    lane = lax.broadcasted_iota(jnp.int32, (BLOCK, BLOCK), 1)
    row = lax.broadcasted_iota(jnp.int32, (BLOCK, BLOCK), 0)
    across = jnp.where((row < HEAD_DIM) != (lane < HEAD_DIM), -1.0, 0.0).astype(BF16)

    def prepare(index, carry):
        span = pl.ds(pl.multiple_of(index * BLOCK, BLOCK), BLOCK)
        for near in range(together):
            lanes = slice(near * BLOCK, near * BLOCK + BLOCK)
            q, k, v, g = q_ref[span, lanes], k_ref[span, lanes], v_ref[span, lanes], gm_ref[span, lanes]
            product = split_two(g.astype(F32) * mixed_ref[span, lanes].astype(F32))
            centre = dot_nn(product[0], across) + dot_nn(product[1], across)
            high, low = split_two(centre)
            first = (lane == 0) | (lane == HEAD_DIM)
            second = (lane == 1) | (lane == HEAD_DIM + 1)
            zero = jnp.zeros_like(q)
            extra = jnp.where(first, high, jnp.where(second, low, zero))
            one = jnp.ones_like(v)
            for half in range(2):
                head = 2 * near + half
                mine = (lane < HEAD_DIM) if half == 0 else (lane >= HEAD_DIM)
                qm_ref[head, span, :] = jnp.where(mine, q, zero)
                km_ref[head, span, :] = jnp.where(mine, k, zero)
                go_ref[head, span, :] = jnp.where(mine, g, zero)
                vx_ref[head, span, :] = jnp.where(mine, v, one)
                gx_ref[head, span, :] = jnp.where(mine, g, extra)
        return carry

    lax.fori_loop(0, rows // BLOCK, prepare, 0)

    def one(block_index, carry):
        slot = block_index % SLOTS
        start = pl.multiple_of(block_index * BLOCK, BLOCK)
        in_copy(block_index).wait()

        @pl.when(block_index + SLOTS - 1 < rows // BLOCK)
        def _():
            in_copy(block_index + SLOTS - 1).start()

        first, count = window_of(bounds, start)
        first = pl.multiple_of(first, BLOCK)
        shift = pl.multiple_of(first - start + SPAN, BLOCK)

        def body(blocks):
            size = blocks * BLOCK
            queries = pl.ds(start, BLOCK)
            keys = pl.ds(first, size)
            spread = [dot_nt(gx_ref[head, queries, :], vx_ref[head, keys, :]) for head in range(2 * together)]
            for near in range(together):
                heads = (2 * near, 2 * near + 1)
                lanes = slice(near * BLOCK, near * BLOCK + BLOCK)
                parts = []
                raised = []
                for head in heads:
                    p = p_ref[slot, head, :, 0:size]
                    grad_scores = p.astype(F32) * spread[head]
                    acc_ref[head, :, pl.ds(shift, size)] += grad_scores
                    parts.append(grad_scores.astype(BF16))
                    raised.append(p)
                q_both = jnp.concatenate([qm_ref[head, queries, :] for head in heads], 0)
                g_both = jnp.concatenate([go_ref[head, queries, :] for head in heads], 0)
                k_both = jnp.concatenate([km_ref[head, keys, :] for head in heads], 0)
                ak_ref[lanes, keys] += dot_tn(q_both, jnp.concatenate(parts, 0))
                av_ref[lanes, keys] += dot_tn(g_both, jnp.concatenate(raised, 0))
                grad_ref[0, queries, lanes] = dot_nn(jnp.concatenate(parts, 1), k_both).astype(BF16)

        for blocks in range(1, WINDOW // BLOCK + 1):
            pl.when(count == blocks)(functools.partial(body, blocks))
        return carry

    lax.fori_loop(0, rows // BLOCK, one, 0)
    for near in range(together):
        lanes = slice(near * BLOCK, near * BLOCK + BLOCK)
        grad_ref[1, :, lanes] = jnp.transpose(ak_ref[lanes, :]).astype(BF16)
        grad_ref[2, :, lanes] = jnp.transpose(av_ref[lanes, :]).astype(BF16)
    for head in range(2 * together):
        padded = jnp.concatenate([jnp.zeros((BLOCK, BLOCK), F32), acc_ref[head]], 1)
        group = padded[0:8]
        for index in range(1, BLOCK // 8):
            group = group + pltpu.roll(padded[8 * index : 8 * index + 8], reach - 8 * index, 1)
        line = group[0:1]
        for index in range(1, 8):
            line = line + pltpu.roll(group, reach - index, 1)[index : index + 1]
        diag_ref[head // 2, head % 2 : head % 2 + 1, :] = line


def attend_grad(lengths, q, k, v, gm, mixed, p, first_pair, pairs, before=()):
    rows, width = q.shape
    together = max(size for size in (1, 2, 3) if pairs % size == 0 and first_pair % size == 0)
    at = first_pair // together
    column = pl.BlockSpec((rows, BLOCK * together), lambda i: (0, at + i))
    return pl.pallas_call(
        functools.partial(attend_grad_kernel, first_pair),
        grid=(pairs // together,),
        in_specs=[smem]
        + [column] * 5
        + [in_hbm]
        + [anywhere] * len(before),
        out_specs=[
            pl.BlockSpec((3, rows, BLOCK * together), lambda i: (0, 0, at + i)),
            pl.BlockSpec((together, 2, WINDOW + BLOCK), lambda i: (at + i, 0, 0)),
        ],
        out_shape=[
            jax.ShapeDtypeStruct((3, rows, width), BF16),
            jax.ShapeDtypeStruct((HEADS // 2, 2, WINDOW + BLOCK), F32),
        ],
        scratch_shapes=[pltpu.VMEM((2 * together, rows, BLOCK), BF16)] * 5
        + [pltpu.VMEM((BLOCK * together, rows), F32)] * 2
        + [
            pltpu.VMEM((2 * together, BLOCK, WINDOW), F32),
            pltpu.VMEM((SLOTS, 2 * together, BLOCK, WINDOW), BF16),
            pltpu.SemaphoreType.DMA((SLOTS,)),
        ],
        input_output_aliases={7 + index: index for index in range(len(before))},
        compiler_params=params(),
        cost_estimate=pl.CostEstimate(
            flops=pairs * 20 * rows * 512 * 64, bytes_accessed=pairs * 5 * MIB, transcendentals=0
        ),
        name="attend_grad",
    )(lengths, q, k, v, gm, mixed, p, *before)


def head_grad_kernel(place_ref, hid_any, grad_any, table_ref, keep_ref, send_ref, hid_ref, grad_ref, result_ref, sems):
    block = result_ref.shape[2]
    pairs = [(hid_any, hid_ref)]
    for matrix in range(3):
        for side in range(2):
            columns = pl.ds(side * block, block)
            pairs.append((grad_any.at[matrix, :, columns], grad_ref.at[matrix, :, columns]))
    pending = start_copies(pairs, sems)
    rows = keep_ref.shape[2]
    for far in range(4):
        for ref, other in ((keep_ref, 0), (send_ref, 1)):
            line = table_ref[pl.ds(owner_of(place_ref, far, other), 1), :]
            block_of = jnp.broadcast_to(line, (rows, 128)).astype(BF16)
            for quarter in range(4):
                ref[quarter, far, :, 3 * block :] = block_of
    pending[0].wait()
    for step in range(6):
        pending[1 + step].wait()
        columns = slice(step % 2 * block, step % 2 * block + block)
        result_ref[step % 2] = dot_tn(hid_ref[...], grad_ref[step // 2, :, columns])
        fold(result_ref.at[step % 2], keep_ref, send_ref, place_ref, step // 3, step % 3 * block)


def head_grad(place, hidden, grads, table):
    rows, width = hidden.shape
    block = width // 2
    slab = (4, 4, width // 16, 3 * block + 128)
    return pl.pallas_call(
        head_grad_kernel,
        in_specs=[smem, in_hbm, in_hbm, in_vmem],
        out_specs=[in_vmem] * 2,
        out_shape=[jax.ShapeDtypeStruct(slab, BF16)] * 2,
        scratch_shapes=[
            pltpu.VMEM((rows, width), BF16),
            pltpu.VMEM((3, rows, width), BF16),
            pltpu.VMEM((2, width, block), F32),
            pltpu.SemaphoreType.DMA((7,)),
        ],
        compiler_params=pltpu.CompilerParams(vmem_limit_bytes=28 * MIB),
        cost_estimate=pl.CostEstimate(flops=6 * rows * width * width, bytes_accessed=12 * MIB, transcendentals=0),
        name="head_grad",
    )(place, hidden, grads, table)


def token_grad_kernel(x_ref, gain_ref, gmid_ref, grad_ref, w_ref, out_ref):
    x = x_ref[...].astype(F32)
    scale = lax.rsqrt(jnp.mean(x * x, -1, keepdims=True) + epsilon)
    normed = x * scale
    grad_hidden = dot_nt(grad_ref[0], w_ref[0]) + dot_nt(grad_ref[1], w_ref[1]) + dot_nt(grad_ref[2], w_ref[2])
    scaled = grad_hidden * gain_ref[...].astype(F32)
    centre = jnp.mean(scaled * normed, -1, keepdims=True)
    out_ref[...] = gmid_ref[...] + scale * (scaled - normed * centre)


def token_grad(x, gain, gmid, grads, weights):
    rows, width = x.shape
    block = rows // 4
    row_spec = pl.BlockSpec((block, width), lambda i: (i, 0))
    return pl.pallas_call(
        token_grad_kernel,
        grid=(4,),
        in_specs=[
            row_spec,
            whole((1, width)),
            row_spec,
            pl.BlockSpec((3, block, width), lambda i: (0, i, 0)),
            whole((3, width, width)),
        ],
        out_specs=row_spec,
        out_shape=jax.ShapeDtypeStruct((rows, width), F32),
        compiler_params=params(),
        cost_estimate=pl.CostEstimate(flops=6 * rows * width * width, bytes_accessed=16 * MIB, transcendentals=0),
        name="token_grad",
    )(x, gain, gmid, grads, weights)


def outer_grad_kernel(place_ref, pieces_ref, glow_ref, out_ref, active_ref):
    units = active_ref.shape[1]
    for near in range(4):
        start = pl.multiple_of((place_ref[2] ^ near) * 64, 64)
        for owner in range(8):
            half = 8 * (owner // 4)
            column = owner % 4 * units
            block = pieces_ref[near].astype(F32)[half : half + 8, column : column + units]
            active_ref[pl.ds(start + 8 * owner, 8), :] = block
    out_ref[...] = dot_tn(active_ref[...].astype(BF16), glow_ref[...])


def outer_grad(place, pieces, glow):
    count, width = glow.shape
    units = pieces.shape[2] // 4
    return pl.pallas_call(
        outer_grad_kernel,
        grid=(1,),
        in_specs=[smem, whole(pieces.shape), whole(glow.shape)],
        out_specs=pl.BlockSpec((units, width), lambda i: (0, 0)),
        out_shape=jax.ShapeDtypeStruct((units, width), F32),
        scratch_shapes=[pltpu.VMEM((count, units), F32)],
        compiler_params=params(),
        cost_estimate=pl.CostEstimate(flops=2 * count * units * width, bytes_accessed=3 * MIB, transcendentals=0),
        name="outer_grad",
    )(place, pieces, glow)


def table_grad(diag):
    reach = WINDOW + BLOCK
    offsets = jnp.arange(reach, dtype=jnp.int32) - (SPAN + BLOCK)
    onehot = (bucket_of(offsets)[:, None] == jnp.arange(BUCKETS, dtype=jnp.int32)[None, :]).astype(F32)
    sums = jnp.dot(diag.reshape(HEADS, reach), onehot, precision=lax.Precision.HIGHEST)
    return sums.T.reshape(BUCKETS * HEADS)


def exchange(value, narrow=0, plane=0, core=0):
    bits = narrow * 8 + plane * 2 + core
    return lax.ppermute(value, ("narrow", "wide"), [(i, i ^ bits) for i in range(32)])


def spread(value):
    return [value] + [exchange(value, narrow=near) for near in range(1, 4)]


def sum_core_kernel(keep_ref, got_ref, *out_refs):
    for quarter, out_ref in enumerate(out_refs):
        for far in range(4):
            out_ref[far] = (keep_ref[quarter, far].astype(F32) + got_ref[quarter, far].astype(F32)).astype(BF16)


def sum_core(keep, got):
    _, _, rows, columns = keep.shape
    return pl.pallas_call(
        sum_core_kernel,
        in_specs=[in_vmem] * 2,
        out_specs=[in_vmem] * 4,
        out_shape=[jax.ShapeDtypeStruct((4, rows, columns), BF16)] * 4,
        compiler_params=small,
        cost_estimate=pl.CostEstimate(flops=0, bytes_accessed=96 * rows * columns, transcendentals=0),
        name="sum_core",
    )(keep, got)


def sum_narrow_kernel(apart, a_ref, b_ref, c_ref, d_ref, *out_refs):
    refs = (a_ref, b_ref, c_ref, d_ref)
    columns = a_ref.shape[2] - (128 if apart else 0)
    for far, out_ref in enumerate(out_refs):
        total = sum(ref[far, :, :columns].astype(F32) for ref in refs)
        out_ref[:, :columns] = total.astype(BF16)
        if apart:
            for near, ref in enumerate(refs):
                out_ref[:, columns + 128 * near : columns + 128 * near + 128] = ref[far, :, columns:]


def sum_narrow(parts, apart):
    _, rows, columns = parts[0].shape
    columns += 3 * 128 if apart else 0
    return pl.pallas_call(
        functools.partial(sum_narrow_kernel, apart),
        in_specs=[in_vmem] * 4,
        out_specs=[in_vmem] * 4,
        out_shape=[jax.ShapeDtypeStruct((rows, columns), BF16)] * 4,
        compiler_params=small,
        cost_estimate=pl.CostEstimate(flops=0, bytes_accessed=40 * rows * columns, transcendentals=0),
        name="sum_narrow",
    )(*parts)


def sum_planes_kernel(a_ref, b_ref, c_ref, d_ref, total_ref, *apart_refs):
    refs = (a_ref, b_ref, c_ref, d_ref)
    columns = total_ref.shape[1]
    total_ref[...] = sum(ref[:, :columns].astype(F32) for ref in refs).astype(BF16)
    for apart_ref in apart_refs:
        for far, ref in enumerate(refs):
            apart_ref[far] = ref[:, columns:]


def sum_planes(parts, apart):
    rows, columns = parts[0].shape
    kept = 4 * 128 if apart else 0
    out_shape = [jax.ShapeDtypeStruct((rows, columns - kept), BF16)]
    if apart:
        out_shape.append(jax.ShapeDtypeStruct((4, rows, kept), BF16))
    return pl.pallas_call(
        sum_planes_kernel,
        in_specs=[in_vmem] * 4,
        out_specs=[in_vmem] * len(out_shape),
        out_shape=out_shape,
        compiler_params=small,
        cost_estimate=pl.CostEstimate(flops=0, bytes_accessed=10 * rows * columns, transcendentals=0),
        name="sum_planes",
    )(*parts)


def cut_kernel(place_ref, part_ref, *out_refs):
    rows, columns = out_refs[0].shape
    rows = rows - 16
    total = part_ref.shape[1]
    units = total * 4 // 5
    for near, out_ref in enumerate(out_refs):
        quarter = place_ref[2] ^ near
        row = pl.ds(pl.multiple_of((quarter % 2) * rows, 16), rows)
        column = pl.multiple_of((quarter // 2) * (units // 2), 128)
        out_ref[0:rows, 0 : units // 2] = part_ref[row, pl.ds(column, units // 2)]
        column = pl.multiple_of(units + (quarter // 2) * (columns - units // 2), 128)
        out_ref[0:rows, units // 2 :] = part_ref[row, pl.ds(column, columns - units // 2)]
        sums = part_ref[2 * rows :, 0:units].astype(F32)
        sums = jnp.concatenate([sums[:, : units // 2], sums[:, units // 2 :]], 0)
        out_ref[rows:, 0 : units // 2] = sums.astype(BF16)
        out_ref[rows:, units // 2 :] = jnp.zeros((16, columns - units // 2), BF16)


def cut(place, part):
    rows, total = part.shape
    shape = ((rows - 8) // 2 + 16, total // 2)
    return pl.pallas_call(
        cut_kernel,
        in_specs=[smem, in_vmem],
        out_specs=[in_vmem] * 4,
        out_shape=[jax.ShapeDtypeStruct(shape, BF16)] * 4,
        compiler_params=small,
        cost_estimate=pl.CostEstimate(flops=0, bytes_accessed=2 * MIB, transcendentals=0),
        name="cut",
    )(place, part)


def sum_quarter_kernel(a_ref, b_ref, c_ref, d_ref, total_ref, apart_ref):
    refs = (a_ref, b_ref, c_ref, d_ref)
    rows = total_ref.shape[0]
    total_ref[...] = sum(ref[0:rows, :].astype(F32) for ref in refs).astype(BF16)
    for near, ref in enumerate(refs):
        apart_ref[near] = ref[rows:, : apart_ref.shape[2]]


def sum_quarter(parts):
    rows, columns = parts[0].shape
    return pl.pallas_call(
        sum_quarter_kernel,
        in_specs=[in_vmem] * 4,
        out_specs=[in_vmem] * 2,
        out_shape=[
            jax.ShapeDtypeStruct((rows - 16, columns), BF16),
            jax.ShapeDtypeStruct((4, 16, columns * 4 // 5), BF16),
        ],
        compiler_params=small,
        cost_estimate=pl.CostEstimate(flops=0, bytes_accessed=2 * MIB, transcendentals=0),
        name="sum_quarter",
    )(*parts)


def as_row(column):
    return jnp.transpose(jnp.broadcast_to(column, (column.shape[0], 128)))[0:1]


def finish_inner_kernel(place_ref, weight_ref, gain_ref, a_ref, b_ref, c_ref, d_ref, out_ref, last_ref, ggain_ref):
    rows = a_ref.shape[0]
    units = weight_ref.shape[1] // 2
    width = last_ref.shape[1] // 2
    for near, ref in enumerate((a_ref, b_ref, c_ref, d_ref)):
        quarter = place_ref[2] ^ near
        row = pl.ds(pl.multiple_of((quarter % 2) * rows, rows), rows)
        half = quarter // 2
        out_ref[row, pl.ds(pl.multiple_of(half * units, 128), units)] = ref[:, :units].astype(F32)
        last_ref[row, pl.ds(pl.multiple_of(half * width, 128), width)] = ref[:, units:].astype(F32)
    along = jnp.sum(out_ref[...] * weight_ref[...].astype(F32), -1, keepdims=True)
    ggain_ref[...] = as_row(along) / gain_ref[...].astype(F32)


def finish_inner(place, weight, gain, parts, width):
    rows, units = weight.shape
    ins = [weight, gain] + list(parts)
    outs = [jax.ShapeDtypeStruct(shape, F32) for shape in ((rows, units), (rows, width), (1, rows))]
    return pl.pallas_call(
        finish_inner_kernel,
        in_specs=[smem] + [in_vmem] * len(ins),
        out_specs=[in_vmem] * len(outs),
        out_shape=outs,
        compiler_params=small,
        cost_estimate=pl.CostEstimate(flops=0, bytes_accessed=3 * MIB, transcendentals=0),
        name="finish_inner",
    )(place, *ins)


def finish_heads_kernel(place_ref, wq_ref, wk_ref, wv_ref, gain_ref, a_ref, b_ref, c_ref, d_ref, *refs):
    *out_refs, table_ref, ggain_ref, result_ref = refs
    rows = a_ref.shape[0]
    width = wq_ref.shape[1]
    half = 3 * width // 2
    for near, ref in enumerate((a_ref, b_ref, c_ref, d_ref)):
        quarter = place_ref[2] ^ near
        row = pl.multiple_of((quarter % 2) * rows, rows)
        column = pl.multiple_of((quarter // 2) * half, 128)
        result_ref[pl.ds(row, rows), pl.ds(column, half)] = ref[:, :half].astype(F32)

        @pl.when(quarter == 0)
        def _():
            table_ref[...] = ref[0:16, half:].astype(F32)[0:1, : table_ref.shape[1]]

    along = jnp.zeros((2 * rows, 1), F32)
    for index, (out_ref, weight_ref) in enumerate(zip(out_refs, (wq_ref, wk_ref, wv_ref))):
        grad = result_ref[:, index * width : (index + 1) * width]
        out_ref[...] = grad
        along = along + jnp.sum(grad * weight_ref[...].astype(F32), -1, keepdims=True)
    ggain_ref[...] = as_row(along) / gain_ref[...].astype(F32)


def finish_heads(place, weights, gain, parts, table_share):
    rows, width = weights[0].shape
    ins = list(weights) + [gain] + list(parts)
    outs = [jax.ShapeDtypeStruct((rows, width), F32)] * 3
    outs += [jax.ShapeDtypeStruct((1, table_share), F32), jax.ShapeDtypeStruct((1, rows), F32)]
    return pl.pallas_call(
        finish_heads_kernel,
        in_specs=[smem] + [in_vmem] * len(ins),
        out_specs=[in_vmem] * len(outs),
        out_shape=outs,
        scratch_shapes=[pltpu.VMEM((rows, 3 * width), F32)],
        compiler_params=small,
        cost_estimate=pl.CostEstimate(flops=0, bytes_accessed=3 * MIB, transcendentals=0),
        name="finish_heads",
    )(place, *ins)


def order_small_kernel(place_ref, own_ref, got_ref, out_ref):
    for other, ref in enumerate((own_ref, got_ref)):
        for far in range(4):
            out_ref[pl.ds(owner_of(place_ref, far, other), 1), :] = ref[far, 0:1, :]


def order_small(place, own, got):
    return pl.pallas_call(
        order_small_kernel,
        grid=(1,),
        in_specs=[smem, whole(own.shape), whole(got.shape)],
        out_specs=pl.BlockSpec((8, own.shape[2]), lambda i: (0, 0)),
        out_shape=jax.ShapeDtypeStruct((8, own.shape[2]), F32),
        name="order_small",
    )(place, own, got)


def gather_messages(message):
    far = jnp.stack([message] + [exchange(message, plane=distance) for distance in range(1, 4)])
    near = jnp.stack(spread(far))
    return near, exchange(near, core=1)


def tie(first, then):
    first, then = lax.optimization_barrier((first, then))
    return first, then


def gather_heads(place, own, small):
    rows, width = own[0].shape
    line = jnp.broadcast_to(jnp.pad(small, (0, width - small.shape[0])), (8, width))
    heads = jnp.stack([jnp.concatenate([weight, line]) for weight in own])
    quarter = lax.dynamic_index_in_dim(heads, place[2], 0, keepdims=False)
    far = jnp.stack([exchange(quarter, plane=distance) for distance in range(1, 4)])
    far, heads = tie(far, heads)
    near = spread(far)
    other = exchange(heads, core=1)
    far_other = exchange(far, core=1)
    lines = lambda first, rest: jnp.concatenate([first[:1, rows:, :256], rest[:, rows:, :256]]).astype(F32)
    ordered = order_small(place, lines(heads, far), lines(other, far_other))
    return near, [heads, other], far_other, ordered


def fetch_inner(narrow, inner_weight, width):
    quarter = lax.dynamic_slice_in_dim(inner_weight, narrow * width, width, 1)
    return [exchange(quarter, plane=far) for far in range(1, 4)]


def layer_specs():
    both = ("narrow", "wide")
    rows, matrix, vector = P(both, None), P("wide", None), P("wide")
    ins = (rows, vector, matrix, matrix, matrix, matrix, vector, vector, matrix, matrix, matrix, rows, P())
    outs = (rows, rows, rows, vector, matrix, matrix, matrix, matrix, vector, vector, matrix, matrix, matrix)
    return ins, outs


def local_permuted(tokens, *arguments):
    *weights_own, lengths, positives = arguments
    attention_gain, query_weight, key_weight, value_weight, output_weight = weights_own[:5]
    bias_table, forward_gain, inner_weight, outer_weight, project_weight = weights_own[5:]
    segs = lengths.shape[1]
    width = tokens.shape[1]
    units = inner_weight.shape[1]
    wide_at = lax.axis_index("wide")
    narrow_at = lax.axis_index("narrow")
    device = narrow_at * 8 + wide_at
    place = jnp.stack([device, wide_at, narrow_at, wide_at // 2, wide_at % 2]).astype(jnp.int32)
    share = attention_gain.shape[0]

    own_heads = (query_weight, key_weight, value_weight, output_weight)
    small = jnp.concatenate([attention_gain, forward_gain, bias_table])
    near, both_heads, far_other, small = gather_heads(place, own_heads, small)
    gain_one = small[:, :share].reshape(1, width)
    gain_two = small[:, share : 2 * share].reshape(1, width)
    table = small[:, 2 * share : 2 * share + bias_table.shape[0]].reshape(BUCKETS, HEADS)
    table = jnp.pad(table, ((0, 0), (0, 4))).astype(BF16)
    _, own_inner = tie(both_heads[1], inner_weight)
    _, own_outer = tie(far_other, outer_weight)
    wu = lax.all_gather(own_outer, "wide", axis=0, tiled=True)
    far = jnp.stack(fetch_inner(narrow_at, own_inner, width))
    (gain_one, gain_two, table), near = tie((gain_one, gain_two, table), near)
    near, far = tie(near, far)
    head_pieces = both_heads + near + [far_other] + [exchange(piece, core=1) for piece in near[1:]]
    near = spread(far)
    other_inner = exchange(own_inner, core=1)

    hid, q, k, v, weights = project(place, tokens, gain_one, head_pieces)
    q, own_last = tie(q, project_weight)
    wp = lax.all_gather(own_last, "wide", axis=0, tiled=True)
    mixed, inv, p = attend(lengths, table, q, k, v, 0, 6)
    mixed, inv, p, near = lax.optimization_barrier((mixed, inv, p, near))
    near_other = [exchange(piece, core=1) for piece in near]
    hidden, slope, active_sum, message, middle, hid_two, wi = forward(
        place, lengths, tokens, mixed, gain_two, weights, wu, units, [own_inner, other_inner] + near + near_other
    )
    loss, grad_wp, glow_all, gmid, gm, grads_out = contrast_back(
        lengths, place, *gather_messages(message), positives[None], wp, gain_two, hid_two, active_sum, wu, slope, wi,
        middle, mixed, inv, weights, project_weight.shape[0],
    )

    part = lax.psum_scatter(grads_out.reshape(-1, units + width), "wide", scatter_dimension=0, tiled=True)
    grad_heads, diag = attend_grad(lengths, q, k, v, gm, mixed, p, 0, 6)
    grad_table = table_grad(diag).reshape(8, -1)
    rows_table = jnp.pad(grad_table, ((0, 0), (0, 128 - grad_table.shape[1])))
    keep, send = head_grad(place, hid, grad_heads, rows_table)
    got = exchange(send, core=1)
    quarters = sum_core(keep, got)
    quarters, gmid = tie(quarters, gmid)
    arrived = [quarters[0]] + [exchange(quarters[near], narrow=near) for near in range(1, 4)]
    grad_tokens = token_grad(tokens, gain_one, gmid, grad_heads, weights)
    grad_tokens, part = tie(grad_tokens, part)
    pieces = cut(place, part)
    pieces = [pieces[0]] + [exchange(pieces[near], narrow=near) for near in range(1, 4)]
    planes = sum_narrow(arrived, False)
    arrived = [planes[0]] + [exchange(planes[far], plane=far) for far in range(1, 4)]
    total, active_pieces = sum_quarter(pieces)
    inner_parts = spread(total)
    grad_outer = outer_grad(place, active_pieces, glow_all)
    grad_outer, arrived = tie(grad_outer, arrived)
    (total,) = sum_planes(arrived, False)
    last_parts = spread(total)
    grad_inner, grad_out, gain_two_grad = finish_inner(place, inner_weight, forward_gain[None], inner_parts, width)
    *grads, table_own, gain_one_grad = finish_heads(
        place, own_heads[:3], attention_gain[None], last_parts, bias_table.shape[0]
    )
    grads.append(grad_out)
    return (
        hidden,
        grad_tokens,
        loss[:, 0].reshape(1, segs),
        gain_one_grad[0],
        *grads,
        table_own[0],
        gain_two_grad[0],
        grad_inner,
        grad_outer,
        grad_wp,
    )


def local_plain(tokens, *arguments):
    *weights_own, lengths, positives = arguments
    attention_gain, query_weight, key_weight, value_weight, output_weight = weights_own[:5]
    bias_table, forward_gain, inner_weight, outer_weight, project_weight = weights_own[5:]
    both = ("narrow", "wide")
    segs = lengths.shape[1]
    width = tokens.shape[1]
    wide_at = lax.axis_index("wide")
    device = lax.axis_index("narrow") * lax.axis_size("wide") + wide_at
    place = jnp.stack([device, wide_at]).astype(jnp.int32)
    share = attention_gain.shape[0]
    gather = lambda a: lax.all_gather(a, "wide", axis=0, tiled=True)
    small = gather(jnp.concatenate([attention_gain, forward_gain, bias_table])[None])
    gain_one = small[:, :share].reshape(1, width)
    gain_two = small[:, share : 2 * share].reshape(1, width)
    table = jnp.pad(small[:, 2 * share :].reshape(BUCKETS, HEADS), ((0, 0), (0, 4)))
    weights = jnp.stack([gather(w) for w in (query_weight, key_weight, value_weight, output_weight)])
    wu = gather(outer_weight)
    hid, q, k, v, weights = project(place, tokens, gain_one, [weights])
    mixed, inv, p = attend(lengths, table, q, k, v, 0, HEADS // 2)
    hidden, slope, active_sum, message, middle, hid_two, wi = forward(
        place, lengths, tokens, mixed, gain_two, weights, wu, inner_weight.shape[1], [gather(inner_weight)]
    )
    messages = lax.all_gather(message, both, axis=0, tiled=True).reshape(-1, 2, 8, 512)
    messages = messages.transpose(0, 2, 1, 3).reshape(-1, 1024)
    loss, grad_wp, glow_all, grows = contrast_plain(
        place,
        messages[:, :width],
        messages[:, width : width + 1].astype(F32),
        positives.reshape(-1, 1),
        gather(project_weight),
        project_weight.shape[0],
    )
    active_all = lax.all_gather(active_sum[:segs], both, axis=0, tiled=True)
    active_own = lax.dynamic_slice_in_dim(active_all, wide_at * outer_weight.shape[0], outer_weight.shape[0], 1)
    grad_outer = dot_tn(active_own, glow_all.astype(F32))
    glow = jnp.pad(grows.astype(BF16), ((0, 16 - segs), (0, 0)))
    gmid, gm, grad_wi, grad_wo = back(
        lengths, place, glow, grows, gain_two, hid_two, active_sum, wu, slope, wi, middle, mixed, inv, weights, False
    )
    grad_heads, diag = attend_grad(lengths, q, k, v, gm, mixed, p, 0, HEADS // 2)
    grad_tokens = token_grad(tokens, gain_one, gmid, grad_heads, weights)

    def total(grad):
        part = lax.psum_scatter(grad, "wide", scatter_dimension=0, tiled=True)
        return lax.psum(part.astype(F32), "narrow")

    grads = [total(dot_tn(hid, grad).astype(BF16)) for grad in grad_heads] + [total(grad_wo)]
    grad_inner = total(grad_wi)
    table_own = total(table_grad(diag).reshape(lax.axis_size("wide"), -1))[0]
    own_heads = jnp.stack([query_weight, key_weight, value_weight])
    along = jnp.sum(jnp.stack(grads[:3]) * own_heads.astype(F32), (0, 2))
    return (
        hidden,
        grad_tokens,
        loss[:, 0].reshape(1, segs),
        along / attention_gain.astype(F32),
        *grads,
        table_own,
        jnp.sum(grad_inner * inner_weight.astype(F32), 1) / forward_gain.astype(F32),
        grad_inner,
        grad_outer,
        grad_wp,
    )


def solution(mesh):
    ins, outs = layer_specs()
    permuted = (mesh.shape["narrow"], mesh.shape["wide"]) == (4, 8)
    body = local_permuted if permuted else local_plain
    return jax.shard_map(body, mesh=mesh, in_specs=ins, out_specs=outs, check_vma=False)
```

```python
import functools

import jax
import jax.numpy as jnp
from jax import lax
from jax.experimental import pallas as pl
from jax.experimental.pallas import tpu as pltpu
from jax.sharding import PartitionSpec as P

HEADS = 12
HEAD_DIM = 64
BUCKETS = 32
SPAN = 256
BLOCK = 128
WINDOW = BLOCK + 2 * SPAN
SLOTS = 4
CHUNK = 1024

epsilon = 1e-06
logit_scale = 50.0
root_half = 0.7071067811865476
inv_root_tau = 0.3989422804014327
MIB = 1 << 20
F32 = jnp.float32
BF16 = jnp.bfloat16


def dot_nn(left, right):
    return lax.dot_general(left, right, (((1,), (0,)), ((), ())), preferred_element_type=F32)


def dot_nt(left, right):
    return lax.dot_general(left, right, (((1,), (1,)), ((), ())), preferred_element_type=F32)


def dot_tn(left, right):
    return lax.dot_general(left, right, (((0,), (0,)), ((), ())), preferred_element_type=F32)


def split(values):
    high = values.astype(BF16)
    rest = values - high.astype(F32)
    middle = rest.astype(BF16)
    return high, middle, (rest - middle.astype(F32)).astype(BF16)


def split_two(values):
    high = values.astype(BF16)
    return high, (values - high.astype(F32)).astype(BF16)


def bucket_of(offset):
    distance = jnp.abs(offset)
    larger = jnp.full_like(distance, 8)
    for step in range(1, 8):
        larger = larger + (distance * distance >= 64 * 2**step).astype(jnp.int32)
    return jnp.where(distance < 8, distance, larger) + jnp.where(offset > 0, 16, 0)


def bounds_of(lengths_ref, count):
    bounds = []
    total = 0
    for index in range(count):
        total = total + lengths_ref[0, index]
        bounds.append(total)
    return bounds


def segment_of(places, bounds):
    segment = jnp.zeros_like(places)
    for bound in bounds:
        segment = segment + (places >= bound).astype(jnp.int32)
    return segment


def window_of(bounds, start):
    low = 0
    high = bounds[-1]
    for bound in bounds[:-1]:
        low = jnp.where(bound <= start, bound, low)
    for bound in reversed(bounds[:-1]):
        high = jnp.where(bound > start + BLOCK - 1, bound, high)
    first = (low // BLOCK) * BLOCK
    blocks = (high - first + BLOCK - 1) // BLOCK
    return first, blocks


def params(mib=60, grid=1):
    return pltpu.CompilerParams(vmem_limit_bytes=mib * MIB, dimension_semantics=("arbitrary",) * grid)


def whole(shape):
    return pl.BlockSpec(shape, lambda *_: (0,) * len(shape), pipeline_mode=pl.Buffered(1))


smem = pl.BlockSpec(memory_space=pltpu.SMEM)
anywhere = pl.BlockSpec(memory_space=pl.ANY)
in_hbm = pl.BlockSpec(memory_space=pltpu.HBM)
in_vmem = pl.BlockSpec(memory_space=pltpu.VMEM)
small = pltpu.CompilerParams(vmem_limit_bytes=12 * MIB)


def owner_of(place_ref, far, other):
    return 2 * (place_ref[3] ^ far) + (place_ref[4] ^ other)


def start_copies(pairs, sems, first=0):
    pending = [pltpu.make_async_copy(source, target, sems.at[first + at]) for at, (source, target) in enumerate(pairs)]
    for copy in pending:
        copy.start()
    return pending


def wait_copies(pending):
    for copy in pending:
        copy.wait()


def head_copies(place_ref, refs, whole_ref):
    rows = whole_ref.shape[1] // 8
    mine = pl.ds(0, rows)
    for other in range(2):
        start = pl.multiple_of(owner_of(place_ref, 0, other) * rows, 16)
        yield refs[other].at[:, mine, :], whole_ref.at[:, pl.ds(start, rows), :]
        for near in range(4):
            piece = refs[2 + 4 * other + near]
            for far in range(1, 4):
                start = pl.multiple_of(owner_of(place_ref, far, other) * rows, 16)
                yield piece.at[far - 1, mine, :], whole_ref.at[place_ref[2] ^ near, pl.ds(start, rows), :]


def project_kernel(place_ref, x_ref, gain_ref, *refs):
    *pieces, hid_ref, q_ref, k_ref, v_ref, out_ref, w_ref, sems, out_sem = refs
    step = pl.program_id(0)
    if len(pieces) == 1:
        pairs = [(pieces[0], w_ref)]
    else:
        pairs = list(head_copies(place_ref, pieces, w_ref))
    whole_copy = pltpu.make_async_copy(w_ref, out_ref, out_sem)

    @pl.when(step == 0)
    def _():
        start_copies(pairs, sems)

    x = x_ref[...].astype(F32)
    scale = lax.rsqrt(jnp.mean(x * x, -1, keepdims=True) + epsilon)
    hidden = (x * scale * gain_ref[...].astype(F32)).astype(BF16)
    hid_ref[...] = hidden

    @pl.when(step == 0)
    def _():
        wait_copies([pltpu.make_async_copy(*pair, sems.at[index]) for index, pair in enumerate(pairs)])
        whole_copy.start()

    q_ref[...] = dot_nn(hidden, w_ref[0]).astype(BF16)
    k_ref[...] = dot_nn(hidden, w_ref[1]).astype(BF16)
    v_ref[...] = dot_nn(hidden, w_ref[2]).astype(BF16)

    @pl.when(step == pl.num_programs(0) - 1)
    def _():
        whole_copy.wait()


def project(place, x, gain, pieces):
    rows, width = x.shape
    block = rows // 4
    row_spec = pl.BlockSpec((block, width), lambda i: (i, 0))
    out = jax.ShapeDtypeStruct((rows, width), BF16)
    return pl.pallas_call(
        project_kernel,
        grid=(4,),
        in_specs=[smem, row_spec, whole((1, width))] + [in_hbm] * len(pieces),
        out_specs=[row_spec] * 4 + [anywhere],
        out_shape=[out] * 4 + [jax.ShapeDtypeStruct((4, width, width), BF16)],
        scratch_shapes=[
            pltpu.VMEM((4, width, width), BF16),
            pltpu.SemaphoreType.DMA((26,)),
            pltpu.SemaphoreType.DMA(()),
        ],
        compiler_params=params(),
        cost_estimate=pl.CostEstimate(
            flops=6 * rows * width * width, bytes_accessed=10 * rows * width + 16 * width * width, transcendentals=0
        ),
        name="project_heads",
    )(place, x, gain, *pieces)


def attend_kernel(first_pair, lengths_ref, table_ref, q_ref, k_ref, v_ref, *refs):
    mixed_ref, inv_ref, p_any, rows_ref, tile_ref, segc_ref, segr_ref, p_ref, sems = refs[-9:]
    together = q_ref.shape[1] // BLOCK
    pair = first_pair + together * pl.program_id(0)
    rows = q_ref.shape[0]
    bounds = bounds_of(lengths_ref, lengths_ref.shape[1])
    reach = WINDOW + BLOCK

    @pl.when(pl.program_id(0) == 0)
    def _():
        segc_ref[...] = segment_of(lax.broadcasted_iota(jnp.int32, segc_ref.shape, 0), bounds)
        segr_ref[...] = segment_of(lax.broadcasted_iota(jnp.int32, segr_ref.shape, 1), bounds)
        offsets = lax.broadcasted_iota(jnp.int32, (BUCKETS, reach), 1) - (SPAN + BLOCK)
        kinds = lax.broadcasted_iota(jnp.int32, (BUCKETS, reach), 0)
        onehot = (bucket_of(offsets) == kinds).astype(F32).astype(BF16)
        rows_ref[...] = dot_tn(table_ref[...], onehot)

    for head in range(2 * together):
        line = rows_ref[pl.ds(2 * pair + head, 1), :]
        skew = pltpu.roll(jnp.broadcast_to(line, (BLOCK, reach)), 0, 1, stride=1, stride_axis=0)
        tile_ref[head] = skew[:, BLOCK:]

    lane = lax.broadcasted_iota(jnp.int32, (BLOCK, BLOCK), 1)
    first_half = lane < HEAD_DIM

    def out_copy(block_index):
        slot = block_index % SLOTS
        target = p_any.at[pl.ds(2 * pair, 2 * together), pl.ds(pl.multiple_of(block_index * BLOCK, BLOCK), BLOCK), :]
        return pltpu.make_async_copy(p_ref.at[slot], target, sems.at[slot])

    def one(block_index, carry):
        slot = block_index % SLOTS
        start = pl.multiple_of(block_index * BLOCK, BLOCK)

        @pl.when(block_index >= SLOTS)
        def _():
            out_copy(block_index - SLOTS).wait()

        first, count = window_of(bounds, start)
        first = pl.multiple_of(first, BLOCK)
        shift = pl.multiple_of(first - start + SPAN, BLOCK)

        def body(blocks):
            size = blocks * BLOCK
            queries = pl.ds(start, BLOCK)
            keys = pl.ds(first, size)
            segc = segc_ref[queries, :]
            segr = segr_ref[0:1, keys]
            same = jnp.concatenate([segc] * blocks, 1) == segr
            wide_lane = lax.broadcasted_iota(jnp.int32, (size, BLOCK), 1) < HEAD_DIM
            scores = []
            for head in range(2 * together):
                lanes = slice(head // 2 * BLOCK, head // 2 * BLOCK + BLOCK)
                mine = first_half if head % 2 == 0 else ~first_half
                q = q_ref[queries, lanes]
                scores.append(dot_nt(jnp.where(mine, q, jnp.zeros_like(q)), k_ref[keys, lanes]))
            raised = []
            for head in range(2 * together):
                score = jnp.where(same, scores[head] + tile_ref[head, :, pl.ds(shift, size)], -1000000000.0)
                power = jnp.exp(score - jnp.max(score, -1, keepdims=True)).astype(BF16)
                p_ref[slot, head, :, 0:size] = power
                raised.append(power)
            for near in range(together):
                lanes = slice(near * BLOCK, near * BLOCK + BLOCK)
                v = v_ref[keys, lanes]
                one = jnp.ones_like(v)
                left = dot_nn(raised[2 * near], jnp.where(wide_lane, v, one))
                right = dot_nn(raised[2 * near + 1], jnp.where(wide_lane, one, v))
                total = pltpu.roll(jnp.where(first_half, right, left), HEAD_DIM, 1)
                inverse = 1.0 / total
                mixed_ref[queries, lanes] = (jnp.where(first_half, left, right) * inverse).astype(BF16)
                inv_ref[queries, lanes] = inverse

        for blocks in range(1, WINDOW // BLOCK + 1):
            pl.when(count == blocks)(functools.partial(body, blocks))
        out_copy(block_index).start()
        return carry

    lax.fori_loop(0, rows // BLOCK, one, 0)
    for block_index in range(rows // BLOCK - SLOTS, rows // BLOCK):
        out_copy(block_index).wait()


def attend(lengths, table, q, k, v, first_pair, pairs, before=()):
    rows, width = q.shape
    together = max(size for size in (1, 2, 3, 6) if pairs % size == 0 and first_pair % size == 0)
    column = pl.BlockSpec((rows, BLOCK * together), lambda p: (0, first_pair // together + p))
    return pl.pallas_call(
        functools.partial(attend_kernel, first_pair),
        grid=(pairs // together,),
        in_specs=[smem, whole(table.shape), column, column, column] + [anywhere] * len(before),
        out_specs=[column, column, anywhere],
        out_shape=[
            jax.ShapeDtypeStruct((rows, width), BF16),
            jax.ShapeDtypeStruct((rows, width), F32),
            jax.ShapeDtypeStruct((HEADS, rows, WINDOW), BF16),
        ],
        scratch_shapes=[
            pltpu.VMEM((16, WINDOW + BLOCK), F32),
            pltpu.VMEM((2 * together, BLOCK, WINDOW), F32),
            pltpu.VMEM((rows, BLOCK), jnp.int32),
            pltpu.VMEM((8, rows), jnp.int32),
            pltpu.VMEM((SLOTS, 2 * together, BLOCK, WINDOW), BF16),
            pltpu.SemaphoreType.DMA((SLOTS,)),
        ],
        input_output_aliases={5 + index: index for index in range(len(before))},
        compiler_params=params(),
        cost_estimate=pl.CostEstimate(
            flops=pairs * 8 * rows * 512 * 128, bytes_accessed=pairs * 6 * MIB, transcendentals=2 * pairs * rows * 512
        ),
        name="attend",
    )(lengths, table, q, k, v, *before)


def gelu_and_slope(v):
    bell = jnp.exp(-0.5 * v * v)
    t = 1.0 / (1.0 + (0.3275911 * root_half) * jnp.abs(v))
    series = t * (
        0.5 * 0.254829592
        + t * (0.5 * -0.284496736 + t * (0.5 * 1.421413741 + t * (0.5 * -1.453152027 + t * (0.5 * 1.061405429))))
    )
    tail = series * bell
    share = jnp.where(v >= 0.0, 1.0 - tail, tail)
    return v * share, share + v * bell * inv_root_tau


def member_of(lengths_ref, rows, count):
    bounds = bounds_of(lengths_ref, lengths_ref.shape[1])
    segment = segment_of(lax.broadcasted_iota(jnp.int32, (rows, count), 0), bounds)
    return (segment == lax.broadcasted_iota(jnp.int32, (rows, count), 1)).astype(F32).astype(BF16)


def member_rows(lengths_ref, rows, count):
    bounds = bounds_of(lengths_ref, lengths_ref.shape[1])
    segment = segment_of(lax.broadcasted_iota(jnp.int32, (count, rows), 1), bounds)
    return (segment == lax.broadcasted_iota(jnp.int32, (count, rows), 0)).astype(F32).astype(BF16)


def inner_copies(place_ref, refs, inner_ref):
    rows = refs[0].shape[0]
    width = inner_ref.shape[0]
    for other in range(2):
        owner = owner_of(place_ref, 0, other)
        yield refs[other], inner_ref.at[pl.ds(pl.multiple_of(owner * rows, 16), rows), :]
        for near in range(4):
            piece = refs[2 + 4 * other + near]
            quarter = place_ref[2] ^ near
            for far in range(1, 4):
                owner = owner_of(place_ref, far, other)
                row = pl.ds(pl.multiple_of(owner * rows, 16), rows)
                column = pl.ds(pl.multiple_of(quarter * width, 128), width)
                yield piece.at[far - 1], inner_ref.at[row, column]


def forward_kernel(place_ref, lengths_ref, x_ref, mixed_ref, gain_ref, heads_ref, wu_any, *refs):
    *pieces, out_ref, slope_ref, active_sum_ref, message_ref, mid_out, hid_out, wi_out = refs[:-12]
    total_ref, mid_ref, hid_ref, member_ref, wo_ref, inner_ref, active_ref = refs[-12:-5]
    wi_ref, wu_ref, sems, out_sems, last_sems = refs[-5:]
    step = pl.program_id(0)
    rows, width = hid_ref.shape
    block = rows // 4
    outs = ((wi_ref, wi_out), (hid_ref, hid_out), (mid_ref, mid_out))
    if len(pieces) == 1:
        groups = [[(pieces[0], wi_ref)], [(wu_any, wu_ref)]]
    else:
        groups = [list(inner_copies(place_ref, pieces, wi_ref)), [(wu_any, wu_ref)]]
    firsts = [0, len(groups[0])]
    spans = [slice(index * block, (index + 1) * block) for index in range(4)]

    def arrive(index):
        pairs = groups[index]
        wait_copies([pltpu.make_async_copy(*pair, sems.at[firsts[index] + at]) for at, pair in enumerate(pairs)])

    @pl.when(step == 0)
    def _():
        output_copy = pltpu.make_async_copy(heads_ref.at[3], wo_ref, last_sems.at[0])
        output_copy.start()
        for group, first in zip(groups, firsts):
            start_copies(group, sems, first)
        member_ref[...] = member_rows(lengths_ref, rows, 16)
        output_copy.wait()
        for span in spans:
            middle = x_ref[span, :].astype(F32) + dot_nn(mixed_ref[span, :], wo_ref[...])
            scale = lax.rsqrt(jnp.mean(middle * middle, -1, keepdims=True) + epsilon)
            total_ref[span, :] = middle
            mid_ref[span, :] = middle
            hid_ref[span, :] = (middle * scale * gain_ref[...].astype(F32)).astype(BF16)
        arrive(0)
        for index, pair in enumerate(outs):
            pltpu.make_async_copy(*pair, out_sems.at[index]).start()

    columns = pl.ds(pl.multiple_of(step * CHUNK, CHUNK), CHUNK)

    def first(span):
        inner_ref[span, :] = dot_nn(hid_ref[span, :], wi_ref[:, columns])

    def second(span):
        for at in range(span.start, span.stop, 32):
            active, slope = gelu_and_slope(inner_ref[at : at + 32, :])
            active_ref[at : at + 32, :] = active.astype(BF16)
            slope_ref[at : at + 32, :] = slope.astype(BF16)

    first(spans[0])
    first(spans[1])
    second(spans[0])

    @pl.when(step == 0)
    def _():
        arrive(1)

    for index, span in enumerate(spans):
        total_ref[span, :] += dot_nn(active_ref[span, :], wu_ref[columns, :])
        if index + 2 < 4:
            first(spans[index + 2])
        if index + 1 < 4:
            second(spans[index + 1])
    active_sum_ref[...] = dot_nn(member_ref[...], active_ref[...])

    @pl.when(step == pl.num_programs(0) - 1)
    def _():
        out_ref[...] = total_ref[...].astype(BF16)
        member = member_ref[...]
        pooled = jnp.zeros((16, width), F32)
        for span in spans:
            for piece in split_two(total_ref[span, :]):
                pooled = pooled + dot_nn(member[:, span], piece)
        row = lax.broadcasted_iota(jnp.int32, (8, 128), 0)
        lens = jnp.zeros((8, 128), jnp.int32)
        for index in range(8):
            lens = jnp.where(row == index, lengths_ref[0, index], lens)
        lens = lens.astype(F32)
        mean = pooled[0:8] / jnp.concatenate([lens] * (width // 128), 1)
        lower = jnp.concatenate([mean[:, 512:], lens, lens], 1)
        message_ref[...] = jnp.concatenate([mean[:, :512], lower], 0).astype(BF16)
        for index, pair in enumerate(outs):
            pltpu.make_async_copy(*pair, out_sems.at[index]).wait()


def forward(place, lengths, x, mixed, gain, heads, wu, units, pieces):
    rows, width = x.shape
    full = whole((rows, width))
    return pl.pallas_call(
        forward_kernel,
        grid=(units // CHUNK,),
        in_specs=[smem, smem, full, full, whole((1, width)), in_hbm, in_hbm] + [in_hbm] * len(pieces),
        out_specs=[
            pl.BlockSpec((rows, width), lambda i: (0, 0)),
            pl.BlockSpec((rows, CHUNK), lambda i: (0, i)),
            pl.BlockSpec((16, CHUNK), lambda i: (0, i)),
            pl.BlockSpec((16, 512), lambda i: (0, 0)),
        ]
        + [anywhere] * 3,
        out_shape=[
            jax.ShapeDtypeStruct((rows, width), BF16),
            jax.ShapeDtypeStruct((rows, units), BF16),
            jax.ShapeDtypeStruct((16, units), F32),
            pltpu.HBM((16, 512), BF16),
            jax.ShapeDtypeStruct((rows, width), F32),
            jax.ShapeDtypeStruct((rows, width), BF16),
            jax.ShapeDtypeStruct((width, units), BF16),
        ],
        scratch_shapes=[
            pltpu.VMEM((rows, width), F32),
            pltpu.VMEM((rows, width), F32),
            pltpu.VMEM((rows, width), BF16),
            pltpu.VMEM((16, rows), BF16),
            pltpu.VMEM((width, width), BF16),
            pltpu.VMEM((rows, CHUNK), F32),
            pltpu.VMEM((rows, CHUNK), BF16),
            pltpu.VMEM((width, units), BF16),
            pltpu.VMEM((units, width), BF16),
            pltpu.SemaphoreType.DMA((27,)),
            pltpu.SemaphoreType.DMA((3,)),
            pltpu.SemaphoreType.DMA((1,)),
        ],
        compiler_params=params(),
        cost_estimate=pl.CostEstimate(
            flops=4 * rows * width * units, bytes_accessed=30 * MIB, transcendentals=2 * rows * units
        ),
        name="feed_forward",
    )(place, lengths, x, mixed, gain, heads, wu, *pieces)


def contrast_kernel(place_ref, own_ref, got_ref, target_ref, wp_any, *refs):
    loss_ref, grad_wp_ref, glow_all_ref, grows_ref, glow_ref = refs[:-7]
    wide_ref, line_ref, full_ref, wp_ref, left_ref, right_ref, sems = refs[-7:]
    count, width = wide_ref.shape
    pending = start_copies([(wp_any, wp_ref)], sems)
    for other, ref in enumerate((own_ref, got_ref)):
        for far in range(4):
            for near in range(4):
                device = (place_ref[2] ^ near) * 8 + owner_of(place_ref, far, other)
                start = pl.multiple_of(device * 8, 8)
                piece = ref[near, far].astype(F32)
                left_ref[pl.ds(start, 8), :] = piece[0:8]
                right_ref[pl.ds(start, 8), :] = piece[8:16]
    rest = width - left_ref.shape[1]
    pooled = jnp.concatenate([left_ref[...], right_ref[:, 0:rest]], 1).astype(BF16)
    lens = right_ref[:, rest : rest + 1]
    wait_copies(pending)
    first = pl.multiple_of(place_ref[0] * 8, 8)
    projected = dot_nn(pooled, wp_ref[...])
    inverse = lax.rsqrt(jnp.sum(projected * projected, -1, keepdims=True) + epsilon)
    embedded = (projected * inverse).astype(BF16)
    row = lax.broadcasted_iota(jnp.int32, (count, count), 0)
    column = lax.broadcasted_iota(jnp.int32, (count, count), 1)
    logits = logit_scale * dot_nt(embedded, embedded)
    logits = jnp.where(row == column, -1000000000.0, logits)
    target_at = jnp.sum(jnp.where(row == column, target_ref[...], 0), -1, keepdims=True)
    hit = column == target_at
    highest = jnp.max(logits, -1, keepdims=True)
    totals = highest + jnp.log(jnp.sum(jnp.exp(logits - highest), -1, keepdims=True))
    target = jnp.sum(jnp.where(hit, logits, 0.0), -1, keepdims=True)
    line_ref[...] = jnp.broadcast_to(totals - target, line_ref.shape)
    loss_ref[...] = line_ref[pl.ds(first, 8), :]
    grad_logits = (jnp.exp(logits - totals) - hit.astype(F32)).astype(BF16)
    grad_embedded = logit_scale * (dot_nn(grad_logits, embedded) + dot_tn(grad_logits, embedded))
    along = jnp.sum(grad_embedded * projected, -1, keepdims=True)
    grad_projected = inverse * grad_embedded - projected * (inverse * inverse * inverse * along)
    high, low = split_two(grad_projected)
    full_ref[...] = dot_tn(pooled, high) + dot_tn(pooled, low)
    share = grad_wp_ref.shape[0]
    grad_wp_ref[...] = full_ref[pl.ds(pl.multiple_of(place_ref[1] * share, share), share), :]
    wp = wp_ref[...]
    grad_rows = (dot_nt(high, wp) + dot_nt(low, wp)) / lens
    glow_all_ref[...] = grad_rows.astype(BF16)
    wide_ref[...] = grad_rows
    own_rows = wide_ref[pl.ds(first, 8), :]
    grows_ref[...] = own_rows
    glow_ref[...] = jnp.concatenate([own_rows, jnp.zeros_like(own_rows)], 0).astype(BF16)


def contrast_plain(place, pooled, lens, targets, wp, share):
    count, width = pooled.shape
    exact = lax.Precision.HIGHEST
    projected = jnp.dot(pooled, wp, preferred_element_type=F32)
    inverse = lax.rsqrt(jnp.sum(projected * projected, -1, keepdims=True) + epsilon)
    embedded = (projected * inverse).astype(BF16)
    numbers = jnp.arange(count, dtype=jnp.int32)
    logits = logit_scale * dot_nt(embedded, embedded)
    logits = jnp.where(numbers[:, None] == numbers[None, :], -1000000000.0, logits)
    hit = numbers[None, :] == targets
    highest = jnp.max(logits, -1, keepdims=True)
    totals = highest + jnp.log(jnp.sum(jnp.exp(logits - highest), -1, keepdims=True))
    loss = totals - jnp.sum(jnp.where(hit, logits, 0.0), -1, keepdims=True)
    grad_logits = (jnp.exp(logits - totals) - hit.astype(F32)).astype(BF16)
    grad_embedded = logit_scale * (dot_nn(grad_logits, embedded) + dot_tn(grad_logits, embedded))
    along = jnp.sum(grad_embedded * projected, -1, keepdims=True)
    grad_projected = inverse * grad_embedded - projected * (inverse * inverse * inverse * along)
    own_columns = lax.dynamic_slice_in_dim(pooled.astype(F32), place[1] * share, share, 1)
    grad_wp = lax.dot_general(own_columns, grad_projected, (((0,), (0,)), ((), ())), precision=exact)
    grad_rows = jnp.dot(grad_projected, wp.astype(F32).T, precision=exact) / lens
    first = place[0] * 8
    own = lambda a: lax.dynamic_slice_in_dim(a, first, 8, 0)
    return jnp.broadcast_to(own(loss), (8, 128)), grad_wp, grad_rows.astype(BF16), own(grad_rows)


def fold(result_ref, keep_ref, send_ref, place_ref, column_half, column):
    narrow, plane, core = place_ref[2], place_ref[3], place_ref[4]
    rows = keep_ref.shape[2]
    for near in range(2):
        quarter = 2 * ((narrow // 2) ^ column_half) + near
        half = (narrow % 2) ^ near
        for far in range(4):
            for ref, owner in ((keep_ref, core), (send_ref, 1 - core)):
                start = pl.multiple_of((2 * (plane ^ far) + owner) * 2 * rows + half * rows, 16)
                block = result_ref[pl.ds(start, rows), :].astype(BF16)
                ref[quarter, far, :, pl.ds(column, block.shape[1])] = block


def back_kernel(
    lengths_ref, place_ref, glow_ref, grows_ref, gain_ref, hid_ref, active_ref, wu_ref, slope_ref, wi_ref,
    mid_any, mixed_any, inv_any, heads_any, gmid_any, gmix_ref, *refs,
):
    *grad_refs, result_ref, total_ref, member_ref, mid_ref, mixed_ref, inv_ref, wo_ref, sems, out_sems, gi_ref = refs
    step = pl.program_id(0)
    last = pl.num_programs(0) - 1
    rows, width = total_ref.shape
    folded = len(grad_refs) == 2 and len(grad_refs[1].shape) == 3
    late = [(mid_any, mid_ref), (mixed_any, mixed_ref), (inv_any, inv_ref), (heads_any.at[3], wo_ref)]

    @pl.when(step == 0)
    def _():
        member = member_of(lengths_ref, rows, 16)
        member_ref[...] = jnp.concatenate([member, member], 1)

    @pl.when(step == 0)
    def _():
        total_ref[...] = jnp.zeros_like(total_ref)

    @pl.when(step == 2)
    def _():
        start_copies(late, sems)

    high, low = split_two(dot_nt(glow_ref[...], wu_ref[...]))
    both = jnp.concatenate([high, low], 0)
    spans = (slice(0, rows // 2), slice(rows // 2, rows))
    for span in spans:
        spread = dot_nn(member_ref[span, :], both)
        gi_ref[span, :] = (spread * slope_ref[span, :].astype(F32)).astype(BF16)
    for span in spans:
        total_ref[span, :] += dot_nt(gi_ref[span, :], wi_ref[...])
    result_ref[:, :CHUNK] = dot_tn(hid_ref[...], gi_ref[...])

    if folded:
        grad_any, grad_ref = grad_refs
        owners, lines, _ = grad_ref.shape
        lines = lines - 8
        units = active_ref.shape[1]
        columns = pl.ds(pl.multiple_of(step * CHUNK, CHUNK), CHUNK)
        for owner in range(owners):
            grad_ref[owner, 0:lines, columns] = result_ref[owner * lines : (owner + 1) * lines, :CHUNK].astype(BF16)

        @pl.when(step == 0)
        def _():
            share = units // owners
            start = pl.multiple_of(place_ref[1] * share, 128)
            for owner in range(owners):
                grad_ref[owner, lines:, 0:units] = jnp.zeros((8, units), BF16)
                grad_ref[owner, lines:, pl.ds(start, share)] = active_ref[0:8, owner * share : (owner + 1) * share].astype(BF16)
    else:
        grad_refs[0][:, pl.ds(pl.multiple_of(step * CHUNK, CHUNK), CHUNK)] = result_ref[:, :CHUNK].astype(BF16)

    @pl.when(step == last)
    def _():
        pending = []
        if folded:
            inner_columns = pl.ds(0, units)
            copy = pltpu.make_async_copy(
                grad_ref.at[:, :, inner_columns], grad_any.at[:, :, inner_columns], out_sems.at[0]
            )
            copy.start()
            pending.append(copy)
        wait_copies([pltpu.make_async_copy(*pair, sems.at[index]) for index, pair in enumerate(late)])
        bounds = bounds_of(lengths_ref, lengths_ref.shape[1])
        block = rows // 8
        for index in range(8):
            span = slice(index * block, (index + 1) * block)
            middle = mid_ref[span, :]
            scale = lax.rsqrt(jnp.mean(middle * middle, -1, keepdims=True) + epsilon)
            normed = middle * scale
            scaled = total_ref[span, :] * gain_ref[...].astype(F32)
            centre = jnp.mean(scaled * normed, -1, keepdims=True)
            segment = segment_of(lax.broadcasted_iota(jnp.int32, (block, 128), 0) + index * block, bounds)
            segment = jnp.concatenate([segment] * (width // 128), 1)
            grad_rows = jnp.zeros((block, width), F32)
            for passage in range(8):
                grad_rows = jnp.where(segment == passage, grows_ref[passage : passage + 1, :], grad_rows)
            total_ref[span, :] = grad_rows + scale * (scaled - normed * centre)
        copy = pltpu.make_async_copy(total_ref, gmid_any, out_sems.at[2])
        copy.start()
        pending.append(copy)
        columns = width // 2
        for side in range(2):
            grad = dot_tn(mixed_ref[...], total_ref[:, side * columns : (side + 1) * columns].astype(BF16))
            if folded:
                span = slice(units + side * columns, units + (side + 1) * columns)
                for owner in range(owners):
                    grad_ref[owner, 0:lines, span] = grad[owner * lines : (owner + 1) * lines].astype(BF16)
            else:
                grad_refs[1][:, side * columns : (side + 1) * columns] = grad.astype(BF16)
        if folded:
            rest = pl.ds(units, width)
            copy = pltpu.make_async_copy(grad_ref.at[:, :, rest], grad_any.at[:, :, rest], out_sems.at[1])
            copy.start()
            pending.append(copy)
        for index in range(4):
            span = slice(index * 2 * block, (index + 1) * 2 * block)
            low_rows = total_ref[span, :].astype(BF16)
            gmix_ref[span, :] = (dot_nt(low_rows, wo_ref[...]) * inv_ref[span, :]).astype(BF16)
        wait_copies(pending)


def back(lengths, place, glow, grows, gain, hidden, active_sum, wu, slope, wi, middle, mixed, inv, heads, folded):
    rows, width = hidden.shape
    units = slope.shape[1]
    full = pl.BlockSpec((rows, width), lambda i: (0, 0))
    if folded:
        slab = (8, width // 8 + 8, units + width)
        grad_shape = [pltpu.HBM(slab, BF16)]
        grad_specs = [anywhere]
        grad_scratch = [pltpu.VMEM(slab, BF16)]
    else:
        shapes = [(width, units), (width, width)]
        grad_shape = [jax.ShapeDtypeStruct(shape, BF16) for shape in shapes]
        grad_specs = [pl.BlockSpec(shape, lambda i: (0, 0)) for shape in shapes]
        grad_scratch = []
    return pl.pallas_call(
        back_kernel,
        grid=(units // CHUNK,),
        in_specs=[
            smem,
            smem,
            whole((16, width)),
            whole((8, width)),
            whole((1, width)),
            whole((rows, width)),
            whole(active_sum.shape),
            pl.BlockSpec((CHUNK, width), lambda i: (i, 0)),
            pl.BlockSpec((rows, CHUNK), lambda i: (0, i)),
            pl.BlockSpec((width, CHUNK), lambda i: (0, i)),
        ]
        + [anywhere] * 4,
        out_specs=[anywhere, full] + grad_specs,
        out_shape=[jax.ShapeDtypeStruct((rows, width), F32), jax.ShapeDtypeStruct((rows, width), BF16)] + grad_shape,
        scratch_shapes=grad_scratch
        + [
            pltpu.VMEM((width, CHUNK), F32),
            pltpu.VMEM((rows, width), F32),
            pltpu.VMEM((rows, 32), BF16),
            pltpu.VMEM((rows, width), F32),
            pltpu.VMEM((rows, width), BF16),
            pltpu.VMEM((rows, width), F32),
            pltpu.VMEM((width, width), BF16),
            pltpu.SemaphoreType.DMA((4,)),
            pltpu.SemaphoreType.DMA((5,)),
            pltpu.VMEM((rows, CHUNK), BF16),
        ],
        compiler_params=params(),
        cost_estimate=pl.CostEstimate(flops=5 * rows * width * units, bytes_accessed=40 * MIB, transcendentals=0),
        name="back",
    )(lengths, place, glow, grows, gain, hidden, active_sum, wu, slope, wi, middle, mixed, inv, heads)


def contrast_back_kernel(
    lengths_ref, place_ref, own_ref, got_ref, target_ref, wp_any, gain_ref, hid_ref, active_ref, wu_ref, slope_ref, wi_ref,
    mid_any, mixed_any, inv_any, heads_any, loss_ref, grad_wp_ref, glow_all_ref, gmid_any, gmix_ref, grad_any, *refs,
):
    back_refs, (grows_ref, glow_ref, *contrast_refs) = refs[:11], refs[11:]

    @pl.when(pl.program_id(0) == 0)
    def _():
        contrast_kernel(
            place_ref, own_ref, got_ref, target_ref, wp_any,
            loss_ref, grad_wp_ref, glow_all_ref, grows_ref, glow_ref, *contrast_refs,
        )

    back_kernel(
        lengths_ref, place_ref, glow_ref, grows_ref, gain_ref, hid_ref, active_ref, wu_ref, slope_ref, wi_ref,
        mid_any, mixed_any, inv_any, heads_any, gmid_any, gmix_ref, grad_any, *back_refs,
    )


def contrast_back(
    lengths, place, own, got, targets, wp, gain, hidden, active_sum, wu, slope, wi, middle, mixed, inv, heads, share
):
    rows, width = hidden.shape
    units = slope.shape[1]
    count = targets.shape[1]
    slab = (8, width // 8 + 8, units + width)
    fixed = lambda shape: pl.BlockSpec(shape, lambda i: (0,) * len(shape))
    return pl.pallas_call(
        contrast_back_kernel,
        grid=(units // CHUNK,),
        in_specs=[smem, smem, whole(own.shape), whole(got.shape), whole(targets.shape), in_hbm]
        + [whole((1, width)), whole((rows, width)), whole(active_sum.shape)]
        + [
            pl.BlockSpec((CHUNK, width), lambda i: (i, 0)),
            pl.BlockSpec((rows, CHUNK), lambda i: (0, i)),
            pl.BlockSpec((width, CHUNK), lambda i: (0, i)),
        ]
        + [anywhere] * 4,
        out_specs=[fixed((8, 128)), fixed((share, width)), fixed((count, width)), anywhere, fixed((rows, width)), anywhere],
        out_shape=[
            jax.ShapeDtypeStruct((8, 128), F32),
            jax.ShapeDtypeStruct((share, width), F32),
            jax.ShapeDtypeStruct((count, width), BF16),
            jax.ShapeDtypeStruct((rows, width), F32),
            jax.ShapeDtypeStruct((rows, width), BF16),
            pltpu.HBM(slab, BF16),
        ],
        scratch_shapes=[
            pltpu.VMEM(slab, BF16),
            pltpu.VMEM((width, CHUNK), F32),
            pltpu.VMEM((rows, width), F32),
            pltpu.VMEM((rows, 32), BF16),
            pltpu.VMEM((rows, width), F32),
            pltpu.VMEM((rows, width), BF16),
            pltpu.VMEM((rows, width), F32),
            pltpu.VMEM((width, width), BF16),
            pltpu.SemaphoreType.DMA((4,)),
            pltpu.SemaphoreType.DMA((5,)),
            pltpu.VMEM((rows, CHUNK), BF16),
            pltpu.VMEM((8, width), F32),
            pltpu.VMEM((16, width), BF16),
            pltpu.VMEM((count, width), F32),
            pltpu.VMEM((count, 128), F32),
            pltpu.VMEM((width, width), F32),
            pltpu.VMEM((width, width), BF16),
            pltpu.VMEM((count, 512), F32),
            pltpu.VMEM((count, 512), F32),
            pltpu.SemaphoreType.DMA((1,)),
        ],
        compiler_params=params(),
        cost_estimate=pl.CostEstimate(flops=5 * rows * width * units, bytes_accessed=40 * MIB, transcendentals=0),
        name="contrast_back",
    )(lengths, place, own, got, targets, wp, gain, hidden, active_sum, wu, slope, wi, middle, mixed, inv, heads)


def attend_grad_kernel(first_pair, lengths_ref, q_ref, k_ref, v_ref, gm_ref, mixed_ref, p_any, *refs):
    grad_ref, diag_ref, qm_ref, km_ref, vx_ref, gx_ref, go_ref, ak_ref, av_ref, acc_ref, p_ref, sems = refs[-12:]
    together = q_ref.shape[1] // BLOCK
    rows = q_ref.shape[0]
    first_head = 2 * (first_pair + together * pl.program_id(0))

    def in_copy(block_index):
        slot = block_index % SLOTS
        source = p_any.at[pl.ds(first_head, 2 * together), pl.ds(pl.multiple_of(block_index * BLOCK, BLOCK), BLOCK), :]
        return pltpu.make_async_copy(source, p_ref.at[slot], sems.at[slot])

    for block_index in range(SLOTS - 1):
        in_copy(block_index).start()
    bounds = bounds_of(lengths_ref, lengths_ref.shape[1])
    reach = WINDOW + BLOCK
    acc_ref[...] = jnp.zeros_like(acc_ref)
    ak_ref[...] = jnp.zeros_like(ak_ref)
    av_ref[...] = jnp.zeros_like(av_ref)

    lane = lax.broadcasted_iota(jnp.int32, (BLOCK, BLOCK), 1)
    row = lax.broadcasted_iota(jnp.int32, (BLOCK, BLOCK), 0)
    across = jnp.where((row < HEAD_DIM) != (lane < HEAD_DIM), -1.0, 0.0).astype(BF16)

    def prepare(index, carry):
        span = pl.ds(pl.multiple_of(index * BLOCK, BLOCK), BLOCK)
        for near in range(together):
            lanes = slice(near * BLOCK, near * BLOCK + BLOCK)
            q, k, v, g = q_ref[span, lanes], k_ref[span, lanes], v_ref[span, lanes], gm_ref[span, lanes]
            product = split_two(g.astype(F32) * mixed_ref[span, lanes].astype(F32))
            centre = dot_nn(product[0], across) + dot_nn(product[1], across)
            high, low = split_two(centre)
            first = (lane == 0) | (lane == HEAD_DIM)
            second = (lane == 1) | (lane == HEAD_DIM + 1)
            zero = jnp.zeros_like(q)
            extra = jnp.where(first, high, jnp.where(second, low, zero))
            one = jnp.ones_like(v)
            for half in range(2):
                head = 2 * near + half
                mine = (lane < HEAD_DIM) if half == 0 else (lane >= HEAD_DIM)
                qm_ref[head, span, :] = jnp.where(mine, q, zero)
                km_ref[head, span, :] = jnp.where(mine, k, zero)
                go_ref[head, span, :] = jnp.where(mine, g, zero)
                vx_ref[head, span, :] = jnp.where(mine, v, one)
                gx_ref[head, span, :] = jnp.where(mine, g, extra)
        return carry

    lax.fori_loop(0, rows // BLOCK, prepare, 0)

    def one(block_index, carry):
        slot = block_index % SLOTS
        start = pl.multiple_of(block_index * BLOCK, BLOCK)
        in_copy(block_index).wait()

        @pl.when(block_index + SLOTS - 1 < rows // BLOCK)
        def _():
            in_copy(block_index + SLOTS - 1).start()

        first, count = window_of(bounds, start)
        first = pl.multiple_of(first, BLOCK)
        shift = pl.multiple_of(first - start + SPAN, BLOCK)

        def body(blocks):
            size = blocks * BLOCK
            queries = pl.ds(start, BLOCK)
            keys = pl.ds(first, size)
            spread = [dot_nt(gx_ref[head, queries, :], vx_ref[head, keys, :]) for head in range(2 * together)]
            for near in range(together):
                heads = (2 * near, 2 * near + 1)
                lanes = slice(near * BLOCK, near * BLOCK + BLOCK)
                parts = []
                raised = []
                for head in heads:
                    p = p_ref[slot, head, :, 0:size]
                    grad_scores = p.astype(F32) * spread[head]
                    acc_ref[head, :, pl.ds(shift, size)] += grad_scores
                    parts.append(grad_scores.astype(BF16))
                    raised.append(p)
                q_both = jnp.concatenate([qm_ref[head, queries, :] for head in heads], 0)
                g_both = jnp.concatenate([go_ref[head, queries, :] for head in heads], 0)
                k_both = jnp.concatenate([km_ref[head, keys, :] for head in heads], 0)
                ak_ref[lanes, keys] += dot_tn(q_both, jnp.concatenate(parts, 0))
                av_ref[lanes, keys] += dot_tn(g_both, jnp.concatenate(raised, 0))
                grad_ref[0, queries, lanes] = dot_nn(jnp.concatenate(parts, 1), k_both).astype(BF16)

        for blocks in range(1, WINDOW // BLOCK + 1):
            pl.when(count == blocks)(functools.partial(body, blocks))
        return carry

    lax.fori_loop(0, rows // BLOCK, one, 0)
    for near in range(together):
        lanes = slice(near * BLOCK, near * BLOCK + BLOCK)
        grad_ref[1, :, lanes] = jnp.transpose(ak_ref[lanes, :]).astype(BF16)
        grad_ref[2, :, lanes] = jnp.transpose(av_ref[lanes, :]).astype(BF16)
    for head in range(2 * together):
        padded = jnp.concatenate([jnp.zeros((BLOCK, BLOCK), F32), acc_ref[head]], 1)
        group = padded[0:8]
        for index in range(1, BLOCK // 8):
            group = group + pltpu.roll(padded[8 * index : 8 * index + 8], reach - 8 * index, 1)
        line = group[0:1]
        for index in range(1, 8):
            line = line + pltpu.roll(group, reach - index, 1)[index : index + 1]
        diag_ref[head // 2, head % 2 : head % 2 + 1, :] = line


def attend_grad(lengths, q, k, v, gm, mixed, p, first_pair, pairs, before=()):
    rows, width = q.shape
    together = max(size for size in (1, 2, 3) if pairs % size == 0 and first_pair % size == 0)
    at = first_pair // together
    column = pl.BlockSpec((rows, BLOCK * together), lambda i: (0, at + i))
    return pl.pallas_call(
        functools.partial(attend_grad_kernel, first_pair),
        grid=(pairs // together,),
        in_specs=[smem]
        + [column] * 5
        + [in_hbm]
        + [anywhere] * len(before),
        out_specs=[
            pl.BlockSpec((3, rows, BLOCK * together), lambda i: (0, 0, at + i)),
            pl.BlockSpec((together, 2, WINDOW + BLOCK), lambda i: (at + i, 0, 0)),
        ],
        out_shape=[
            jax.ShapeDtypeStruct((3, rows, width), BF16),
            jax.ShapeDtypeStruct((HEADS // 2, 2, WINDOW + BLOCK), F32),
        ],
        scratch_shapes=[pltpu.VMEM((2 * together, rows, BLOCK), BF16)] * 5
        + [pltpu.VMEM((BLOCK * together, rows), F32)] * 2
        + [
            pltpu.VMEM((2 * together, BLOCK, WINDOW), F32),
            pltpu.VMEM((SLOTS, 2 * together, BLOCK, WINDOW), BF16),
            pltpu.SemaphoreType.DMA((SLOTS,)),
        ],
        input_output_aliases={7 + index: index for index in range(len(before))},
        compiler_params=params(),
        cost_estimate=pl.CostEstimate(
            flops=pairs * 20 * rows * 512 * 64, bytes_accessed=pairs * 5 * MIB, transcendentals=0
        ),
        name="attend_grad",
    )(lengths, q, k, v, gm, mixed, p, *before)


def head_grad_kernel(place_ref, hid_any, grad_any, table_ref, keep_ref, send_ref, hid_ref, grad_ref, result_ref, sems):
    block = result_ref.shape[2]
    pairs = [(hid_any, hid_ref)]
    for matrix in range(3):
        for side in range(2):
            columns = pl.ds(side * block, block)
            pairs.append((grad_any.at[matrix, :, columns], grad_ref.at[matrix, :, columns]))
    pending = start_copies(pairs, sems)
    rows = keep_ref.shape[2]
    for far in range(4):
        for ref, other in ((keep_ref, 0), (send_ref, 1)):
            line = table_ref[pl.ds(owner_of(place_ref, far, other), 1), :]
            block_of = jnp.broadcast_to(line, (rows, 128)).astype(BF16)
            for quarter in range(4):
                ref[quarter, far, :, 3 * block :] = block_of
    pending[0].wait()
    for step in range(6):
        pending[1 + step].wait()
        columns = slice(step % 2 * block, step % 2 * block + block)
        result_ref[step % 2] = dot_tn(hid_ref[...], grad_ref[step // 2, :, columns])
        fold(result_ref.at[step % 2], keep_ref, send_ref, place_ref, step // 3, step % 3 * block)


def head_grad(place, hidden, grads, table):
    rows, width = hidden.shape
    block = width // 2
    slab = (4, 4, width // 16, 3 * block + 128)
    return pl.pallas_call(
        head_grad_kernel,
        in_specs=[smem, in_hbm, in_hbm, in_vmem],
        out_specs=[in_vmem] * 2,
        out_shape=[jax.ShapeDtypeStruct(slab, BF16)] * 2,
        scratch_shapes=[
            pltpu.VMEM((rows, width), BF16),
            pltpu.VMEM((3, rows, width), BF16),
            pltpu.VMEM((2, width, block), F32),
            pltpu.SemaphoreType.DMA((7,)),
        ],
        compiler_params=pltpu.CompilerParams(vmem_limit_bytes=28 * MIB),
        cost_estimate=pl.CostEstimate(flops=6 * rows * width * width, bytes_accessed=12 * MIB, transcendentals=0),
        name="head_grad",
    )(place, hidden, grads, table)


def token_grad_kernel(x_ref, gain_ref, gmid_ref, grad_ref, w_ref, out_ref):
    x = x_ref[...].astype(F32)
    scale = lax.rsqrt(jnp.mean(x * x, -1, keepdims=True) + epsilon)
    normed = x * scale
    grad_hidden = dot_nt(grad_ref[0], w_ref[0]) + dot_nt(grad_ref[1], w_ref[1]) + dot_nt(grad_ref[2], w_ref[2])
    scaled = grad_hidden * gain_ref[...].astype(F32)
    centre = jnp.mean(scaled * normed, -1, keepdims=True)
    out_ref[...] = gmid_ref[...] + scale * (scaled - normed * centre)


def token_grad(x, gain, gmid, grads, weights):
    rows, width = x.shape
    block = rows // 4
    row_spec = pl.BlockSpec((block, width), lambda i: (i, 0))
    return pl.pallas_call(
        token_grad_kernel,
        grid=(4,),
        in_specs=[
            row_spec,
            whole((1, width)),
            row_spec,
            pl.BlockSpec((3, block, width), lambda i: (0, i, 0)),
            whole((3, width, width)),
        ],
        out_specs=row_spec,
        out_shape=jax.ShapeDtypeStruct((rows, width), F32),
        compiler_params=params(),
        cost_estimate=pl.CostEstimate(flops=6 * rows * width * width, bytes_accessed=16 * MIB, transcendentals=0),
        name="token_grad",
    )(x, gain, gmid, grads, weights)


def outer_grad_kernel(place_ref, pieces_ref, glow_ref, out_ref, active_ref):
    units = active_ref.shape[1]
    for near in range(4):
        start = pl.multiple_of((place_ref[2] ^ near) * 64, 64)
        for owner in range(8):
            half = 8 * (owner // 4)
            column = owner % 4 * units
            block = pieces_ref[near].astype(F32)[half : half + 8, column : column + units]
            active_ref[pl.ds(start + 8 * owner, 8), :] = block
    out_ref[...] = dot_tn(active_ref[...].astype(BF16), glow_ref[...])


def outer_grad(place, pieces, glow):
    count, width = glow.shape
    units = pieces.shape[2] // 4
    return pl.pallas_call(
        outer_grad_kernel,
        grid=(1,),
        in_specs=[smem, whole(pieces.shape), whole(glow.shape)],
        out_specs=pl.BlockSpec((units, width), lambda i: (0, 0)),
        out_shape=jax.ShapeDtypeStruct((units, width), F32),
        scratch_shapes=[pltpu.VMEM((count, units), F32)],
        compiler_params=params(),
        cost_estimate=pl.CostEstimate(flops=2 * count * units * width, bytes_accessed=3 * MIB, transcendentals=0),
        name="outer_grad",
    )(place, pieces, glow)


def table_grad(diag):
    reach = WINDOW + BLOCK
    offsets = jnp.arange(reach, dtype=jnp.int32) - (SPAN + BLOCK)
    onehot = (bucket_of(offsets)[:, None] == jnp.arange(BUCKETS, dtype=jnp.int32)[None, :]).astype(F32)
    sums = jnp.dot(diag.reshape(HEADS, reach), onehot, precision=lax.Precision.HIGHEST)
    return sums.T.reshape(BUCKETS * HEADS)


def exchange(value, narrow=0, plane=0, core=0):
    bits = narrow * 8 + plane * 2 + core
    return lax.ppermute(value, ("narrow", "wide"), [(i, i ^ bits) for i in range(32)])


def spread(value):
    return [value] + [exchange(value, narrow=near) for near in range(1, 4)]


def sum_core_kernel(keep_ref, got_ref, *out_refs):
    for quarter, out_ref in enumerate(out_refs):
        for far in range(4):
            out_ref[far] = (keep_ref[quarter, far].astype(F32) + got_ref[quarter, far].astype(F32)).astype(BF16)


def sum_core(keep, got):
    _, _, rows, columns = keep.shape
    return pl.pallas_call(
        sum_core_kernel,
        in_specs=[in_vmem] * 2,
        out_specs=[in_vmem] * 4,
        out_shape=[jax.ShapeDtypeStruct((4, rows, columns), BF16)] * 4,
        compiler_params=small,
        cost_estimate=pl.CostEstimate(flops=0, bytes_accessed=96 * rows * columns, transcendentals=0),
        name="sum_core",
    )(keep, got)


def sum_narrow_kernel(apart, a_ref, b_ref, c_ref, d_ref, *out_refs):
    refs = (a_ref, b_ref, c_ref, d_ref)
    columns = a_ref.shape[2] - (128 if apart else 0)
    for far, out_ref in enumerate(out_refs):
        total = sum(ref[far, :, :columns].astype(F32) for ref in refs)
        out_ref[:, :columns] = total.astype(BF16)
        if apart:
            for near, ref in enumerate(refs):
                out_ref[:, columns + 128 * near : columns + 128 * near + 128] = ref[far, :, columns:]


def sum_narrow(parts, apart):
    _, rows, columns = parts[0].shape
    columns += 3 * 128 if apart else 0
    return pl.pallas_call(
        functools.partial(sum_narrow_kernel, apart),
        in_specs=[in_vmem] * 4,
        out_specs=[in_vmem] * 4,
        out_shape=[jax.ShapeDtypeStruct((rows, columns), BF16)] * 4,
        compiler_params=small,
        cost_estimate=pl.CostEstimate(flops=0, bytes_accessed=40 * rows * columns, transcendentals=0),
        name="sum_narrow",
    )(*parts)


def sum_planes_kernel(a_ref, b_ref, c_ref, d_ref, total_ref, *apart_refs):
    refs = (a_ref, b_ref, c_ref, d_ref)
    columns = total_ref.shape[1]
    total_ref[...] = sum(ref[:, :columns].astype(F32) for ref in refs).astype(BF16)
    for apart_ref in apart_refs:
        for far, ref in enumerate(refs):
            apart_ref[far] = ref[:, columns:]


def sum_planes(parts, apart):
    rows, columns = parts[0].shape
    kept = 4 * 128 if apart else 0
    out_shape = [jax.ShapeDtypeStruct((rows, columns - kept), BF16)]
    if apart:
        out_shape.append(jax.ShapeDtypeStruct((4, rows, kept), BF16))
    return pl.pallas_call(
        sum_planes_kernel,
        in_specs=[in_vmem] * 4,
        out_specs=[in_vmem] * len(out_shape),
        out_shape=out_shape,
        compiler_params=small,
        cost_estimate=pl.CostEstimate(flops=0, bytes_accessed=10 * rows * columns, transcendentals=0),
        name="sum_planes",
    )(*parts)


def cut_kernel(place_ref, part_ref, *out_refs):
    rows, columns = out_refs[0].shape
    rows = rows - 16
    total = part_ref.shape[1]
    units = total * 4 // 5
    for near, out_ref in enumerate(out_refs):
        quarter = place_ref[2] ^ near
        row = pl.ds(pl.multiple_of((quarter % 2) * rows, 16), rows)
        column = pl.multiple_of((quarter // 2) * (units // 2), 128)
        out_ref[0:rows, 0 : units // 2] = part_ref[row, pl.ds(column, units // 2)]
        column = pl.multiple_of(units + (quarter // 2) * (columns - units // 2), 128)
        out_ref[0:rows, units // 2 :] = part_ref[row, pl.ds(column, columns - units // 2)]
        sums = part_ref[2 * rows :, 0:units].astype(F32)
        sums = jnp.concatenate([sums[:, : units // 2], sums[:, units // 2 :]], 0)
        out_ref[rows:, 0 : units // 2] = sums.astype(BF16)
        out_ref[rows:, units // 2 :] = jnp.zeros((16, columns - units // 2), BF16)


def cut(place, part):
    rows, total = part.shape
    shape = ((rows - 8) // 2 + 16, total // 2)
    return pl.pallas_call(
        cut_kernel,
        in_specs=[smem, in_vmem],
        out_specs=[in_vmem] * 4,
        out_shape=[jax.ShapeDtypeStruct(shape, BF16)] * 4,
        compiler_params=small,
        cost_estimate=pl.CostEstimate(flops=0, bytes_accessed=2 * MIB, transcendentals=0),
        name="cut",
    )(place, part)


def sum_quarter_kernel(a_ref, b_ref, c_ref, d_ref, total_ref, apart_ref):
    refs = (a_ref, b_ref, c_ref, d_ref)
    rows = total_ref.shape[0]
    total_ref[...] = sum(ref[0:rows, :].astype(F32) for ref in refs).astype(BF16)
    for near, ref in enumerate(refs):
        apart_ref[near] = ref[rows:, : apart_ref.shape[2]]


def sum_quarter(parts):
    rows, columns = parts[0].shape
    return pl.pallas_call(
        sum_quarter_kernel,
        in_specs=[in_vmem] * 4,
        out_specs=[in_vmem] * 2,
        out_shape=[
            jax.ShapeDtypeStruct((rows - 16, columns), BF16),
            jax.ShapeDtypeStruct((4, 16, columns * 4 // 5), BF16),
        ],
        compiler_params=small,
        cost_estimate=pl.CostEstimate(flops=0, bytes_accessed=2 * MIB, transcendentals=0),
        name="sum_quarter",
    )(*parts)


def as_row(column):
    return jnp.transpose(jnp.broadcast_to(column, (column.shape[0], 128)))[0:1]


def finish_inner_kernel(place_ref, weight_ref, gain_ref, a_ref, b_ref, c_ref, d_ref, out_ref, last_ref, ggain_ref):
    rows = a_ref.shape[0]
    units = weight_ref.shape[1] // 2
    width = last_ref.shape[1] // 2
    for near, ref in enumerate((a_ref, b_ref, c_ref, d_ref)):
        quarter = place_ref[2] ^ near
        row = pl.ds(pl.multiple_of((quarter % 2) * rows, rows), rows)
        half = quarter // 2
        out_ref[row, pl.ds(pl.multiple_of(half * units, 128), units)] = ref[:, :units].astype(F32)
        last_ref[row, pl.ds(pl.multiple_of(half * width, 128), width)] = ref[:, units:].astype(F32)
    along = jnp.sum(out_ref[...] * weight_ref[...].astype(F32), -1, keepdims=True)
    ggain_ref[...] = as_row(along) / gain_ref[...].astype(F32)


def finish_inner(place, weight, gain, parts, width):
    rows, units = weight.shape
    ins = [weight, gain] + list(parts)
    outs = [jax.ShapeDtypeStruct(shape, F32) for shape in ((rows, units), (rows, width), (1, rows))]
    return pl.pallas_call(
        finish_inner_kernel,
        in_specs=[smem] + [in_vmem] * len(ins),
        out_specs=[in_vmem] * len(outs),
        out_shape=outs,
        compiler_params=small,
        cost_estimate=pl.CostEstimate(flops=0, bytes_accessed=3 * MIB, transcendentals=0),
        name="finish_inner",
    )(place, *ins)


def finish_heads_kernel(place_ref, wq_ref, wk_ref, wv_ref, gain_ref, a_ref, b_ref, c_ref, d_ref, *refs):
    *out_refs, table_ref, ggain_ref, result_ref = refs
    rows = a_ref.shape[0]
    width = wq_ref.shape[1]
    half = 3 * width // 2
    for near, ref in enumerate((a_ref, b_ref, c_ref, d_ref)):
        quarter = place_ref[2] ^ near
        row = pl.multiple_of((quarter % 2) * rows, rows)
        column = pl.multiple_of((quarter // 2) * half, 128)
        result_ref[pl.ds(row, rows), pl.ds(column, half)] = ref[:, :half].astype(F32)

        @pl.when(quarter == 0)
        def _():
            table_ref[...] = ref[0:16, half:].astype(F32)[0:1, : table_ref.shape[1]]

    along = jnp.zeros((2 * rows, 1), F32)
    for index, (out_ref, weight_ref) in enumerate(zip(out_refs, (wq_ref, wk_ref, wv_ref))):
        grad = result_ref[:, index * width : (index + 1) * width]
        out_ref[...] = grad
        along = along + jnp.sum(grad * weight_ref[...].astype(F32), -1, keepdims=True)
    ggain_ref[...] = as_row(along) / gain_ref[...].astype(F32)


def finish_heads(place, weights, gain, parts, table_share):
    rows, width = weights[0].shape
    ins = list(weights) + [gain] + list(parts)
    outs = [jax.ShapeDtypeStruct((rows, width), F32)] * 3
    outs += [jax.ShapeDtypeStruct((1, table_share), F32), jax.ShapeDtypeStruct((1, rows), F32)]
    return pl.pallas_call(
        finish_heads_kernel,
        in_specs=[smem] + [in_vmem] * len(ins),
        out_specs=[in_vmem] * len(outs),
        out_shape=outs,
        scratch_shapes=[pltpu.VMEM((rows, 3 * width), F32)],
        compiler_params=small,
        cost_estimate=pl.CostEstimate(flops=0, bytes_accessed=3 * MIB, transcendentals=0),
        name="finish_heads",
    )(place, *ins)


def order_small_kernel(place_ref, own_ref, got_ref, out_ref):
    for other, ref in enumerate((own_ref, got_ref)):
        for far in range(4):
            out_ref[pl.ds(owner_of(place_ref, far, other), 1), :] = ref[far, 0:1, :]


def order_small(place, own, got):
    return pl.pallas_call(
        order_small_kernel,
        grid=(1,),
        in_specs=[smem, whole(own.shape), whole(got.shape)],
        out_specs=pl.BlockSpec((8, own.shape[2]), lambda i: (0, 0)),
        out_shape=jax.ShapeDtypeStruct((8, own.shape[2]), F32),
        name="order_small",
    )(place, own, got)


def gather_messages(message):
    far = jnp.stack([message] + [exchange(message, plane=distance) for distance in range(1, 4)])
    near = jnp.stack(spread(far))
    return near, exchange(near, core=1)


def tie(first, then):
    first, then = lax.optimization_barrier((first, then))
    return first, then


def gather_heads(place, own, small):
    rows, width = own[0].shape
    line = jnp.broadcast_to(jnp.pad(small, (0, width - small.shape[0])), (8, width))
    heads = jnp.stack([jnp.concatenate([weight, line]) for weight in own])
    quarter = lax.dynamic_index_in_dim(heads, place[2], 0, keepdims=False)
    far = jnp.stack([exchange(quarter, plane=distance) for distance in range(1, 4)])
    far, heads = tie(far, heads)
    near = spread(far)
    other = exchange(heads, core=1)
    far_other = exchange(far, core=1)
    lines = lambda first, rest: jnp.concatenate([first[:1, rows:, :256], rest[:, rows:, :256]]).astype(F32)
    ordered = order_small(place, lines(heads, far), lines(other, far_other))
    return near, [heads, other], far_other, ordered


def fetch_inner(narrow, inner_weight, width):
    quarter = lax.dynamic_slice_in_dim(inner_weight, narrow * width, width, 1)
    return [exchange(quarter, plane=far) for far in range(1, 4)]


def layer_specs():
    both = ("narrow", "wide")
    rows, matrix, vector = P(both, None), P("wide", None), P("wide")
    ins = (rows, vector, matrix, matrix, matrix, matrix, vector, vector, matrix, matrix, matrix, rows, P())
    outs = (rows, rows, rows, vector, matrix, matrix, matrix, matrix, vector, vector, matrix, matrix, matrix)
    return ins, outs


def local_permuted(tokens, *arguments):
    *weights_own, lengths, positives = arguments
    attention_gain, query_weight, key_weight, value_weight, output_weight = weights_own[:5]
    bias_table, forward_gain, inner_weight, outer_weight, project_weight = weights_own[5:]
    segs = lengths.shape[1]
    width = tokens.shape[1]
    units = inner_weight.shape[1]
    wide_at = lax.axis_index("wide")
    narrow_at = lax.axis_index("narrow")
    device = narrow_at * 8 + wide_at
    place = jnp.stack([device, wide_at, narrow_at, wide_at // 2, wide_at % 2]).astype(jnp.int32)
    share = attention_gain.shape[0]

    own_heads = (query_weight, key_weight, value_weight, output_weight)
    small = jnp.concatenate([attention_gain, forward_gain, bias_table])
    near, both_heads, far_other, small = gather_heads(place, own_heads, small)
    gain_one = small[:, :share].reshape(1, width)
    gain_two = small[:, share : 2 * share].reshape(1, width)
    table = small[:, 2 * share : 2 * share + bias_table.shape[0]].reshape(BUCKETS, HEADS)
    table = jnp.pad(table, ((0, 0), (0, 4))).astype(BF16)
    _, own_inner = tie(both_heads[1], inner_weight)
    _, own_outer = tie(far_other, outer_weight)
    wu = lax.all_gather(own_outer, "wide", axis=0, tiled=True)
    far = jnp.stack(fetch_inner(narrow_at, own_inner, width))
    (gain_one, gain_two, table), near = tie((gain_one, gain_two, table), near)
    near, far = tie(near, far)
    head_pieces = both_heads + near + [far_other] + [exchange(piece, core=1) for piece in near[1:]]
    near = spread(far)
    other_inner = exchange(own_inner, core=1)

    hid, q, k, v, weights = project(place, tokens, gain_one, head_pieces)
    q, own_last = tie(q, project_weight)
    wp = lax.all_gather(own_last, "wide", axis=0, tiled=True)
    mixed, inv, p = attend(lengths, table, q, k, v, 0, 6)
    mixed, inv, p, near = lax.optimization_barrier((mixed, inv, p, near))
    near_other = [exchange(piece, core=1) for piece in near]
    hidden, slope, active_sum, message, middle, hid_two, wi = forward(
        place, lengths, tokens, mixed, gain_two, weights, wu, units, [own_inner, other_inner] + near + near_other
    )
    loss, grad_wp, glow_all, gmid, gm, grads_out = contrast_back(
        lengths, place, *gather_messages(message), positives[None], wp, gain_two, hid_two, active_sum, wu, slope, wi,
        middle, mixed, inv, weights, project_weight.shape[0],
    )

    part = lax.psum_scatter(grads_out.reshape(-1, units + width), "wide", scatter_dimension=0, tiled=True)
    grad_heads, diag = attend_grad(lengths, q, k, v, gm, mixed, p, 0, 6)
    grad_table = table_grad(diag).reshape(8, -1)
    rows_table = jnp.pad(grad_table, ((0, 0), (0, 128 - grad_table.shape[1])))
    keep, send = head_grad(place, hid, grad_heads, rows_table)
    got = exchange(send, core=1)
    quarters = sum_core(keep, got)
    quarters, gmid = tie(quarters, gmid)
    arrived = [quarters[0]] + [exchange(quarters[near], narrow=near) for near in range(1, 4)]
    grad_tokens = token_grad(tokens, gain_one, gmid, grad_heads, weights)
    grad_tokens, part = tie(grad_tokens, part)
    pieces = cut(place, part)
    pieces = [pieces[0]] + [exchange(pieces[near], narrow=near) for near in range(1, 4)]
    planes = sum_narrow(arrived, False)
    arrived = [planes[0]] + [exchange(planes[far], plane=far) for far in range(1, 4)]
    total, active_pieces = sum_quarter(pieces)
    inner_parts = spread(total)
    grad_outer = outer_grad(place, active_pieces, glow_all)
    grad_outer, arrived = tie(grad_outer, arrived)
    (total,) = sum_planes(arrived, False)
    last_parts = spread(total)
    grad_inner, grad_out, gain_two_grad = finish_inner(place, inner_weight, forward_gain[None], inner_parts, width)
    *grads, table_own, gain_one_grad = finish_heads(
        place, own_heads[:3], attention_gain[None], last_parts, bias_table.shape[0]
    )
    grads.append(grad_out)
    return (
        hidden,
        grad_tokens,
        loss[:, 0].reshape(1, segs),
        gain_one_grad[0],
        *grads,
        table_own[0],
        gain_two_grad[0],
        grad_inner,
        grad_outer,
        grad_wp,
    )


def local_plain(tokens, *arguments):
    *weights_own, lengths, positives = arguments
    attention_gain, query_weight, key_weight, value_weight, output_weight = weights_own[:5]
    bias_table, forward_gain, inner_weight, outer_weight, project_weight = weights_own[5:]
    both = ("narrow", "wide")
    segs = lengths.shape[1]
    width = tokens.shape[1]
    wide_at = lax.axis_index("wide")
    device = lax.axis_index("narrow") * lax.axis_size("wide") + wide_at
    place = jnp.stack([device, wide_at]).astype(jnp.int32)
    share = attention_gain.shape[0]
    gather = lambda a: lax.all_gather(a, "wide", axis=0, tiled=True)
    small = gather(jnp.concatenate([attention_gain, forward_gain, bias_table])[None])
    gain_one = small[:, :share].reshape(1, width)
    gain_two = small[:, share : 2 * share].reshape(1, width)
    table = jnp.pad(small[:, 2 * share :].reshape(BUCKETS, HEADS), ((0, 0), (0, 4)))
    weights = jnp.stack([gather(w) for w in (query_weight, key_weight, value_weight, output_weight)])
    wu = gather(outer_weight)
    hid, q, k, v, weights = project(place, tokens, gain_one, [weights])
    mixed, inv, p = attend(lengths, table, q, k, v, 0, HEADS // 2)
    hidden, slope, active_sum, message, middle, hid_two, wi = forward(
        place, lengths, tokens, mixed, gain_two, weights, wu, inner_weight.shape[1], [gather(inner_weight)]
    )
    messages = lax.all_gather(message, both, axis=0, tiled=True).reshape(-1, 2, 8, 512)
    messages = messages.transpose(0, 2, 1, 3).reshape(-1, 1024)
    loss, grad_wp, glow_all, grows = contrast_plain(
        place,
        messages[:, :width],
        messages[:, width : width + 1].astype(F32),
        positives.reshape(-1, 1),
        gather(project_weight),
        project_weight.shape[0],
    )
    active_all = lax.all_gather(active_sum[:segs], both, axis=0, tiled=True)
    active_own = lax.dynamic_slice_in_dim(active_all, wide_at * outer_weight.shape[0], outer_weight.shape[0], 1)
    grad_outer = dot_tn(active_own, glow_all.astype(F32))
    glow = jnp.pad(grows.astype(BF16), ((0, 16 - segs), (0, 0)))
    gmid, gm, grad_wi, grad_wo = back(
        lengths, place, glow, grows, gain_two, hid_two, active_sum, wu, slope, wi, middle, mixed, inv, weights, False
    )
    grad_heads, diag = attend_grad(lengths, q, k, v, gm, mixed, p, 0, HEADS // 2)
    grad_tokens = token_grad(tokens, gain_one, gmid, grad_heads, weights)

    def total(grad):
        part = lax.psum_scatter(grad, "wide", scatter_dimension=0, tiled=True)
        return lax.psum(part.astype(F32), "narrow")

    grads = [total(dot_tn(hid, grad).astype(BF16)) for grad in grad_heads] + [total(grad_wo)]
    grad_inner = total(grad_wi)
    table_own = total(table_grad(diag).reshape(lax.axis_size("wide"), -1))[0]
    own_heads = jnp.stack([query_weight, key_weight, value_weight])
    along = jnp.sum(jnp.stack(grads[:3]) * own_heads.astype(F32), (0, 2))
    return (
        hidden,
        grad_tokens,
        loss[:, 0].reshape(1, segs),
        along / attention_gain.astype(F32),
        *grads,
        table_own,
        jnp.sum(grad_inner * inner_weight.astype(F32), 1) / forward_gain.astype(F32),
        grad_inner,
        grad_outer,
        grad_wp,
    )


def solution(mesh):
    ins, outs = layer_specs()
    permuted = (mesh.shape["narrow"], mesh.shape["wide"]) == (4, 8)
    body = local_permuted if permuted else local_plain
    return jax.shard_map(body, mesh=mesh, in_specs=ins, out_specs=outs, check_vma=False)
```

```python
import functools

import jax
import jax.numpy as jnp
from jax import lax
from jax.experimental import pallas as pl
from jax.experimental.pallas import tpu as pltpu
from jax.sharding import PartitionSpec as P

HEADS = 12
HEAD_DIM = 64
BUCKETS = 32
SPAN = 256
BLOCK = 128
WINDOW = BLOCK + 2 * SPAN
SLOTS = 3
CHUNK = 1024

epsilon = 1e-06
logit_scale = 50.0
root_half = 0.7071067811865476
inv_root_tau = 0.3989422804014327
MIB = 1 << 20
F32 = jnp.float32
BF16 = jnp.bfloat16


def dot_nn(left, right):
    return lax.dot_general(left, right, (((1,), (0,)), ((), ())), preferred_element_type=F32)


def dot_nt(left, right):
    return lax.dot_general(left, right, (((1,), (1,)), ((), ())), preferred_element_type=F32)


def dot_tn(left, right):
    return lax.dot_general(left, right, (((0,), (0,)), ((), ())), preferred_element_type=F32)


def split(values):
    high = values.astype(BF16)
    rest = values - high.astype(F32)
    middle = rest.astype(BF16)
    return high, middle, (rest - middle.astype(F32)).astype(BF16)


def split_two(values):
    high = values.astype(BF16)
    return high, (values - high.astype(F32)).astype(BF16)


def bucket_of(offset):
    distance = jnp.abs(offset)
    larger = jnp.full_like(distance, 8)
    for step in range(1, 8):
        larger = larger + (distance * distance >= 64 * 2**step).astype(jnp.int32)
    return jnp.where(distance < 8, distance, larger) + jnp.where(offset > 0, 16, 0)


def bounds_of(lengths_ref, count):
    bounds = []
    total = 0
    for index in range(count):
        total = total + lengths_ref[0, index]
        bounds.append(total)
    return bounds


def segment_of(places, bounds):
    segment = jnp.zeros_like(places)
    for bound in bounds:
        segment = segment + (places >= bound).astype(jnp.int32)
    return segment


def window_of(bounds, start):
    low = 0
    high = bounds[-1]
    for bound in bounds[:-1]:
        low = jnp.where(bound <= start, bound, low)
    for bound in reversed(bounds[:-1]):
        high = jnp.where(bound > start + BLOCK - 1, bound, high)
    first = (low // BLOCK) * BLOCK
    blocks = (high - first + BLOCK - 1) // BLOCK
    return first, blocks


def params(mib=60, grid=1):
    return pltpu.CompilerParams(vmem_limit_bytes=mib * MIB, dimension_semantics=("arbitrary",) * grid)


def whole(shape):
    return pl.BlockSpec(shape, lambda *_: (0,) * len(shape), pipeline_mode=pl.Buffered(1))


smem = pl.BlockSpec(memory_space=pltpu.SMEM)
anywhere = pl.BlockSpec(memory_space=pl.ANY)
in_hbm = pl.BlockSpec(memory_space=pltpu.HBM)
in_vmem = pl.BlockSpec(memory_space=pltpu.VMEM)
small = pltpu.CompilerParams(vmem_limit_bytes=12 * MIB)


def owner_of(place_ref, far, other):
    return 2 * (place_ref[3] ^ far) + (place_ref[4] ^ other)


def start_copies(pairs, sems, first=0):
    pending = [pltpu.make_async_copy(source, target, sems.at[first + at]) for at, (source, target) in enumerate(pairs)]
    for copy in pending:
        copy.start()
    return pending


def wait_copies(pending):
    for copy in pending:
        copy.wait()


def head_copies(place_ref, refs, whole_ref):
    rows = whole_ref.shape[1] // 8
    mine = pl.ds(0, rows)
    for other in range(2):
        start = pl.multiple_of(owner_of(place_ref, 0, other) * rows, 16)
        yield refs[other].at[:, mine, :], whole_ref.at[:, pl.ds(start, rows), :]
        for near in range(4):
            piece = refs[2 + 4 * other + near]
            for far in range(1, 4):
                start = pl.multiple_of(owner_of(place_ref, far, other) * rows, 16)
                yield piece.at[far - 1, mine, :], whole_ref.at[place_ref[2] ^ near, pl.ds(start, rows), :]


def project_kernel(place_ref, x_ref, gain_ref, *refs):
    *pieces, hid_ref, q_ref, k_ref, v_ref, out_ref, w_ref, sems, out_sem = refs
    step = pl.program_id(0)
    if len(pieces) == 1:
        pairs = [(pieces[0], w_ref)]
    else:
        pairs = list(head_copies(place_ref, pieces, w_ref))
    whole_copy = pltpu.make_async_copy(w_ref, out_ref, out_sem)

    @pl.when(step == 0)
    def _():
        start_copies(pairs, sems)

    x = x_ref[...].astype(F32)
    scale = lax.rsqrt(jnp.mean(x * x, -1, keepdims=True) + epsilon)
    hidden = (x * scale * gain_ref[...].astype(F32)).astype(BF16)
    hid_ref[...] = hidden

    @pl.when(step == 0)
    def _():
        wait_copies([pltpu.make_async_copy(*pair, sems.at[index]) for index, pair in enumerate(pairs)])
        whole_copy.start()

    q_ref[...] = dot_nn(hidden, w_ref[0]).astype(BF16)
    k_ref[...] = dot_nn(hidden, w_ref[1]).astype(BF16)
    v_ref[...] = dot_nn(hidden, w_ref[2]).astype(BF16)

    @pl.when(step == pl.num_programs(0) - 1)
    def _():
        whole_copy.wait()


def project(place, x, gain, pieces):
    rows, width = x.shape
    block = rows // 4
    row_spec = pl.BlockSpec((block, width), lambda i: (i, 0))
    out = jax.ShapeDtypeStruct((rows, width), BF16)
    return pl.pallas_call(
        project_kernel,
        grid=(4,),
        in_specs=[smem, row_spec, whole((1, width))] + [in_hbm] * len(pieces),
        out_specs=[row_spec] * 4 + [anywhere],
        out_shape=[out] * 4 + [jax.ShapeDtypeStruct((4, width, width), BF16)],
        scratch_shapes=[
            pltpu.VMEM((4, width, width), BF16),
            pltpu.SemaphoreType.DMA((26,)),
            pltpu.SemaphoreType.DMA(()),
        ],
        compiler_params=params(),
        cost_estimate=pl.CostEstimate(
            flops=6 * rows * width * width, bytes_accessed=10 * rows * width + 16 * width * width, transcendentals=0
        ),
        name="project_heads",
    )(place, x, gain, *pieces)


def attend_kernel(first_pair, lengths_ref, table_ref, q_ref, k_ref, v_ref, *refs):
    mixed_ref, inv_ref, p_any, rows_ref, tile_ref, segc_ref, segr_ref, p_ref, sems = refs[-9:]
    together = q_ref.shape[1] // BLOCK
    pair = first_pair + together * pl.program_id(0)
    rows = q_ref.shape[0]
    bounds = bounds_of(lengths_ref, lengths_ref.shape[1])
    reach = WINDOW + BLOCK

    @pl.when(pl.program_id(0) == 0)
    def _():
        segc_ref[...] = segment_of(lax.broadcasted_iota(jnp.int32, segc_ref.shape, 0), bounds)
        segr_ref[...] = segment_of(lax.broadcasted_iota(jnp.int32, segr_ref.shape, 1), bounds)
        offsets = lax.broadcasted_iota(jnp.int32, (BUCKETS, reach), 1) - (SPAN + BLOCK)
        kinds = lax.broadcasted_iota(jnp.int32, (BUCKETS, reach), 0)
        onehot = (bucket_of(offsets) == kinds).astype(F32).astype(BF16)
        rows_ref[...] = dot_tn(table_ref[...], onehot)

    for head in range(2 * together):
        line = rows_ref[pl.ds(2 * pair + head, 1), :]
        skew = pltpu.roll(jnp.broadcast_to(line, (BLOCK, reach)), 0, 1, stride=1, stride_axis=0)
        tile_ref[head] = skew[:, BLOCK:]

    lane = lax.broadcasted_iota(jnp.int32, (BLOCK, BLOCK), 1)
    first_half = lane < HEAD_DIM

    def out_copy(block_index):
        slot = block_index % SLOTS
        target = p_any.at[pl.ds(2 * pair, 2 * together), pl.ds(pl.multiple_of(block_index * BLOCK, BLOCK), BLOCK), :]
        return pltpu.make_async_copy(p_ref.at[slot], target, sems.at[slot])

    def one(block_index, carry):
        slot = block_index % SLOTS
        start = pl.multiple_of(block_index * BLOCK, BLOCK)

        @pl.when(block_index >= SLOTS)
        def _():
            out_copy(block_index - SLOTS).wait()

        first, count = window_of(bounds, start)
        first = pl.multiple_of(first, BLOCK)
        shift = pl.multiple_of(first - start + SPAN, BLOCK)

        def body(blocks):
            size = blocks * BLOCK
            queries = pl.ds(start, BLOCK)
            keys = pl.ds(first, size)
            segc = segc_ref[queries, :]
            segr = segr_ref[0:1, keys]
            same = jnp.concatenate([segc] * blocks, 1) == segr
            wide_lane = lax.broadcasted_iota(jnp.int32, (size, BLOCK), 1) < HEAD_DIM
            scores = []
            for head in range(2 * together):
                lanes = slice(head // 2 * BLOCK, head // 2 * BLOCK + BLOCK)
                mine = first_half if head % 2 == 0 else ~first_half
                q = q_ref[queries, lanes]
                scores.append(dot_nt(jnp.where(mine, q, jnp.zeros_like(q)), k_ref[keys, lanes]))
            raised = []
            for head in range(2 * together):
                score = jnp.where(same, scores[head] + tile_ref[head, :, pl.ds(shift, size)], -1000000000.0)
                power = jnp.exp(score - jnp.max(score, -1, keepdims=True)).astype(BF16)
                p_ref[slot, head, :, 0:size] = power
                raised.append(power)
            for near in range(together):
                lanes = slice(near * BLOCK, near * BLOCK + BLOCK)
                v = v_ref[keys, lanes]
                one = jnp.ones_like(v)
                left = dot_nn(raised[2 * near], jnp.where(wide_lane, v, one))
                right = dot_nn(raised[2 * near + 1], jnp.where(wide_lane, one, v))
                total = pltpu.roll(jnp.where(first_half, right, left), HEAD_DIM, 1)
                inverse = 1.0 / total
                mixed_ref[queries, lanes] = (jnp.where(first_half, left, right) * inverse).astype(BF16)
                inv_ref[queries, lanes] = inverse

        for blocks in range(1, WINDOW // BLOCK + 1):
            pl.when(count == blocks)(functools.partial(body, blocks))
        out_copy(block_index).start()
        return carry

    lax.fori_loop(0, rows // BLOCK, one, 0)
    for block_index in range(rows // BLOCK - SLOTS, rows // BLOCK):
        out_copy(block_index).wait()


def attend(lengths, table, q, k, v, first_pair, pairs, before=()):
    rows, width = q.shape
    together = max(size for size in (1, 2, 3, 6) if pairs % size == 0 and first_pair % size == 0)
    column = pl.BlockSpec((rows, BLOCK * together), lambda p: (0, first_pair // together + p))
    return pl.pallas_call(
        functools.partial(attend_kernel, first_pair),
        grid=(pairs // together,),
        in_specs=[smem, whole(table.shape), column, column, column] + [anywhere] * len(before),
        out_specs=[column, column, anywhere],
        out_shape=[
            jax.ShapeDtypeStruct((rows, width), BF16),
            jax.ShapeDtypeStruct((rows, width), F32),
            jax.ShapeDtypeStruct((HEADS, rows, WINDOW), BF16),
        ],
        scratch_shapes=[
            pltpu.VMEM((16, WINDOW + BLOCK), F32),
            pltpu.VMEM((2 * together, BLOCK, WINDOW), F32),
            pltpu.VMEM((rows, BLOCK), jnp.int32),
            pltpu.VMEM((8, rows), jnp.int32),
            pltpu.VMEM((SLOTS, 2 * together, BLOCK, WINDOW), BF16),
            pltpu.SemaphoreType.DMA((SLOTS,)),
        ],
        input_output_aliases={5 + index: index for index in range(len(before))},
        compiler_params=params(),
        cost_estimate=pl.CostEstimate(
            flops=pairs * 8 * rows * 512 * 128, bytes_accessed=pairs * 6 * MIB, transcendentals=2 * pairs * rows * 512
        ),
        name="attend",
    )(lengths, table, q, k, v, *before)


def gelu_and_slope(v):
    bell = jnp.exp(-0.5 * v * v)
    t = 1.0 / (1.0 + (0.3275911 * root_half) * jnp.abs(v))
    series = t * (
        0.5 * 0.254829592
        + t * (0.5 * -0.284496736 + t * (0.5 * 1.421413741 + t * (0.5 * -1.453152027 + t * (0.5 * 1.061405429))))
    )
    tail = series * bell
    share = jnp.where(v >= 0.0, 1.0 - tail, tail)
    return v * share, share + v * bell * inv_root_tau


def member_of(lengths_ref, rows, count):
    bounds = bounds_of(lengths_ref, lengths_ref.shape[1])
    segment = segment_of(lax.broadcasted_iota(jnp.int32, (rows, count), 0), bounds)
    return (segment == lax.broadcasted_iota(jnp.int32, (rows, count), 1)).astype(F32).astype(BF16)


def member_rows(lengths_ref, rows, count):
    bounds = bounds_of(lengths_ref, lengths_ref.shape[1])
    segment = segment_of(lax.broadcasted_iota(jnp.int32, (count, rows), 1), bounds)
    return (segment == lax.broadcasted_iota(jnp.int32, (count, rows), 0)).astype(F32).astype(BF16)


def inner_copies(place_ref, refs, inner_ref):
    rows = refs[0].shape[0]
    width = inner_ref.shape[0]
    for other in range(2):
        owner = owner_of(place_ref, 0, other)
        yield refs[other], inner_ref.at[pl.ds(pl.multiple_of(owner * rows, 16), rows), :]
        for near in range(4):
            piece = refs[2 + 4 * other + near]
            quarter = place_ref[2] ^ near
            for far in range(1, 4):
                owner = owner_of(place_ref, far, other)
                row = pl.ds(pl.multiple_of(owner * rows, 16), rows)
                column = pl.ds(pl.multiple_of(quarter * width, 128), width)
                yield piece.at[far - 1], inner_ref.at[row, column]


def forward_kernel(place_ref, lengths_ref, x_ref, mixed_ref, gain_ref, heads_ref, wu_any, *refs):
    *pieces, out_ref, slope_ref, active_sum_ref, message_ref, mid_out, hid_out, wi_out = refs[:-12]
    total_ref, mid_ref, hid_ref, member_ref, wo_ref, inner_ref, active_ref = refs[-12:-5]
    wi_ref, wu_ref, sems, out_sems, last_sems = refs[-5:]
    step = pl.program_id(0)
    rows, width = hid_ref.shape
    block = rows // 4
    outs = ((wi_ref, wi_out), (hid_ref, hid_out), (mid_ref, mid_out))
    if len(pieces) == 1:
        groups = [[(pieces[0], wi_ref)], [(wu_any, wu_ref)]]
    else:
        groups = [list(inner_copies(place_ref, pieces, wi_ref)), [(wu_any, wu_ref)]]
    firsts = [0, len(groups[0])]
    spans = [slice(index * block, (index + 1) * block) for index in range(4)]

    def arrive(index):
        pairs = groups[index]
        wait_copies([pltpu.make_async_copy(*pair, sems.at[firsts[index] + at]) for at, pair in enumerate(pairs)])

    @pl.when(step == 0)
    def _():
        output_copy = pltpu.make_async_copy(heads_ref.at[3], wo_ref, last_sems.at[0])
        output_copy.start()
        for group, first in zip(groups, firsts):
            start_copies(group, sems, first)
        member_ref[...] = member_rows(lengths_ref, rows, 16)
        output_copy.wait()
        for span in spans:
            middle = x_ref[span, :].astype(F32) + dot_nn(mixed_ref[span, :], wo_ref[...])
            scale = lax.rsqrt(jnp.mean(middle * middle, -1, keepdims=True) + epsilon)
            total_ref[span, :] = middle
            mid_ref[span, :] = middle
            hid_ref[span, :] = (middle * scale * gain_ref[...].astype(F32)).astype(BF16)
        arrive(0)
        for index, pair in enumerate(outs):
            pltpu.make_async_copy(*pair, out_sems.at[index]).start()

    columns = pl.ds(pl.multiple_of(step * CHUNK, CHUNK), CHUNK)

    def first(span):
        inner_ref[span, :] = dot_nn(hid_ref[span, :], wi_ref[:, columns])

    def second(span):
        for at in range(span.start, span.stop, 32):
            active, slope = gelu_and_slope(inner_ref[at : at + 32, :])
            active_ref[at : at + 32, :] = active.astype(BF16)
            slope_ref[at : at + 32, :] = slope.astype(BF16)

    first(spans[0])
    first(spans[1])
    second(spans[0])

    @pl.when(step == 0)
    def _():
        arrive(1)

    for index, span in enumerate(spans):
        total_ref[span, :] += dot_nn(active_ref[span, :], wu_ref[columns, :])
        if index + 2 < 4:
            first(spans[index + 2])
        if index + 1 < 4:
            second(spans[index + 1])
    active_sum_ref[...] = dot_nn(member_ref[...], active_ref[...])

    @pl.when(step == pl.num_programs(0) - 1)
    def _():
        out_ref[...] = total_ref[...].astype(BF16)
        member = member_ref[...]
        pooled = jnp.zeros((16, width), F32)
        for span in spans:
            for piece in split_two(total_ref[span, :]):
                pooled = pooled + dot_nn(member[:, span], piece)
        row = lax.broadcasted_iota(jnp.int32, (8, 128), 0)
        lens = jnp.zeros((8, 128), jnp.int32)
        for index in range(8):
            lens = jnp.where(row == index, lengths_ref[0, index], lens)
        lens = lens.astype(F32)
        mean = pooled[0:8] / jnp.concatenate([lens] * (width // 128), 1)
        lower = jnp.concatenate([mean[:, 512:], lens, lens], 1)
        message_ref[...] = jnp.concatenate([mean[:, :512], lower], 0).astype(BF16)
        for index, pair in enumerate(outs):
            pltpu.make_async_copy(*pair, out_sems.at[index]).wait()


def forward(place, lengths, x, mixed, gain, heads, wu, units, pieces):
    rows, width = x.shape
    full = whole((rows, width))
    return pl.pallas_call(
        forward_kernel,
        grid=(units // CHUNK,),
        in_specs=[smem, smem, full, full, whole((1, width)), in_hbm, in_hbm] + [in_hbm] * len(pieces),
        out_specs=[
            pl.BlockSpec((rows, width), lambda i: (0, 0)),
            pl.BlockSpec((rows, CHUNK), lambda i: (0, i)),
            pl.BlockSpec((16, CHUNK), lambda i: (0, i)),
            pl.BlockSpec((16, 512), lambda i: (0, 0)),
        ]
        + [anywhere] * 3,
        out_shape=[
            jax.ShapeDtypeStruct((rows, width), BF16),
            jax.ShapeDtypeStruct((rows, units), BF16),
            jax.ShapeDtypeStruct((16, units), F32),
            pltpu.HBM((16, 512), BF16),
            jax.ShapeDtypeStruct((rows, width), F32),
            jax.ShapeDtypeStruct((rows, width), BF16),
            jax.ShapeDtypeStruct((width, units), BF16),
        ],
        scratch_shapes=[
            pltpu.VMEM((rows, width), F32),
            pltpu.VMEM((rows, width), F32),
            pltpu.VMEM((rows, width), BF16),
            pltpu.VMEM((16, rows), BF16),
            pltpu.VMEM((width, width), BF16),
            pltpu.VMEM((rows, CHUNK), F32),
            pltpu.VMEM((rows, CHUNK), BF16),
            pltpu.VMEM((width, units), BF16),
            pltpu.VMEM((units, width), BF16),
            pltpu.SemaphoreType.DMA((27,)),
            pltpu.SemaphoreType.DMA((3,)),
            pltpu.SemaphoreType.DMA((1,)),
        ],
        compiler_params=params(),
        cost_estimate=pl.CostEstimate(
            flops=4 * rows * width * units, bytes_accessed=30 * MIB, transcendentals=2 * rows * units
        ),
        name="feed_forward",
    )(place, lengths, x, mixed, gain, heads, wu, *pieces)


def contrast_kernel(place_ref, own_ref, got_ref, target_ref, wp_any, *refs):
    loss_ref, grad_wp_ref, glow_all_ref, grows_ref, glow_ref = refs[:-7]
    wide_ref, line_ref, full_ref, wp_ref, left_ref, right_ref, sems = refs[-7:]
    count, width = wide_ref.shape
    pending = start_copies([(wp_any, wp_ref)], sems)
    for other, ref in enumerate((own_ref, got_ref)):
        for far in range(4):
            for near in range(4):
                device = (place_ref[2] ^ near) * 8 + owner_of(place_ref, far, other)
                start = pl.multiple_of(device * 8, 8)
                piece = ref[near, far].astype(F32)
                left_ref[pl.ds(start, 8), :] = piece[0:8]
                right_ref[pl.ds(start, 8), :] = piece[8:16]
    rest = width - left_ref.shape[1]
    pooled = jnp.concatenate([left_ref[...], right_ref[:, 0:rest]], 1).astype(BF16)
    lens = right_ref[:, rest : rest + 1]
    wait_copies(pending)
    first = pl.multiple_of(place_ref[0] * 8, 8)
    projected = dot_nn(pooled, wp_ref[...])
    inverse = lax.rsqrt(jnp.sum(projected * projected, -1, keepdims=True) + epsilon)
    embedded = (projected * inverse).astype(BF16)
    row = lax.broadcasted_iota(jnp.int32, (count, count), 0)
    column = lax.broadcasted_iota(jnp.int32, (count, count), 1)
    logits = logit_scale * dot_nt(embedded, embedded)
    logits = jnp.where(row == column, -1000000000.0, logits)
    target_at = jnp.sum(jnp.where(row == column, target_ref[...], 0), -1, keepdims=True)
    hit = column == target_at
    highest = jnp.max(logits, -1, keepdims=True)
    totals = highest + jnp.log(jnp.sum(jnp.exp(logits - highest), -1, keepdims=True))
    target = jnp.sum(jnp.where(hit, logits, 0.0), -1, keepdims=True)
    line_ref[...] = jnp.broadcast_to(totals - target, line_ref.shape)
    loss_ref[...] = line_ref[pl.ds(first, 8), :]
    grad_logits = (jnp.exp(logits - totals) - hit.astype(F32)).astype(BF16)
    grad_embedded = logit_scale * (dot_nn(grad_logits, embedded) + dot_tn(grad_logits, embedded))
    along = jnp.sum(grad_embedded * projected, -1, keepdims=True)
    grad_projected = inverse * grad_embedded - projected * (inverse * inverse * inverse * along)
    high, low = split_two(grad_projected)
    full_ref[...] = dot_tn(pooled, high) + dot_tn(pooled, low)
    share = grad_wp_ref.shape[0]
    grad_wp_ref[...] = full_ref[pl.ds(pl.multiple_of(place_ref[1] * share, share), share), :]
    wp = wp_ref[...]
    grad_rows = (dot_nt(high, wp) + dot_nt(low, wp)) / lens
    glow_all_ref[...] = grad_rows.astype(BF16)
    wide_ref[...] = grad_rows
    own_rows = wide_ref[pl.ds(first, 8), :]
    grows_ref[...] = own_rows
    glow_ref[...] = jnp.concatenate([own_rows, jnp.zeros_like(own_rows)], 0).astype(BF16)


def contrast_plain(place, pooled, lens, targets, wp, share):
    count, width = pooled.shape
    exact = lax.Precision.HIGHEST
    projected = jnp.dot(pooled, wp, preferred_element_type=F32)
    inverse = lax.rsqrt(jnp.sum(projected * projected, -1, keepdims=True) + epsilon)
    embedded = (projected * inverse).astype(BF16)
    numbers = jnp.arange(count, dtype=jnp.int32)
    logits = logit_scale * dot_nt(embedded, embedded)
    logits = jnp.where(numbers[:, None] == numbers[None, :], -1000000000.0, logits)
    hit = numbers[None, :] == targets
    highest = jnp.max(logits, -1, keepdims=True)
    totals = highest + jnp.log(jnp.sum(jnp.exp(logits - highest), -1, keepdims=True))
    loss = totals - jnp.sum(jnp.where(hit, logits, 0.0), -1, keepdims=True)
    grad_logits = (jnp.exp(logits - totals) - hit.astype(F32)).astype(BF16)
    grad_embedded = logit_scale * (dot_nn(grad_logits, embedded) + dot_tn(grad_logits, embedded))
    along = jnp.sum(grad_embedded * projected, -1, keepdims=True)
    grad_projected = inverse * grad_embedded - projected * (inverse * inverse * inverse * along)
    own_columns = lax.dynamic_slice_in_dim(pooled.astype(F32), place[1] * share, share, 1)
    grad_wp = lax.dot_general(own_columns, grad_projected, (((0,), (0,)), ((), ())), precision=exact)
    grad_rows = jnp.dot(grad_projected, wp.astype(F32).T, precision=exact) / lens
    first = place[0] * 8
    own = lambda a: lax.dynamic_slice_in_dim(a, first, 8, 0)
    return jnp.broadcast_to(own(loss), (8, 128)), grad_wp, grad_rows.astype(BF16), own(grad_rows)


def fold(result_ref, keep_ref, send_ref, place_ref, column_half, column):
    narrow, plane, core = place_ref[2], place_ref[3], place_ref[4]
    rows = keep_ref.shape[2]
    for near in range(2):
        quarter = 2 * ((narrow // 2) ^ column_half) + near
        half = (narrow % 2) ^ near
        for far in range(4):
            for ref, owner in ((keep_ref, core), (send_ref, 1 - core)):
                start = pl.multiple_of((2 * (plane ^ far) + owner) * 2 * rows + half * rows, 16)
                block = result_ref[pl.ds(start, rows), :].astype(BF16)
                ref[quarter, far, :, pl.ds(column, block.shape[1])] = block


def back_kernel(
    lengths_ref, place_ref, glow_ref, grows_ref, gain_ref, hid_ref, active_ref, wu_ref, slope_ref, wi_ref,
    mid_any, mixed_any, inv_any, heads_any, gmid_any, gmix_ref, *refs,
):
    *grad_refs, result_ref, total_ref, member_ref, mid_ref, mixed_ref, inv_ref, wo_ref, sems, out_sems, gi_ref = refs
    step = pl.program_id(0)
    last = pl.num_programs(0) - 1
    rows, width = total_ref.shape
    folded = len(grad_refs) == 2 and len(grad_refs[1].shape) == 3
    late = [(mid_any, mid_ref), (mixed_any, mixed_ref), (inv_any, inv_ref), (heads_any.at[3], wo_ref)]

    @pl.when(step == 0)
    def _():
        member = member_of(lengths_ref, rows, 16)
        member_ref[...] = jnp.concatenate([member, member], 1)

    @pl.when(step == 0)
    def _():
        total_ref[...] = jnp.zeros_like(total_ref)

    @pl.when(step == 2)
    def _():
        start_copies(late, sems)

    high, low = split_two(dot_nt(glow_ref[...], wu_ref[...]))
    both = jnp.concatenate([high, low], 0)
    spans = (slice(0, rows // 2), slice(rows // 2, rows))
    for span in spans:
        spread = dot_nn(member_ref[span, :], both)
        gi_ref[span, :] = (spread * slope_ref[span, :].astype(F32)).astype(BF16)
    for span in spans:
        total_ref[span, :] += dot_nt(gi_ref[span, :], wi_ref[...])
    result_ref[:, :CHUNK] = dot_tn(hid_ref[...], gi_ref[...])

    if folded:
        grad_any, grad_ref = grad_refs
        owners, lines, _ = grad_ref.shape
        lines = lines - 8
        units = active_ref.shape[1]
        columns = pl.ds(pl.multiple_of(step * CHUNK, CHUNK), CHUNK)
        for owner in range(owners):
            grad_ref[owner, 0:lines, columns] = result_ref[owner * lines : (owner + 1) * lines, :CHUNK].astype(BF16)

        @pl.when(step == 0)
        def _():
            share = units // owners
            start = pl.multiple_of(place_ref[1] * share, 128)
            for owner in range(owners):
                grad_ref[owner, lines:, 0:units] = jnp.zeros((8, units), BF16)
                grad_ref[owner, lines:, pl.ds(start, share)] = active_ref[0:8, owner * share : (owner + 1) * share].astype(BF16)
    else:
        grad_refs[0][:, pl.ds(pl.multiple_of(step * CHUNK, CHUNK), CHUNK)] = result_ref[:, :CHUNK].astype(BF16)

    @pl.when(step == last)
    def _():
        pending = []
        if folded:
            inner_columns = pl.ds(0, units)
            copy = pltpu.make_async_copy(
                grad_ref.at[:, :, inner_columns], grad_any.at[:, :, inner_columns], out_sems.at[0]
            )
            copy.start()
            pending.append(copy)
        wait_copies([pltpu.make_async_copy(*pair, sems.at[index]) for index, pair in enumerate(late)])
        bounds = bounds_of(lengths_ref, lengths_ref.shape[1])
        block = rows // 8
        for index in range(8):
            span = slice(index * block, (index + 1) * block)
            middle = mid_ref[span, :]
            scale = lax.rsqrt(jnp.mean(middle * middle, -1, keepdims=True) + epsilon)
            normed = middle * scale
            scaled = total_ref[span, :] * gain_ref[...].astype(F32)
            centre = jnp.mean(scaled * normed, -1, keepdims=True)
            segment = segment_of(lax.broadcasted_iota(jnp.int32, (block, 128), 0) + index * block, bounds)
            segment = jnp.concatenate([segment] * (width // 128), 1)
            grad_rows = jnp.zeros((block, width), F32)
            for passage in range(8):
                grad_rows = jnp.where(segment == passage, grows_ref[passage : passage + 1, :], grad_rows)
            total_ref[span, :] = grad_rows + scale * (scaled - normed * centre)
        copy = pltpu.make_async_copy(total_ref, gmid_any, out_sems.at[2])
        copy.start()
        pending.append(copy)
        columns = width // 2
        for side in range(2):
            grad = dot_tn(mixed_ref[...], total_ref[:, side * columns : (side + 1) * columns].astype(BF16))
            if folded:
                span = slice(units + side * columns, units + (side + 1) * columns)
                for owner in range(owners):
                    grad_ref[owner, 0:lines, span] = grad[owner * lines : (owner + 1) * lines].astype(BF16)
            else:
                grad_refs[1][:, side * columns : (side + 1) * columns] = grad.astype(BF16)
        if folded:
            rest = pl.ds(units, width)
            copy = pltpu.make_async_copy(grad_ref.at[:, :, rest], grad_any.at[:, :, rest], out_sems.at[1])
            copy.start()
            pending.append(copy)
        for index in range(4):
            span = slice(index * 2 * block, (index + 1) * 2 * block)
            low_rows = total_ref[span, :].astype(BF16)
            gmix_ref[span, :] = (dot_nt(low_rows, wo_ref[...]) * inv_ref[span, :]).astype(BF16)
        wait_copies(pending)


def back(lengths, place, glow, grows, gain, hidden, active_sum, wu, slope, wi, middle, mixed, inv, heads, folded):
    rows, width = hidden.shape
    units = slope.shape[1]
    full = pl.BlockSpec((rows, width), lambda i: (0, 0))
    if folded:
        slab = (8, width // 8 + 8, units + width)
        grad_shape = [pltpu.HBM(slab, BF16)]
        grad_specs = [anywhere]
        grad_scratch = [pltpu.VMEM(slab, BF16)]
    else:
        shapes = [(width, units), (width, width)]
        grad_shape = [jax.ShapeDtypeStruct(shape, BF16) for shape in shapes]
        grad_specs = [pl.BlockSpec(shape, lambda i: (0, 0)) for shape in shapes]
        grad_scratch = []
    return pl.pallas_call(
        back_kernel,
        grid=(units // CHUNK,),
        in_specs=[
            smem,
            smem,
            whole((16, width)),
            whole((8, width)),
            whole((1, width)),
            whole((rows, width)),
            whole(active_sum.shape),
            pl.BlockSpec((CHUNK, width), lambda i: (i, 0)),
            pl.BlockSpec((rows, CHUNK), lambda i: (0, i)),
            pl.BlockSpec((width, CHUNK), lambda i: (0, i)),
        ]
        + [anywhere] * 4,
        out_specs=[anywhere, full] + grad_specs,
        out_shape=[jax.ShapeDtypeStruct((rows, width), F32), jax.ShapeDtypeStruct((rows, width), BF16)] + grad_shape,
        scratch_shapes=grad_scratch
        + [
            pltpu.VMEM((width, CHUNK), F32),
            pltpu.VMEM((rows, width), F32),
            pltpu.VMEM((rows, 32), BF16),
            pltpu.VMEM((rows, width), F32),
            pltpu.VMEM((rows, width), BF16),
            pltpu.VMEM((rows, width), F32),
            pltpu.VMEM((width, width), BF16),
            pltpu.SemaphoreType.DMA((4,)),
            pltpu.SemaphoreType.DMA((5,)),
            pltpu.VMEM((rows, CHUNK), BF16),
        ],
        compiler_params=params(),
        cost_estimate=pl.CostEstimate(flops=5 * rows * width * units, bytes_accessed=40 * MIB, transcendentals=0),
        name="back",
    )(lengths, place, glow, grows, gain, hidden, active_sum, wu, slope, wi, middle, mixed, inv, heads)


def contrast_back_kernel(
    lengths_ref, place_ref, own_ref, got_ref, target_ref, wp_any, gain_ref, hid_ref, active_ref, wu_ref, slope_ref, wi_ref,
    mid_any, mixed_any, inv_any, heads_any, loss_ref, grad_wp_ref, glow_all_ref, gmid_any, gmix_ref, grad_any, *refs,
):
    back_refs, (grows_ref, glow_ref, *contrast_refs) = refs[:11], refs[11:]

    @pl.when(pl.program_id(0) == 0)
    def _():
        contrast_kernel(
            place_ref, own_ref, got_ref, target_ref, wp_any,
            loss_ref, grad_wp_ref, glow_all_ref, grows_ref, glow_ref, *contrast_refs,
        )

    back_kernel(
        lengths_ref, place_ref, glow_ref, grows_ref, gain_ref, hid_ref, active_ref, wu_ref, slope_ref, wi_ref,
        mid_any, mixed_any, inv_any, heads_any, gmid_any, gmix_ref, grad_any, *back_refs,
    )


def contrast_back(
    lengths, place, own, got, targets, wp, gain, hidden, active_sum, wu, slope, wi, middle, mixed, inv, heads, share
):
    rows, width = hidden.shape
    units = slope.shape[1]
    count = targets.shape[1]
    slab = (8, width // 8 + 8, units + width)
    fixed = lambda shape: pl.BlockSpec(shape, lambda i: (0,) * len(shape))
    return pl.pallas_call(
        contrast_back_kernel,
        grid=(units // CHUNK,),
        in_specs=[smem, smem, whole(own.shape), whole(got.shape), whole(targets.shape), in_hbm]
        + [whole((1, width)), whole((rows, width)), whole(active_sum.shape)]
        + [
            pl.BlockSpec((CHUNK, width), lambda i: (i, 0)),
            pl.BlockSpec((rows, CHUNK), lambda i: (0, i)),
            pl.BlockSpec((width, CHUNK), lambda i: (0, i)),
        ]
        + [anywhere] * 4,
        out_specs=[fixed((8, 128)), fixed((share, width)), fixed((count, width)), anywhere, fixed((rows, width)), anywhere],
        out_shape=[
            jax.ShapeDtypeStruct((8, 128), F32),
            jax.ShapeDtypeStruct((share, width), F32),
            jax.ShapeDtypeStruct((count, width), BF16),
            jax.ShapeDtypeStruct((rows, width), F32),
            jax.ShapeDtypeStruct((rows, width), BF16),
            pltpu.HBM(slab, BF16),
        ],
        scratch_shapes=[
            pltpu.VMEM(slab, BF16),
            pltpu.VMEM((width, CHUNK), F32),
            pltpu.VMEM((rows, width), F32),
            pltpu.VMEM((rows, 32), BF16),
            pltpu.VMEM((rows, width), F32),
            pltpu.VMEM((rows, width), BF16),
            pltpu.VMEM((rows, width), F32),
            pltpu.VMEM((width, width), BF16),
            pltpu.SemaphoreType.DMA((4,)),
            pltpu.SemaphoreType.DMA((5,)),
            pltpu.VMEM((rows, CHUNK), BF16),
            pltpu.VMEM((8, width), F32),
            pltpu.VMEM((16, width), BF16),
            pltpu.VMEM((count, width), F32),
            pltpu.VMEM((count, 128), F32),
            pltpu.VMEM((width, width), F32),
            pltpu.VMEM((width, width), BF16),
            pltpu.VMEM((count, 512), F32),
            pltpu.VMEM((count, 512), F32),
            pltpu.SemaphoreType.DMA((1,)),
        ],
        compiler_params=params(),
        cost_estimate=pl.CostEstimate(flops=5 * rows * width * units, bytes_accessed=40 * MIB, transcendentals=0),
        name="contrast_back",
    )(lengths, place, own, got, targets, wp, gain, hidden, active_sum, wu, slope, wi, middle, mixed, inv, heads)


def attend_grad_kernel(first_pair, lengths_ref, q_ref, k_ref, v_ref, gm_ref, mixed_ref, p_any, *refs):
    grad_ref, diag_ref, qm_ref, km_ref, vx_ref, gx_ref, go_ref, ak_ref, av_ref, acc_ref, p_ref, sems = refs[-12:]
    together = q_ref.shape[1] // BLOCK
    rows = q_ref.shape[0]
    first_head = 2 * (first_pair + together * pl.program_id(0))

    def in_copy(block_index):
        slot = block_index % SLOTS
        source = p_any.at[pl.ds(first_head, 2 * together), pl.ds(pl.multiple_of(block_index * BLOCK, BLOCK), BLOCK), :]
        return pltpu.make_async_copy(source, p_ref.at[slot], sems.at[slot])

    for block_index in range(SLOTS - 1):
        in_copy(block_index).start()
    bounds = bounds_of(lengths_ref, lengths_ref.shape[1])
    reach = WINDOW + BLOCK
    acc_ref[...] = jnp.zeros_like(acc_ref)
    ak_ref[...] = jnp.zeros_like(ak_ref)
    av_ref[...] = jnp.zeros_like(av_ref)

    lane = lax.broadcasted_iota(jnp.int32, (BLOCK, BLOCK), 1)
    row = lax.broadcasted_iota(jnp.int32, (BLOCK, BLOCK), 0)
    across = jnp.where((row < HEAD_DIM) != (lane < HEAD_DIM), -1.0, 0.0).astype(BF16)

    def prepare(index, carry):
        span = pl.ds(pl.multiple_of(index * BLOCK, BLOCK), BLOCK)
        for near in range(together):
            lanes = slice(near * BLOCK, near * BLOCK + BLOCK)
            q, k, v, g = q_ref[span, lanes], k_ref[span, lanes], v_ref[span, lanes], gm_ref[span, lanes]
            product = split_two(g.astype(F32) * mixed_ref[span, lanes].astype(F32))
            centre = dot_nn(product[0], across) + dot_nn(product[1], across)
            high, low = split_two(centre)
            first = (lane == 0) | (lane == HEAD_DIM)
            second = (lane == 1) | (lane == HEAD_DIM + 1)
            zero = jnp.zeros_like(q)
            extra = jnp.where(first, high, jnp.where(second, low, zero))
            one = jnp.ones_like(v)
            for half in range(2):
                head = 2 * near + half
                mine = (lane < HEAD_DIM) if half == 0 else (lane >= HEAD_DIM)
                qm_ref[head, span, :] = jnp.where(mine, q, zero)
                km_ref[head, span, :] = jnp.where(mine, k, zero)
                go_ref[head, span, :] = jnp.where(mine, g, zero)
                vx_ref[head, span, :] = jnp.where(mine, v, one)
                gx_ref[head, span, :] = jnp.where(mine, g, extra)
        return carry

    lax.fori_loop(0, rows // BLOCK, prepare, 0)

    def one(block_index, carry):
        slot = block_index % SLOTS
        start = pl.multiple_of(block_index * BLOCK, BLOCK)
        in_copy(block_index).wait()

        @pl.when(block_index + SLOTS - 1 < rows // BLOCK)
        def _():
            in_copy(block_index + SLOTS - 1).start()

        first, count = window_of(bounds, start)
        first = pl.multiple_of(first, BLOCK)
        shift = pl.multiple_of(first - start + SPAN, BLOCK)

        def body(blocks):
            size = blocks * BLOCK
            queries = pl.ds(start, BLOCK)
            keys = pl.ds(first, size)
            spread = [dot_nt(gx_ref[head, queries, :], vx_ref[head, keys, :]) for head in range(2 * together)]
            for near in range(together):
                heads = (2 * near, 2 * near + 1)
                lanes = slice(near * BLOCK, near * BLOCK + BLOCK)
                parts = []
                raised = []
                for head in heads:
                    p = p_ref[slot, head, :, 0:size]
                    grad_scores = p.astype(F32) * spread[head]
                    acc_ref[head, :, pl.ds(shift, size)] += grad_scores
                    parts.append(grad_scores.astype(BF16))
                    raised.append(p)
                q_both = jnp.concatenate([qm_ref[head, queries, :] for head in heads], 0)
                g_both = jnp.concatenate([go_ref[head, queries, :] for head in heads], 0)
                k_both = jnp.concatenate([km_ref[head, keys, :] for head in heads], 0)
                ak_ref[lanes, keys] += dot_tn(q_both, jnp.concatenate(parts, 0))
                av_ref[lanes, keys] += dot_tn(g_both, jnp.concatenate(raised, 0))
                grad_ref[0, queries, lanes] = dot_nn(jnp.concatenate(parts, 1), k_both).astype(BF16)

        for blocks in range(1, WINDOW // BLOCK + 1):
            pl.when(count == blocks)(functools.partial(body, blocks))
        return carry

    lax.fori_loop(0, rows // BLOCK, one, 0)
    for near in range(together):
        lanes = slice(near * BLOCK, near * BLOCK + BLOCK)
        grad_ref[1, :, lanes] = jnp.transpose(ak_ref[lanes, :]).astype(BF16)
        grad_ref[2, :, lanes] = jnp.transpose(av_ref[lanes, :]).astype(BF16)
    for head in range(2 * together):
        padded = jnp.concatenate([jnp.zeros((BLOCK, BLOCK), F32), acc_ref[head]], 1)
        group = padded[0:8]
        for index in range(1, BLOCK // 8):
            group = group + pltpu.roll(padded[8 * index : 8 * index + 8], reach - 8 * index, 1)
        line = group[0:1]
        for index in range(1, 8):
            line = line + pltpu.roll(group, reach - index, 1)[index : index + 1]
        diag_ref[head // 2, head % 2 : head % 2 + 1, :] = line


def attend_grad(lengths, q, k, v, gm, mixed, p, first_pair, pairs, before=()):
    rows, width = q.shape
    together = max(size for size in (1, 2, 3, 6) if pairs % size == 0 and first_pair % size == 0)
    at = first_pair // together
    column = pl.BlockSpec((rows, BLOCK * together), lambda i: (0, at + i), pipeline_mode=pl.Buffered(1 if together == 6 else 2))
    return pl.pallas_call(
        functools.partial(attend_grad_kernel, first_pair),
        grid=(pairs // together,),
        in_specs=[smem]
        + [column] * 5
        + [in_hbm]
        + [anywhere] * len(before),
        out_specs=[
            pl.BlockSpec((3, rows, BLOCK * together), lambda i: (0, 0, at + i)),
            pl.BlockSpec((together, 2, WINDOW + BLOCK), lambda i: (at + i, 0, 0)),
        ],
        out_shape=[
            jax.ShapeDtypeStruct((3, rows, width), BF16),
            jax.ShapeDtypeStruct((HEADS // 2, 2, WINDOW + BLOCK), F32),
        ],
        scratch_shapes=[pltpu.VMEM((2 * together, rows, BLOCK), BF16)] * 5
        + [pltpu.VMEM((BLOCK * together, rows), F32)] * 2
        + [
            pltpu.VMEM((2 * together, BLOCK, WINDOW), F32),
            pltpu.VMEM((SLOTS, 2 * together, BLOCK, WINDOW), BF16),
            pltpu.SemaphoreType.DMA((SLOTS,)),
        ],
        input_output_aliases={7 + index: index for index in range(len(before))},
        compiler_params=params(),
        cost_estimate=pl.CostEstimate(
            flops=pairs * 20 * rows * 512 * 64, bytes_accessed=pairs * 5 * MIB, transcendentals=0
        ),
        name="attend_grad",
    )(lengths, q, k, v, gm, mixed, p, *before)


def head_grad_kernel(place_ref, hid_any, grad_any, table_ref, keep_ref, send_ref, hid_ref, grad_ref, result_ref, sems):
    block = result_ref.shape[2]
    pairs = [(hid_any, hid_ref)]
    for matrix in range(3):
        for side in range(2):
            columns = pl.ds(side * block, block)
            pairs.append((grad_any.at[matrix, :, columns], grad_ref.at[matrix, :, columns]))
    pending = start_copies(pairs, sems)
    rows = keep_ref.shape[2]
    for far in range(4):
        for ref, other in ((keep_ref, 0), (send_ref, 1)):
            line = table_ref[pl.ds(owner_of(place_ref, far, other), 1), :]
            block_of = jnp.broadcast_to(line, (rows, 128)).astype(BF16)
            for quarter in range(4):
                ref[quarter, far, :, 3 * block :] = block_of
    pending[0].wait()
    for step in range(6):
        pending[1 + step].wait()
        columns = slice(step % 2 * block, step % 2 * block + block)
        result_ref[step % 2] = dot_tn(hid_ref[...], grad_ref[step // 2, :, columns])
        fold(result_ref.at[step % 2], keep_ref, send_ref, place_ref, step // 3, step % 3 * block)


def head_grad(place, hidden, grads, table):
    rows, width = hidden.shape
    block = width // 2
    slab = (4, 4, width // 16, 3 * block + 128)
    return pl.pallas_call(
        head_grad_kernel,
        in_specs=[smem, in_hbm, in_hbm, in_vmem],
        out_specs=[in_vmem] * 2,
        out_shape=[jax.ShapeDtypeStruct(slab, BF16)] * 2,
        scratch_shapes=[
            pltpu.VMEM((rows, width), BF16),
            pltpu.VMEM((3, rows, width), BF16),
            pltpu.VMEM((2, width, block), F32),
            pltpu.SemaphoreType.DMA((7,)),
        ],
        compiler_params=pltpu.CompilerParams(vmem_limit_bytes=28 * MIB),
        cost_estimate=pl.CostEstimate(flops=6 * rows * width * width, bytes_accessed=12 * MIB, transcendentals=0),
        name="head_grad",
    )(place, hidden, grads, table)


def token_grad_kernel(x_ref, gain_ref, gmid_ref, grad_ref, w_ref, out_ref):
    x = x_ref[...].astype(F32)
    scale = lax.rsqrt(jnp.mean(x * x, -1, keepdims=True) + epsilon)
    normed = x * scale
    grad_hidden = dot_nt(grad_ref[0], w_ref[0]) + dot_nt(grad_ref[1], w_ref[1]) + dot_nt(grad_ref[2], w_ref[2])
    scaled = grad_hidden * gain_ref[...].astype(F32)
    centre = jnp.mean(scaled * normed, -1, keepdims=True)
    out_ref[...] = gmid_ref[...] + scale * (scaled - normed * centre)


def token_grad(x, gain, gmid, grads, weights):
    rows, width = x.shape
    block = rows // 4
    row_spec = pl.BlockSpec((block, width), lambda i: (i, 0))
    return pl.pallas_call(
        token_grad_kernel,
        grid=(4,),
        in_specs=[
            row_spec,
            whole((1, width)),
            row_spec,
            pl.BlockSpec((3, block, width), lambda i: (0, i, 0)),
            whole((3, width, width)),
        ],
        out_specs=row_spec,
        out_shape=jax.ShapeDtypeStruct((rows, width), F32),
        compiler_params=params(),
        cost_estimate=pl.CostEstimate(flops=6 * rows * width * width, bytes_accessed=16 * MIB, transcendentals=0),
        name="token_grad",
    )(x, gain, gmid, grads, weights)


def outer_grad_kernel(place_ref, pieces_ref, glow_ref, out_ref, active_ref):
    units = active_ref.shape[1]
    for near in range(4):
        start = pl.multiple_of((place_ref[2] ^ near) * 64, 64)
        for owner in range(8):
            half = 8 * (owner // 4)
            column = owner % 4 * units
            block = pieces_ref[near].astype(F32)[half : half + 8, column : column + units]
            active_ref[pl.ds(start + 8 * owner, 8), :] = block
    out_ref[...] = dot_tn(active_ref[...].astype(BF16), glow_ref[...])


def outer_grad(place, pieces, glow):
    count, width = glow.shape
    units = pieces.shape[2] // 4
    return pl.pallas_call(
        outer_grad_kernel,
        grid=(1,),
        in_specs=[smem, whole(pieces.shape), whole(glow.shape)],
        out_specs=pl.BlockSpec((units, width), lambda i: (0, 0)),
        out_shape=jax.ShapeDtypeStruct((units, width), F32),
        scratch_shapes=[pltpu.VMEM((count, units), F32)],
        compiler_params=params(),
        cost_estimate=pl.CostEstimate(flops=2 * count * units * width, bytes_accessed=3 * MIB, transcendentals=0),
        name="outer_grad",
    )(place, pieces, glow)


def table_grad(diag):
    reach = WINDOW + BLOCK
    offsets = jnp.arange(reach, dtype=jnp.int32) - (SPAN + BLOCK)
    onehot = (bucket_of(offsets)[:, None] == jnp.arange(BUCKETS, dtype=jnp.int32)[None, :]).astype(F32)
    sums = jnp.dot(diag.reshape(HEADS, reach), onehot, precision=lax.Precision.HIGHEST)
    return sums.T.reshape(BUCKETS * HEADS)


def exchange(value, narrow=0, plane=0, core=0):
    bits = narrow * 8 + plane * 2 + core
    return lax.ppermute(value, ("narrow", "wide"), [(i, i ^ bits) for i in range(32)])


def spread(value):
    return [value] + [exchange(value, narrow=near) for near in range(1, 4)]


def sum_core_kernel(keep_ref, got_ref, *out_refs):
    for quarter, out_ref in enumerate(out_refs):
        for far in range(4):
            out_ref[far] = (keep_ref[quarter, far].astype(F32) + got_ref[quarter, far].astype(F32)).astype(BF16)


def sum_core(keep, got):
    _, _, rows, columns = keep.shape
    return pl.pallas_call(
        sum_core_kernel,
        in_specs=[in_vmem] * 2,
        out_specs=[in_vmem] * 4,
        out_shape=[jax.ShapeDtypeStruct((4, rows, columns), BF16)] * 4,
        compiler_params=small,
        cost_estimate=pl.CostEstimate(flops=0, bytes_accessed=96 * rows * columns, transcendentals=0),
        name="sum_core",
    )(keep, got)


def sum_narrow_kernel(apart, a_ref, b_ref, c_ref, d_ref, *out_refs):
    refs = (a_ref, b_ref, c_ref, d_ref)
    columns = a_ref.shape[2] - (128 if apart else 0)
    for far, out_ref in enumerate(out_refs):
        total = sum(ref[far, :, :columns].astype(F32) for ref in refs)
        out_ref[:, :columns] = total.astype(BF16)
        if apart:
            for near, ref in enumerate(refs):
                out_ref[:, columns + 128 * near : columns + 128 * near + 128] = ref[far, :, columns:]


def sum_narrow(parts, apart):
    _, rows, columns = parts[0].shape
    columns += 3 * 128 if apart else 0
    return pl.pallas_call(
        functools.partial(sum_narrow_kernel, apart),
        in_specs=[in_vmem] * 4,
        out_specs=[in_vmem] * 4,
        out_shape=[jax.ShapeDtypeStruct((rows, columns), BF16)] * 4,
        compiler_params=small,
        cost_estimate=pl.CostEstimate(flops=0, bytes_accessed=40 * rows * columns, transcendentals=0),
        name="sum_narrow",
    )(*parts)


def sum_planes_kernel(a_ref, b_ref, c_ref, d_ref, total_ref, *apart_refs):
    refs = (a_ref, b_ref, c_ref, d_ref)
    columns = total_ref.shape[1]
    total_ref[...] = sum(ref[:, :columns].astype(F32) for ref in refs).astype(BF16)
    for apart_ref in apart_refs:
        for far, ref in enumerate(refs):
            apart_ref[far] = ref[:, columns:]


def sum_planes(parts, apart):
    rows, columns = parts[0].shape
    kept = 4 * 128 if apart else 0
    out_shape = [jax.ShapeDtypeStruct((rows, columns - kept), BF16)]
    if apart:
        out_shape.append(jax.ShapeDtypeStruct((4, rows, kept), BF16))
    return pl.pallas_call(
        sum_planes_kernel,
        in_specs=[in_vmem] * 4,
        out_specs=[in_vmem] * len(out_shape),
        out_shape=out_shape,
        compiler_params=small,
        cost_estimate=pl.CostEstimate(flops=0, bytes_accessed=10 * rows * columns, transcendentals=0),
        name="sum_planes",
    )(*parts)


def cut_kernel(place_ref, part_ref, *out_refs):
    rows, columns = out_refs[0].shape
    rows = rows - 16
    total = part_ref.shape[1]
    units = total * 4 // 5
    for near, out_ref in enumerate(out_refs):
        quarter = place_ref[2] ^ near
        row = pl.ds(pl.multiple_of((quarter % 2) * rows, 16), rows)
        column = pl.multiple_of((quarter // 2) * (units // 2), 128)
        out_ref[0:rows, 0 : units // 2] = part_ref[row, pl.ds(column, units // 2)]
        column = pl.multiple_of(units + (quarter // 2) * (columns - units // 2), 128)
        out_ref[0:rows, units // 2 :] = part_ref[row, pl.ds(column, columns - units // 2)]
        sums = part_ref[2 * rows :, 0:units].astype(F32)
        sums = jnp.concatenate([sums[:, : units // 2], sums[:, units // 2 :]], 0)
        out_ref[rows:, 0 : units // 2] = sums.astype(BF16)
        out_ref[rows:, units // 2 :] = jnp.zeros((16, columns - units // 2), BF16)


def cut(place, part):
    rows, total = part.shape
    shape = ((rows - 8) // 2 + 16, total // 2)
    return pl.pallas_call(
        cut_kernel,
        in_specs=[smem, in_vmem],
        out_specs=[in_vmem] * 4,
        out_shape=[jax.ShapeDtypeStruct(shape, BF16)] * 4,
        compiler_params=small,
        cost_estimate=pl.CostEstimate(flops=0, bytes_accessed=2 * MIB, transcendentals=0),
        name="cut",
    )(place, part)


def sum_quarter_kernel(a_ref, b_ref, c_ref, d_ref, total_ref, apart_ref):
    refs = (a_ref, b_ref, c_ref, d_ref)
    rows = total_ref.shape[0]
    total_ref[...] = sum(ref[0:rows, :].astype(F32) for ref in refs).astype(BF16)
    for near, ref in enumerate(refs):
        apart_ref[near] = ref[rows:, : apart_ref.shape[2]]


def sum_quarter(parts):
    rows, columns = parts[0].shape
    return pl.pallas_call(
        sum_quarter_kernel,
        in_specs=[in_vmem] * 4,
        out_specs=[in_vmem] * 2,
        out_shape=[
            jax.ShapeDtypeStruct((rows - 16, columns), BF16),
            jax.ShapeDtypeStruct((4, 16, columns * 4 // 5), BF16),
        ],
        compiler_params=small,
        cost_estimate=pl.CostEstimate(flops=0, bytes_accessed=2 * MIB, transcendentals=0),
        name="sum_quarter",
    )(*parts)


def as_row(column):
    return jnp.transpose(jnp.broadcast_to(column, (column.shape[0], 128)))[0:1]


def finish_inner_kernel(place_ref, weight_ref, gain_ref, a_ref, b_ref, c_ref, d_ref, out_ref, last_ref, ggain_ref):
    rows = a_ref.shape[0]
    units = weight_ref.shape[1] // 2
    width = last_ref.shape[1] // 2
    for near, ref in enumerate((a_ref, b_ref, c_ref, d_ref)):
        quarter = place_ref[2] ^ near
        row = pl.ds(pl.multiple_of((quarter % 2) * rows, rows), rows)
        half = quarter // 2
        out_ref[row, pl.ds(pl.multiple_of(half * units, 128), units)] = ref[:, :units].astype(F32)
        last_ref[row, pl.ds(pl.multiple_of(half * width, 128), width)] = ref[:, units:].astype(F32)
    along = jnp.sum(out_ref[...] * weight_ref[...].astype(F32), -1, keepdims=True)
    ggain_ref[...] = as_row(along) / gain_ref[...].astype(F32)


def finish_inner(place, weight, gain, parts, width):
    rows, units = weight.shape
    ins = [weight, gain] + list(parts)
    outs = [jax.ShapeDtypeStruct(shape, F32) for shape in ((rows, units), (rows, width), (1, rows))]
    return pl.pallas_call(
        finish_inner_kernel,
        in_specs=[smem] + [in_vmem] * len(ins),
        out_specs=[in_vmem] * len(outs),
        out_shape=outs,
        compiler_params=small,
        cost_estimate=pl.CostEstimate(flops=0, bytes_accessed=3 * MIB, transcendentals=0),
        name="finish_inner",
    )(place, *ins)


def finish_heads_kernel(place_ref, wq_ref, wk_ref, wv_ref, gain_ref, a_ref, b_ref, c_ref, d_ref, *refs):
    *out_refs, table_ref, ggain_ref, result_ref = refs
    rows = a_ref.shape[0]
    width = wq_ref.shape[1]
    half = 3 * width // 2
    for near, ref in enumerate((a_ref, b_ref, c_ref, d_ref)):
        quarter = place_ref[2] ^ near
        row = pl.multiple_of((quarter % 2) * rows, rows)
        column = pl.multiple_of((quarter // 2) * half, 128)
        result_ref[pl.ds(row, rows), pl.ds(column, half)] = ref[:, :half].astype(F32)

        @pl.when(quarter == 0)
        def _():
            table_ref[...] = ref[0:16, half:].astype(F32)[0:1, : table_ref.shape[1]]

    along = jnp.zeros((2 * rows, 1), F32)
    for index, (out_ref, weight_ref) in enumerate(zip(out_refs, (wq_ref, wk_ref, wv_ref))):
        grad = result_ref[:, index * width : (index + 1) * width]
        out_ref[...] = grad
        along = along + jnp.sum(grad * weight_ref[...].astype(F32), -1, keepdims=True)
    ggain_ref[...] = as_row(along) / gain_ref[...].astype(F32)


def finish_heads(place, weights, gain, parts, table_share):
    rows, width = weights[0].shape
    ins = list(weights) + [gain] + list(parts)
    outs = [jax.ShapeDtypeStruct((rows, width), F32)] * 3
    outs += [jax.ShapeDtypeStruct((1, table_share), F32), jax.ShapeDtypeStruct((1, rows), F32)]
    return pl.pallas_call(
        finish_heads_kernel,
        in_specs=[smem] + [in_vmem] * len(ins),
        out_specs=[in_vmem] * len(outs),
        out_shape=outs,
        scratch_shapes=[pltpu.VMEM((rows, 3 * width), F32)],
        compiler_params=small,
        cost_estimate=pl.CostEstimate(flops=0, bytes_accessed=3 * MIB, transcendentals=0),
        name="finish_heads",
    )(place, *ins)


def order_small_kernel(place_ref, own_ref, got_ref, out_ref):
    for other, ref in enumerate((own_ref, got_ref)):
        for far in range(4):
            out_ref[pl.ds(owner_of(place_ref, far, other), 1), :] = ref[far, 0:1, :]


def order_small(place, own, got):
    return pl.pallas_call(
        order_small_kernel,
        grid=(1,),
        in_specs=[smem, whole(own.shape), whole(got.shape)],
        out_specs=pl.BlockSpec((8, own.shape[2]), lambda i: (0, 0)),
        out_shape=jax.ShapeDtypeStruct((8, own.shape[2]), F32),
        name="order_small",
    )(place, own, got)


def gather_messages(message):
    far = jnp.stack([message] + [exchange(message, plane=distance) for distance in range(1, 4)])
    near = jnp.stack(spread(far))
    return near, exchange(near, core=1)


def tie(first, then):
    first, then = lax.optimization_barrier((first, then))
    return first, then


def gather_heads(place, own, small):
    rows, width = own[0].shape
    line = jnp.broadcast_to(jnp.pad(small, (0, width - small.shape[0])), (8, width))
    heads = jnp.stack([jnp.concatenate([weight, line]) for weight in own])
    quarter = lax.dynamic_index_in_dim(heads, place[2], 0, keepdims=False)
    far = jnp.stack([exchange(quarter, plane=distance) for distance in range(1, 4)])
    far, heads = tie(far, heads)
    near = spread(far)
    other = exchange(heads, core=1)
    far_other = exchange(far, core=1)
    lines = lambda first, rest: jnp.concatenate([first[:1, rows:, :256], rest[:, rows:, :256]]).astype(F32)
    ordered = order_small(place, lines(heads, far), lines(other, far_other))
    return near, [heads, other], far_other, ordered


def fetch_inner(narrow, inner_weight, width):
    quarter = lax.dynamic_slice_in_dim(inner_weight, narrow * width, width, 1)
    return [exchange(quarter, plane=far) for far in range(1, 4)]


def layer_specs():
    both = ("narrow", "wide")
    rows, matrix, vector = P(both, None), P("wide", None), P("wide")
    ins = (rows, vector, matrix, matrix, matrix, matrix, vector, vector, matrix, matrix, matrix, rows, P())
    outs = (rows, rows, rows, vector, matrix, matrix, matrix, matrix, vector, vector, matrix, matrix, matrix)
    return ins, outs


def local_permuted(tokens, *arguments):
    *weights_own, lengths, positives = arguments
    attention_gain, query_weight, key_weight, value_weight, output_weight = weights_own[:5]
    bias_table, forward_gain, inner_weight, outer_weight, project_weight = weights_own[5:]
    segs = lengths.shape[1]
    width = tokens.shape[1]
    units = inner_weight.shape[1]
    wide_at = lax.axis_index("wide")
    narrow_at = lax.axis_index("narrow")
    device = narrow_at * 8 + wide_at
    place = jnp.stack([device, wide_at, narrow_at, wide_at // 2, wide_at % 2]).astype(jnp.int32)
    share = attention_gain.shape[0]

    own_heads = (query_weight, key_weight, value_weight, output_weight)
    small = jnp.concatenate([attention_gain, forward_gain, bias_table])
    near, both_heads, far_other, small = gather_heads(place, own_heads, small)
    gain_one = small[:, :share].reshape(1, width)
    gain_two = small[:, share : 2 * share].reshape(1, width)
    table = small[:, 2 * share : 2 * share + bias_table.shape[0]].reshape(BUCKETS, HEADS)
    table = jnp.pad(table, ((0, 0), (0, 4))).astype(BF16)
    _, own_inner = tie(both_heads[1], inner_weight)
    _, own_outer = tie(far_other, outer_weight)
    wu = lax.all_gather(own_outer, "wide", axis=0, tiled=True)
    far = jnp.stack(fetch_inner(narrow_at, own_inner, width))
    (gain_one, gain_two, table), near = tie((gain_one, gain_two, table), near)
    near, far = tie(near, far)
    head_pieces = both_heads + near + [far_other] + [exchange(piece, core=1) for piece in near[1:]]
    near = spread(far)
    other_inner = exchange(own_inner, core=1)

    hid, q, k, v, weights = project(place, tokens, gain_one, head_pieces)
    q, own_last = tie(q, project_weight)
    wp = lax.all_gather(own_last, "wide", axis=0, tiled=True)
    mixed, inv, p = attend(lengths, table, q, k, v, 0, 6)
    mixed, inv, p, near = lax.optimization_barrier((mixed, inv, p, near))
    near_other = [exchange(piece, core=1) for piece in near]
    hidden, slope, active_sum, message, middle, hid_two, wi = forward(
        place, lengths, tokens, mixed, gain_two, weights, wu, units, [own_inner, other_inner] + near + near_other
    )
    loss, grad_wp, glow_all, gmid, gm, grads_out = contrast_back(
        lengths, place, *gather_messages(message), positives[None], wp, gain_two, hid_two, active_sum, wu, slope, wi,
        middle, mixed, inv, weights, project_weight.shape[0],
    )

    part = lax.psum_scatter(grads_out.reshape(-1, units + width), "wide", scatter_dimension=0, tiled=True)
    grad_heads, diag = attend_grad(lengths, q, k, v, gm, mixed, p, 0, 6)
    grad_table = table_grad(diag).reshape(8, -1)
    rows_table = jnp.pad(grad_table, ((0, 0), (0, 128 - grad_table.shape[1])))
    keep, send = head_grad(place, hid, grad_heads, rows_table)
    got = exchange(send, core=1)
    quarters = sum_core(keep, got)
    quarters, gmid = tie(quarters, gmid)
    arrived = [quarters[0]] + [exchange(quarters[near], narrow=near) for near in range(1, 4)]
    grad_tokens = token_grad(tokens, gain_one, gmid, grad_heads, weights)
    grad_tokens, arrived = tie(grad_tokens, arrived)
    planes = sum_narrow(arrived, False)
    planes, part = tie(planes, part)
    arrived = [planes[0]] + [exchange(planes[far], plane=far) for far in range(1, 4)]
    pieces = cut(place, part)
    pieces = [pieces[0]] + [exchange(pieces[near], narrow=near) for near in range(1, 4)]
    total, active_pieces = sum_quarter(pieces)
    inner_parts = spread(total)
    grad_outer = outer_grad(place, active_pieces, glow_all)
    grad_outer, arrived = tie(grad_outer, arrived)
    (total,) = sum_planes(arrived, False)
    last_parts = spread(total)
    grad_inner, grad_out, gain_two_grad = finish_inner(place, inner_weight, forward_gain[None], inner_parts, width)
    *grads, table_own, gain_one_grad = finish_heads(
        place, own_heads[:3], attention_gain[None], last_parts, bias_table.shape[0]
    )
    grads.append(grad_out)
    return (
        hidden,
        grad_tokens,
        loss[:, 0].reshape(1, segs),
        gain_one_grad[0],
        *grads,
        table_own[0],
        gain_two_grad[0],
        grad_inner,
        grad_outer,
        grad_wp,
    )


def local_plain(tokens, *arguments):
    *weights_own, lengths, positives = arguments
    attention_gain, query_weight, key_weight, value_weight, output_weight = weights_own[:5]
    bias_table, forward_gain, inner_weight, outer_weight, project_weight = weights_own[5:]
    both = ("narrow", "wide")
    segs = lengths.shape[1]
    width = tokens.shape[1]
    wide_at = lax.axis_index("wide")
    device = lax.axis_index("narrow") * lax.axis_size("wide") + wide_at
    place = jnp.stack([device, wide_at]).astype(jnp.int32)
    share = attention_gain.shape[0]
    gather = lambda a: lax.all_gather(a, "wide", axis=0, tiled=True)
    small = gather(jnp.concatenate([attention_gain, forward_gain, bias_table])[None])
    gain_one = small[:, :share].reshape(1, width)
    gain_two = small[:, share : 2 * share].reshape(1, width)
    table = jnp.pad(small[:, 2 * share :].reshape(BUCKETS, HEADS), ((0, 0), (0, 4)))
    weights = jnp.stack([gather(w) for w in (query_weight, key_weight, value_weight, output_weight)])
    wu = gather(outer_weight)
    hid, q, k, v, weights = project(place, tokens, gain_one, [weights])
    mixed, inv, p = attend(lengths, table, q, k, v, 0, HEADS // 2)
    hidden, slope, active_sum, message, middle, hid_two, wi = forward(
        place, lengths, tokens, mixed, gain_two, weights, wu, inner_weight.shape[1], [gather(inner_weight)]
    )
    messages = lax.all_gather(message, both, axis=0, tiled=True).reshape(-1, 2, 8, 512)
    messages = messages.transpose(0, 2, 1, 3).reshape(-1, 1024)
    loss, grad_wp, glow_all, grows = contrast_plain(
        place,
        messages[:, :width],
        messages[:, width : width + 1].astype(F32),
        positives.reshape(-1, 1),
        gather(project_weight),
        project_weight.shape[0],
    )
    active_all = lax.all_gather(active_sum[:segs], both, axis=0, tiled=True)
    active_own = lax.dynamic_slice_in_dim(active_all, wide_at * outer_weight.shape[0], outer_weight.shape[0], 1)
    grad_outer = dot_tn(active_own, glow_all.astype(F32))
    glow = jnp.pad(grows.astype(BF16), ((0, 16 - segs), (0, 0)))
    gmid, gm, grad_wi, grad_wo = back(
        lengths, place, glow, grows, gain_two, hid_two, active_sum, wu, slope, wi, middle, mixed, inv, weights, False
    )
    grad_heads, diag = attend_grad(lengths, q, k, v, gm, mixed, p, 0, HEADS // 2)
    grad_tokens = token_grad(tokens, gain_one, gmid, grad_heads, weights)

    def total(grad):
        part = lax.psum_scatter(grad, "wide", scatter_dimension=0, tiled=True)
        return lax.psum(part.astype(F32), "narrow")

    grads = [total(dot_tn(hid, grad).astype(BF16)) for grad in grad_heads] + [total(grad_wo)]
    grad_inner = total(grad_wi)
    table_own = total(table_grad(diag).reshape(lax.axis_size("wide"), -1))[0]
    own_heads = jnp.stack([query_weight, key_weight, value_weight])
    along = jnp.sum(jnp.stack(grads[:3]) * own_heads.astype(F32), (0, 2))
    return (
        hidden,
        grad_tokens,
        loss[:, 0].reshape(1, segs),
        along / attention_gain.astype(F32),
        *grads,
        table_own,
        jnp.sum(grad_inner * inner_weight.astype(F32), 1) / forward_gain.astype(F32),
        grad_inner,
        grad_outer,
        grad_wp,
    )


def solution(mesh):
    ins, outs = layer_specs()
    permuted = (mesh.shape["narrow"], mesh.shape["wide"]) == (4, 8)
    body = local_permuted if permuted else local_plain
    return jax.shard_map(body, mesh=mesh, in_specs=ins, out_specs=outs, check_vma=False)
```
